32 devices in a mesh: gx: 4 (over z), gy: 8 (over y, x, core).
Axes of the slice: x: 2, y: 2, z: 4, core: 2. Of those that a mesh axis runs over, the one named last changes fastest.
Arguments:
- rhs: float32 [2048, 2048], P('gx', 'gy'), may hold values from -6 to 6, as said below
- pressure: float32 [2048, 2048], P('gx', 'gy'), may hold values from -6 to 6
- wet_mask: int32 [2048, 2048], P('gx', 'gy'), may hold values 0 or 1
- bathy_class: int32 [2048, 2048], P('gx', 'gy'), may hold values from 0 to 7
Outputs:
- new_pressure: float32 [2048, 2048], P('gx', 'gy')
- final_residual: float32 [2048, 2048], P('gx', 'gy')
The draws below stay inside these ranges and needn't reach their ends.
Inputs may be any that keep to these rules, and one draw needn't show every extreme that they name: `rhs`: real-valued and rough from cell to cell.
All inputs are finite; a program needn't handle non-finite values. No bound on the sum of `wet_mask` on one device may be relied on, other than what follows from the above.
Results may differ from the reference program's by a relative error of at most 0.0003.
Values sent between devices are 32-bit elements; how exact they have to be, the bound alone decides.
No kernel may reach another device: no remote copies, remote signals or barrier semaphores. Data moves between devices by JAX's collectives and lax.ppermute only.
A program may use at most 128 MiB of HBM per device.

```python
import jax
import jax.numpy as jnp

LEVELS = 4
SWEEPS = 12
NX = 2048
NY = 2048


def draw_rhs(key, part):
    return jnp.clip(jax.random.normal(key, (NX, NY), jnp.float32), -6.0, 6.0)


def touch_ends(values, key, smallest, top_value):
    place = [jax.random.randint(jax.random.fold_in(key, axis), (), 0, length) for axis, length in enumerate(values.shape)]
    longest = values.shape.index(max(values.shape))
    next_to = place[:longest] + [(place[longest] + 1) % values.shape[longest]] + place[longest + 1:]
    return values.at[tuple(place)].set(smallest).at[tuple(next_to)].set(top_value)


def level_of(rng, shape, split, low, largest):
    def one(position, blocks):
        draws = jax.random.uniform(jax.random.fold_in(jax.random.fold_in(rng, 6), position), (blocks,), jnp.float32, low / len(split), largest / len(split))
        return jnp.repeat(jnp.exp(draws), shape[position] // blocks).reshape((-1,) + (1,) * (len(shape) - position - 1))

    factor_of = one(*split[0])
    for cut in split[1:]:
        factor_of = factor_of * one(*cut)
    return factor_of


def normal_values(own_key, extent, spread, limit, split=(), kind=jnp.bfloat16):
    drawn = spread * jax.random.normal(own_key, extent, jnp.float32)
    if split:
        drawn = drawn * level_of(own_key, extent, split, -0.22, 0.18)
    return jnp.clip(drawn, -limit, limit).astype(kind)


def setup_inputs(seed: int = 0) -> dict:
    key_list = jax.random.split(jax.random.key(seed), 5)
    rhs = draw_rhs(jax.random.fold_in(key_list[4], 71), 0)
    pressure = normal_values(key_list[1], (NX, NY), 1.0, 6.0, ((0, 4), (1, 8)), jnp.float32)
    wet_mask = touch_ends((jax.random.randint(key_list[2], (NX, NY), 0, 8) < 7).astype(jnp.int32), jax.random.fold_in(key_list[2], 1), 0, 1)
    bathy_class = touch_ends(jax.random.randint(key_list[3], (NX, NY), 0, 8), jax.random.fold_in(key_list[3], 1), 0, 7).astype(jnp.int32)
    return dict(rhs=rhs, pressure=pressure, wet_mask=wet_mask, bathy_class=bathy_class)


damping = 0.01
relaxation = 0.8


def mean_blocks(field):
    height, width = field.shape
    return field.reshape(height // 2, 2, width // 2, 2).sum(axis=(1, 3)) * 0.25


def padded(field):
    return jnp.pad(field, 1)


def face_couplings(weight_pad, level_scale):
    middle = weight_pad[1:-1, 1:-1]
    to_north = level_scale * jnp.minimum(middle, weight_pad[:-2, 1:-1])
    to_south = level_scale * jnp.minimum(middle, weight_pad[2:, 1:-1])
    to_west = level_scale * jnp.minimum(middle, weight_pad[1:-1, :-2])
    to_east = level_scale * jnp.minimum(middle, weight_pad[1:-1, 2:])
    diagonal = damping + to_north + to_south + to_west + to_east
    return (to_north, to_south, to_west, to_east, diagonal)


def apply_operator(field_pad, coeffs):
    to_north, to_south, to_west, to_east, diagonal = coeffs
    middle = field_pad[1:-1, 1:-1]
    beside = to_north * field_pad[:-2, 1:-1] + to_south * field_pad[2:, 1:-1]
    beside = beside + to_west * field_pad[1:-1, :-2] + to_east * field_pad[1:-1, 2:]
    return diagonal * middle - beside


def jacobi_step(field_pad, source, coeffs):
    middle = field_pad[1:-1, 1:-1]
    return middle + relaxation * (source - apply_operator(field_pad, coeffs)) / coeffs[4]


def prolong(field):
    return jnp.repeat(jnp.repeat(field, 2, axis=0), 2, axis=1)


def reference(rhs, pressure, wet_mask, bathy_class):
    wet_cells = wet_mask.astype(jnp.float32)
    weight = wet_cells * (1.0 + 0.5 * bathy_class.astype(jnp.float32))
    source = wet_cells * rhs
    first_guess = wet_cells * pressure
    level_coeffs = []
    for level in range(LEVELS + 1):
        level_coeffs.append(face_couplings(padded(weight), 0.5 ** level))
        if level < LEVELS:
            weight = mean_blocks(weight)
    sources = [source]
    iterates = []
    iterate = jacobi_step(padded(first_guess), source, level_coeffs[0])
    for level in range(LEVELS):
        if level > 0:
            iterate = relaxation * sources[level] / level_coeffs[level][4]
        iterates.append(iterate)
        residual_now = sources[level] - apply_operator(padded(iterate), level_coeffs[level])
        sources.append(mean_blocks(residual_now))
    current = jnp.zeros_like(sources[LEVELS])
    for sweep_index in range(SWEEPS):
        current = jacobi_step(padded(current), sources[LEVELS], level_coeffs[LEVELS])
    for level in range(LEVELS - 1, -1, -1):
        summed = iterates[level] + prolong(current)
        current = jacobi_step(padded(summed), sources[level], level_coeffs[level])
    final_residual = source - apply_operator(padded(current), level_coeffs[0])
    return current, final_residual
```

```python
import functools

import jax
import jax.numpy as jnp
from jax import lax
from jax.experimental import pallas as pl
from jax.experimental.pallas import tpu as pltpu
from jax.sharding import PartitionSpec as P

LEVELS = 4
SWEEPS = 12

damping = 0.01
relaxation = 0.8

HALO = 24
LANES = 128
GUARD = 8
PIECES = 5
VMEM_LIMIT = 40 * 1024 * 1024
TALL = 16


def lane_of(x):
    return lax.broadcasted_iota(jnp.int32, x.shape, x.ndim - 1)


def roll(x, amount):
    amount %= LANES
    return x if amount == 0 else pltpu.roll(x, amount, x.ndim - 1)


def from_west(tiles, step):
    moved = [roll(t, step) for t in tiles]
    edge = lane_of(tiles[0]) < step
    return [jnp.where(edge, moved[i - 1], moved[i]) for i in range(len(tiles))]


def from_east(tiles, step):
    moved = [roll(t, -step) for t in tiles]
    edge = lane_of(tiles[0]) >= LANES - step
    count = len(tiles)
    return [jnp.where(edge, moved[(i + 1) % count], moved[i]) for i in range(count)]


def lane_pairs(x, step):
    first = (lane_of(x) // step) % 2 == 0
    return x + jnp.where(first, roll(x, -step), roll(x, step))


def chunks_of(rows, largest):
    count = 1
    while rows % count or rows // count > largest or (rows // count) % 2:
        count += 1
    return count, rows // count


def for_chunks(rows, body, largest=112):
    count, size = chunks_of(rows, largest)
    if count == 1:
        body(0, size)
        return

    def step(i, carry):
        body(i * size, size)
        return carry

    lax.fori_loop(0, count, step, 0)


def load(ref, start, size):
    return [ref[t, pl.ds(GUARD + start, size), :] for t in range(3)]


def store(ref, start, size, tiles):
    for t in range(3):
        ref[t, pl.ds(GUARD + start, size), :] = tiles[t]


def clear_guards(ref, rows):
    zeros = jnp.zeros((GUARD, LANES), jnp.float32)
    for t in range(ref.shape[0]):
        ref[t, 0:GUARD, :] = zeros
        ref[t, GUARD + rows : 2 * GUARD + rows, :] = zeros


def operator(mid, north, south, c_west, c_north, c_south, step):
    west = from_west(mid, step)
    flux = [c_west[t] * (mid[t] - west[t]) for t in range(3)]
    out = from_east(flux, step)
    return [
        damping * mid[t]
        + (flux[t] - out[t])
        + (c_north[t] * (mid[t] - north[t]) + c_south[t] * (mid[t] - south[t]))
        for t in range(3)
    ]


def pool_rows(ref, start, size, step):
    half = size // 2
    out = []
    for t in range(3):
        even = ref[t, pl.ds(GUARD + start, half, stride=2), :]
        odd = ref[t, pl.ds(GUARD + start + 1, half, stride=2), :]
        out.append(lane_pairs(even + odd, step))
    return out


def pack_kernel(rhs, pressure, wet, kind, above, below, own_ref, west_ref, east_ref):
    rows = rhs.shape[0]
    total = rows + 2 * HALO
    for t in range(2):
        columns = slice(t * LANES, (t + 1) * LANES)
        is_wet = wet[:, columns].astype(jnp.float32)
        middle = (
            is_wet * rhs[:, columns],
            is_wet * pressure[:, columns],
            is_wet * (1.0 + 0.5 * kind[:, columns].astype(jnp.float32)),
        )
        zeros = jnp.zeros((GUARD, LANES), jnp.float32)
        for k in range(3):
            own_ref[k, t, 0:GUARD, :] = zeros
            own_ref[k, t, GUARD : GUARD + HALO, :] = above[k, :, columns]
            own_ref[k, t, GUARD + HALO : GUARD + HALO + rows, :] = middle[k]
            own_ref[k, t, GUARD + HALO + rows : GUARD + total, :] = below[k, :, columns]
            own_ref[k, t, GUARD + total :, :] = zeros
    piece = total // PIECES
    for k in range(3):
        for tile, first, ref in ((0, 0, west_ref), (1, LANES - HALO, east_ref)):
            packed = jnp.zeros((piece, LANES), jnp.float32)
            for p in range(PIECES):
                part = own_ref[k, tile, GUARD + p * piece : GUARD + (p + 1) * piece, :]
                lane = lane_of(part)
                here = (lane >= p * HALO) & (lane < (p + 1) * HALO)
                packed = jnp.where(here, roll(part, p * HALO - first), packed)
            ref[k] = packed


def down_kernel(own, from_left, from_right, *refs):
    rows = own.shape[2] - 2 * GUARD
    state, coarse_ref = refs[: 4 * LEVELS + 1], refs[4 * LEVELS + 1]
    scratch = refs[4 * LEVELS + 2 :]
    field, weights, sources = scratch[0], scratch[1 : 2 + LEVELS], scratch[2 + LEVELS : 3 + 2 * LEVELS]
    guess, resid = scratch[3 + 2 * LEVELS], scratch[4 + 2 * LEVELS]
    piece = rows // PIECES
    for k, ref in ((0, state[-1]), (1, guess), (2, weights[0])):
        clear_guards(ref, rows)
        for p in range(PIECES):
            span = slice(GUARD + p * piece, GUARD + (p + 1) * piece)
            left, right = from_left[k], from_right[k]
            lane = lane_of(left)
            left = roll(left, LANES - HALO - p * HALO)
            right = roll(right, -p * HALO)
            ref[0, span, :] = own[k, 0, span, :]
            ref[1, span, :] = own[k, 1, span, :]
            ref[2, span, :] = jnp.where(lane < HALO, right, jnp.where(lane >= LANES - HALO, left, 0.0))
    clear_guards(field, rows)
    for level in range(LEVELS):
        step, height = 2**level, rows >> level
        weight, source = weights[level], state[-1] if level == 0 else sources[level]
        c_west_ref, c_north_ref, scale_ref, smooth_ref = state[4 * level : 4 * level + 4]
        clear_guards(c_north_ref, height)
        if level > 0:
            clear_guards(weight, height)
            clear_guards(field, height)

        def first_pass(start, size, level=level, step=step, weight=weight, source=source):
            w = load(weight, start, size)
            w_north = load(weight, start - 1, size)
            w_south = load(weight, start + 1, size)
            w_west = from_west(w, step)
            c_north = [jnp.minimum(a, b) for a, b in zip(w, w_north)]
            c_south = [jnp.minimum(a, b) for a, b in zip(w, w_south)]
            c_west = [jnp.minimum(a, b) for a, b in zip(w, w_west)]
            c_east = from_east(c_west, step)
            scale = [
                relaxation / (damping + c_north[t] + c_south[t] + c_west[t] + c_east[t]) for t in range(3)
            ]
            store(c_north_ref, start, size, c_north)
            store(c_west_ref, start, size, c_west)
            store(scale_ref, start, size, scale)
            b = load(source, start, size)
            if level == 0:
                mid = load(guess, start, size)
                applied = operator(
                    mid, load(guess, start - 1, size), load(guess, start + 1, size), c_west, c_north, c_south, step
                )
                value = [mid[t] + scale[t] * (b[t] - applied[t]) for t in range(3)]
            else:
                value = [scale[t] * b[t] for t in range(3)]
            store(field, start, size, value)
            pooled = pool_rows(weight, start, size, step)
            half = [0.125 * p for p in pooled]
            store(weights[level + 1], start // 2, size // 2, half)

        def second_pass(start, size, level=level, step=step, source=source):
            mid = load(field, start, size)
            applied = operator(
                mid,
                load(field, start - 1, size),
                load(field, start + 1, size),
                load(c_west_ref, start, size),
                load(c_north_ref, start, size),
                load(c_north_ref, start + 1, size),
                step,
            )
            b = load(source, start, size)
            rest = [b[t] - applied[t] for t in range(3)]
            scale = load(scale_ref, start, size)
            store(smooth_ref, start, size, [mid[t] + scale[t] * rest[t] for t in range(3)])
            store(resid, start, size, rest)
            pooled = pool_rows(resid, start, size, step) if level < LEVELS - 1 else None
            if pooled is not None:
                store(sources[level + 1], start // 2, size // 2, [0.25 * p for p in pooled])

        for_chunks(height, first_pass)
        for_chunks(height, second_pass)
    level = LEVELS - 1
    step, halo = 2**level, HALO >> level
    coarse_rows = ((rows >> level) - 2 * halo) // 2
    packed = jnp.zeros((coarse_rows, LANES), jnp.float32)
    lane = lane_of(packed)
    per_tile = LANES // 2**LEVELS
    pooled_b = pool_rows(resid, halo, 2 * coarse_rows, step)
    pooled_w = pool_rows(weights[level], halo, 2 * coarse_rows, step)
    index = (lane % per_tile) * 2**LEVELS
    place = lane // per_tile
    for group, (values, factor) in enumerate(((pooled_b, 0.25), (pooled_w, 0.125))):
        for t in range(2):
            taken = jnp.take_along_axis(factor * values[t], index, axis=1)
            packed = jnp.where(place == 2 * group + t, taken, packed)
    coarse_ref[...] = packed


def up_kernel(left, own, right, *refs):
    state = refs[: 4 * LEVELS + 1]
    out_ref, resid_ref = refs[4 * LEVELS + 1 : 4 * LEVELS + 3]
    prolonged = refs[4 * LEVELS + 3 : 5 * LEVELS + 3]
    final = refs[5 * LEVELS + 3]
    rows = out_ref.shape[0] + 2 * HALO
    width = out_ref.shape[1] >> LEVELS

    lane = lane_of(own)
    here, beside = lane < 2 * width, lane < 3 * width
    b = jnp.where(lane < width, left[...], jnp.where(here, roll(own[...], width), roll(right[...], 2 * width)))
    w = jnp.where(lane < width, roll(left[...], -width), jnp.where(here, own[...], roll(right[...], width)))
    b, w = jnp.where(beside, b, 0.0), jnp.where(beside, w, 0.0)

    def north_of(x):
        return pltpu.roll(x, 1, 0)

    def south_of(x):
        return pltpu.roll(x, x.shape[0] - 1, 0)

    c_west = jnp.minimum(w, roll(w, 1))
    c_north = jnp.minimum(w, north_of(w))
    c_east, c_south = roll(c_west, -1), south_of(c_north)
    scale = relaxation / (damping + c_north + c_south + c_west + c_east)
    first = scale * b

    def sweep(_, e):
        applied = (
            damping * e
            + (c_west * (e - roll(e, 1)) + c_east * (e - roll(e, -1)))
            + (c_north * (e - north_of(e)) + c_south * (e - south_of(e)))
        )
        return e + (first - scale * applied)

    e = lax.fori_loop(0, SWEEPS - 1, sweep, first)

    level = LEVELS - 1
    halo = HALO >> level
    height = rows >> level
    pe = prolonged[level]
    coarse_rows = (height - 2 * halo) // 2
    picked = e[TALL - 8 : TALL + coarse_rows + 8]
    lane = lane_of(picked)
    for t in range(3):
        group = (lane + t * LANES) // 2**LEVELS
        if t == 2:
            group = jnp.where(lane < LANES // 2, group, group - 3 * LANES // 2**LEVELS)
        taken = jnp.take_along_axis(picked, jnp.clip(group + width, 0, LANES - 1), axis=1)[7 : 7 + coarse_rows + 2]
        pe[t, 0 : 2 * GUARD, :] = jnp.zeros((2 * GUARD, LANES), jnp.float32)
        pe[t, height : height + 2 * GUARD, :] = jnp.zeros((2 * GUARD, LANES), jnp.float32)
        pe[t, pl.ds(GUARD + halo - 2, coarse_rows + 2, stride=2), :] = taken
        pe[t, pl.ds(GUARD + halo - 1, coarse_rows + 2, stride=2), :] = taken

    for level in range(LEVELS - 1, -1, -1):
        step, height = 2**level, rows >> level
        c_west_ref, c_north_ref, scale_ref, smooth_ref = state[4 * level : 4 * level + 4]
        pe = prolonged[level]
        if level < LEVELS - 1:
            clear_guards(pe, height)

        def climb(start, size, level=level, step=step, pe=pe):
            mid = load(pe, start, size)
            applied = operator(
                mid,
                load(pe, start - 1, size),
                load(pe, start + 1, size),
                load(c_west_ref, start, size),
                load(c_north_ref, start, size),
                load(c_north_ref, start + 1, size),
                step,
            )
            smooth, scale = load(smooth_ref, start, size), load(scale_ref, start, size)
            value = [smooth[t] + (mid[t] - scale[t] * applied[t]) for t in range(3)]
            if level == 0:
                store(final, start, size, value)
            else:
                above = prolonged[level - 1]
                for t in range(3):
                    above[t, pl.ds(GUARD + 2 * start, size, stride=2), :] = value[t]
                    above[t, pl.ds(GUARD + 2 * start + 1, size, stride=2), :] = value[t]

        for_chunks(height, climb)

    c_west_ref, c_north_ref = state[0], state[1]

    def last(start, size):
        base = start + HALO
        mid = load(final, base, size)
        applied = operator(
            mid,
            load(final, base - 1, size),
            load(final, base + 1, size),
            load(c_west_ref, base, size),
            load(c_north_ref, base, size),
            load(c_north_ref, base + 1, size),
            1,
        )
        b = load(state[-1], base, size)
        for t in range(2):
            out_ref[pl.ds(start, size), t * LANES : (t + 1) * LANES] = mid[t]
            resid_ref[pl.ds(start, size), t * LANES : (t + 1) * LANES] = b[t] - applied[t]

    for_chunks(out_ref.shape[0], last, 128)


def level_shape(rows, level):
    return (3, (rows >> level) + 2 * GUARD, LANES)


def call(kernel, out_shape, scratch, flops, moved):
    return pl.pallas_call(
        kernel,
        out_shape=out_shape,
        scratch_shapes=scratch,
        compiler_params=pltpu.CompilerParams(vmem_limit_bytes=VMEM_LIMIT),
        cost_estimate=pl.CostEstimate(flops=flops, bytes_accessed=moved, transcendentals=0),
    )


def exchange(first, last, axis):
    count = lax.axis_size(axis)
    up = [(i, i + 1) for i in range(count - 1)]
    down = [(j, i) for i, j in up]
    return lax.ppermute(last, axis, up), lax.ppermute(first, axis, down)


def local(rhs, pressure, wet_mask, bathy_class):
    rows, columns = rhs.shape
    total = rows + 2 * HALO
    f32 = functools.partial(jax.ShapeDtypeStruct, dtype=jnp.float32)

    def edge(start):
        cut = [lax.slice_in_dim(x, start, start + HALO, axis=0) for x in (rhs, pressure, wet_mask, bathy_class)]
        wet = cut[2].astype(jnp.float32)
        return jnp.stack((wet * cut[0], wet * cut[1], wet * (1.0 + 0.5 * cut[3].astype(jnp.float32))))

    above, below = exchange(edge(0), edge(rows - HALO), "gx")
    piece = total // PIECES
    own, west, east = call(
        pack_kernel,
        (f32((3, 2, total + 2 * GUARD, LANES)), f32((3, piece, LANES)), f32((3, piece, LANES))),
        (),
        10 * rows * columns,
        24 * rows * columns,
    )(rhs, pressure, wet_mask, bathy_class, above, below)
    from_left, from_right = exchange(west, east, "gy")

    state_shapes = [f32(level_shape(total, level)) for level in range(LEVELS) for _ in range(4)]
    state_shapes.append(f32(level_shape(total, 0)))
    vmem = lambda level: pltpu.VMEM(level_shape(total, level), jnp.float32)
    scratch = [vmem(0)]
    scratch += [vmem(level) for level in range(LEVELS + 1)]
    scratch += [vmem(level) if level else pltpu.VMEM((8, LANES), jnp.float32) for level in range(LEVELS + 1)]
    scratch += [vmem(0), vmem(0)]
    coarse_rows = rows >> LEVELS
    *state, coarse = call(
        down_kernel,
        (*state_shapes, f32((coarse_rows, LANES))),
        scratch,
        100 * rows * columns,
        40 * rows * columns,
    )(own, from_left, from_right)

    north, south = exchange(coarse[:TALL], coarse[coarse_rows - TALL :], "gx")
    tall = jnp.concatenate((north, coarse, south), axis=0)
    left, right = exchange(tall, tall, "gy")
    scratch = [vmem(level) for level in range(LEVELS)] + [vmem(0)]
    return call(
        up_kernel,
        (f32((rows, columns)), f32((rows, columns))),
        scratch,
        60 * rows * columns,
        40 * rows * columns,
    )(left, tall, right, *state)


def solution(mesh):
    placed = (P("gx", "gy"), P("gx", "gy"), P("gx", "gy"), P("gx", "gy"))
    return jax.shard_map(
        local, mesh=mesh, in_specs=placed, out_specs=(P("gx", "gy"), P("gx", "gy")), check_vma=False
    )
```

```python
import functools

import jax
import jax.numpy as jnp
from jax import lax
from jax.experimental import pallas as pl
from jax.experimental.pallas import tpu as pltpu
from jax.sharding import PartitionSpec as P

LEVELS = 4
SWEEPS = 12

damping = 0.01
relaxation = 0.8

HALO = 24
LANES = 128
GUARD = 8
PIECES = 5
VMEM_LIMIT = 40 * 1024 * 1024
TALL = 16


def lane_of(x):
    return lax.broadcasted_iota(jnp.int32, x.shape, x.ndim - 1)


def roll(x, amount):
    amount %= LANES
    return x if amount == 0 else pltpu.roll(x, amount, x.ndim - 1)


def from_west(tiles, step):
    moved = [roll(t, step) for t in tiles]
    edge = lane_of(tiles[0]) < step
    return [jnp.where(edge, moved[i - 1], moved[i]) for i in range(len(tiles))]


def from_east(tiles, step):
    moved = [roll(t, -step) for t in tiles]
    edge = lane_of(tiles[0]) >= LANES - step
    count = len(tiles)
    return [jnp.where(edge, moved[(i + 1) % count], moved[i]) for i in range(count)]


def lane_pairs(x, step):
    first = (lane_of(x) // step) % 2 == 0
    return x + jnp.where(first, roll(x, -step), roll(x, step))


def chunks_of(rows, largest):
    count = 1
    while rows % count or rows // count > largest or (rows // count) % 2:
        count += 1
    return count, rows // count


def for_chunks(rows, body, largest=112):
    count, size = chunks_of(rows, largest)
    if count == 1:
        body(0, size)
        return

    def step(i, carry):
        body(i * size, size)
        return carry

    lax.fori_loop(0, count, step, 0)


def load(ref, start, size):
    return [ref[t, pl.ds(GUARD + start, size), :] for t in range(3)]


def store(ref, start, size, tiles):
    for t in range(3):
        ref[t, pl.ds(GUARD + start, size), :] = tiles[t]


def clear_guards(ref, rows):
    zeros = jnp.zeros((GUARD, LANES), jnp.float32)
    for t in range(ref.shape[0]):
        ref[t, 0:GUARD, :] = zeros
        ref[t, GUARD + rows : 2 * GUARD + rows, :] = zeros


def operator(mid, north, south, c_west, c_north, c_south, step):
    west = from_west(mid, step)
    flux = [c_west[t] * (mid[t] - west[t]) for t in range(3)]
    out = from_east(flux, step)
    return [
        damping * mid[t]
        + (flux[t] - out[t])
        + (c_north[t] * (mid[t] - north[t]) + c_south[t] * (mid[t] - south[t]))
        for t in range(3)
    ]


def pool_rows(ref, start, size, step):
    half = size // 2
    out = []
    for t in range(3):
        even = ref[t, pl.ds(GUARD + start, half, stride=2), :]
        odd = ref[t, pl.ds(GUARD + start + 1, half, stride=2), :]
        out.append(lane_pairs(even + odd, step))
    return out


def load_kernel(rhs_hbm, pressure_hbm, wet_hbm, kind_hbm, own_ref, rhs, pressure, wet, kind, sems):
    rows = rhs.shape[0]
    parts = 4
    size = rows // parts
    pairs = ((rhs_hbm, rhs), (pressure_hbm, pressure), (wet_hbm, wet), (kind_hbm, kind))
    copies = []
    for p in range(parts):
        span = pl.ds(p * size, size)
        copies.append([
            pltpu.make_async_copy(src.at[span], dst.at[span], sems.at[4 * p + k]) for k, (src, dst) in enumerate(pairs)
        ])
        for copy in copies[-1]:
            copy.start()
    for p in range(parts):
        for copy in copies[p]:
            copy.wait()
        for t in range(2):
            here = (slice(p * size, (p + 1) * size), slice(t * LANES, (t + 1) * LANES))
            is_wet = wet[here].astype(jnp.float32)
            span = slice(GUARD + HALO + p * size, GUARD + HALO + (p + 1) * size)
            own_ref[0, t, span, :] = is_wet * rhs[here]
            own_ref[1, t, span, :] = is_wet * pressure[here]
            own_ref[2, t, span, :] = is_wet * (1.0 + 0.5 * kind[here].astype(jnp.float32))


def pack_kernel(_, above, below, own_ref, west_ref, east_ref):
    total = own_ref.shape[2] - 2 * GUARD
    zeros = jnp.zeros((GUARD, LANES), jnp.float32)
    for k in range(3):
        for t in range(2):
            columns = slice(t * LANES, (t + 1) * LANES)
            own_ref[k, t, 0:GUARD, :] = zeros
            own_ref[k, t, GUARD : GUARD + HALO, :] = above[k, :, columns]
            own_ref[k, t, GUARD + total - HALO : GUARD + total, :] = below[k, :, columns]
            own_ref[k, t, GUARD + total :, :] = zeros
    piece = total // PIECES
    for k in range(3):
        for tile, first, ref in ((0, 0, west_ref), (1, LANES - HALO, east_ref)):
            packed = jnp.zeros((piece, LANES), jnp.float32)
            for p in range(PIECES):
                part = own_ref[k, tile, GUARD + p * piece : GUARD + (p + 1) * piece, :]
                lane = lane_of(part)
                here = (lane >= p * HALO) & (lane < (p + 1) * HALO)
                packed = jnp.where(here, roll(part, p * HALO - first), packed)
            ref[k] = packed


def down_kernel(own, from_left, from_right, *refs):
    rows = own.shape[2] - 2 * GUARD
    state, coarse_ref = refs[: 4 * LEVELS + 1], refs[4 * LEVELS + 1]
    scratch = refs[4 * LEVELS + 2 :]
    field, weights, sources = scratch[0], scratch[1 : 2 + LEVELS], scratch[2 + LEVELS : 3 + 2 * LEVELS]
    guess, resid = scratch[3 + 2 * LEVELS], scratch[4 + 2 * LEVELS]
    piece = rows // PIECES
    for k, ref in ((0, state[-1]), (1, guess), (2, weights[0])):
        clear_guards(ref, rows)
        for p in range(PIECES):
            span = slice(GUARD + p * piece, GUARD + (p + 1) * piece)
            left, right = from_left[k], from_right[k]
            lane = lane_of(left)
            left = roll(left, LANES - HALO - p * HALO)
            right = roll(right, -p * HALO)
            ref[0, span, :] = own[k, 0, span, :]
            ref[1, span, :] = own[k, 1, span, :]
            ref[2, span, :] = jnp.where(lane < HALO, right, jnp.where(lane >= LANES - HALO, left, 0.0))
    clear_guards(field, rows)
    for level in range(LEVELS):
        step, height = 2**level, rows >> level
        weight, source = weights[level], state[-1] if level == 0 else sources[level]
        c_west_ref, c_north_ref, scale_ref, smooth_ref = state[4 * level : 4 * level + 4]
        clear_guards(c_north_ref, height)
        if level > 0:
            clear_guards(weight, height)
            clear_guards(field, height)

        def first_pass(start, size, level=level, step=step, weight=weight, source=source):
            w = load(weight, start, size)
            w_north = load(weight, start - 1, size)
            w_south = load(weight, start + 1, size)
            w_west = from_west(w, step)
            c_north = [jnp.minimum(a, b) for a, b in zip(w, w_north)]
            c_south = [jnp.minimum(a, b) for a, b in zip(w, w_south)]
            c_west = [jnp.minimum(a, b) for a, b in zip(w, w_west)]
            c_east = from_east(c_west, step)
            scale = [
                relaxation / (damping + c_north[t] + c_south[t] + c_west[t] + c_east[t]) for t in range(3)
            ]
            store(c_north_ref, start, size, c_north)
            store(c_west_ref, start, size, c_west)
            store(scale_ref, start, size, scale)
            b = load(source, start, size)
            if level == 0:
                mid = load(guess, start, size)
                applied = operator(
                    mid, load(guess, start - 1, size), load(guess, start + 1, size), c_west, c_north, c_south, step
                )
                value = [mid[t] + scale[t] * (b[t] - applied[t]) for t in range(3)]
            else:
                value = [scale[t] * b[t] for t in range(3)]
            store(field, start, size, value)
            pooled = pool_rows(weight, start, size, step)
            half = [0.125 * p for p in pooled]
            store(weights[level + 1], start // 2, size // 2, half)

        def second_pass(start, size, level=level, step=step, source=source):
            mid = load(field, start, size)
            applied = operator(
                mid,
                load(field, start - 1, size),
                load(field, start + 1, size),
                load(c_west_ref, start, size),
                load(c_north_ref, start, size),
                load(c_north_ref, start + 1, size),
                step,
            )
            b = load(source, start, size)
            rest = [b[t] - applied[t] for t in range(3)]
            scale = load(scale_ref, start, size)
            store(smooth_ref, start, size, [mid[t] + scale[t] * rest[t] for t in range(3)])
            store(resid, start, size, rest)
            pooled = pool_rows(resid, start, size, step) if level < LEVELS - 1 else None
            if pooled is not None:
                store(sources[level + 1], start // 2, size // 2, [0.25 * p for p in pooled])

        for_chunks(height, first_pass)
        for_chunks(height, second_pass)
    level = LEVELS - 1
    step, halo = 2**level, HALO >> level
    coarse_rows = ((rows >> level) - 2 * halo) // 2
    dense = jnp.zeros((8, LANES), jnp.float32)
    lane = lane_of(dense)
    per_tile = LANES // 2**LEVELS
    pooled_b = pool_rows(resid, halo, 2 * coarse_rows, step)
    pooled_w = pool_rows(weights[level], halo, 2 * coarse_rows, step)
    index = (lane % per_tile) * 2**LEVELS
    place = lane // per_tile
    for g in range(coarse_rows // 8):
        for group, (values, factor) in enumerate(((pooled_b, 0.25), (pooled_w, 0.125))):
            for t in range(2):
                taken = jnp.take_along_axis(factor * values[t][8 * g : 8 * g + 8], index, axis=1)
                dense = jnp.where(place == 4 * g + 2 * group + t, taken, dense)
    coarse_ref[...] = dense


def up_kernel(all_ref, *refs):
    state = refs[: 4 * LEVELS + 1]
    out_ref, resid_ref = refs[4 * LEVELS + 1 : 4 * LEVELS + 3]
    prolonged = refs[4 * LEVELS + 3 : 5 * LEVELS + 3]
    final = refs[5 * LEVELS + 3]
    rows = out_ref.shape[0] + 2 * HALO
    width = out_ref.shape[1] >> LEVELS
    groups = (out_ref.shape[0] >> LEVELS) // 8

    x, nx = lax.axis_index("gx"), lax.axis_size("gx")
    y, ny = lax.axis_index("gy"), lax.axis_size("gy")
    tiles = []
    for dx in (-1, 0, 1):
        for dy in (-1, 0, 1):
            inside = (x + dx >= 0) & (x + dx < nx) & (y + dy >= 0) & (y + dy < ny)
            tile = all_ref[jnp.where(inside, (x + dx) * ny + y + dy, 0)]
            tiles.append(jnp.where(inside, tile, 0.0))
    lane = lane_of(tiles[0])
    blocks = [(0, g) for g in range(groups - TALL // 8, groups)]
    blocks += [(1, g) for g in range(groups)] + [(2, g) for g in range(TALL // 8)]
    b, w = [], []
    for band, g in blocks:
        b_rows = w_rows = jnp.zeros_like(tiles[0])
        for side in range(3):
            tile = tiles[3 * band + side]
            here = (lane >= side * width) & (lane < (side + 1) * width)
            b_rows = jnp.where(here, roll(tile, (side - 2 * g) * width), b_rows)
            w_rows = jnp.where(here, roll(tile, (side - 2 * g - 1) * width), w_rows)
        b.append(b_rows)
        w.append(w_rows)
    b, w = jnp.concatenate(b, axis=0), jnp.concatenate(w, axis=0)

    def north_of(x):
        return pltpu.roll(x, 1, 0)

    def south_of(x):
        return pltpu.roll(x, x.shape[0] - 1, 0)

    c_west = jnp.minimum(w, roll(w, 1))
    c_north = jnp.minimum(w, north_of(w))
    c_east, c_south = roll(c_west, -1), south_of(c_north)
    scale = relaxation / (damping + c_north + c_south + c_west + c_east)
    first = scale * b

    def sweep(_, e):
        applied = (
            damping * e
            + (c_west * (e - roll(e, 1)) + c_east * (e - roll(e, -1)))
            + (c_north * (e - north_of(e)) + c_south * (e - south_of(e)))
        )
        return e + (first - scale * applied)

    e = lax.fori_loop(0, SWEEPS - 1, sweep, first)

    level = LEVELS - 1
    halo = HALO >> level
    height = rows >> level
    pe = prolonged[level]
    coarse_rows = (height - 2 * halo) // 2
    picked = e[TALL - 8 : TALL + coarse_rows + 8]
    lane = lane_of(picked)
    for t in range(3):
        group = (lane + t * LANES) // 2**LEVELS
        if t == 2:
            group = jnp.where(lane < LANES // 2, group, group - 3 * LANES // 2**LEVELS)
        taken = jnp.take_along_axis(picked, jnp.clip(group + width, 0, LANES - 1), axis=1)[7 : 7 + coarse_rows + 2]
        pe[t, 0 : 2 * GUARD, :] = jnp.zeros((2 * GUARD, LANES), jnp.float32)
        pe[t, height : height + 2 * GUARD, :] = jnp.zeros((2 * GUARD, LANES), jnp.float32)
        pe[t, pl.ds(GUARD + halo - 2, coarse_rows + 2, stride=2), :] = taken
        pe[t, pl.ds(GUARD + halo - 1, coarse_rows + 2, stride=2), :] = taken

    for level in range(LEVELS - 1, -1, -1):
        step, height = 2**level, rows >> level
        c_west_ref, c_north_ref, scale_ref, smooth_ref = state[4 * level : 4 * level + 4]
        pe = prolonged[level]
        if level < LEVELS - 1:
            clear_guards(pe, height)

        def climb(start, size, level=level, step=step, pe=pe):
            mid = load(pe, start, size)
            applied = operator(
                mid,
                load(pe, start - 1, size),
                load(pe, start + 1, size),
                load(c_west_ref, start, size),
                load(c_north_ref, start, size),
                load(c_north_ref, start + 1, size),
                step,
            )
            smooth, scale = load(smooth_ref, start, size), load(scale_ref, start, size)
            value = [smooth[t] + (mid[t] - scale[t] * applied[t]) for t in range(3)]
            if level == 0:
                store(final, start, size, value)
            else:
                above = prolonged[level - 1]
                for t in range(3):
                    above[t, pl.ds(GUARD + 2 * start, size, stride=2), :] = value[t]
                    above[t, pl.ds(GUARD + 2 * start + 1, size, stride=2), :] = value[t]

        for_chunks(height, climb)

    c_west_ref, c_north_ref = state[0], state[1]

    def last(start, size):
        base = start + HALO
        mid = load(final, base, size)
        applied = operator(
            mid,
            load(final, base - 1, size),
            load(final, base + 1, size),
            load(c_west_ref, base, size),
            load(c_north_ref, base, size),
            load(c_north_ref, base + 1, size),
            1,
        )
        b = load(state[-1], base, size)
        for t in range(2):
            out_ref[pl.ds(start, size), t * LANES : (t + 1) * LANES] = mid[t]
            resid_ref[pl.ds(start, size), t * LANES : (t + 1) * LANES] = b[t] - applied[t]

    for_chunks(out_ref.shape[0], last, 128)


def level_shape(rows, level):
    return (3, (rows >> level) + 2 * GUARD, LANES)


def call(kernel, out_shape, scratch, flops, moved, limit=VMEM_LIMIT, **more):
    return pl.pallas_call(
        kernel,
        out_shape=out_shape,
        scratch_shapes=scratch,
        compiler_params=pltpu.CompilerParams(vmem_limit_bytes=limit),
        cost_estimate=pl.CostEstimate(flops=flops, bytes_accessed=moved, transcendentals=0),
        **more,
    )


def exchange(first, last, axis):
    count = lax.axis_size(axis)
    up = [(i, i + 1) for i in range(count - 1)]
    down = [(j, i) for i, j in up]
    return lax.ppermute(last, axis, up), lax.ppermute(first, axis, down)


def local(rhs, pressure, wet_mask, bathy_class):
    rows, columns = rhs.shape
    total = rows + 2 * HALO
    f32 = functools.partial(jax.ShapeDtypeStruct, dtype=jnp.float32)

    def edge(start):
        cut = [lax.slice_in_dim(x, start, start + HALO, axis=0) for x in (rhs, pressure, wet_mask, bathy_class)]
        wet = cut[2].astype(jnp.float32)
        return jnp.stack((wet * cut[0], wet * cut[1], wet * (1.0 + 0.5 * cut[3].astype(jnp.float32))))

    above, below = exchange(edge(0), edge(rows - HALO), "gx")
    piece = total // PIECES
    own_shape = f32((3, 2, total + 2 * GUARD, LANES))
    given = (rhs, pressure, wet_mask, bathy_class)
    own = call(
        load_kernel,
        own_shape,
        [pltpu.VMEM(x.shape, x.dtype) for x in given] + [pltpu.SemaphoreType.DMA((16,))],
        5 * rows * columns,
        16 * rows * columns,
        in_specs=[pl.BlockSpec(memory_space=pltpu.HBM)] * 4,
    )(*given)
    own, west, east = call(
        pack_kernel,
        (own_shape, f32((3, piece, LANES)), f32((3, piece, LANES))),
        (),
        10 * HALO * rows,
        10 * HALO * rows,
        input_output_aliases={0: 0},
    )(own, above, below)
    from_left, from_right = exchange(west, east, "gy")

    state_shapes = [f32(level_shape(total, level)) for level in range(LEVELS) for _ in range(4)]
    state_shapes.append(f32(level_shape(total, 0)))
    vmem = lambda level: pltpu.VMEM(level_shape(total, level), jnp.float32)
    scratch = [vmem(0)]
    scratch += [vmem(level) for level in range(LEVELS + 1)]
    scratch += [vmem(level) if level else pltpu.VMEM((8, LANES), jnp.float32) for level in range(LEVELS + 1)]
    scratch += [vmem(0), vmem(0)]
    coarse_rows = rows >> LEVELS
    *state, coarse = call(
        down_kernel,
        (*state_shapes, f32((8, LANES))),
        scratch,
        100 * rows * columns,
        40 * rows * columns,
    )(own, from_left, from_right)

    gathered = lax.all_gather(coarse, ("gx", "gy"))
    scratch = [vmem(level) for level in range(LEVELS)] + [vmem(0)]
    return call(
        up_kernel,
        (f32((rows, columns)), f32((rows, columns))),
        scratch,
        60 * rows * columns,
        40 * rows * columns,
    )(gathered, *state)


def solution(mesh):
    placed = (P("gx", "gy"), P("gx", "gy"), P("gx", "gy"), P("gx", "gy"))
    return jax.shard_map(
        local, mesh=mesh, in_specs=placed, out_specs=(P("gx", "gy"), P("gx", "gy")), check_vma=False
    )
```

```python
import functools

import jax
import jax.numpy as jnp
from jax import lax
from jax.experimental import pallas as pl
from jax.experimental.pallas import tpu as pltpu
from jax.sharding import PartitionSpec as P

LEVELS = 4
SWEEPS = 12

damping = 0.01
relaxation = 0.8

HALO = 24
LANES = 128
GUARD = 8
PIECES = 5
VMEM_LIMIT = 40 * 1024 * 1024
TALL = 16


def lane_of(x):
    return lax.broadcasted_iota(jnp.int32, x.shape, x.ndim - 1)


def roll(x, amount):
    amount %= LANES
    return x if amount == 0 else pltpu.roll(x, amount, x.ndim - 1)


def from_west(tiles, step):
    moved = [roll(t, step) for t in tiles]
    edge = lane_of(tiles[0]) < step
    return [jnp.where(edge, moved[i - 1], moved[i]) for i in range(len(tiles))]


def from_east(tiles, step):
    moved = [roll(t, -step) for t in tiles]
    edge = lane_of(tiles[0]) >= LANES - step
    count = len(tiles)
    return [jnp.where(edge, moved[(i + 1) % count], moved[i]) for i in range(count)]


def lane_pairs(x, step):
    first = (lane_of(x) // step) % 2 == 0
    return x + jnp.where(first, roll(x, -step), roll(x, step))


def chunks_of(rows, largest):
    count = 1
    while rows % count or rows // count > largest or (rows // count) % 2:
        count += 1
    return count, rows // count


def for_chunks(rows, body, largest=112):
    count, size = chunks_of(rows, largest)
    if count == 1:
        body(0, size)
        return

    def step(i, carry):
        body(i * size, size)
        return carry

    lax.fori_loop(0, count, step, 0)


def load(ref, start, size):
    return [ref[t, pl.ds(GUARD + start, size), :] for t in range(3)]


def store(ref, start, size, tiles):
    for t in range(3):
        ref[t, pl.ds(GUARD + start, size), :] = tiles[t]


def clear_guards(ref, rows):
    zeros = jnp.zeros((GUARD, LANES), jnp.float32)
    for t in range(ref.shape[0]):
        ref[t, 0:GUARD, :] = zeros
        ref[t, GUARD + rows : 2 * GUARD + rows, :] = zeros


def operator(mid, north, south, c_west, c_north, c_south, step):
    west = from_west(mid, step)
    flux = [c_west[t] * (mid[t] - west[t]) for t in range(3)]
    out = from_east(flux, step)
    return [
        damping * mid[t]
        + (flux[t] - out[t])
        + (c_north[t] * (mid[t] - north[t]) + c_south[t] * (mid[t] - south[t]))
        for t in range(3)
    ]


def pool_rows(ref, start, size, step):
    half = size // 2
    out = []
    for t in range(3):
        even = ref[t, pl.ds(GUARD + start, half, stride=2), :]
        odd = ref[t, pl.ds(GUARD + start + 1, half, stride=2), :]
        out.append(lane_pairs(even + odd, step))
    return out


def load_kernel(rhs_hbm, pressure_hbm, wet_hbm, kind_hbm, own_ref, rhs, pressure, wet, kind, sems):
    rows = rhs.shape[0]
    parts = 4
    size = rows // parts
    pairs = ((rhs_hbm, rhs), (pressure_hbm, pressure), (wet_hbm, wet), (kind_hbm, kind))
    copies = []
    for p in range(parts):
        span = pl.ds(p * size, size)
        copies.append([
            pltpu.make_async_copy(src.at[span], dst.at[span], sems.at[4 * p + k]) for k, (src, dst) in enumerate(pairs)
        ])
        for copy in copies[-1]:
            copy.start()
    for p in range(parts):
        for copy in copies[p]:
            copy.wait()
        for t in range(2):
            here = (slice(p * size, (p + 1) * size), slice(t * LANES, (t + 1) * LANES))
            is_wet = wet[here].astype(jnp.float32)
            span = slice(GUARD + HALO + p * size, GUARD + HALO + (p + 1) * size)
            own_ref[0, t, span, :] = is_wet * rhs[here]
            own_ref[1, t, span, :] = is_wet * pressure[here]
            own_ref[2, t, span, :] = is_wet * (1.0 + 0.5 * kind[here].astype(jnp.float32))


def pack_kernel(_, above, below, own_ref, west_ref, east_ref):
    total = own_ref.shape[2] - 2 * GUARD
    zeros = jnp.zeros((GUARD, LANES), jnp.float32)
    for k in range(3):
        for t in range(2):
            columns = slice(t * LANES, (t + 1) * LANES)
            own_ref[k, t, 0:GUARD, :] = zeros
            own_ref[k, t, GUARD : GUARD + HALO, :] = above[k, :, columns]
            own_ref[k, t, GUARD + total - HALO : GUARD + total, :] = below[k, :, columns]
            own_ref[k, t, GUARD + total :, :] = zeros
    piece = total // PIECES
    for k in range(3):
        for tile, first, ref in ((0, 0, west_ref), (1, LANES - HALO, east_ref)):
            packed = jnp.zeros((piece, LANES), jnp.float32)
            for p in range(PIECES):
                part = own_ref[k, tile, GUARD + p * piece : GUARD + (p + 1) * piece, :]
                lane = lane_of(part)
                here = (lane >= p * HALO) & (lane < (p + 1) * HALO)
                packed = jnp.where(here, roll(part, p * HALO - first), packed)
            ref[k] = packed


def down_kernel(own, from_left, from_right, *refs):
    rows = own.shape[2] - 2 * GUARD
    state, coarse_ref = refs[: 4 * LEVELS + 1], refs[4 * LEVELS + 1]
    scratch = refs[4 * LEVELS + 2 :]
    field, weights, sources = scratch[0], scratch[1 : 2 + LEVELS], scratch[2 + LEVELS : 3 + 2 * LEVELS]
    guess, resid = scratch[3 + 2 * LEVELS], scratch[4 + 2 * LEVELS]
    piece = rows // PIECES
    for k, ref in ((0, state[-1]), (1, guess), (2, weights[0])):
        clear_guards(ref, rows)
        for p in range(PIECES):
            span = slice(GUARD + p * piece, GUARD + (p + 1) * piece)
            left, right = from_left[k], from_right[k]
            lane = lane_of(left)
            left = roll(left, LANES - HALO - p * HALO)
            right = roll(right, -p * HALO)
            ref[0, span, :] = own[k, 0, span, :]
            ref[1, span, :] = own[k, 1, span, :]
            ref[2, span, :] = jnp.where(lane < HALO, right, jnp.where(lane >= LANES - HALO, left, 0.0))
    clear_guards(field, rows)
    for level in range(LEVELS):
        step, height = 2**level, rows >> level
        weight, source = weights[level], state[-1] if level == 0 else sources[level]
        c_west_ref, c_north_ref, scale_ref, smooth_ref = state[4 * level : 4 * level + 4]
        clear_guards(c_north_ref, height)
        if level > 0:
            clear_guards(weight, height)
            clear_guards(field, height)

        def first_pass(start, size, level=level, step=step, weight=weight, source=source):
            w = load(weight, start, size)
            w_north = load(weight, start - 1, size)
            w_south = load(weight, start + 1, size)
            w_west = from_west(w, step)
            c_north = [jnp.minimum(a, b) for a, b in zip(w, w_north)]
            c_south = [jnp.minimum(a, b) for a, b in zip(w, w_south)]
            c_west = [jnp.minimum(a, b) for a, b in zip(w, w_west)]
            c_east = from_east(c_west, step)
            scale = [
                relaxation / (damping + c_north[t] + c_south[t] + c_west[t] + c_east[t]) for t in range(3)
            ]
            store(c_north_ref, start, size, c_north)
            store(c_west_ref, start, size, c_west)
            store(scale_ref, start, size, scale)
            b = load(source, start, size)
            if level == 0:
                mid = load(guess, start, size)
                applied = operator(
                    mid, load(guess, start - 1, size), load(guess, start + 1, size), c_west, c_north, c_south, step
                )
                value = [mid[t] + scale[t] * (b[t] - applied[t]) for t in range(3)]
            else:
                value = [scale[t] * b[t] for t in range(3)]
            store(field, start, size, value)
            pooled = pool_rows(weight, start, size, step)
            half = [0.125 * p for p in pooled]
            store(weights[level + 1], start // 2, size // 2, half)

        def second_pass(start, size, level=level, step=step, source=source):
            mid = load(field, start, size)
            applied = operator(
                mid,
                load(field, start - 1, size),
                load(field, start + 1, size),
                load(c_west_ref, start, size),
                load(c_north_ref, start, size),
                load(c_north_ref, start + 1, size),
                step,
            )
            b = load(source, start, size)
            rest = [b[t] - applied[t] for t in range(3)]
            scale = load(scale_ref, start, size)
            store(smooth_ref, start, size, [mid[t] + scale[t] * rest[t] for t in range(3)])
            store(resid, start, size, rest)
            pooled = pool_rows(resid, start, size, step) if level < LEVELS - 1 else None
            if pooled is not None:
                store(sources[level + 1], start // 2, size // 2, [0.25 * p for p in pooled])

        for_chunks(height, first_pass)
        for_chunks(height, second_pass)
    level = LEVELS - 1
    step, halo = 2**level, HALO >> level
    coarse_rows = ((rows >> level) - 2 * halo) // 2
    dense = jnp.zeros((8, LANES), jnp.float32)
    lane = lane_of(dense)
    per_tile = LANES // 2**LEVELS
    pooled_b = pool_rows(resid, halo, 2 * coarse_rows, step)
    pooled_w = pool_rows(weights[level], halo, 2 * coarse_rows, step)
    index = (lane % per_tile) * 2**LEVELS
    place = lane // per_tile
    for g in range(coarse_rows // 8):
        for group, (values, factor) in enumerate(((pooled_b, 0.25), (pooled_w, 0.125))):
            for t in range(2):
                taken = jnp.take_along_axis(factor * values[t][8 * g : 8 * g + 8], index, axis=1)
                dense = jnp.where(place == 4 * g + 2 * group + t, taken, dense)
    coarse_ref[...] = jnp.broadcast_to(dense[None], coarse_ref.shape)


def up_kernel(all_ref, *refs):
    state = refs[: 4 * LEVELS + 1]
    out_ref, resid_ref = refs[4 * LEVELS + 1 : 4 * LEVELS + 3]
    prolonged = refs[4 * LEVELS + 3 : 5 * LEVELS + 3]
    final = refs[5 * LEVELS + 3]
    rows = out_ref.shape[0] + 2 * HALO
    width = out_ref.shape[1] >> LEVELS
    groups = (out_ref.shape[0] >> LEVELS) // 8

    x, nx = lax.axis_index("gx"), lax.axis_size("gx")
    y, ny = lax.axis_index("gy"), lax.axis_size("gy")
    tiles = []
    for dx in (-1, 0, 1):
        for dy in (-1, 0, 1):
            inside = (x + dx >= 0) & (x + dx < nx) & (y + dy >= 0) & (y + dy < ny)
            tile = all_ref[jnp.where(inside, (x + dx) * ny + y + dy, 0)]
            tiles.append(jnp.where(inside, tile, 0.0))
    lane = lane_of(tiles[0])
    blocks = [(0, g) for g in range(groups - TALL // 8, groups)]
    blocks += [(1, g) for g in range(groups)] + [(2, g) for g in range(TALL // 8)]
    b, w = [], []
    for band, g in blocks:
        b_rows = w_rows = jnp.zeros_like(tiles[0])
        for side in range(3):
            tile = tiles[3 * band + side]
            here = (lane >= side * width) & (lane < (side + 1) * width)
            b_rows = jnp.where(here, roll(tile, (side - 2 * g) * width), b_rows)
            w_rows = jnp.where(here, roll(tile, (side - 2 * g - 1) * width), w_rows)
        b.append(b_rows)
        w.append(w_rows)
    b, w = jnp.concatenate(b, axis=0), jnp.concatenate(w, axis=0)

    def north_of(x):
        return pltpu.roll(x, 1, 0)

    def south_of(x):
        return pltpu.roll(x, x.shape[0] - 1, 0)

    c_west = jnp.minimum(w, roll(w, 1))
    c_north = jnp.minimum(w, north_of(w))
    c_east, c_south = roll(c_west, -1), south_of(c_north)
    scale = relaxation / (damping + c_north + c_south + c_west + c_east)
    first = scale * b

    def sweep(_, e):
        applied = (
            damping * e
            + (c_west * (e - roll(e, 1)) + c_east * (e - roll(e, -1)))
            + (c_north * (e - north_of(e)) + c_south * (e - south_of(e)))
        )
        return e + (first - scale * applied)

    e = lax.fori_loop(0, SWEEPS - 1, sweep, first)

    level = LEVELS - 1
    halo = HALO >> level
    height = rows >> level
    pe = prolonged[level]
    coarse_rows = (height - 2 * halo) // 2
    picked = e[TALL - 8 : TALL + coarse_rows + 8]
    lane = lane_of(picked)
    for t in range(3):
        group = (lane + t * LANES) // 2**LEVELS
        if t == 2:
            group = jnp.where(lane < LANES // 2, group, group - 3 * LANES // 2**LEVELS)
        taken = jnp.take_along_axis(picked, jnp.clip(group + width, 0, LANES - 1), axis=1)[7 : 7 + coarse_rows + 2]
        pe[t, 0 : 2 * GUARD, :] = jnp.zeros((2 * GUARD, LANES), jnp.float32)
        pe[t, height : height + 2 * GUARD, :] = jnp.zeros((2 * GUARD, LANES), jnp.float32)
        pe[t, pl.ds(GUARD + halo - 2, coarse_rows + 2, stride=2), :] = taken
        pe[t, pl.ds(GUARD + halo - 1, coarse_rows + 2, stride=2), :] = taken

    for level in range(LEVELS - 1, -1, -1):
        step, height = 2**level, rows >> level
        c_west_ref, c_north_ref, scale_ref, smooth_ref = state[4 * level : 4 * level + 4]
        pe = prolonged[level]
        if level < LEVELS - 1:
            clear_guards(pe, height)

        def climb(start, size, level=level, step=step, pe=pe):
            mid = load(pe, start, size)
            applied = operator(
                mid,
                load(pe, start - 1, size),
                load(pe, start + 1, size),
                load(c_west_ref, start, size),
                load(c_north_ref, start, size),
                load(c_north_ref, start + 1, size),
                step,
            )
            smooth, scale = load(smooth_ref, start, size), load(scale_ref, start, size)
            value = [smooth[t] + (mid[t] - scale[t] * applied[t]) for t in range(3)]
            if level == 0:
                store(final, start, size, value)
            else:
                above = prolonged[level - 1]
                for t in range(3):
                    above[t, pl.ds(GUARD + 2 * start, size, stride=2), :] = value[t]
                    above[t, pl.ds(GUARD + 2 * start + 1, size, stride=2), :] = value[t]

        for_chunks(height, climb)

    c_west_ref, c_north_ref = state[0], state[1]

    def last(start, size):
        base = start + HALO
        mid = load(final, base, size)
        applied = operator(
            mid,
            load(final, base - 1, size),
            load(final, base + 1, size),
            load(c_west_ref, base, size),
            load(c_north_ref, base, size),
            load(c_north_ref, base + 1, size),
            1,
        )
        b = load(state[-1], base, size)
        for t in range(2):
            out_ref[pl.ds(start, size), t * LANES : (t + 1) * LANES] = mid[t]
            resid_ref[pl.ds(start, size), t * LANES : (t + 1) * LANES] = b[t] - applied[t]

    for_chunks(out_ref.shape[0], last, 128)


def level_shape(rows, level):
    return (3, (rows >> level) + 2 * GUARD, LANES)


def call(kernel, out_shape, scratch, flops, moved, limit=VMEM_LIMIT, **more):
    return pl.pallas_call(
        kernel,
        out_shape=out_shape,
        scratch_shapes=scratch,
        compiler_params=pltpu.CompilerParams(vmem_limit_bytes=limit),
        cost_estimate=pl.CostEstimate(flops=flops, bytes_accessed=moved, transcendentals=0),
        **more,
    )


def exchange(first, last, axis):
    count = lax.axis_size(axis)
    up = [(i, i + 1) for i in range(count - 1)]
    down = [(j, i) for i, j in up]
    return lax.ppermute(last, axis, up), lax.ppermute(first, axis, down)


def local(rhs, pressure, wet_mask, bathy_class):
    rows, columns = rhs.shape
    total = rows + 2 * HALO
    f32 = functools.partial(jax.ShapeDtypeStruct, dtype=jnp.float32)

    def edge(start):
        cut = [lax.slice_in_dim(x, start, start + HALO, axis=0) for x in (rhs, pressure, wet_mask, bathy_class)]
        wet = cut[2].astype(jnp.float32)
        return jnp.stack((wet * cut[0], wet * cut[1], wet * (1.0 + 0.5 * cut[3].astype(jnp.float32))))

    above, below = exchange(edge(0), edge(rows - HALO), "gx")
    piece = total // PIECES
    own_shape = f32((3, 2, total + 2 * GUARD, LANES))
    given = (rhs, pressure, wet_mask, bathy_class)
    own = call(
        load_kernel,
        own_shape,
        [pltpu.VMEM(x.shape, x.dtype) for x in given] + [pltpu.SemaphoreType.DMA((16,))],
        5 * rows * columns,
        16 * rows * columns,
        in_specs=[pl.BlockSpec(memory_space=pltpu.HBM)] * 4,
    )(*given)
    own, west, east = call(
        pack_kernel,
        (own_shape, f32((3, piece, LANES)), f32((3, piece, LANES))),
        (),
        10 * HALO * rows,
        10 * HALO * rows,
        input_output_aliases={0: 0},
    )(own, above, below)
    from_left, from_right = exchange(west, east, "gy")

    state_shapes = [f32(level_shape(total, level)) for level in range(LEVELS) for _ in range(4)]
    state_shapes.append(f32(level_shape(total, 0)))
    vmem = lambda level: pltpu.VMEM(level_shape(total, level), jnp.float32)
    scratch = [vmem(0)]
    scratch += [vmem(level) for level in range(LEVELS + 1)]
    scratch += [vmem(level) if level else pltpu.VMEM((8, LANES), jnp.float32) for level in range(LEVELS + 1)]
    scratch += [vmem(0), vmem(0)]
    devices = lax.axis_size("gx") * lax.axis_size("gy")
    *state, coarse = call(
        down_kernel,
        (*state_shapes, f32((devices, 8, LANES))),
        scratch,
        100 * rows * columns,
        40 * rows * columns,
    )(own, from_left, from_right)

    gathered = lax.all_to_all(coarse, ("gx", "gy"), 0, 0)
    scratch = [vmem(level) for level in range(LEVELS)] + [vmem(0)]
    return call(
        up_kernel,
        (f32((rows, columns)), f32((rows, columns))),
        scratch,
        60 * rows * columns,
        40 * rows * columns,
    )(gathered, *state)


def solution(mesh):
    placed = (P("gx", "gy"), P("gx", "gy"), P("gx", "gy"), P("gx", "gy"))
    return jax.shard_map(
        local, mesh=mesh, in_specs=placed, out_specs=(P("gx", "gy"), P("gx", "gy")), check_vma=False
    )
```

```python
import functools

import jax
import jax.numpy as jnp
from jax import lax
from jax.experimental import pallas as pl
from jax.experimental.pallas import tpu as pltpu
from jax.sharding import PartitionSpec as P

LEVELS = 4
SWEEPS = 12

damping = 0.01
relaxation = 0.8

HALO = 24
LANES = 128
GUARD = 8
PIECES = 5
VMEM_LIMIT = 40 * 1024 * 1024
TALL = 16


def lane_of(x):
    return lax.broadcasted_iota(jnp.int32, x.shape, x.ndim - 1)


def roll(x, amount):
    amount %= LANES
    return x if amount == 0 else pltpu.roll(x, amount, x.ndim - 1)


def from_west(tiles, step):
    moved = [roll(t, step) for t in tiles]
    edge = lane_of(tiles[0]) < step
    return [jnp.where(edge, moved[i - 1], moved[i]) for i in range(len(tiles))]


def from_east(tiles, step):
    moved = [roll(t, -step) for t in tiles]
    edge = lane_of(tiles[0]) >= LANES - step
    count = len(tiles)
    return [jnp.where(edge, moved[(i + 1) % count], moved[i]) for i in range(count)]


def lane_pairs(x, step):
    first = (lane_of(x) // step) % 2 == 0
    return x + jnp.where(first, roll(x, -step), roll(x, step))


def chunks_of(rows, largest):
    count = 1
    while rows % count or rows // count > largest or (rows // count) % 2:
        count += 1
    return count, rows // count


def for_chunks(rows, body, largest=112):
    count, size = chunks_of(rows, largest)
    if count == 1:
        body(0, size)
        return

    def step(i, carry):
        body(i * size, size)
        return carry

    lax.fori_loop(0, count, step, 0)


def load(ref, start, size):
    return [ref[t, pl.ds(GUARD + start, size), :] for t in range(3)]


def store(ref, start, size, tiles):
    for t in range(3):
        ref[t, pl.ds(GUARD + start, size), :] = tiles[t]


def clear_guards(ref, rows):
    zeros = jnp.zeros((GUARD, LANES), jnp.float32)
    for t in range(ref.shape[0]):
        ref[t, 0:GUARD, :] = zeros
        ref[t, GUARD + rows : 2 * GUARD + rows, :] = zeros


def operator(mid, north, south, c_west, c_north, c_south, step):
    west = from_west(mid, step)
    flux = [c_west[t] * (mid[t] - west[t]) for t in range(3)]
    out = from_east(flux, step)
    return [
        damping * mid[t]
        + (flux[t] - out[t])
        + (c_north[t] * (mid[t] - north[t]) + c_south[t] * (mid[t] - south[t]))
        for t in range(3)
    ]


def pool_rows(ref, start, size, step):
    half = size // 2
    out = []
    for t in range(3):
        even = ref[t, pl.ds(GUARD + start, half, stride=2), :]
        odd = ref[t, pl.ds(GUARD + start + 1, half, stride=2), :]
        out.append(lane_pairs(even + odd, step))
    return out


def load_kernel(rhs, pressure, wet, kind, own_ref):
    rows = rhs.shape[0]
    span = slice(GUARD + HALO, GUARD + HALO + rows)
    for t in range(2):
        columns = slice(t * LANES, (t + 1) * LANES)
        is_wet = wet[:, columns].astype(jnp.float32)
        own_ref[0, t, span, :] = is_wet * rhs[:, columns]
        own_ref[1, t, span, :] = is_wet * pressure[:, columns]
        own_ref[2, t, span, :] = is_wet * (1.0 + 0.5 * kind[:, columns].astype(jnp.float32))


def pack_kernel(_, above, below, own_ref, cross_ref, pair_ref):
    even = lax.axis_index("gy") % 2 == 0
    total = own_ref.shape[2] - 2 * GUARD
    zeros = jnp.zeros((GUARD, LANES), jnp.float32)
    for k in range(3):
        for t in range(2):
            columns = slice(t * LANES, (t + 1) * LANES)
            own_ref[k, t, 0:GUARD, :] = zeros
            own_ref[k, t, GUARD : GUARD + HALO, :] = above[k, :, columns]
            own_ref[k, t, GUARD + total - HALO : GUARD + total, :] = below[k, :, columns]
            own_ref[k, t, GUARD + total :, :] = zeros
    piece = total // PIECES
    for k in range(3):
        sides = []
        for tile, first in ((0, 0), (1, LANES - HALO)):
            packed = jnp.zeros((piece, LANES), jnp.float32)
            for p in range(PIECES):
                part = own_ref[k, tile, GUARD + p * piece : GUARD + (p + 1) * piece, :]
                lane = lane_of(part)
                here = (lane >= p * HALO) & (lane < (p + 1) * HALO)
                packed = jnp.where(here, roll(part, p * HALO - first), packed)
            sides.append(packed)
        west, east = sides
        cross_ref[k] = jnp.where(even, west, east)
        pair_ref[k] = jnp.where(even, east, west)


def down_kernel(own, from_cross, from_pair, *refs):
    even = lax.axis_index("gy") % 2 == 0
    rows = own.shape[2] - 2 * GUARD
    state, coarse_ref = refs[: 4 * LEVELS + 1], refs[4 * LEVELS + 1]
    scratch = refs[4 * LEVELS + 2 :]
    field, weights, sources = scratch[0], scratch[1 : 2 + LEVELS], scratch[2 + LEVELS : 3 + 2 * LEVELS]
    guess, resid = scratch[3 + 2 * LEVELS], scratch[4 + 2 * LEVELS]
    piece = rows // PIECES
    for k, ref in ((0, state[-1]), (1, guess), (2, weights[0])):
        clear_guards(ref, rows)
        for p in range(PIECES):
            span = slice(GUARD + p * piece, GUARD + (p + 1) * piece)
            left = jnp.where(even, from_cross[k], from_pair[k])
            right = jnp.where(even, from_pair[k], from_cross[k])
            lane = lane_of(left)
            left = roll(left, LANES - HALO - p * HALO)
            right = roll(right, -p * HALO)
            ref[0, span, :] = own[k, 0, span, :]
            ref[1, span, :] = own[k, 1, span, :]
            ref[2, span, :] = jnp.where(lane < HALO, right, jnp.where(lane >= LANES - HALO, left, 0.0))
    clear_guards(field, rows)
    for level in range(LEVELS):
        step, height = 2**level, rows >> level
        weight, source = weights[level], state[-1] if level == 0 else sources[level]
        c_west_ref, c_north_ref, scale_ref, smooth_ref = state[4 * level : 4 * level + 4]
        clear_guards(c_north_ref, height)
        if level > 0:
            clear_guards(weight, height)
            clear_guards(field, height)

        def first_pass(start, size, level=level, step=step, weight=weight, source=source):
            w = load(weight, start, size)
            w_north = load(weight, start - 1, size)
            w_south = load(weight, start + 1, size)
            w_west = from_west(w, step)
            c_north = [jnp.minimum(a, b) for a, b in zip(w, w_north)]
            c_south = [jnp.minimum(a, b) for a, b in zip(w, w_south)]
            c_west = [jnp.minimum(a, b) for a, b in zip(w, w_west)]
            c_east = from_east(c_west, step)
            scale = [
                relaxation / (damping + c_north[t] + c_south[t] + c_west[t] + c_east[t]) for t in range(3)
            ]
            store(c_north_ref, start, size, c_north)
            store(c_west_ref, start, size, c_west)
            store(scale_ref, start, size, scale)
            b = load(source, start, size)
            if level == 0:
                mid = load(guess, start, size)
                applied = operator(
                    mid, load(guess, start - 1, size), load(guess, start + 1, size), c_west, c_north, c_south, step
                )
                value = [mid[t] + scale[t] * (b[t] - applied[t]) for t in range(3)]
            else:
                value = [scale[t] * b[t] for t in range(3)]
            store(field, start, size, value)
            pooled = pool_rows(weight, start, size, step)
            half = [0.125 * p for p in pooled]
            store(weights[level + 1], start // 2, size // 2, half)

        def second_pass(start, size, level=level, step=step, source=source):
            mid = load(field, start, size)
            applied = operator(
                mid,
                load(field, start - 1, size),
                load(field, start + 1, size),
                load(c_west_ref, start, size),
                load(c_north_ref, start, size),
                load(c_north_ref, start + 1, size),
                step,
            )
            b = load(source, start, size)
            rest = [b[t] - applied[t] for t in range(3)]
            scale = load(scale_ref, start, size)
            store(smooth_ref, start, size, [mid[t] + scale[t] * rest[t] for t in range(3)])
            store(resid, start, size, rest)
            pooled = pool_rows(resid, start, size, step) if level < LEVELS - 1 else None
            if pooled is not None:
                store(sources[level + 1], start // 2, size // 2, [0.25 * p for p in pooled])

        for_chunks(height, first_pass)
        for_chunks(height, second_pass)
    level = LEVELS - 1
    step, halo = 2**level, HALO >> level
    coarse_rows = ((rows >> level) - 2 * halo) // 2
    dense = jnp.zeros((8, LANES), jnp.float32)
    lane = lane_of(dense)
    per_tile = LANES // 2**LEVELS
    pooled_b = pool_rows(resid, halo, 2 * coarse_rows, step)
    pooled_w = pool_rows(weights[level], halo, 2 * coarse_rows, step)
    index = (lane % per_tile) * 2**LEVELS
    place = lane // per_tile
    for g in range(coarse_rows // 8):
        for group, (values, factor) in enumerate(((pooled_b, 0.25), (pooled_w, 0.125))):
            for t in range(2):
                taken = jnp.take_along_axis(factor * values[t][8 * g : 8 * g + 8], index, axis=1)
                dense = jnp.where(place == 4 * g + 2 * group + t, taken, dense)
    coarse_ref[...] = jnp.broadcast_to(dense[None], coarse_ref.shape)


def up_kernel(all_ref, *refs):
    state = refs[: 4 * LEVELS + 1]
    out_ref, resid_ref = refs[4 * LEVELS + 1 : 4 * LEVELS + 3]
    prolonged = refs[4 * LEVELS + 3 : 5 * LEVELS + 3]
    final = refs[5 * LEVELS + 3]
    rows = out_ref.shape[0] + 2 * HALO
    width = out_ref.shape[1] >> LEVELS
    groups = (out_ref.shape[0] >> LEVELS) // 8

    x, nx = lax.axis_index("gx"), lax.axis_size("gx")
    y, ny = lax.axis_index("gy"), lax.axis_size("gy")
    tiles = []
    for dx in (-1, 0, 1):
        for dy in (-1, 0, 1):
            inside = (x + dx >= 0) & (x + dx < nx) & (y + dy >= 0) & (y + dy < ny)
            tile = all_ref[jnp.where(inside, (x + dx) * ny + y + dy, 0)]
            tiles.append(jnp.where(inside, tile, 0.0))
    lane = lane_of(tiles[0])
    blocks = [(0, g) for g in range(groups - TALL // 8, groups)]
    blocks += [(1, g) for g in range(groups)] + [(2, g) for g in range(TALL // 8)]
    b, w = [], []
    for band, g in blocks:
        b_rows = w_rows = jnp.zeros_like(tiles[0])
        for side in range(3):
            tile = tiles[3 * band + side]
            here = (lane >= side * width) & (lane < (side + 1) * width)
            b_rows = jnp.where(here, roll(tile, (side - 2 * g) * width), b_rows)
            w_rows = jnp.where(here, roll(tile, (side - 2 * g - 1) * width), w_rows)
        b.append(b_rows)
        w.append(w_rows)
    b, w = jnp.concatenate(b, axis=0), jnp.concatenate(w, axis=0)

    def north_of(x):
        return pltpu.roll(x, 1, 0)

    def south_of(x):
        return pltpu.roll(x, x.shape[0] - 1, 0)

    c_west = jnp.minimum(w, roll(w, 1))
    c_north = jnp.minimum(w, north_of(w))
    c_east, c_south = roll(c_west, -1), south_of(c_north)
    scale = relaxation / (damping + c_north + c_south + c_west + c_east)
    first = scale * b

    def sweep(_, e):
        applied = (
            damping * e
            + (c_west * (e - roll(e, 1)) + c_east * (e - roll(e, -1)))
            + (c_north * (e - north_of(e)) + c_south * (e - south_of(e)))
        )
        return e + (first - scale * applied)

    e = lax.fori_loop(0, SWEEPS - 1, sweep, first)

    level = LEVELS - 1
    halo = HALO >> level
    height = rows >> level
    pe = prolonged[level]
    coarse_rows = (height - 2 * halo) // 2
    picked = e[TALL - 8 : TALL + coarse_rows + 8]
    lane = lane_of(picked)
    for t in range(3):
        group = (lane + t * LANES) // 2**LEVELS
        if t == 2:
            group = jnp.where(lane < LANES // 2, group, group - 3 * LANES // 2**LEVELS)
        taken = jnp.take_along_axis(picked, jnp.clip(group + width, 0, LANES - 1), axis=1)[7 : 7 + coarse_rows + 2]
        pe[t, 0 : 2 * GUARD, :] = jnp.zeros((2 * GUARD, LANES), jnp.float32)
        pe[t, height : height + 2 * GUARD, :] = jnp.zeros((2 * GUARD, LANES), jnp.float32)
        pe[t, pl.ds(GUARD + halo - 2, coarse_rows + 2, stride=2), :] = taken
        pe[t, pl.ds(GUARD + halo - 1, coarse_rows + 2, stride=2), :] = taken

    for level in range(LEVELS - 1, -1, -1):
        step, height = 2**level, rows >> level
        c_west_ref, c_north_ref, scale_ref, smooth_ref = state[4 * level : 4 * level + 4]
        pe = prolonged[level]
        if level < LEVELS - 1:
            clear_guards(pe, height)

        def climb(start, size, level=level, step=step, pe=pe):
            mid = load(pe, start, size)
            applied = operator(
                mid,
                load(pe, start - 1, size),
                load(pe, start + 1, size),
                load(c_west_ref, start, size),
                load(c_north_ref, start, size),
                load(c_north_ref, start + 1, size),
                step,
            )
            smooth, scale = load(smooth_ref, start, size), load(scale_ref, start, size)
            value = [smooth[t] + (mid[t] - scale[t] * applied[t]) for t in range(3)]
            if level == 0:
                store(final, start, size, value)
            else:
                above = prolonged[level - 1]
                for t in range(3):
                    above[t, pl.ds(GUARD + 2 * start, size, stride=2), :] = value[t]
                    above[t, pl.ds(GUARD + 2 * start + 1, size, stride=2), :] = value[t]

        for_chunks(height, climb)

    c_west_ref, c_north_ref = state[0], state[1]

    def last(start, size):
        base = start + HALO
        mid = load(final, base, size)
        applied = operator(
            mid,
            load(final, base - 1, size),
            load(final, base + 1, size),
            load(c_west_ref, base, size),
            load(c_north_ref, base, size),
            load(c_north_ref, base + 1, size),
            1,
        )
        b = load(state[-1], base, size)
        for t in range(2):
            out_ref[pl.ds(start, size), t * LANES : (t + 1) * LANES] = mid[t]
            resid_ref[pl.ds(start, size), t * LANES : (t + 1) * LANES] = b[t] - applied[t]

    for_chunks(out_ref.shape[0], last, 128)


def level_shape(rows, level):
    return (3, (rows >> level) + 2 * GUARD, LANES)


def call(kernel, out_shape, scratch, flops, moved, limit=VMEM_LIMIT, **more):
    return pl.pallas_call(
        kernel,
        out_shape=out_shape,
        scratch_shapes=scratch,
        compiler_params=pltpu.CompilerParams(vmem_limit_bytes=limit),
        cost_estimate=pl.CostEstimate(flops=flops, bytes_accessed=moved, transcendentals=0),
        **more,
    )


def exchange(first, last, axis):
    count = lax.axis_size(axis)
    up = [(i, i + 1) for i in range(count - 1)]
    down = [(j, i) for i, j in up]
    return lax.ppermute(last, axis, up), lax.ppermute(first, axis, down)


def swap(x, axis, first):
    pairs = [(i, i + 1) for i in range(first, lax.axis_size(axis) - 1, 2)]
    return lax.ppermute(x, axis, pairs + [(j, i) for i, j in pairs])


def local(rhs, pressure, wet_mask, bathy_class):
    rows, columns = rhs.shape
    total = rows + 2 * HALO
    f32 = functools.partial(jax.ShapeDtypeStruct, dtype=jnp.float32)

    def edge(start):
        cut = [lax.slice_in_dim(x, start, start + HALO, axis=0) for x in (rhs, pressure, wet_mask, bathy_class)]
        wet = cut[2].astype(jnp.float32)
        return jnp.stack((wet * cut[0], wet * cut[1], wet * (1.0 + 0.5 * cut[3].astype(jnp.float32))))

    above, below = exchange(edge(0), edge(rows - HALO), "gx")
    piece = total // PIECES
    own_shape = f32((3, 2, total + 2 * GUARD, LANES))
    given = (rhs, pressure, wet_mask, bathy_class)
    own = call(
        load_kernel,
        own_shape,
        (),
        5 * rows * columns,
        16 * rows * columns,
    )(*given)
    own, to_cross, to_pair = call(
        pack_kernel,
        (own_shape, f32((3, piece, LANES)), f32((3, piece, LANES))),
        (),
        10 * HALO * rows,
        10 * HALO * rows,
        input_output_aliases={0: 0},
    )(own, above, below)
    from_cross = swap(to_cross, "gy", 1)
    from_pair = swap(to_pair, "gy", 0)

    state_shapes = [f32(level_shape(total, level)) for level in range(LEVELS) for _ in range(4)]
    state_shapes.append(f32(level_shape(total, 0)))
    vmem = lambda level: pltpu.VMEM(level_shape(total, level), jnp.float32)
    scratch = [vmem(0)]
    scratch += [vmem(level) for level in range(LEVELS + 1)]
    scratch += [vmem(level) if level else pltpu.VMEM((8, LANES), jnp.float32) for level in range(LEVELS + 1)]
    scratch += [vmem(0), vmem(0)]
    devices = lax.axis_size("gx") * lax.axis_size("gy")
    *state, coarse = call(
        down_kernel,
        (*state_shapes, f32((devices, 8, LANES))),
        scratch,
        100 * rows * columns,
        40 * rows * columns,
    )(own, from_cross, from_pair)

    gathered = lax.all_to_all(coarse, ("gx", "gy"), 0, 0)
    scratch = [vmem(level) for level in range(LEVELS)] + [vmem(0)]
    return call(
        up_kernel,
        (f32((rows, columns)), f32((rows, columns))),
        scratch,
        60 * rows * columns,
        40 * rows * columns,
    )(gathered, *state)


def solution(mesh):
    placed = (P("gx", "gy"), P("gx", "gy"), P("gx", "gy"), P("gx", "gy"))
    return jax.shard_map(
        local, mesh=mesh, in_specs=placed, out_specs=(P("gx", "gy"), P("gx", "gy")), check_vma=False
    )
```

```python
import jax
import jax.numpy as jnp
from jax import lax
from jax.experimental import pallas as pl
from jax.experimental.pallas import tpu as pltpu
from jax.sharding import PartitionSpec as P

LEVELS = 4
SWEEPS = 12

damping = 0.01
relaxation = 0.8

HALO = 24
LANES = 128
INNER = LANES // 2 - HALO
GUARD = 8
PIECES = 5
TALL = 16
VMEM_LIMIT = 40 * 1024 * 1024


def lane_of(x):
    return lax.broadcasted_iota(jnp.int32, x.shape, x.ndim - 1)


def roll(x, amount):
    amount %= LANES
    return x if amount == 0 else pltpu.roll(x, amount, x.ndim - 1)


def from_west(tiles, step):
    moved = [roll(t, step) for t in tiles]
    if len(tiles) == 1:
        return moved
    edge = lane_of(tiles[0]) < step
    return [jnp.where(edge, moved[i - 1], moved[i]) for i in range(len(tiles))]


def from_east(tiles, step):
    moved = [roll(t, -step) for t in tiles]
    count = len(tiles)
    if count == 1:
        return moved
    edge = lane_of(tiles[0]) >= LANES - step
    return [jnp.where(edge, moved[(i + 1) % count], moved[i]) for i in range(count)]


def lane_pairs(x, step):
    first = (lane_of(x) // step) % 2 == 0
    return x + jnp.where(first, roll(x, -step), roll(x, step))


def for_chunks(rows, body, largest):
    sizes = [size for size in range(8, largest + 1, 8) if rows % size == 0]
    if rows <= largest or not sizes:
        body(0, rows)
        return

    def step(i, carry):
        body(i * sizes[-1], sizes[-1])
        return carry

    lax.fori_loop(0, rows // sizes[-1], step, 0)


def load(ref, start, size):
    return [ref[t, pl.ds(GUARD + start, size), :] for t in range(ref.shape[0])]


def store(ref, start, size, tiles):
    for t, tile in enumerate(tiles):
        ref[t, pl.ds(GUARD + start, size), :] = tile


def store_twice(ref, start, size, tiles):
    for t, tile in enumerate(tiles):
        ref[t, pl.ds(GUARD + 2 * start, size, stride=2), :] = tile
        ref[t, pl.ds(GUARD + 2 * start + 1, size, stride=2), :] = tile


def clear_guards(ref, rows):
    zeros = jnp.zeros((GUARD, LANES), jnp.float32)
    for t in range(ref.shape[0]):
        ref[t, 0:GUARD, :] = zeros
        ref[t, GUARD + rows : 2 * GUARD + rows, :] = zeros


def operator(mid, north, south, c_west, c_north, c_south, step):
    west = from_west(mid, step)
    tiles = range(len(mid))
    flux = [c_west[t] * (mid[t] - west[t]) for t in tiles]
    out = from_east(flux, step)
    return [
        damping * mid[t]
        + (flux[t] - out[t])
        + (c_north[t] * (mid[t] - north[t]) + c_south[t] * (mid[t] - south[t]))
        for t in tiles
    ]


def applied_to(ref, coeffs, start, size, step):
    c_west_ref, c_north_ref = coeffs
    mid = load(ref, start, size)
    north, south = load(ref, start - 1, size), load(ref, start + 1, size)
    c_west, c_north = load(c_west_ref, start, size), load(c_north_ref, start, size)
    return mid, operator(mid, north, south, c_west, c_north, load(c_north_ref, start + 1, size), step)


def pool_rows(ref, start, size, step):
    out = []
    for t in range(ref.shape[0]):
        even = ref[t, pl.ds(GUARD + start, size // 2, stride=2), :]
        odd = ref[t, pl.ds(GUARD + start + 1, size // 2, stride=2), :]
        out.append(lane_pairs(even + odd, step))
    return out


def descend(level, height, weight, source, guess, state, field, resid, next_weight, next_source, largest):
    step = 2**level
    c_west_ref, c_north_ref, scale_ref, smooth_ref = state
    for ref in (weight, field, c_north_ref):
        clear_guards(ref, height)

    def first_pass(start, size):
        w, w_north, w_south = (load(weight, start + k, size) for k in (0, -1, 1))
        c_north = [jnp.minimum(a, b) for a, b in zip(w, w_north)]
        c_south = [jnp.minimum(a, b) for a, b in zip(w, w_south)]
        c_west = [jnp.minimum(a, b) for a, b in zip(w, from_west(w, step))]
        c_east = from_east(c_west, step)
        scale = [
            relaxation / (damping + c_north[t] + c_south[t] + c_west[t] + c_east[t]) for t in range(len(w))
        ]
        store(c_north_ref, start, size, c_north)
        store(c_west_ref, start, size, c_west)
        store(scale_ref, start, size, scale)
        value = load(source, start, size)
        if guess is not None:
            mid, north, south = (load(guess, start + k, size) for k in (0, -1, 1))
            applied = operator(mid, north, south, c_west, c_north, c_south, step)
            value = [value[t] - applied[t] for t in range(len(w))]
        value = [scale[t] * value[t] for t in range(len(w))]
        if guess is not None:
            value = [mid[t] + value[t] for t in range(len(w))]
        store(field, start, size, value)
        if next_weight is not None:
            pooled = [0.125 * p for p in pool_rows(weight, start, size, step)]
            store(next_weight, start // 2, size // 2, pooled)

    def second_pass(start, size):
        mid, applied = applied_to(field, (c_west_ref, c_north_ref), start, size, step)
        b, scale = load(source, start, size), load(scale_ref, start, size)
        rest = [b[t] - applied[t] for t in range(len(b))]
        store(smooth_ref, start, size, [mid[t] + scale[t] * rest[t] for t in range(len(b))])
        store(resid, start, size, rest)
        if next_source is not None:
            pooled = [0.25 * p for p in pool_rows(resid, start, size, step)]
            store(next_source, start // 2, size // 2, pooled)

    for_chunks(height, first_pass, largest)
    for_chunks(height, second_pass, largest)


def descend_all(rows, sources, guess, weights, states, field, resid, largest):
    for level in range(LEVELS - 1):
        descend(
            level,
            rows >> level,
            weights[level],
            sources[level],
            guess if level == 0 else None,
            states[4 * level : 4 * level + 4],
            field,
            resid,
            weights[level + 1],
            sources[level + 1],
            largest,
        )


def pack_kernel(source, guess, weight, first_rows, second_rows, own_source, own_guess, own_weight, cross_ref, pair_ref):
    rows = source.shape[0]
    total = rows + 2 * HALO
    even_x, even_y = lax.axis_index("gx") % 2 == 0, lax.axis_index("gy") % 2 == 0
    own = (own_source, own_guess, own_weight)
    for k, block in enumerate((source, guess, weight)):
        clear_guards(own[k], total)
        above = jnp.where(even_x, first_rows[k], second_rows[k])
        below = jnp.where(even_x, second_rows[k], first_rows[k])
        for t in range(2):
            columns = slice(t * LANES, (t + 1) * LANES)
            own[k][t, GUARD : GUARD + HALO, :] = above[:, columns]
            own[k][t, GUARD + HALO : GUARD + HALO + rows, :] = block[:, columns]
            own[k][t, GUARD + HALO + rows : GUARD + total, :] = below[:, columns]
    piece = total // PIECES
    for k in range(3):
        sides = []
        for tile, first in ((0, 0), (1, LANES - HALO)):
            packed = jnp.zeros((piece, LANES), jnp.float32)
            for p in range(PIECES):
                part = own[k][tile, GUARD + p * piece : GUARD + (p + 1) * piece, :]
                lane = lane_of(part)
                here = (lane >= p * HALO) & (lane < (p + 1) * HALO)
                packed = jnp.where(here, roll(part, p * HALO - first), packed)
            sides.append(packed)
        west, east = sides
        cross_ref[k] = jnp.where(even_y, west, east)
        pair_ref[k] = jnp.where(even_y, east, west)


def body_kernel(source, guess, weight, *refs):
    states = refs[: 4 * (LEVELS - 1)]
    last_weight, last_source, field, resid, guess_in, *inner = refs[4 * (LEVELS - 1) :]
    rows = source.shape[1] - 2 * GUARD
    depth = LEVELS - 2
    weights = (guess_in, *inner[:depth], last_weight)
    sources = (source, *inner[depth:], last_source)
    weights[0][...] = weight[...]
    descend_all(rows, sources, guess, weights, states, field, resid, 112)


def frame_kernel(own_source, own_guess, own_weight, from_cross, from_pair, body_weight, body_source, *refs):
    even = lax.axis_index("gy") % 2 == 0
    states, refs = refs[: 4 * (LEVELS - 1)], refs[4 * (LEVELS - 1) :]
    frame_source, ring_state, coarse_ref = refs[0], refs[1:5], refs[5]
    frame_guess, frame_weight, field, resid, ring_weight, ring_source, ring_field, ring_resid, *inner = refs[6:]
    rows = own_source.shape[1] - 2 * GUARD
    weights = (frame_weight, *inner[: LEVELS - 1])
    sources = (frame_source, *inner[LEVELS - 1 :])
    piece = rows // PIECES
    for k, (own, frame) in enumerate(
        ((own_source, frame_source), (own_guess, frame_guess), (own_weight, frame_weight))
    ):
        clear_guards(frame, rows)
        left = jnp.where(even, from_cross[k], from_pair[k])
        right = jnp.where(even, from_pair[k], from_cross[k])
        lane = lane_of(left)
        for p in range(PIECES):
            span = slice(GUARD + p * piece, GUARD + (p + 1) * piece)
            inside = jnp.where(lane < LANES // 2, roll(own[0, span, :], HALO), roll(own[1, span, :], -HALO))
            inside = jnp.where(lane < HALO, roll(left, -p * HALO), inside)
            frame[0, span, :] = jnp.where(lane >= LANES - HALO, roll(right, -(p + 1) * HALO), inside)
    descend_all(rows, sources, frame_guess, weights, states, field, resid, 280)

    level = LEVELS - 1
    step, halo, height = 2**level, HALO >> level, rows >> level
    for body, frame, ring in (
        (body_weight, weights[level], ring_weight),
        (body_source, sources[level], ring_source),
    ):
        middle = load(body, 0, height)
        around = load(frame, 0, height)[0]
        lane = lane_of(around)
        ahead, back = roll(around, HALO), roll(around, -HALO)
        store(
            ring,
            0,
            height,
            [
                jnp.where(lane < 2 * step, back, middle[0]),
                jnp.where(lane >= LANES - 2 * step, ahead, middle[1]),
                jnp.where(lane < LANES // 2, ahead, back),
            ],
        )
    descend(level, height, ring_weight, ring_source, None, ring_state, ring_field, ring_resid, None, None, height)

    coarse_rows = (height - 2 * halo) // 2
    dense = jnp.zeros((8, LANES), jnp.float32)
    lane = lane_of(dense)
    per_tile = LANES // 2**LEVELS
    pooled_b = pool_rows(ring_resid, halo, 2 * coarse_rows, step)
    pooled_w = pool_rows(ring_weight, halo, 2 * coarse_rows, step)
    index = (lane % per_tile) * 2**LEVELS
    place = lane // per_tile
    for g in range(coarse_rows // 8):
        for group, (values, factor) in enumerate(((pooled_b, 0.25), (pooled_w, 0.125))):
            for t in range(2):
                taken = jnp.take_along_axis(factor * values[t][8 * g : 8 * g + 8], index, axis=1)
                dense = jnp.where(place == 4 * g + 2 * group + t, taken, dense)
    coarse_ref[...] = jnp.broadcast_to(dense[None], coarse_ref.shape)


def coarse_solve(all_ref, width, groups):
    x, nx = lax.axis_index("gx"), lax.axis_size("gx")
    y, ny = lax.axis_index("gy"), lax.axis_size("gy")
    tiles = []
    for dx in (-1, 0, 1):
        for dy in (-1, 0, 1):
            inside = (x + dx >= 0) & (x + dx < nx) & (y + dy >= 0) & (y + dy < ny)
            tile = all_ref[jnp.where(inside, (x + dx) * ny + y + dy, 0)]
            tiles.append(jnp.where(inside, tile, 0.0))
    lane = lane_of(tiles[0])
    blocks = [(0, g) for g in range(groups - TALL // 8, groups)]
    blocks += [(1, g) for g in range(groups)] + [(2, g) for g in range(TALL // 8)]
    b, w = [], []
    for band, g in blocks:
        b_rows = w_rows = jnp.zeros_like(tiles[0])
        for side in range(3):
            tile = tiles[3 * band + side]
            here = (lane >= side * width) & (lane < (side + 1) * width)
            b_rows = jnp.where(here, roll(tile, (side - 2 * g) * width), b_rows)
            w_rows = jnp.where(here, roll(tile, (side - 2 * g - 1) * width), w_rows)
        b.append(b_rows)
        w.append(w_rows)
    b, w = jnp.concatenate(b, axis=0), jnp.concatenate(w, axis=0)

    def north_of(x):
        return pltpu.roll(x, 1, 0)

    def south_of(x):
        return pltpu.roll(x, x.shape[0] - 1, 0)

    c_west = jnp.minimum(w, roll(w, 1))
    c_north = jnp.minimum(w, north_of(w))
    c_east, c_south = roll(c_west, -1), south_of(c_north)
    scale = relaxation / (damping + c_north + c_south + c_west + c_east)
    first = scale * b

    def sweep(_, e):
        applied = (
            damping * e
            + (c_west * (e - roll(e, 1)) + c_east * (e - roll(e, -1)))
            + (c_north * (e - north_of(e)) + c_south * (e - south_of(e)))
        )
        return e + (first - scale * applied)

    return lax.fori_loop(0, SWEEPS - 1, sweep, first)


def up_kernel(all_ref, own_source, frame_source, *refs):
    count = 4 * (LEVELS - 1)
    body_state, frame_state, ring_state = refs[:count], refs[count : 2 * count], refs[2 * count : 2 * count + 4]
    out_ref, resid_ref = refs[2 * count + 4 : 2 * count + 6]
    ring_pe, body_final, frame_final, *inner = refs[2 * count + 6 :]
    body_pe, frame_pe = inner[: LEVELS - 1], inner[LEVELS - 1 :]
    rows = out_ref.shape[0] + 2 * HALO
    width = out_ref.shape[1] >> LEVELS
    e = coarse_solve(all_ref, width, (out_ref.shape[0] >> LEVELS) // 8)

    level = LEVELS - 1
    step, halo, height = 2**level, HALO >> level, rows >> level
    coarse_rows = (height - 2 * halo) // 2
    picked = e[TALL - 8 : TALL + coarse_rows + 8]
    lane = lane_of(picked)
    for t in range(3):
        group = (lane + t * LANES) // 2**LEVELS
        if t == 2:
            group = jnp.where(lane < LANES // 2, group, group - 3 * LANES // 2**LEVELS)
        taken = jnp.take_along_axis(picked, jnp.clip(group + width, 0, LANES - 1), axis=1)[7 : 7 + coarse_rows + 2]
        ring_pe[t, 0 : 2 * GUARD, :] = jnp.zeros((2 * GUARD, LANES), jnp.float32)
        ring_pe[t, height : height + 2 * GUARD, :] = jnp.zeros((2 * GUARD, LANES), jnp.float32)
        ring_pe[t, pl.ds(GUARD + halo - 2, coarse_rows + 2, stride=2), :] = taken
        ring_pe[t, pl.ds(GUARD + halo - 1, coarse_rows + 2, stride=2), :] = taken

    def climbed(pe, state, start, size, step):
        mid, applied = applied_to(pe, state[:2], start, size, step)
        scale, smooth = load(state[2], start, size), load(state[3], start, size)
        return [smooth[t] + (mid[t] - scale[t] * applied[t]) for t in range(len(mid))]

    ring = climbed(ring_pe, ring_state, 0, height, step)
    lane = lane_of(ring[0])
    around = jnp.where(
        lane < LANES // 2,
        jnp.where(lane < HALO, roll(ring[2], HALO), roll(ring[0], HALO)),
        jnp.where(lane < LANES - HALO, roll(ring[1], -HALO), roll(ring[2], -HALO)),
    )
    store_twice(body_pe[level - 1], 0, height, ring[:2])
    store_twice(frame_pe[level - 1], 0, height, [around])

    for level in range(LEVELS - 2, -1, -1):
        step, height = 2**level, rows >> level
        for pes, states, final, largest in (
            (body_pe, body_state, body_final, 112),
            (frame_pe, frame_state, frame_final, 280),
        ):
            state = states[4 * level : 4 * level + 4]
            clear_guards(pes[level], height)

            def climb(start, size, level=level, step=step, pes=pes, state=state, final=final):
                value = climbed(pes[level], state, start, size, step)
                if level == 0:
                    store(final, start, size, value)
                else:
                    store_twice(pes[level - 1], start, size, value)

            for_chunks(height, climb, largest)

    def last(start, size):
        base = start + HALO
        body = applied_to(body_final, body_state[:2], base, size, 1)
        frame = applied_to(frame_final, frame_state[:2], base, size, 1)
        b, b_frame = load(own_source, base, size), load(frame_source, base, size)
        body = (body[0], [b[t] - body[1][t] for t in range(2)])
        frame = (frame[0][0], b_frame[0] - frame[1][0])
        lane = lane_of(frame[0])
        near = HALO - 4
        span = pl.ds(start, size)
        for ref, middle, around in ((out_ref, body[0], frame[0]), (resid_ref, body[1], frame[1])):
            ref[span, :LANES] = jnp.where(lane < near, roll(around, -HALO), middle[0])
            ref[span, LANES:] = jnp.where(lane >= LANES - near, roll(around, HALO), middle[1])

    for_chunks(out_ref.shape[0], last, 128)


def call(kernel, out_shape, scratch, flops, moved):
    return pl.pallas_call(
        kernel,
        out_shape=out_shape,
        scratch_shapes=scratch,
        compiler_params=pltpu.CompilerParams(vmem_limit_bytes=VMEM_LIMIT),
        cost_estimate=pl.CostEstimate(flops=flops, bytes_accessed=moved, transcendentals=0),
    )


def swap(x, axis, first):
    pairs = [(i, i + 1) for i in range(first, lax.axis_size(axis) - 1, 2)]
    return lax.ppermute(x, axis, pairs + [(j, i) for i, j in pairs])


def local(rhs, pressure, wet_mask, bathy_class):
    rows, columns = rhs.shape
    cells = rows * columns
    total = rows + 2 * HALO
    levels = range(LEVELS - 1)

    def shape(tiles, level):
        return (tiles, (total >> level) + 2 * GUARD, LANES)

    def out(*dims):
        return jax.ShapeDtypeStruct(dims, jnp.float32)

    def vmem(tiles, level):
        return pltpu.VMEM(shape(tiles, level), jnp.float32)

    def fields(r, p, m, c):
        wet = m.astype(jnp.float32)
        return wet * r, wet * p, wet * (1.0 + 0.5 * c.astype(jnp.float32))

    given = (rhs, pressure, wet_mask, bathy_class)

    def edge(start):
        return jnp.stack(fields(*(lax.dynamic_slice_in_dim(x, start, HALO, axis=0) for x in given)))

    even = lax.axis_index("gx") % 2 == 0
    first_rows = swap(edge(jnp.where(even, 0, rows - HALO)), "gx", 1)
    second_rows = swap(edge(jnp.where(even, rows - HALO, 0)), "gx", 0)
    piece = total // PIECES
    own_shapes = [out(*shape(2, 0))] * 3
    *own, to_cross, to_pair = call(
        pack_kernel, (*own_shapes, out(3, piece, LANES), out(3, piece, LANES)), (), 10 * cells, 10 * cells
    )(*fields(*given), first_rows, second_rows)
    from_cross = swap(to_cross, "gy", 1)
    from_pair = swap(to_pair, "gy", 0)

    state_count = 4 * (LEVELS - 1)
    *body_state, body_weight, body_source = call(
        body_kernel,
        [out(*shape(2, level)) for level in levels for _ in range(4)] + [out(*shape(2, LEVELS - 1))] * 2,
        [vmem(2, 0)] * 3 + [vmem(2, level) for level in levels[1:]] * 2,
        100 * cells,
        40 * cells,
    )(*own)
    devices = lax.axis_size("gx") * lax.axis_size("gy")
    ring = LEVELS - 1
    *state, coarse = call(
        frame_kernel,
        [out(*shape(1, level)) for level in levels for _ in range(4)]
        + [out(*shape(1, 0))]
        + [out(*shape(3, ring))] * 4
        + [out(devices, 8, LANES)],
        [vmem(1, 0)] * 4 + [vmem(3, ring)] * 4 + [vmem(1, level) for level in range(1, LEVELS)] * 2,
        50 * cells,
        20 * cells,
    )(*own, from_cross, from_pair, body_weight, body_source)
    frame_state, frame_source, ring_state = state[:state_count], state[state_count], state[state_count + 1 :]
    gathered = lax.all_to_all(coarse, ("gx", "gy"), 0, 0)
    return call(
        up_kernel,
        (out(rows, columns), out(rows, columns)),
        [vmem(3, ring), vmem(2, 0), vmem(1, 0)]
        + [vmem(2, level) for level in levels]
        + [vmem(1, level) for level in levels],
        60 * cells,
        40 * cells,
    )(gathered, own[0], frame_source, *body_state, *frame_state, *ring_state)


def solution(mesh):
    placed = (P("gx", "gy"), P("gx", "gy"), P("gx", "gy"), P("gx", "gy"))
    return jax.shard_map(
        local, mesh=mesh, in_specs=placed, out_specs=(P("gx", "gy"), P("gx", "gy")), check_vma=False
    )
```

```python
import jax
import jax.numpy as jnp
from jax import lax
from jax.experimental import pallas as pl
from jax.experimental.pallas import tpu as pltpu
from jax.sharding import PartitionSpec as P

LEVELS = 4
SWEEPS = 12

damping = 0.01
relaxation = 0.8

HALO = 24
LANES = 128
INNER = LANES // 2 - HALO
GUARD = 8
PIECES = 5
TALL = 16
VMEM_LIMIT = 40 * 1024 * 1024


def lane_of(x):
    return lax.broadcasted_iota(jnp.int32, x.shape, x.ndim - 1)


def roll(x, amount):
    amount %= LANES
    return x if amount == 0 else pltpu.roll(x, amount, x.ndim - 1)


def from_west(tiles, step):
    moved = [roll(t, step) for t in tiles]
    if len(tiles) == 1:
        return moved
    edge = lane_of(tiles[0]) < step
    return [jnp.where(edge, moved[i - 1], moved[i]) for i in range(len(tiles))]


def from_east(tiles, step):
    moved = [roll(t, -step) for t in tiles]
    count = len(tiles)
    if count == 1:
        return moved
    edge = lane_of(tiles[0]) >= LANES - step
    return [jnp.where(edge, moved[(i + 1) % count], moved[i]) for i in range(count)]


def lane_pairs(x, step):
    first = (lane_of(x) // step) % 2 == 0
    return x + jnp.where(first, roll(x, -step), roll(x, step))


def for_parts(start, size, body, part):
    for offset in range(0, size, part):
        body(start + offset, min(part, size - offset))


def for_chunks(rows, body, largest, part):
    sizes = [size for size in range(8, largest + 1, 8) if rows % size == 0]
    if rows <= largest or not sizes:
        for_parts(0, rows, body, part)
        return

    def step(i, carry):
        for_parts(i * sizes[-1], sizes[-1], body, part)
        return carry

    lax.fori_loop(0, rows // sizes[-1], step, 0)


def load(ref, start, size):
    return [ref[t, pl.ds(GUARD + start, size), :] for t in range(ref.shape[0])]


def store(ref, start, size, tiles):
    for t, tile in enumerate(tiles):
        ref[t, pl.ds(GUARD + start, size), :] = tile


def store_twice(ref, start, size, tiles):
    for t, tile in enumerate(tiles):
        ref[t, pl.ds(GUARD + 2 * start, size, stride=2), :] = tile
        ref[t, pl.ds(GUARD + 2 * start + 1, size, stride=2), :] = tile


def clear_guards(ref, rows):
    zeros = jnp.zeros((GUARD, LANES), jnp.float32)
    for t in range(ref.shape[0]):
        ref[t, 0:GUARD, :] = zeros
        ref[t, GUARD + rows : 2 * GUARD + rows, :] = zeros


def operator(mid, north, south, c_west, c_north, c_south, step):
    west = from_west(mid, step)
    tiles = range(len(mid))
    flux = [c_west[t] * (mid[t] - west[t]) for t in tiles]
    out = from_east(flux, step)
    return [
        damping * mid[t]
        + (flux[t] - out[t])
        + (c_north[t] * (mid[t] - north[t]) + c_south[t] * (mid[t] - south[t]))
        for t in tiles
    ]


def applied_to(ref, coeffs, start, size, step):
    c_west_ref, c_north_ref = coeffs
    mid = load(ref, start, size)
    north, south = load(ref, start - 1, size), load(ref, start + 1, size)
    c_west, c_north = load(c_west_ref, start, size), load(c_north_ref, start, size)
    return mid, operator(mid, north, south, c_west, c_north, load(c_north_ref, start + 1, size), step)


def pool_rows(ref, start, size, step):
    out = []
    for t in range(ref.shape[0]):
        even = ref[t, pl.ds(GUARD + start, size // 2, stride=2), :]
        odd = ref[t, pl.ds(GUARD + start + 1, size // 2, stride=2), :]
        out.append(lane_pairs(even + odd, step))
    return out


def descend(level, height, weight, source, guess, state, field, resid, next_weight, next_source, largest, part):
    step = 2**level
    c_west_ref, c_north_ref, scale_ref, smooth_ref = state
    for ref in (weight, field, c_north_ref):
        clear_guards(ref, height)

    def first_pass(start, size):
        w, w_north, w_south = (load(weight, start + k, size) for k in (0, -1, 1))
        c_north = [jnp.minimum(a, b) for a, b in zip(w, w_north)]
        c_south = [jnp.minimum(a, b) for a, b in zip(w, w_south)]
        c_west = [jnp.minimum(a, b) for a, b in zip(w, from_west(w, step))]
        c_east = from_east(c_west, step)
        scale = [
            relaxation / (damping + c_north[t] + c_south[t] + c_west[t] + c_east[t]) for t in range(len(w))
        ]
        store(c_north_ref, start, size, c_north)
        store(c_west_ref, start, size, c_west)
        store(scale_ref, start, size, scale)
        value = load(source, start, size)
        if guess is not None:
            mid, north, south = (load(guess, start + k, size) for k in (0, -1, 1))
            applied = operator(mid, north, south, c_west, c_north, c_south, step)
            value = [value[t] - applied[t] for t in range(len(w))]
        value = [scale[t] * value[t] for t in range(len(w))]
        if guess is not None:
            value = [mid[t] + value[t] for t in range(len(w))]
        store(field, start, size, value)
        if next_weight is not None:
            pooled = [0.125 * p for p in pool_rows(weight, start, size, step)]
            store(next_weight, start // 2, size // 2, pooled)

    def second_pass(start, size):
        mid, applied = applied_to(field, (c_west_ref, c_north_ref), start, size, step)
        b, scale = load(source, start, size), load(scale_ref, start, size)
        rest = [b[t] - applied[t] for t in range(len(b))]
        store(smooth_ref, start, size, [mid[t] + scale[t] * rest[t] for t in range(len(b))])
        store(resid, start, size, rest)
        if next_source is not None:
            pooled = [0.25 * p for p in pool_rows(resid, start, size, step)]
            store(next_source, start // 2, size // 2, pooled)

    for_chunks(height, first_pass, largest, part)
    for_chunks(height, second_pass, largest, part)


def descend_all(rows, sources, guess, weights, states, field, resid, largest, part):
    for level in range(LEVELS - 1):
        descend(
            level,
            rows >> level,
            weights[level],
            sources[level],
            guess if level == 0 else None,
            states[4 * level : 4 * level + 4],
            field,
            resid,
            weights[level + 1],
            sources[level + 1],
            largest,
            part,
        )


def pack_kernel(source, guess, weight, first_rows, second_rows, own_source, own_guess, own_weight, cross_ref, pair_ref):
    rows = source.shape[0]
    total = rows + 2 * HALO
    even_x, even_y = lax.axis_index("gx") % 2 == 0, lax.axis_index("gy") % 2 == 0
    own = (own_source, own_guess, own_weight)
    for k, block in enumerate((source, guess, weight)):
        clear_guards(own[k], total)
        above = jnp.where(even_x, first_rows[k], second_rows[k])
        below = jnp.where(even_x, second_rows[k], first_rows[k])
        for t in range(2):
            columns = slice(t * LANES, (t + 1) * LANES)
            own[k][t, GUARD : GUARD + HALO, :] = above[:, columns]
            own[k][t, GUARD + HALO : GUARD + HALO + rows, :] = block[:, columns]
            own[k][t, GUARD + HALO + rows : GUARD + total, :] = below[:, columns]
    piece = total // PIECES
    for k in range(3):
        sides = []
        for tile, first in ((0, 0), (1, LANES - HALO)):
            packed = jnp.zeros((piece, LANES), jnp.float32)
            for p in range(PIECES):
                part = own[k][tile, GUARD + p * piece : GUARD + (p + 1) * piece, :]
                lane = lane_of(part)
                here = (lane >= p * HALO) & (lane < (p + 1) * HALO)
                packed = jnp.where(here, roll(part, p * HALO - first), packed)
            sides.append(packed)
        west, east = sides
        cross_ref[k] = jnp.where(even_y, west, east)
        pair_ref[k] = jnp.where(even_y, east, west)


def body_kernel(source, guess, weight, *refs):
    states = refs[: 4 * (LEVELS - 1)]
    last_weight, last_source, field, resid, guess_in, *inner = refs[4 * (LEVELS - 1) :]
    rows = source.shape[1] - 2 * GUARD
    depth = LEVELS - 2
    weights = (guess_in, *inner[:depth], last_weight)
    sources = (source, *inner[depth:], last_source)
    weights[0][...] = weight[...]
    descend_all(rows, sources, guess, weights, states, field, resid, 112, 16)


def frame_kernel(own_source, own_guess, own_weight, from_cross, from_pair, body_weight, body_source, *refs):
    even = lax.axis_index("gy") % 2 == 0
    states, refs = refs[: 4 * (LEVELS - 1)], refs[4 * (LEVELS - 1) :]
    frame_source, ring_state, coarse_ref = refs[0], refs[1:5], refs[5]
    frame_guess, frame_weight, field, resid, ring_weight, ring_source, ring_field, ring_resid, *inner = refs[6:]
    rows = own_source.shape[1] - 2 * GUARD
    weights = (frame_weight, *inner[: LEVELS - 1])
    sources = (frame_source, *inner[LEVELS - 1 :])
    piece = rows // PIECES
    for k, (own, frame) in enumerate(
        ((own_source, frame_source), (own_guess, frame_guess), (own_weight, frame_weight))
    ):
        clear_guards(frame, rows)
        left = jnp.where(even, from_cross[k], from_pair[k])
        right = jnp.where(even, from_pair[k], from_cross[k])
        lane = lane_of(left)
        for p in range(PIECES):
            span = slice(GUARD + p * piece, GUARD + (p + 1) * piece)
            inside = jnp.where(lane < LANES // 2, roll(own[0, span, :], HALO), roll(own[1, span, :], -HALO))
            inside = jnp.where(lane < HALO, roll(left, -p * HALO), inside)
            frame[0, span, :] = jnp.where(lane >= LANES - HALO, roll(right, -(p + 1) * HALO), inside)
    descend_all(rows, sources, frame_guess, weights, states, field, resid, 280, 32)

    level = LEVELS - 1
    step, halo, height = 2**level, HALO >> level, rows >> level
    for body, frame, ring in (
        (body_weight, weights[level], ring_weight),
        (body_source, sources[level], ring_source),
    ):
        middle = load(body, 0, height)
        around = load(frame, 0, height)[0]
        lane = lane_of(around)
        ahead, back = roll(around, HALO), roll(around, -HALO)
        store(
            ring,
            0,
            height,
            [
                jnp.where(lane < 2 * step, back, middle[0]),
                jnp.where(lane >= LANES - 2 * step, ahead, middle[1]),
                jnp.where(lane < LANES // 2, ahead, back),
            ],
        )
    descend(level, height, ring_weight, ring_source, None, ring_state, ring_field, ring_resid, None, None, height, 16)

    coarse_rows = (height - 2 * halo) // 2
    dense = jnp.zeros((8, LANES), jnp.float32)
    lane = lane_of(dense)
    per_tile = LANES // 2**LEVELS
    pooled_b = pool_rows(ring_resid, halo, 2 * coarse_rows, step)
    pooled_w = pool_rows(ring_weight, halo, 2 * coarse_rows, step)
    index = (lane % per_tile) * 2**LEVELS
    place = lane // per_tile
    for g in range(coarse_rows // 8):
        for group, (values, factor) in enumerate(((pooled_b, 0.25), (pooled_w, 0.125))):
            for t in range(2):
                taken = jnp.take_along_axis(factor * values[t][8 * g : 8 * g + 8], index, axis=1)
                dense = jnp.where(place == 4 * g + 2 * group + t, taken, dense)
    coarse_ref[...] = jnp.broadcast_to(dense[None], coarse_ref.shape)


def coarse_solve(all_ref, width, groups):
    x, nx = lax.axis_index("gx"), lax.axis_size("gx")
    y, ny = lax.axis_index("gy"), lax.axis_size("gy")
    tiles = []
    for dx in (-1, 0, 1):
        for dy in (-1, 0, 1):
            inside = (x + dx >= 0) & (x + dx < nx) & (y + dy >= 0) & (y + dy < ny)
            tile = all_ref[jnp.where(inside, (x + dx) * ny + y + dy, 0)]
            tiles.append(jnp.where(inside, tile, 0.0))
    lane = lane_of(tiles[0])
    blocks = [(0, g) for g in range(groups - TALL // 8, groups)]
    blocks += [(1, g) for g in range(groups)] + [(2, g) for g in range(TALL // 8)]
    b, w = [], []
    for band, g in blocks:
        b_rows = w_rows = jnp.zeros_like(tiles[0])
        for side in range(3):
            tile = tiles[3 * band + side]
            here = (lane >= side * width) & (lane < (side + 1) * width)
            b_rows = jnp.where(here, roll(tile, (side - 2 * g) * width), b_rows)
            w_rows = jnp.where(here, roll(tile, (side - 2 * g - 1) * width), w_rows)
        b.append(b_rows)
        w.append(w_rows)
    b, w = jnp.concatenate(b, axis=0), jnp.concatenate(w, axis=0)

    def north_of(x):
        return pltpu.roll(x, 1, 0)

    def south_of(x):
        return pltpu.roll(x, x.shape[0] - 1, 0)

    c_west = jnp.minimum(w, roll(w, 1))
    c_north = jnp.minimum(w, north_of(w))
    c_east, c_south = roll(c_west, -1), south_of(c_north)
    scale = relaxation / (damping + c_north + c_south + c_west + c_east)
    first = scale * b

    def sweep(_, e):
        applied = (
            damping * e
            + (c_west * (e - roll(e, 1)) + c_east * (e - roll(e, -1)))
            + (c_north * (e - north_of(e)) + c_south * (e - south_of(e)))
        )
        return e + (first - scale * applied)

    return lax.fori_loop(0, SWEEPS - 1, sweep, first)


def up_kernel(all_ref, own_source, frame_source, *refs):
    count = 4 * (LEVELS - 1)
    body_state, frame_state, ring_state = refs[:count], refs[count : 2 * count], refs[2 * count : 2 * count + 4]
    out_ref, resid_ref = refs[2 * count + 4 : 2 * count + 6]
    ring_pe, body_final, frame_final, sems, *inner = refs[2 * count + 6 :]
    outs, inner = inner[:2], inner[2:]
    body_pe, frame_pe = inner[: LEVELS - 1], inner[LEVELS - 1 :]
    rows = out_ref.shape[0] + 2 * HALO
    width = out_ref.shape[1] >> LEVELS
    e = coarse_solve(all_ref, width, (out_ref.shape[0] >> LEVELS) // 8)

    level = LEVELS - 1
    step, halo, height = 2**level, HALO >> level, rows >> level
    coarse_rows = (height - 2 * halo) // 2
    picked = e[TALL - 8 : TALL + coarse_rows + 8]
    lane = lane_of(picked)
    for t in range(3):
        group = (lane + t * LANES) // 2**LEVELS
        if t == 2:
            group = jnp.where(lane < LANES // 2, group, group - 3 * LANES // 2**LEVELS)
        taken = jnp.take_along_axis(picked, jnp.clip(group + width, 0, LANES - 1), axis=1)[7 : 7 + coarse_rows + 2]
        ring_pe[t, 0 : 2 * GUARD, :] = jnp.zeros((2 * GUARD, LANES), jnp.float32)
        ring_pe[t, height : height + 2 * GUARD, :] = jnp.zeros((2 * GUARD, LANES), jnp.float32)
        ring_pe[t, pl.ds(GUARD + halo - 2, coarse_rows + 2, stride=2), :] = taken
        ring_pe[t, pl.ds(GUARD + halo - 1, coarse_rows + 2, stride=2), :] = taken

    def climbed(pe, state, start, size, step):
        mid, applied = applied_to(pe, state[:2], start, size, step)
        scale, smooth = load(state[2], start, size), load(state[3], start, size)
        return [smooth[t] + (mid[t] - scale[t] * applied[t]) for t in range(len(mid))]

    def climb_ring(start, size, level=level, step=step):
        ring = climbed(ring_pe, ring_state, start, size, step)
        lane = lane_of(ring[0])
        around = jnp.where(
            lane < LANES // 2,
            jnp.where(lane < HALO, roll(ring[2], HALO), roll(ring[0], HALO)),
            jnp.where(lane < LANES - HALO, roll(ring[1], -HALO), roll(ring[2], -HALO)),
        )
        store_twice(body_pe[level - 1], start, size, ring[:2])
        store_twice(frame_pe[level - 1], start, size, [around])

    for_chunks(height, climb_ring, height, 16)

    for level in range(LEVELS - 2, -1, -1):
        step, height = 2**level, rows >> level
        for pes, states, final, largest, part in (
            (body_pe, body_state, body_final, 112, 16),
            (frame_pe, frame_state, frame_final, 280, 32),
        ):
            state = states[4 * level : 4 * level + 4]
            clear_guards(pes[level], height)

            def climb(start, size, level=level, step=step, pes=pes, state=state, final=final):
                value = climbed(pes[level], state, start, size, step)
                if level == 0:
                    store(final, start, size, value)
                else:
                    store_twice(pes[level - 1], start, size, value)

            for_chunks(height, climb, largest, part)

    def last(start, size):
        base = start + HALO
        body = applied_to(body_final, body_state[:2], base, size, 1)
        frame = applied_to(frame_final, frame_state[:2], base, size, 1)
        b, b_frame = load(own_source, base, size), load(frame_source, base, size)
        body = (body[0], [b[t] - body[1][t] for t in range(2)])
        frame = (frame[0][0], b_frame[0] - frame[1][0])
        lane = lane_of(frame[0])
        near = HALO - 4
        span = pl.ds(start, size)
        for ref, middle, around in ((outs[0], body[0], frame[0]), (outs[1], body[1], frame[1])):
            ref[span, :LANES] = jnp.where(lane < near, roll(around, -HALO), middle[0])
            ref[span, LANES:] = jnp.where(lane >= LANES - near, roll(around, HALO), middle[1])

    parts = sems.shape[0] // 2
    size = out_ref.shape[0] // parts

    def copies(p):
        span = pl.ds(p * size, size)
        return [
            pltpu.make_async_copy(outs[k].at[span], ref.at[span], sems.at[2 * p + k])
            for k, ref in enumerate((out_ref, resid_ref))
        ]

    def finish(p, carry):
        for_parts(p * size, size, last, 16)
        for copy in copies(p):
            copy.start()
        return carry

    lax.fori_loop(0, parts, finish, 0)
    for p in range(parts):
        for copy in copies(p):
            copy.wait()


def call(kernel, out_shape, scratch, flops, moved, **more):
    return pl.pallas_call(
        kernel,
        out_shape=out_shape,
        scratch_shapes=scratch,
        compiler_params=pltpu.CompilerParams(vmem_limit_bytes=VMEM_LIMIT),
        cost_estimate=pl.CostEstimate(flops=flops, bytes_accessed=moved, transcendentals=0),
        **more,
    )


def swap(x, axis, first):
    pairs = [(i, i + 1) for i in range(first, lax.axis_size(axis) - 1, 2)]
    return lax.ppermute(x, axis, pairs + [(j, i) for i, j in pairs])


def local(rhs, pressure, wet_mask, bathy_class):
    rows, columns = rhs.shape
    cells = rows * columns
    total = rows + 2 * HALO
    levels = range(LEVELS - 1)

    def shape(tiles, level):
        return (tiles, (total >> level) + 2 * GUARD, LANES)

    def out(*dims):
        return jax.ShapeDtypeStruct(dims, jnp.float32)

    def vmem(tiles, level):
        return pltpu.VMEM(shape(tiles, level), jnp.float32)

    def fields(r, p, m, c):
        wet = m.astype(jnp.float32)
        return wet * r, wet * p, wet * (1.0 + 0.5 * c.astype(jnp.float32))

    given = (rhs, pressure, wet_mask, bathy_class)

    def edge(start):
        return jnp.stack(fields(*(lax.dynamic_slice_in_dim(x, start, HALO, axis=0) for x in given)))

    even = lax.axis_index("gx") % 2 == 0
    first_rows = swap(edge(jnp.where(even, 0, rows - HALO)), "gx", 1)
    second_rows = swap(edge(jnp.where(even, rows - HALO, 0)), "gx", 0)
    piece = total // PIECES
    own_shapes = [out(*shape(2, 0))] * 3
    *own, to_cross, to_pair = call(
        pack_kernel, (*own_shapes, out(3, piece, LANES), out(3, piece, LANES)), (), 10 * cells, 10 * cells
    )(*fields(*given), first_rows, second_rows)
    from_cross = swap(to_cross, "gy", 1)
    from_pair = swap(to_pair, "gy", 0)

    state_count = 4 * (LEVELS - 1)
    *body_state, body_weight, body_source = call(
        body_kernel,
        [out(*shape(2, level)) for level in levels for _ in range(4)] + [out(*shape(2, LEVELS - 1))] * 2,
        [vmem(2, 0)] * 3 + [vmem(2, level) for level in levels[1:]] * 2,
        100 * cells,
        40 * cells,
    )(*own)
    devices = lax.axis_size("gx") * lax.axis_size("gy")
    ring = LEVELS - 1
    *state, coarse = call(
        frame_kernel,
        [out(*shape(1, level)) for level in levels for _ in range(4)]
        + [out(*shape(1, 0))]
        + [out(*shape(3, ring))] * 4
        + [out(devices, 8, LANES)],
        [vmem(1, 0)] * 4 + [vmem(3, ring)] * 4 + [vmem(1, level) for level in range(1, LEVELS)] * 2,
        50 * cells,
        20 * cells,
    )(*own, from_cross, from_pair, body_weight, body_source)
    frame_state, frame_source, ring_state = state[:state_count], state[state_count], state[state_count + 1 :]
    gathered = lax.all_to_all(coarse, ("gx", "gy"), 0, 0)
    return call(
        up_kernel,
        (out(rows, columns), out(rows, columns)),
        [vmem(3, ring), vmem(2, 0), vmem(1, 0), pltpu.SemaphoreType.DMA((8,))]
        + [pltpu.VMEM((rows, columns), jnp.float32)] * 2
        + [vmem(2, level) for level in levels]
        + [vmem(1, level) for level in levels],
        60 * cells,
        40 * cells,
        out_specs=[pl.BlockSpec(memory_space=pl.ANY)] * 2,
    )(gathered, own[0], frame_source, *body_state, *frame_state, *ring_state)


def solution(mesh):
    placed = (P("gx", "gy"), P("gx", "gy"), P("gx", "gy"), P("gx", "gy"))
    return jax.shard_map(
        local, mesh=mesh, in_specs=placed, out_specs=(P("gx", "gy"), P("gx", "gy")), check_vma=False
    )
```

```python
import jax
import jax.numpy as jnp
from jax import lax
from jax.experimental import pallas as pl
from jax.experimental.pallas import tpu as pltpu
from jax.sharding import PartitionSpec as P

LEVELS = 4
SWEEPS = 12

damping = 0.01
relaxation = 0.8

HALO = 24
LANES = 128
INNER = LANES // 2 - HALO
GUARD = 8
PIECES = 5
TALL = 16
VMEM_LIMIT = 40 * 1024 * 1024


def lane_of(x):
    return lax.broadcasted_iota(jnp.int32, x.shape, x.ndim - 1)


def roll(x, amount):
    amount %= LANES
    return x if amount == 0 else pltpu.roll(x, amount, x.ndim - 1)


def from_west(tiles, step):
    moved = [roll(t, step) for t in tiles]
    if len(tiles) == 1:
        return moved
    edge = lane_of(tiles[0]) < step
    return [jnp.where(edge, moved[i - 1], moved[i]) for i in range(len(tiles))]


def from_east(tiles, step):
    moved = [roll(t, -step) for t in tiles]
    count = len(tiles)
    if count == 1:
        return moved
    edge = lane_of(tiles[0]) >= LANES - step
    return [jnp.where(edge, moved[(i + 1) % count], moved[i]) for i in range(count)]


def lane_pairs(x, step):
    first = (lane_of(x) // step) % 2 == 0
    return x + jnp.where(first, roll(x, -step), roll(x, step))


def for_parts(start, size, body, part):
    for offset in range(0, size, part):
        body(start + offset, min(part, size - offset))


def for_chunks(rows, body, largest, part):
    sizes = [size for size in range(8, largest + 1, 8) if rows % size == 0]
    if rows <= largest or not sizes:
        for_parts(0, rows, body, part)
        return

    def step(i, carry):
        for_parts(i * sizes[-1], sizes[-1], body, part)
        return carry

    lax.fori_loop(0, rows // sizes[-1], step, 0)


def load(ref, start, size):
    return [ref[t, pl.ds(GUARD + start, size), :] for t in range(ref.shape[0])]


def store(ref, start, size, tiles):
    for t, tile in enumerate(tiles):
        ref[t, pl.ds(GUARD + start, size), :] = tile


def store_twice(ref, start, size, tiles):
    for t, tile in enumerate(tiles):
        ref[t, pl.ds(GUARD + 2 * start, size, stride=2), :] = tile
        ref[t, pl.ds(GUARD + 2 * start + 1, size, stride=2), :] = tile


def clear_guards(ref, rows):
    zeros = jnp.zeros((GUARD, LANES), jnp.float32)
    for t in range(ref.shape[0]):
        ref[t, 0:GUARD, :] = zeros
        ref[t, GUARD + rows : 2 * GUARD + rows, :] = zeros


def scale_of(couplings):
    diagonal = damping + couplings
    inverse = pl.reciprocal(diagonal, approx=True)
    for _ in range(2):
        inverse = inverse * (2.0 - diagonal * inverse)
    return relaxation * inverse


def operator(mid, north, south, c_west, c_north, c_south, step):
    west = from_west(mid, step)
    tiles = range(len(mid))
    flux = [c_west[t] * (mid[t] - west[t]) for t in tiles]
    out = from_east(flux, step)
    return [
        damping * mid[t]
        + (flux[t] - out[t])
        + (c_north[t] * (mid[t] - north[t]) + c_south[t] * (mid[t] - south[t]))
        for t in tiles
    ]


def applied_to(ref, coeffs, start, size, step):
    c_west_ref, c_north_ref = coeffs
    mid = load(ref, start, size)
    north, south = load(ref, start - 1, size), load(ref, start + 1, size)
    c_west, c_north = load(c_west_ref, start, size), load(c_north_ref, start, size)
    return mid, operator(mid, north, south, c_west, c_north, load(c_north_ref, start + 1, size), step)


def pool_rows(ref, start, size, step):
    out = []
    for t in range(ref.shape[0]):
        even = ref[t, pl.ds(GUARD + start, size // 2, stride=2), :]
        odd = ref[t, pl.ds(GUARD + start + 1, size // 2, stride=2), :]
        out.append(lane_pairs(even + odd, step))
    return out


def descend(level, height, weight, source, guess, state, field, resid, next_weight, next_source, largest, part):
    step = 2**level
    c_west_ref, c_north_ref, scale_ref, smooth_ref = state
    for ref in (weight, field, c_north_ref):
        clear_guards(ref, height)

    def first_pass(start, size):
        w, w_north, w_south = (load(weight, start + k, size) for k in (0, -1, 1))
        c_north = [jnp.minimum(a, b) for a, b in zip(w, w_north)]
        c_south = [jnp.minimum(a, b) for a, b in zip(w, w_south)]
        c_west = [jnp.minimum(a, b) for a, b in zip(w, from_west(w, step))]
        c_east = from_east(c_west, step)
        scale = [scale_of(c_north[t] + c_south[t] + c_west[t] + c_east[t]) for t in range(len(w))]
        store(c_north_ref, start, size, c_north)
        store(c_west_ref, start, size, c_west)
        store(scale_ref, start, size, scale)
        value = load(source, start, size)
        if guess is not None:
            mid, north, south = (load(guess, start + k, size) for k in (0, -1, 1))
            applied = operator(mid, north, south, c_west, c_north, c_south, step)
            value = [value[t] - applied[t] for t in range(len(w))]
        value = [scale[t] * value[t] for t in range(len(w))]
        if guess is not None:
            value = [mid[t] + value[t] for t in range(len(w))]
        store(field, start, size, value)
        if next_weight is not None:
            pooled = [0.125 * p for p in pool_rows(weight, start, size, step)]
            store(next_weight, start // 2, size // 2, pooled)

    def second_pass(start, size):
        mid, applied = applied_to(field, (c_west_ref, c_north_ref), start, size, step)
        b, scale = load(source, start, size), load(scale_ref, start, size)
        rest = [b[t] - applied[t] for t in range(len(b))]
        store(smooth_ref, start, size, [mid[t] + scale[t] * rest[t] for t in range(len(b))])
        store(resid, start, size, rest)
        if next_source is not None:
            pooled = [0.25 * p for p in pool_rows(resid, start, size, step)]
            store(next_source, start // 2, size // 2, pooled)

    for_chunks(height, first_pass, largest, part)
    for_chunks(height, second_pass, largest, part)


def descend_all(rows, sources, guess, weights, states, field, resid, largest, part):
    for level in range(LEVELS - 1):
        descend(
            level,
            rows >> level,
            weights[level],
            sources[level],
            guess if level == 0 else None,
            states[4 * level : 4 * level + 4],
            field,
            resid,
            weights[level + 1],
            sources[level + 1],
            largest,
            part,
        )


def pack_kernel(source, guess, weight, first_rows, second_rows, own_source, own_guess, own_weight, cross_ref, pair_ref):
    rows = source.shape[0]
    total = rows + 2 * HALO
    even_x, even_y = lax.axis_index("gx") % 2 == 0, lax.axis_index("gy") % 2 == 0
    own = (own_source, own_guess, own_weight)
    for k, block in enumerate((source, guess, weight)):
        clear_guards(own[k], total)
        above = jnp.where(even_x, first_rows[k], second_rows[k])
        below = jnp.where(even_x, second_rows[k], first_rows[k])
        for t in range(2):
            columns = slice(t * LANES, (t + 1) * LANES)
            own[k][t, GUARD : GUARD + HALO, :] = above[:, columns]
            own[k][t, GUARD + HALO : GUARD + HALO + rows, :] = block[:, columns]
            own[k][t, GUARD + HALO + rows : GUARD + total, :] = below[:, columns]
    piece = total // PIECES
    for k in range(3):
        sides = []
        for tile, first in ((0, 0), (1, LANES - HALO)):
            packed = jnp.zeros((piece, LANES), jnp.float32)
            for p in range(PIECES):
                part = own[k][tile, GUARD + p * piece : GUARD + (p + 1) * piece, :]
                lane = lane_of(part)
                here = (lane >= p * HALO) & (lane < (p + 1) * HALO)
                packed = jnp.where(here, roll(part, p * HALO - first), packed)
            sides.append(packed)
        west, east = sides
        cross_ref[k] = jnp.where(even_y, west, east)
        pair_ref[k] = jnp.where(even_y, east, west)


def body_kernel(source, guess, weight, *refs):
    states = refs[: 4 * (LEVELS - 1)]
    last_weight, last_source, field, resid, guess_in, *inner = refs[4 * (LEVELS - 1) :]
    rows = source.shape[1] - 2 * GUARD
    depth = LEVELS - 2
    weights = (guess_in, *inner[:depth], last_weight)
    sources = (source, *inner[depth:], last_source)
    weights[0][...] = weight[...]
    descend_all(rows, sources, guess, weights, states, field, resid, 112, 56)


def frame_kernel(own_source, own_guess, own_weight, from_cross, from_pair, body_weight, body_source, *refs):
    even = lax.axis_index("gy") % 2 == 0
    states, refs = refs[: 4 * (LEVELS - 1)], refs[4 * (LEVELS - 1) :]
    frame_source, ring_state, coarse_ref = refs[0], refs[1:5], refs[5]
    frame_guess, frame_weight, field, resid, ring_weight, ring_source, ring_field, ring_resid, *inner = refs[6:]
    rows = own_source.shape[1] - 2 * GUARD
    weights = (frame_weight, *inner[: LEVELS - 1])
    sources = (frame_source, *inner[LEVELS - 1 :])
    piece = rows // PIECES
    for k, (own, frame) in enumerate(
        ((own_source, frame_source), (own_guess, frame_guess), (own_weight, frame_weight))
    ):
        clear_guards(frame, rows)
        left = jnp.where(even, from_cross[k], from_pair[k])
        right = jnp.where(even, from_pair[k], from_cross[k])
        lane = lane_of(left)
        for p in range(PIECES):
            span = slice(GUARD + p * piece, GUARD + (p + 1) * piece)
            inside = jnp.where(lane < LANES // 2, roll(own[0, span, :], HALO), roll(own[1, span, :], -HALO))
            inside = jnp.where(lane < HALO, roll(left, -p * HALO), inside)
            frame[0, span, :] = jnp.where(lane >= LANES - HALO, roll(right, -(p + 1) * HALO), inside)
    descend_all(rows, sources, frame_guess, weights, states, field, resid, 280, 16)

    level = LEVELS - 1
    step, halo, height = 2**level, HALO >> level, rows >> level
    for body, frame, ring in (
        (body_weight, weights[level], ring_weight),
        (body_source, sources[level], ring_source),
    ):
        middle = load(body, 0, height)
        around = load(frame, 0, height)[0]
        lane = lane_of(around)
        ahead, back = roll(around, HALO), roll(around, -HALO)
        store(
            ring,
            0,
            height,
            [
                jnp.where(lane < 2 * step, back, middle[0]),
                jnp.where(lane >= LANES - 2 * step, ahead, middle[1]),
                jnp.where(lane < LANES // 2, ahead, back),
            ],
        )
    descend(level, height, ring_weight, ring_source, None, ring_state, ring_field, ring_resid, None, None, height, 16)

    coarse_rows = (height - 2 * halo) // 2
    dense = jnp.zeros((8, LANES), jnp.float32)
    lane = lane_of(dense)
    per_tile = LANES // 2**LEVELS
    pooled_b = pool_rows(ring_resid, halo, 2 * coarse_rows, step)
    pooled_w = pool_rows(ring_weight, halo, 2 * coarse_rows, step)
    index = (lane % per_tile) * 2**LEVELS
    place = lane // per_tile
    for g in range(coarse_rows // 8):
        for group, (values, factor) in enumerate(((pooled_b, 0.25), (pooled_w, 0.125))):
            for t in range(2):
                taken = jnp.take_along_axis(factor * values[t][8 * g : 8 * g + 8], index, axis=1)
                dense = jnp.where(place == 4 * g + 2 * group + t, taken, dense)
    coarse_ref[...] = jnp.broadcast_to(dense[None], coarse_ref.shape)


def coarse_solve(all_ref, width, groups):
    x, nx = lax.axis_index("gx"), lax.axis_size("gx")
    y, ny = lax.axis_index("gy"), lax.axis_size("gy")
    tiles = []
    for dx in (-1, 0, 1):
        for dy in (-1, 0, 1):
            inside = (x + dx >= 0) & (x + dx < nx) & (y + dy >= 0) & (y + dy < ny)
            tile = all_ref[jnp.where(inside, (x + dx) * ny + y + dy, 0)]
            tiles.append(jnp.where(inside, tile, 0.0))
    lane = lane_of(tiles[0])
    blocks = [(0, g) for g in range(groups - TALL // 8, groups)]
    blocks += [(1, g) for g in range(groups)] + [(2, g) for g in range(TALL // 8)]
    b, w = [], []
    for band, g in blocks:
        b_rows = w_rows = jnp.zeros_like(tiles[0])
        for side in range(3):
            tile = tiles[3 * band + side]
            here = (lane >= side * width) & (lane < (side + 1) * width)
            b_rows = jnp.where(here, roll(tile, (side - 2 * g) * width), b_rows)
            w_rows = jnp.where(here, roll(tile, (side - 2 * g - 1) * width), w_rows)
        b.append(b_rows)
        w.append(w_rows)
    b, w = jnp.concatenate(b, axis=0), jnp.concatenate(w, axis=0)

    def north_of(x):
        return pltpu.roll(x, 1, 0)

    def south_of(x):
        return pltpu.roll(x, x.shape[0] - 1, 0)

    c_west = jnp.minimum(w, roll(w, 1))
    c_north = jnp.minimum(w, north_of(w))
    c_east, c_south = roll(c_west, -1), south_of(c_north)
    scale = scale_of(c_north + c_south + c_west + c_east)
    first = scale * b

    def sweep(_, e):
        applied = (
            damping * e
            + (c_west * (e - roll(e, 1)) + c_east * (e - roll(e, -1)))
            + (c_north * (e - north_of(e)) + c_south * (e - south_of(e)))
        )
        return e + (first - scale * applied)

    return lax.fori_loop(0, SWEEPS - 1, sweep, first)


def up_kernel(all_ref, own_source, frame_source, *refs):
    count = 4 * (LEVELS - 1)
    body_state, frame_state, ring_state = refs[:count], refs[count : 2 * count], refs[2 * count : 2 * count + 4]
    out_ref, resid_ref = refs[2 * count + 4 : 2 * count + 6]
    ring_pe, body_final, frame_final, sems, *inner = refs[2 * count + 6 :]
    outs, inner = inner[:2], inner[2:]
    body_pe, frame_pe = inner[: LEVELS - 1], inner[LEVELS - 1 :]
    rows = out_ref.shape[0] + 2 * HALO
    width = out_ref.shape[1] >> LEVELS
    e = coarse_solve(all_ref, width, (out_ref.shape[0] >> LEVELS) // 8)

    level = LEVELS - 1
    step, halo, height = 2**level, HALO >> level, rows >> level
    coarse_rows = (height - 2 * halo) // 2
    picked = e[TALL - 8 : TALL + coarse_rows + 8]
    lane = lane_of(picked)
    for t in range(3):
        group = (lane + t * LANES) // 2**LEVELS
        if t == 2:
            group = jnp.where(lane < LANES // 2, group, group - 3 * LANES // 2**LEVELS)
        taken = jnp.take_along_axis(picked, jnp.clip(group + width, 0, LANES - 1), axis=1)[7 : 7 + coarse_rows + 2]
        ring_pe[t, 0 : 2 * GUARD, :] = jnp.zeros((2 * GUARD, LANES), jnp.float32)
        ring_pe[t, height : height + 2 * GUARD, :] = jnp.zeros((2 * GUARD, LANES), jnp.float32)
        ring_pe[t, pl.ds(GUARD + halo - 2, coarse_rows + 2, stride=2), :] = taken
        ring_pe[t, pl.ds(GUARD + halo - 1, coarse_rows + 2, stride=2), :] = taken

    def climbed(pe, state, start, size, step):
        mid, applied = applied_to(pe, state[:2], start, size, step)
        scale, smooth = load(state[2], start, size), load(state[3], start, size)
        return [smooth[t] + (mid[t] - scale[t] * applied[t]) for t in range(len(mid))]

    def climb_ring(start, size, level=level, step=step):
        ring = climbed(ring_pe, ring_state, start, size, step)
        lane = lane_of(ring[0])
        around = jnp.where(
            lane < LANES // 2,
            jnp.where(lane < HALO, roll(ring[2], HALO), roll(ring[0], HALO)),
            jnp.where(lane < LANES - HALO, roll(ring[1], -HALO), roll(ring[2], -HALO)),
        )
        store_twice(body_pe[level - 1], start, size, ring[:2])
        store_twice(frame_pe[level - 1], start, size, [around])

    for_chunks(height, climb_ring, height, height)

    for level in range(LEVELS - 2, -1, -1):
        step, height = 2**level, rows >> level
        for pes, states, final, largest, part in (
            (body_pe, body_state, body_final, 112, 56),
            (frame_pe, frame_state, frame_final, 280, 140),
        ):
            state = states[4 * level : 4 * level + 4]
            clear_guards(pes[level], height)

            def climb(start, size, level=level, step=step, pes=pes, state=state, final=final):
                value = climbed(pes[level], state, start, size, step)
                if level == 0:
                    store(final, start, size, value)
                else:
                    store_twice(pes[level - 1], start, size, value)

            for_chunks(height, climb, largest, part)

    def last(start, size):
        base = start + HALO
        body = applied_to(body_final, body_state[:2], base, size, 1)
        frame = applied_to(frame_final, frame_state[:2], base, size, 1)
        b, b_frame = load(own_source, base, size), load(frame_source, base, size)
        body = (body[0], [b[t] - body[1][t] for t in range(2)])
        frame = (frame[0][0], b_frame[0] - frame[1][0])
        lane = lane_of(frame[0])
        near = HALO - 4
        span = pl.ds(start, size)
        for ref, middle, around in ((outs[0], body[0], frame[0]), (outs[1], body[1], frame[1])):
            ref[span, :LANES] = jnp.where(lane < near, roll(around, -HALO), middle[0])
            ref[span, LANES:] = jnp.where(lane >= LANES - near, roll(around, HALO), middle[1])

    parts = sems.shape[0] // 2
    size = out_ref.shape[0] // parts

    def copies(p):
        span = pl.ds(p * size, size)
        return [
            pltpu.make_async_copy(outs[k].at[span], ref.at[span], sems.at[2 * p + k])
            for k, ref in enumerate((out_ref, resid_ref))
        ]

    def finish(p, carry):
        for_parts(p * size, size, last, 64)
        for copy in copies(p):
            copy.start()
        return carry

    lax.fori_loop(0, parts, finish, 0)
    for p in range(parts):
        for copy in copies(p):
            copy.wait()


def call(kernel, out_shape, scratch, flops, moved, **more):
    return pl.pallas_call(
        kernel,
        out_shape=out_shape,
        scratch_shapes=scratch,
        compiler_params=pltpu.CompilerParams(vmem_limit_bytes=VMEM_LIMIT),
        cost_estimate=pl.CostEstimate(flops=flops, bytes_accessed=moved, transcendentals=0),
        **more,
    )


def swap(x, axis, first):
    pairs = [(i, i + 1) for i in range(first, lax.axis_size(axis) - 1, 2)]
    return lax.ppermute(x, axis, pairs + [(j, i) for i, j in pairs])


def local(rhs, pressure, wet_mask, bathy_class):
    rows, columns = rhs.shape
    cells = rows * columns
    total = rows + 2 * HALO
    levels = range(LEVELS - 1)

    def shape(tiles, level):
        return (tiles, (total >> level) + 2 * GUARD, LANES)

    def out(*dims):
        return jax.ShapeDtypeStruct(dims, jnp.float32)

    def vmem(tiles, level):
        return pltpu.VMEM(shape(tiles, level), jnp.float32)

    def fields(r, p, m, c):
        wet = m.astype(jnp.float32)
        return wet * r, wet * p, wet * (1.0 + 0.5 * c.astype(jnp.float32))

    given = (rhs, pressure, wet_mask, bathy_class)

    def edge(start):
        return jnp.stack(fields(*(lax.dynamic_slice_in_dim(x, start, HALO, axis=0) for x in given)))

    even = lax.axis_index("gx") % 2 == 0
    first_rows = swap(edge(jnp.where(even, 0, rows - HALO)), "gx", 1)
    second_rows = swap(edge(jnp.where(even, rows - HALO, 0)), "gx", 0)
    piece = total // PIECES
    own_shapes = [out(*shape(2, 0))] * 3
    *own, to_cross, to_pair = call(
        pack_kernel, (*own_shapes, out(3, piece, LANES), out(3, piece, LANES)), (), 10 * cells, 10 * cells
    )(*fields(*given), first_rows, second_rows)
    from_cross = swap(to_cross, "gy", 1)
    from_pair = swap(to_pair, "gy", 0)

    state_count = 4 * (LEVELS - 1)
    *body_state, body_weight, body_source = call(
        body_kernel,
        [out(*shape(2, level)) for level in levels for _ in range(4)] + [out(*shape(2, LEVELS - 1))] * 2,
        [vmem(2, 0)] * 3 + [vmem(2, level) for level in levels[1:]] * 2,
        100 * cells,
        40 * cells,
    )(*own)
    devices = lax.axis_size("gx") * lax.axis_size("gy")
    ring = LEVELS - 1
    *state, coarse = call(
        frame_kernel,
        [out(*shape(1, level)) for level in levels for _ in range(4)]
        + [out(*shape(1, 0))]
        + [out(*shape(3, ring))] * 4
        + [out(devices, 8, LANES)],
        [vmem(1, 0)] * 4 + [vmem(3, ring)] * 4 + [vmem(1, level) for level in range(1, LEVELS)] * 2,
        50 * cells,
        20 * cells,
    )(*own, from_cross, from_pair, body_weight, body_source)
    frame_state, frame_source, ring_state = state[:state_count], state[state_count], state[state_count + 1 :]
    gathered = lax.all_to_all(coarse, ("gx", "gy"), 0, 0)
    return call(
        up_kernel,
        (out(rows, columns), out(rows, columns)),
        [vmem(3, ring), vmem(2, 0), vmem(1, 0), pltpu.SemaphoreType.DMA((8,))]
        + [pltpu.VMEM((rows, columns), jnp.float32)] * 2
        + [vmem(2, level) for level in levels]
        + [vmem(1, level) for level in levels],
        60 * cells,
        40 * cells,
        out_specs=[pl.BlockSpec(memory_space=pl.ANY)] * 2,
    )(gathered, own[0], frame_source, *body_state, *frame_state, *ring_state)


def solution(mesh):
    placed = (P("gx", "gy"), P("gx", "gy"), P("gx", "gy"), P("gx", "gy"))
    return jax.shard_map(
        local, mesh=mesh, in_specs=placed, out_specs=(P("gx", "gy"), P("gx", "gy")), check_vma=False
    )
```

```python
import jax
import jax.numpy as jnp
from jax import lax
from jax.experimental import pallas as pl
from jax.experimental.pallas import tpu as pltpu
from jax.sharding import PartitionSpec as P

LEVELS = 4
SWEEPS = 12

damping = 0.01
relaxation = 0.8

HALO = 24
LANES = 128
INNER = LANES // 2 - HALO
GUARD = 8
PIECES = 5
TALL = 16
VMEM_LIMIT = 40 * 1024 * 1024


def lane_of(x):
    return lax.broadcasted_iota(jnp.int32, x.shape, x.ndim - 1)


def roll(x, amount):
    amount %= LANES
    return x if amount == 0 else pltpu.roll(x, amount, x.ndim - 1)


def from_west(tiles, step):
    moved = [roll(t, step) for t in tiles]
    if len(tiles) == 1:
        return moved
    edge = lane_of(tiles[0]) < step
    return [jnp.where(edge, moved[i - 1], moved[i]) for i in range(len(tiles))]


def from_east(tiles, step):
    moved = [roll(t, -step) for t in tiles]
    count = len(tiles)
    if count == 1:
        return moved
    edge = lane_of(tiles[0]) >= LANES - step
    return [jnp.where(edge, moved[(i + 1) % count], moved[i]) for i in range(count)]


def lane_pairs(x, step):
    first = (lane_of(x) // step) % 2 == 0
    return x + jnp.where(first, roll(x, -step), roll(x, step))


def for_parts(start, size, body, part):
    for offset in range(0, size, part):
        body(start + offset, min(part, size - offset))


def for_chunks(rows, body, largest, part):
    sizes = [size for size in range(8, largest + 1, 8) if rows % size == 0]
    if rows <= largest or not sizes:
        for_parts(0, rows, body, part)
        return

    def step(i, carry):
        for_parts(i * sizes[-1], sizes[-1], body, part)
        return carry

    lax.fori_loop(0, rows // sizes[-1], step, 0)


def load(ref, start, size):
    return [ref[t, pl.ds(GUARD + start, size), :] for t in range(ref.shape[0])]


def store(ref, start, size, tiles):
    for t, tile in enumerate(tiles):
        ref[t, pl.ds(GUARD + start, size), :] = tile


def store_twice(ref, start, size, tiles):
    for t, tile in enumerate(tiles):
        ref[t, pl.ds(GUARD + 2 * start, size, stride=2), :] = tile
        ref[t, pl.ds(GUARD + 2 * start + 1, size, stride=2), :] = tile


def clear_guards(ref, rows):
    zeros = jnp.zeros((GUARD, LANES), jnp.float32)
    for t in range(ref.shape[0]):
        ref[t, 0:GUARD, :] = zeros
        ref[t, GUARD + rows : 2 * GUARD + rows, :] = zeros


def operator(mid, north, south, c_west, c_north, c_south, step):
    west = from_west(mid, step)
    tiles = range(len(mid))
    flux = [c_west[t] * (mid[t] - west[t]) for t in tiles]
    out = from_east(flux, step)
    return [
        damping * mid[t]
        + (flux[t] - out[t])
        + (c_north[t] * (mid[t] - north[t]) + c_south[t] * (mid[t] - south[t]))
        for t in tiles
    ]


def applied_to(ref, coeffs, start, size, step):
    c_west_ref, c_north_ref = coeffs
    mid = load(ref, start, size)
    north, south = load(ref, start - 1, size), load(ref, start + 1, size)
    c_west, c_north = load(c_west_ref, start, size), load(c_north_ref, start, size)
    return mid, operator(mid, north, south, c_west, c_north, load(c_north_ref, start + 1, size), step)


def pool_rows(ref, start, size, step):
    out = []
    for t in range(ref.shape[0]):
        even = ref[t, pl.ds(GUARD + start, size // 2, stride=2), :]
        odd = ref[t, pl.ds(GUARD + start + 1, size // 2, stride=2), :]
        out.append(lane_pairs(even + odd, step))
    return out


def descend(level, height, weight, source, guess, state, field, resid, next_weight, next_source, largest, part):
    step = 2**level
    c_west_ref, c_north_ref, scale_ref, smooth_ref = state
    for ref in (weight, field, c_north_ref):
        clear_guards(ref, height)

    def first_pass(start, size):
        w, w_north, w_south = (load(weight, start + k, size) for k in (0, -1, 1))
        c_north = [jnp.minimum(a, b) for a, b in zip(w, w_north)]
        c_south = [jnp.minimum(a, b) for a, b in zip(w, w_south)]
        c_west = [jnp.minimum(a, b) for a, b in zip(w, from_west(w, step))]
        c_east = from_east(c_west, step)
        scale = [
            relaxation / (damping + c_north[t] + c_south[t] + c_west[t] + c_east[t]) for t in range(len(w))
        ]
        store(c_north_ref, start, size, c_north)
        store(c_west_ref, start, size, c_west)
        store(scale_ref, start, size, scale)
        value = load(source, start, size)
        if guess is not None:
            mid, north, south = (load(guess, start + k, size) for k in (0, -1, 1))
            applied = operator(mid, north, south, c_west, c_north, c_south, step)
            value = [value[t] - applied[t] for t in range(len(w))]
        value = [scale[t] * value[t] for t in range(len(w))]
        if guess is not None:
            value = [mid[t] + value[t] for t in range(len(w))]
        store(field, start, size, value)
        if next_weight is not None:
            pooled = [0.125 * p for p in pool_rows(weight, start, size, step)]
            store(next_weight, start // 2, size // 2, pooled)

    def second_pass(start, size):
        mid, applied = applied_to(field, (c_west_ref, c_north_ref), start, size, step)
        b, scale = load(source, start, size), load(scale_ref, start, size)
        rest = [b[t] - applied[t] for t in range(len(b))]
        store(smooth_ref, start, size, [mid[t] + scale[t] * rest[t] for t in range(len(b))])
        store(resid, start, size, rest)
        if next_source is not None:
            pooled = [0.25 * p for p in pool_rows(resid, start, size, step)]
            store(next_source, start // 2, size // 2, pooled)

    for_chunks(height, first_pass, largest, part)
    for_chunks(height, second_pass, largest, part)


def descend_all(rows, sources, guess, weights, states, field, resid, largest, part):
    for level in range(LEVELS - 1):
        descend(
            level,
            rows >> level,
            weights[level],
            sources[level],
            guess if level == 0 else None,
            states[4 * level : 4 * level + 4],
            field,
            resid,
            weights[level + 1],
            sources[level + 1],
            largest,
            part,
        )


def pack_kernel(source, guess, weight, first_rows, second_rows, own_source, own_guess, own_weight, cross_ref, pair_ref):
    rows = source.shape[0]
    total = rows + 2 * HALO
    even_x, even_y = lax.axis_index("gx") % 2 == 0, lax.axis_index("gy") % 2 == 0
    own = (own_source, own_guess, own_weight)
    for k, block in enumerate((source, guess, weight)):
        clear_guards(own[k], total)
        above = jnp.where(even_x, first_rows[k], second_rows[k])
        below = jnp.where(even_x, second_rows[k], first_rows[k])
        for t in range(2):
            columns = slice(t * LANES, (t + 1) * LANES)
            own[k][t, GUARD : GUARD + HALO, :] = above[:, columns]
            own[k][t, GUARD + HALO : GUARD + HALO + rows, :] = block[:, columns]
            own[k][t, GUARD + HALO + rows : GUARD + total, :] = below[:, columns]
    piece = total // PIECES
    for k in range(3):
        sides = []
        for tile, first in ((0, 0), (1, LANES - HALO)):
            packed = jnp.zeros((piece, LANES), jnp.float32)
            for p in range(PIECES):
                part = own[k][tile, GUARD + p * piece : GUARD + (p + 1) * piece, :]
                lane = lane_of(part)
                here = (lane >= p * HALO) & (lane < (p + 1) * HALO)
                packed = jnp.where(here, roll(part, p * HALO - first), packed)
            sides.append(packed)
        west, east = sides
        cross_ref[k] = jnp.where(even_y, west, east)
        pair_ref[k] = jnp.where(even_y, east, west)


def body_kernel(source, guess, weight, *refs):
    states = refs[: 4 * (LEVELS - 1)]
    last_weight, last_source, field, resid, guess_in, *inner = refs[4 * (LEVELS - 1) :]
    rows = source.shape[1] - 2 * GUARD
    depth = LEVELS - 2
    weights = (guess_in, *inner[:depth], last_weight)
    sources = (source, *inner[depth:], last_source)
    weights[0][...] = weight[...]
    descend_all(rows, sources, guess, weights, states, field, resid, 112, 16)


def frame_kernel(own_source, own_guess, own_weight, from_cross, from_pair, body_weight, body_source, *refs):
    even = lax.axis_index("gy") % 2 == 0
    states, refs = refs[: 4 * (LEVELS - 1)], refs[4 * (LEVELS - 1) :]
    frame_source, ring_state, coarse_ref = refs[0], refs[1:5], refs[5]
    frame_guess, frame_weight, field, resid, ring_weight, ring_source, ring_field, ring_resid, *inner = refs[6:]
    rows = own_source.shape[1] - 2 * GUARD
    weights = (frame_weight, *inner[: LEVELS - 1])
    sources = (frame_source, *inner[LEVELS - 1 :])
    piece = rows // PIECES
    for k, (own, frame) in enumerate(
        ((own_source, frame_source), (own_guess, frame_guess), (own_weight, frame_weight))
    ):
        clear_guards(frame, rows)
        left = jnp.where(even, from_cross[k], from_pair[k])
        right = jnp.where(even, from_pair[k], from_cross[k])
        lane = lane_of(left)
        for p in range(PIECES):
            span = slice(GUARD + p * piece, GUARD + (p + 1) * piece)
            inside = jnp.where(lane < LANES // 2, roll(own[0, span, :], HALO), roll(own[1, span, :], -HALO))
            inside = jnp.where(lane < HALO, roll(left, -p * HALO), inside)
            frame[0, span, :] = jnp.where(lane >= LANES - HALO, roll(right, -(p + 1) * HALO), inside)
    descend_all(rows, sources, frame_guess, weights, states, field, resid, 280, 280)

    level = LEVELS - 1
    step, halo, height = 2**level, HALO >> level, rows >> level
    for body, frame, ring in (
        (body_weight, weights[level], ring_weight),
        (body_source, sources[level], ring_source),
    ):
        middle = load(body, 0, height)
        around = load(frame, 0, height)[0]
        lane = lane_of(around)
        ahead, back = roll(around, HALO), roll(around, -HALO)
        store(
            ring,
            0,
            height,
            [
                jnp.where(lane < 2 * step, back, middle[0]),
                jnp.where(lane >= LANES - 2 * step, ahead, middle[1]),
                jnp.where(lane < LANES // 2, ahead, back),
            ],
        )
    descend(level, height, ring_weight, ring_source, None, ring_state, ring_field, ring_resid, None, None, height, 16)

    coarse_rows = (height - 2 * halo) // 2
    dense = jnp.zeros((8, LANES), jnp.float32)
    lane = lane_of(dense)
    per_tile = LANES // 2**LEVELS
    pooled_b = pool_rows(ring_resid, halo, 2 * coarse_rows, step)
    pooled_w = pool_rows(ring_weight, halo, 2 * coarse_rows, step)
    index = (lane % per_tile) * 2**LEVELS
    place = lane // per_tile
    for g in range(coarse_rows // 8):
        for group, (values, factor) in enumerate(((pooled_b, 0.25), (pooled_w, 0.125))):
            for t in range(2):
                taken = jnp.take_along_axis(factor * values[t][8 * g : 8 * g + 8], index, axis=1)
                dense = jnp.where(place == 4 * g + 2 * group + t, taken, dense)
    coarse_ref[...] = jnp.broadcast_to(dense[None], coarse_ref.shape)


def coarse_solve(all_ref, width, groups):
    x, nx = lax.axis_index("gx"), lax.axis_size("gx")
    y, ny = lax.axis_index("gy"), lax.axis_size("gy")
    tiles = []
    for dx in (-1, 0, 1):
        for dy in (-1, 0, 1):
            inside = (x + dx >= 0) & (x + dx < nx) & (y + dy >= 0) & (y + dy < ny)
            tile = all_ref[jnp.where(inside, y + dy, 0), jnp.where(inside, x + dx, 0)]
            tiles.append(jnp.where(inside, tile, 0.0))
    lane = lane_of(tiles[0])
    blocks = [(0, g) for g in range(groups - TALL // 8, groups)]
    blocks += [(1, g) for g in range(groups)] + [(2, g) for g in range(TALL // 8)]
    b, w = [], []
    for band, g in blocks:
        b_rows = w_rows = jnp.zeros_like(tiles[0])
        for side in range(3):
            tile = tiles[3 * band + side]
            here = (lane >= side * width) & (lane < (side + 1) * width)
            b_rows = jnp.where(here, roll(tile, (side - 2 * g) * width), b_rows)
            w_rows = jnp.where(here, roll(tile, (side - 2 * g - 1) * width), w_rows)
        b.append(b_rows)
        w.append(w_rows)
    b, w = jnp.concatenate(b, axis=0), jnp.concatenate(w, axis=0)

    def north_of(x):
        return pltpu.roll(x, 1, 0)

    def south_of(x):
        return pltpu.roll(x, x.shape[0] - 1, 0)

    c_west = jnp.minimum(w, roll(w, 1))
    c_north = jnp.minimum(w, north_of(w))
    c_east, c_south = roll(c_west, -1), south_of(c_north)
    scale = relaxation / (damping + c_north + c_south + c_west + c_east)
    first = scale * b

    def sweep(_, e):
        applied = (
            damping * e
            + (c_west * (e - roll(e, 1)) + c_east * (e - roll(e, -1)))
            + (c_north * (e - north_of(e)) + c_south * (e - south_of(e)))
        )
        return e + (first - scale * applied)

    return lax.fori_loop(0, SWEEPS - 1, sweep, first)


def up_kernel(all_ref, own_source, frame_source, *refs):
    count = 4 * (LEVELS - 1)
    body_state, frame_state, ring_state = refs[:count], refs[count : 2 * count], refs[2 * count : 2 * count + 4]
    out_ref, resid_ref = refs[2 * count + 4 : 2 * count + 6]
    ring_pe, body_final, frame_final, sems, *inner = refs[2 * count + 6 :]
    outs, inner = inner[:2], inner[2:]
    body_pe, frame_pe = inner[: LEVELS - 1], inner[LEVELS - 1 :]
    rows = out_ref.shape[0] + 2 * HALO
    width = out_ref.shape[1] >> LEVELS
    e = coarse_solve(all_ref, width, (out_ref.shape[0] >> LEVELS) // 8)

    level = LEVELS - 1
    step, halo, height = 2**level, HALO >> level, rows >> level
    coarse_rows = (height - 2 * halo) // 2
    picked = e[TALL - 8 : TALL + coarse_rows + 8]
    lane = lane_of(picked)
    for t in range(3):
        group = (lane + t * LANES) // 2**LEVELS
        if t == 2:
            group = jnp.where(lane < LANES // 2, group, group - 3 * LANES // 2**LEVELS)
        taken = jnp.take_along_axis(picked, jnp.clip(group + width, 0, LANES - 1), axis=1)[7 : 7 + coarse_rows + 2]
        ring_pe[t, 0 : 2 * GUARD, :] = jnp.zeros((2 * GUARD, LANES), jnp.float32)
        ring_pe[t, height : height + 2 * GUARD, :] = jnp.zeros((2 * GUARD, LANES), jnp.float32)
        ring_pe[t, pl.ds(GUARD + halo - 2, coarse_rows + 2, stride=2), :] = taken
        ring_pe[t, pl.ds(GUARD + halo - 1, coarse_rows + 2, stride=2), :] = taken

    def climbed(pe, state, start, size, step):
        mid, applied = applied_to(pe, state[:2], start, size, step)
        scale, smooth = load(state[2], start, size), load(state[3], start, size)
        return [smooth[t] + (mid[t] - scale[t] * applied[t]) for t in range(len(mid))]

    def climb_ring(start, size, level=level, step=step):
        ring = climbed(ring_pe, ring_state, start, size, step)
        lane = lane_of(ring[0])
        around = jnp.where(
            lane < LANES // 2,
            jnp.where(lane < HALO, roll(ring[2], HALO), roll(ring[0], HALO)),
            jnp.where(lane < LANES - HALO, roll(ring[1], -HALO), roll(ring[2], -HALO)),
        )
        store_twice(body_pe[level - 1], start, size, ring[:2])
        store_twice(frame_pe[level - 1], start, size, [around])

    for_chunks(height, climb_ring, height, 16)

    for level in range(LEVELS - 2, -1, -1):
        step, height = 2**level, rows >> level
        for pes, states, final, largest, part in (
            (body_pe, body_state, body_final, 112, 16),
            (frame_pe, frame_state, frame_final, 280, 32),
        ):
            state = states[4 * level : 4 * level + 4]
            clear_guards(pes[level], height)

            def climb(start, size, level=level, step=step, pes=pes, state=state, final=final):
                value = climbed(pes[level], state, start, size, step)
                if level == 0:
                    store(final, start, size, value)
                else:
                    store_twice(pes[level - 1], start, size, value)

            for_chunks(height, climb, largest, part)

    def last(start, size):
        base = start + HALO
        body = applied_to(body_final, body_state[:2], base, size, 1)
        frame = applied_to(frame_final, frame_state[:2], base, size, 1)
        b, b_frame = load(own_source, base, size), load(frame_source, base, size)
        body = (body[0], [b[t] - body[1][t] for t in range(2)])
        frame = (frame[0][0], b_frame[0] - frame[1][0])
        lane = lane_of(frame[0])
        near = HALO - 4
        span = pl.ds(start, size)
        for ref, middle, around in ((outs[0], body[0], frame[0]), (outs[1], body[1], frame[1])):
            ref[span, :LANES] = jnp.where(lane < near, roll(around, -HALO), middle[0])
            ref[span, LANES:] = jnp.where(lane >= LANES - near, roll(around, HALO), middle[1])

    parts = sems.shape[0] // 2
    size = out_ref.shape[0] // parts

    def copies(p):
        span = pl.ds(p * size, size)
        return [
            pltpu.make_async_copy(outs[k].at[span], ref.at[span], sems.at[2 * p + k])
            for k, ref in enumerate((out_ref, resid_ref))
        ]

    def finish(p, carry):
        for_parts(p * size, size, last, 16)
        for copy in copies(p):
            copy.start()
        return carry

    lax.fori_loop(0, parts, finish, 0)
    for p in range(parts):
        for copy in copies(p):
            copy.wait()


def call(kernel, out_shape, scratch, flops, moved, **more):
    return pl.pallas_call(
        kernel,
        out_shape=out_shape,
        scratch_shapes=scratch,
        compiler_params=pltpu.CompilerParams(vmem_limit_bytes=VMEM_LIMIT),
        cost_estimate=pl.CostEstimate(flops=flops, bytes_accessed=moved, transcendentals=0),
        **more,
    )


def swap(x, axis, first):
    pairs = [(i, i + 1) for i in range(first, lax.axis_size(axis) - 1, 2)]
    return lax.ppermute(x, axis, pairs + [(j, i) for i, j in pairs])


def local(rhs, pressure, wet_mask, bathy_class):
    rows, columns = rhs.shape
    cells = rows * columns
    total = rows + 2 * HALO
    levels = range(LEVELS - 1)

    def shape(tiles, level):
        return (tiles, (total >> level) + 2 * GUARD, LANES)

    def out(*dims):
        return jax.ShapeDtypeStruct(dims, jnp.float32)

    def vmem(tiles, level):
        return pltpu.VMEM(shape(tiles, level), jnp.float32)

    def fields(r, p, m, c):
        wet = m.astype(jnp.float32)
        return wet * r, wet * p, wet * (1.0 + 0.5 * c.astype(jnp.float32))

    given = (rhs, pressure, wet_mask, bathy_class)

    def edge(start):
        return jnp.stack(fields(*(lax.dynamic_slice_in_dim(x, start, HALO, axis=0) for x in given)))

    even = lax.axis_index("gx") % 2 == 0
    first_rows = swap(edge(jnp.where(even, 0, rows - HALO)), "gx", 1)
    second_rows = swap(edge(jnp.where(even, rows - HALO, 0)), "gx", 0)
    piece = total // PIECES
    own_shapes = [out(*shape(2, 0))] * 3
    *own, to_cross, to_pair = call(
        pack_kernel, (*own_shapes, out(3, piece, LANES), out(3, piece, LANES)), (), 10 * cells, 10 * cells
    )(*fields(*given), first_rows, second_rows)
    from_cross = swap(to_cross, "gy", 1)
    from_pair = swap(to_pair, "gy", 0)

    state_count = 4 * (LEVELS - 1)
    *body_state, body_weight, body_source = call(
        body_kernel,
        [out(*shape(2, level)) for level in levels for _ in range(4)] + [out(*shape(2, LEVELS - 1))] * 2,
        [vmem(2, 0)] * 3 + [vmem(2, level) for level in levels[1:]] * 2,
        100 * cells,
        40 * cells,
    )(*own)
    ring = LEVELS - 1
    *state, coarse = call(
        frame_kernel,
        [out(*shape(1, level)) for level in levels for _ in range(4)]
        + [out(*shape(1, 0))]
        + [out(*shape(3, ring))] * 4
        + [out(lax.axis_size("gx"), 8, LANES)],
        [vmem(1, 0)] * 4 + [vmem(3, ring)] * 4 + [vmem(1, level) for level in range(1, LEVELS)] * 2,
        50 * cells,
        20 * cells,
    )(*own, from_cross, from_pair, body_weight, body_source)
    frame_state, frame_source, ring_state = state[:state_count], state[state_count], state[state_count + 1 :]
    places = lax.axis_size("gy")
    line = lax.all_to_all(coarse, "gx", 0, 0)
    gathered = lax.all_to_all(jnp.broadcast_to(line, (places, *line.shape)), "gy", 0, 0)
    return call(
        up_kernel,
        (out(rows, columns), out(rows, columns)),
        [vmem(3, ring), vmem(2, 0), vmem(1, 0), pltpu.SemaphoreType.DMA((8,))]
        + [pltpu.VMEM((rows, columns), jnp.float32)] * 2
        + [vmem(2, level) for level in levels]
        + [vmem(1, level) for level in levels],
        60 * cells,
        40 * cells,
        out_specs=[pl.BlockSpec(memory_space=pl.ANY)] * 2,
    )(gathered, own[0], frame_source, *body_state, *frame_state, *ring_state)


def solution(mesh):
    placed = (P("gx", "gy"), P("gx", "gy"), P("gx", "gy"), P("gx", "gy"))
    return jax.shard_map(
        local, mesh=mesh, in_specs=placed, out_specs=(P("gx", "gy"), P("gx", "gy")), check_vma=False
    )
```

```python
import jax
import jax.numpy as jnp
from jax import lax
from jax.experimental import pallas as pl
from jax.experimental.pallas import tpu as pltpu
from jax.sharding import PartitionSpec as P

LEVELS = 4
SWEEPS = 12

damping = 0.01
relaxation = 0.8

HALO = 24
LANES = 128
INNER = LANES // 2 - HALO
GUARD = 8
PIECES = 5
TALL = 16
VMEM_LIMIT = 40 * 1024 * 1024


def lane_of(x):
    return lax.broadcasted_iota(jnp.int32, x.shape, x.ndim - 1)


def roll(x, amount):
    amount %= LANES
    return x if amount == 0 else pltpu.roll(x, amount, x.ndim - 1)


def from_west(tiles, step):
    moved = [roll(t, step) for t in tiles]
    if len(tiles) == 1:
        return moved
    edge = lane_of(tiles[0]) < step
    return [jnp.where(edge, moved[i - 1], moved[i]) for i in range(len(tiles))]


def from_east(tiles, step):
    moved = [roll(t, -step) for t in tiles]
    count = len(tiles)
    if count == 1:
        return moved
    edge = lane_of(tiles[0]) >= LANES - step
    return [jnp.where(edge, moved[(i + 1) % count], moved[i]) for i in range(count)]


def spread(tiles, step):
    second = (lane_of(tiles[0]) // step) % 2 == 1
    return [jnp.where(second, roll(t, step), t) for t in tiles]


def for_parts(start, size, body, part):
    for offset in range(0, size, part):
        body(start + offset, min(part, size - offset))


def for_chunks(rows, body, largest, part):
    sizes = [size for size in range(8, largest + 1, 8) if rows % size == 0]
    if rows <= largest or not sizes:
        for_parts(0, rows, body, part)
        return

    def step(i, carry):
        for_parts(i * sizes[-1], sizes[-1], body, part)
        return carry

    lax.fori_loop(0, rows // sizes[-1], step, 0)


def load(ref, start, size):
    return [ref[t, pl.ds(GUARD + start, size), :] for t in range(ref.shape[0])]


def store(ref, start, size, tiles):
    for t, tile in enumerate(tiles):
        ref[t, pl.ds(GUARD + start, size), :] = tile


def store_twice(ref, start, size, tiles):
    for t, tile in enumerate(tiles):
        ref[t, pl.ds(GUARD + 2 * start, size, stride=2), :] = tile
        ref[t, pl.ds(GUARD + 2 * start + 1, size, stride=2), :] = tile


def clear_guards(ref, rows):
    zeros = jnp.zeros((GUARD, LANES), jnp.float32)
    for t in range(ref.shape[0]):
        ref[t, 0:GUARD, :] = zeros
        ref[t, GUARD + rows : 2 * GUARD + rows, :] = zeros


def beside(mid, north, south, c_west, c_north, c_south, step):
    west = from_west(mid, step)
    east = from_east([c * m for c, m in zip(c_west, mid)], step)
    return [
        (c_west[t] * west[t] + east[t]) + (c_north[t] * north[t] + c_south[t] * south[t]) for t in range(len(mid))
    ]


def beside_of(ref, coeffs, start, size, step):
    c_west_ref, c_north_ref = coeffs
    mid = load(ref, start, size)
    north, south = load(ref, start - 1, size), load(ref, start + 1, size)
    c_west, c_north = load(c_west_ref, start, size), load(c_north_ref, start, size)
    return mid, beside(mid, north, south, c_west, c_north, load(c_north_ref, start + 1, size), step)


def pool_rows(ref, start, size, step):
    out = []
    for t in range(ref.shape[0]):
        even = ref[t, pl.ds(GUARD + start, size // 2, stride=2), :]
        odd = ref[t, pl.ds(GUARD + start + 1, size // 2, stride=2), :]
        both = even + odd
        out.append(both + roll(both, -step))
    return out


def descend(level, height, weight, source, guess, state, diagonal_ref, field, resid, next_weight, next_source, largest, part):
    step = 2**level
    c_west_ref, c_north_ref, scale_ref, smooth_ref = state
    for ref in (weight, field, c_north_ref):
        clear_guards(ref, height)

    def first_pass(start, size):
        w, w_north, w_south = (load(weight, start + k, size) for k in (0, -1, 1))
        c_north = [jnp.minimum(a, b) for a, b in zip(w, w_north)]
        c_south = [jnp.minimum(a, b) for a, b in zip(w, w_south)]
        c_west = [jnp.minimum(a, b) for a, b in zip(w, from_west(w, step))]
        c_east = from_east(c_west, step)
        diagonal = [damping + c_north[t] + c_south[t] + c_west[t] + c_east[t] for t in range(len(w))]
        scale = [relaxation / d for d in diagonal]
        store(c_north_ref, start, size, c_north)
        store(c_west_ref, start, size, c_west)
        store(scale_ref, start, size, scale)
        store(diagonal_ref, start, size, diagonal)
        value = load(source, start, size)
        if guess is None:
            value = [scale[t] * value[t] for t in range(len(w))]
        else:
            mid, north, south = (load(guess, start + k, size) for k in (0, -1, 1))
            around = beside(mid, north, south, c_west, c_north, c_south, step)
            value = [
                (1.0 - relaxation) * mid[t] + scale[t] * (value[t] + around[t]) for t in range(len(w))
            ]
        store(field, start, size, value)
        if next_weight is not None:
            pooled = [0.125 * p for p in pool_rows(weight, start, size, step)]
            store(next_weight, start // 2, size // 2, pooled)

    def second_pass(start, size):
        mid, around = beside_of(field, (c_west_ref, c_north_ref), start, size, step)
        b, scale, diagonal = (load(ref, start, size) for ref in (source, scale_ref, diagonal_ref))
        rest = [(b[t] + around[t]) - diagonal[t] * mid[t] for t in range(len(b))]
        store(smooth_ref, start, size, [mid[t] + scale[t] * rest[t] for t in range(len(b))])
        store(resid, start, size, rest)
        if next_source is not None:
            pooled = [0.25 * p for p in pool_rows(resid, start, size, step)]
            store(next_source, start // 2, size // 2, pooled)

    for_chunks(height, first_pass, largest, part)
    for_chunks(height, second_pass, largest, part)


def descend_all(rows, sources, guess, weights, states, diagonal, field, resid, largest, part):
    for level in range(LEVELS - 1):
        descend(
            level,
            rows >> level,
            weights[level],
            sources[level],
            guess if level == 0 else None,
            states[4 * level : 4 * level + 4],
            diagonal[level],
            field,
            resid,
            weights[level + 1],
            sources[level + 1],
            largest,
            part,
        )


def to_sides(west, east, cross_ref, pair_ref, k, rows):
    even = lax.axis_index("gy") % 2 == 0
    cross_ref[k, rows, :] = jnp.where(even, west, east)
    pair_ref[k, rows, :] = jnp.where(even, east, west)


def layout_kernel(source, guess, weight, own_source, own_guess, own_weight, cross_ref, pair_ref):
    rows = source.shape[0]
    piece = cross_ref.shape[1]
    tail = rows - (PIECES - 1) * piece
    for k, (block, own) in enumerate(zip((source, guess, weight), (own_source, own_guess, own_weight))):
        clear_guards(own, rows + 2 * HALO)
        sides = []
        for t in range(2):
            own[t, GUARD + HALO : GUARD + HALO + rows, :] = block[:, t * LANES : (t + 1) * LANES]
        for tile, first in ((0, 0), (1, LANES - HALO)):
            columns = slice(tile * LANES, (tile + 1) * LANES)
            last = roll(block[(PIECES - 1) * piece :, columns], (PIECES - 1) * HALO - first)
            packed = jnp.concatenate((last, jnp.zeros((piece - tail, LANES), jnp.float32)), axis=0)
            for p in range(PIECES - 1):
                part = block[p * piece : (p + 1) * piece, columns]
                packed = jnp.where(lane_of(part) // HALO == p, roll(part, p * HALO - first), packed)
            sides.append(packed)
        to_sides(*sides, cross_ref, pair_ref, k, slice(0, piece))


def halo_kernel(*refs):
    first_rows, second_rows, *own, cross_ref, pair_ref = refs[5:]
    total = own[0].shape[1] - 2 * GUARD
    piece = cross_ref.shape[1]
    even = lax.axis_index("gx") % 2 == 0
    shift = (PIECES - 1) * HALO
    for k in range(3):
        above = jnp.where(even, first_rows[k], second_rows[k])
        below = jnp.where(even, second_rows[k], first_rows[k])
        for rows, row, first in ((above, 0, piece - 2 * HALO), (below, total - HALO, piece - HALO)):
            body = [rows[:, t * LANES : (t + 1) * LANES] for t in range(2)]
            for t in range(2):
                own[k][t, GUARD + row : GUARD + row + HALO, :] = body[t]
            span = slice(first, first + HALO)
            here = lane_of(body[0]) >= shift
            cross, pair = cross_ref[k, span, :], pair_ref[k, span, :]
            west, east = roll(body[0], shift), roll(body[1], shift + HALO - LANES)
            even_y = lax.axis_index("gy") % 2 == 0
            cross_ref[k, span, :] = jnp.where(here, jnp.where(even_y, west, east), cross)
            pair_ref[k, span, :] = jnp.where(here, jnp.where(even_y, east, west), pair)


def body_kernel(source, guess, weight, *refs):
    states = refs[: 4 * (LEVELS - 1)]
    last_weight, last_source, first_diagonal, field, resid, weight_in, *inner = refs[4 * (LEVELS - 1) :]
    rows = source.shape[1] - 2 * GUARD
    depth = LEVELS - 2
    weights = (weight_in, *inner[:depth], last_weight)
    sources = (source, *inner[depth : 2 * depth], last_source)
    diagonal = (first_diagonal, *inner[2 * depth :])
    weights[0][...] = weight[...]
    descend_all(rows, sources, guess, weights, states, diagonal, field, resid, 112, 16)


def frame_kernel(own_source, own_guess, own_weight, from_cross, from_pair, body_weight, body_source, *refs):
    even = lax.axis_index("gy") % 2 == 0
    states, refs = refs[: 4 * (LEVELS - 1)], refs[4 * (LEVELS - 1) :]
    frame_source, first_diagonal, ring_state, coarse_ref = refs[0], refs[1], refs[2:6], refs[6]
    frame_guess, frame_weight, field, resid, *refs = refs[7:]
    ring_weight, ring_source, ring_field, ring_resid, ring_diagonal, *inner = refs
    rows = own_source.shape[1] - 2 * GUARD
    depth = LEVELS - 1
    weights = (frame_weight, *inner[:depth])
    sources = (frame_source, *inner[depth : 2 * depth])
    diagonals = (first_diagonal, *inner[2 * depth :])
    piece = rows // PIECES
    for k, (own, frame) in enumerate(
        ((own_source, frame_source), (own_guess, frame_guess), (own_weight, frame_weight))
    ):
        clear_guards(frame, rows)
        left = jnp.where(even, from_cross[k], from_pair[k])
        right = jnp.where(even, from_pair[k], from_cross[k])
        spans = [(p, 0, HALO + p * piece, piece) for p in range(PIECES - 1)]
        spans.append((PIECES - 1, 0, HALO + (PIECES - 1) * piece, piece - 2 * HALO))
        spans += [(PIECES - 1, piece - 2 * HALO, 0, HALO), (PIECES - 1, piece - HALO, rows - HALO, HALO)]
        for p, first, start, size in spans:
            span = slice(GUARD + start, GUARD + start + size)
            west = roll(left[first : first + size], -p * HALO)
            east = roll(right[first : first + size], -(p + 1) * HALO)
            lane = lane_of(west)
            inside = jnp.where(lane < LANES // 2, roll(own[0, span, :], HALO), roll(own[1, span, :], -HALO))
            inside = jnp.where(lane < HALO, west, inside)
            frame[0, span, :] = jnp.where(lane >= LANES - HALO, east, inside)
    descend_all(rows, sources, frame_guess, weights, states, diagonals, field, resid, 280, 280)

    level = LEVELS - 1
    step, halo, height = 2**level, HALO >> level, rows >> level
    for body, frame, ring in (
        (body_weight, weights[level], ring_weight),
        (body_source, sources[level], ring_source),
    ):
        middle = load(body, 0, height)
        around = load(frame, 0, height)[0]
        lane = lane_of(around)
        ahead, back = roll(around, HALO), roll(around, -HALO)
        store(
            ring,
            0,
            height,
            [
                jnp.where(lane < 2 * step, back, middle[0]),
                jnp.where(lane >= LANES - 2 * step, ahead, middle[1]),
                jnp.where(lane < LANES // 2, ahead, back),
            ],
        )
    descend(
        level,
        height,
        ring_weight,
        ring_source,
        None,
        ring_state,
        ring_diagonal,
        ring_field,
        ring_resid,
        None,
        None,
        height,
        height,
    )

    coarse_rows = (height - 2 * halo) // 2
    dense = jnp.zeros((8, LANES), jnp.float32)
    lane = lane_of(dense)
    per_tile = LANES // 2**LEVELS
    pooled_b = pool_rows(ring_resid, halo, 2 * coarse_rows, step)
    pooled_w = pool_rows(ring_weight, halo, 2 * coarse_rows, step)
    index = (lane % per_tile) * 2**LEVELS
    place = lane // per_tile
    for g in range(coarse_rows // 8):
        for group, (values, factor) in enumerate(((pooled_b, 0.25), (pooled_w, 0.125))):
            for t in range(2):
                taken = jnp.take_along_axis(factor * values[t][8 * g : 8 * g + 8], index, axis=1)
                dense = jnp.where(place == 4 * g + 2 * group + t, taken, dense)
    coarse_ref[...] = jnp.broadcast_to(dense[None], coarse_ref.shape)


def coarse_solve(all_ref, width, groups):
    x, nx = lax.axis_index("gx"), lax.axis_size("gx")
    y, ny = lax.axis_index("gy"), lax.axis_size("gy")
    tiles = []
    for dx in (-1, 0, 1):
        for dy in (-1, 0, 1):
            inside = (x + dx >= 0) & (x + dx < nx) & (y + dy >= 0) & (y + dy < ny)
            tile = all_ref[jnp.where(inside, (x + dx) * ny + y + dy, 0)]
            tiles.append(jnp.where(inside, tile, 0.0))
    lane = lane_of(tiles[0])
    blocks = [(0, g) for g in range(groups - TALL // 8, groups)]
    blocks += [(1, g) for g in range(groups)] + [(2, g) for g in range(TALL // 8)]
    b, w = [], []
    for band, g in blocks:
        b_rows = w_rows = jnp.zeros_like(tiles[0])
        for side in range(3):
            tile = tiles[3 * band + side]
            here = (lane >= side * width) & (lane < (side + 1) * width)
            b_rows = jnp.where(here, roll(tile, (side - 2 * g) * width), b_rows)
            w_rows = jnp.where(here, roll(tile, (side - 2 * g - 1) * width), w_rows)
        b.append(b_rows)
        w.append(w_rows)
    b, w = jnp.concatenate(b, axis=0), jnp.concatenate(w, axis=0)

    def north_of(x):
        return pltpu.roll(x, 1, 0)

    def south_of(x):
        return pltpu.roll(x, x.shape[0] - 1, 0)

    c_west = jnp.minimum(w, roll(w, 1))
    c_north = jnp.minimum(w, north_of(w))
    c_east, c_south = roll(c_west, -1), south_of(c_north)
    scale = relaxation / (damping + c_north + c_south + c_west + c_east)
    first = scale * b
    c_west, c_east, c_north, c_south = (scale * c for c in (c_west, c_east, c_north, c_south))

    def sweep(_, e):
        around = (c_west * roll(e, 1) + c_east * roll(e, -1)) + (c_north * north_of(e) + c_south * south_of(e))
        return ((1.0 - relaxation) * e + first) + around

    return lax.fori_loop(0, SWEEPS - 1, sweep, first)


def up_kernel(all_ref, own_source, frame_source, own_diagonal, frame_diagonal, *refs):
    count = 4 * (LEVELS - 1)
    body_state, frame_state, ring_state = refs[:count], refs[count : 2 * count], refs[2 * count : 2 * count + 4]
    out_ref, resid_ref = refs[2 * count + 4 : 2 * count + 6]
    ring_pe, body_final, frame_final, sems, *inner = refs[2 * count + 6 :]
    outs, inner = inner[:2], inner[2:]
    body_pe, frame_pe = inner[: LEVELS - 1], inner[LEVELS - 1 :]
    rows = out_ref.shape[0] + 2 * HALO
    width = out_ref.shape[1] >> LEVELS
    e = coarse_solve(all_ref, width, (out_ref.shape[0] >> LEVELS) // 8)

    level = LEVELS - 1
    step, halo, height = 2**level, HALO >> level, rows >> level
    coarse_rows = (height - 2 * halo) // 2
    picked = e[TALL - 8 : TALL + coarse_rows + 8]
    lane = lane_of(picked)
    for t in range(3):
        group = (lane + t * LANES) // 2**LEVELS
        if t == 2:
            group = jnp.where(lane < LANES // 2, group, group - 3 * LANES // 2**LEVELS)
        taken = jnp.take_along_axis(picked, jnp.clip(group + width, 0, LANES - 1), axis=1)[7 : 7 + coarse_rows + 2]
        ring_pe[t, 0 : 2 * GUARD, :] = jnp.zeros((2 * GUARD, LANES), jnp.float32)
        ring_pe[t, height : height + 2 * GUARD, :] = jnp.zeros((2 * GUARD, LANES), jnp.float32)
        ring_pe[t, pl.ds(GUARD + halo - 2, coarse_rows + 2, stride=2), :] = taken
        ring_pe[t, pl.ds(GUARD + halo - 1, coarse_rows + 2, stride=2), :] = taken

    def climbed(pe, state, start, size, step):
        mid, around = beside_of(pe, state[:2], start, size, step)
        scale, smooth = load(state[2], start, size), load(state[3], start, size)
        return [(smooth[t] + (1.0 - relaxation) * mid[t]) + scale[t] * around[t] for t in range(len(mid))]

    def climb_ring(start, size, level=level, step=step):
        ring = spread(climbed(ring_pe, ring_state, start, size, step), step // 2)
        lane = lane_of(ring[0])
        around = jnp.where(
            lane < LANES // 2,
            jnp.where(lane < HALO, roll(ring[2], HALO), roll(ring[0], HALO)),
            jnp.where(lane < LANES - HALO, roll(ring[1], -HALO), roll(ring[2], -HALO)),
        )
        store_twice(body_pe[level - 1], start, size, ring[:2])
        store_twice(frame_pe[level - 1], start, size, [around])

    for_chunks(height, climb_ring, height, 16)

    for level in range(LEVELS - 2, -1, -1):
        step, height = 2**level, rows >> level
        for pes, states, final, largest, part in (
            (body_pe, body_state, body_final, 112, 16),
            (frame_pe, frame_state, frame_final, 280, 32),
        ):
            state = states[4 * level : 4 * level + 4]
            clear_guards(pes[level], height)

            def climb(start, size, level=level, step=step, pes=pes, state=state, final=final):
                value = climbed(pes[level], state, start, size, step)
                if level == 0:
                    store(final, start, size, value)
                else:
                    store_twice(pes[level - 1], start, size, spread(value, step // 2))

            for_chunks(height, climb, largest, part)

    def last(start, size):
        base = start + HALO
        body, around = beside_of(body_final, body_state[:2], base, size, 1)
        frame, frame_around = beside_of(frame_final, frame_state[:2], base, size, 1)
        b, d = load(own_source, base, size), load(own_diagonal, base, size)
        b_frame, d_frame = load(frame_source, base, size), load(frame_diagonal, base, size)
        body = (body, [(b[t] + around[t]) - d[t] * body[t] for t in range(2)])
        frame = (frame[0], (b_frame[0] + frame_around[0]) - d_frame[0] * frame[0])
        lane = lane_of(frame[0])
        near = HALO - 4
        span = pl.ds(start, size)
        for ref, middle, around in ((outs[0], body[0], frame[0]), (outs[1], body[1], frame[1])):
            ref[span, :LANES] = jnp.where(lane < near, roll(around, -HALO), middle[0])
            ref[span, LANES:] = jnp.where(lane >= LANES - near, roll(around, HALO), middle[1])

    parts = sems.shape[0] // 2
    size = out_ref.shape[0] // parts

    def copies(p):
        span = pl.ds(p * size, size)
        return [
            pltpu.make_async_copy(outs[k].at[span], ref.at[span], sems.at[2 * p + k])
            for k, ref in enumerate((out_ref, resid_ref))
        ]

    def finish(p, carry):
        for_parts(p * size, size, last, 16)
        for copy in copies(p):
            copy.start()
        return carry

    lax.fori_loop(0, parts, finish, 0)
    for p in range(parts):
        for copy in copies(p):
            copy.wait()


def call(kernel, out_shape, scratch, flops, moved, **more):
    return pl.pallas_call(
        kernel,
        out_shape=out_shape,
        scratch_shapes=scratch,
        compiler_params=pltpu.CompilerParams(vmem_limit_bytes=VMEM_LIMIT),
        cost_estimate=pl.CostEstimate(flops=flops, bytes_accessed=moved, transcendentals=0),
        **more,
    )


def swap(x, axis, first):
    pairs = [(i, i + 1) for i in range(first, lax.axis_size(axis) - 1, 2)]
    return lax.ppermute(x, axis, pairs + [(j, i) for i, j in pairs])


def local(rhs, pressure, wet_mask, bathy_class):
    rows, columns = rhs.shape
    cells = rows * columns
    total = rows + 2 * HALO
    levels = range(LEVELS - 1)

    def shape(tiles, level):
        return (tiles, (total >> level) + 2 * GUARD, LANES)

    def out(*dims):
        return jax.ShapeDtypeStruct(dims, jnp.float32)

    def vmem(tiles, level):
        return pltpu.VMEM(shape(tiles, level), jnp.float32)

    def fields(r, p, m, c):
        wet = m.astype(jnp.float32)
        return wet * r, wet * p, wet * (1.0 + 0.5 * c.astype(jnp.float32))

    given = (rhs, pressure, wet_mask, bathy_class)

    def edge(start):
        return jnp.stack(fields(*(lax.dynamic_slice_in_dim(x, start, HALO, axis=0) for x in given)))

    even = lax.axis_index("gx") % 2 == 0
    first_rows = swap(edge(jnp.where(even, 0, rows - HALO)), "gx", 1)
    second_rows = swap(edge(jnp.where(even, rows - HALO, 0)), "gx", 0)
    piece = total // PIECES
    own_shapes = [out(*shape(2, 0))] * 3
    laid_out = [*own_shapes, out(3, piece, LANES), out(3, piece, LANES)]
    begun = call(layout_kernel, laid_out, (), 10 * cells, 10 * cells)(*fields(*given))
    *own, to_cross, to_pair = call(
        halo_kernel, laid_out, (), cells, cells, input_output_aliases={k: k for k in range(5)}
    )(*begun, first_rows, second_rows)
    from_cross = swap(to_cross, "gy", 1)
    from_pair = swap(to_pair, "gy", 0)

    state_count = 4 * (LEVELS - 1)
    *body_state, body_weight, body_source, diagonal = call(
        body_kernel,
        [out(*shape(2, level)) for level in levels for _ in range(4)]
        + [out(*shape(2, LEVELS - 1))] * 2
        + [out(*shape(2, 0))],
        [vmem(2, 0)] * 3 + [vmem(2, level) for level in levels[1:]] * 3,
        100 * cells,
        40 * cells,
    )(*own)
    devices = lax.axis_size("gx") * lax.axis_size("gy")
    ring = LEVELS - 1
    *state, coarse = call(
        frame_kernel,
        [out(*shape(1, level)) for level in levels for _ in range(4)]
        + [out(*shape(1, 0))] * 2
        + [out(*shape(3, ring))] * 4
        + [out(devices, 8, LANES)],
        [vmem(1, 0)] * 4 + [vmem(3, ring)] * 5 + [vmem(1, level) for level in range(1, LEVELS)] * 3,
        50 * cells,
        20 * cells,
    )(*own, from_cross, from_pair, body_weight, body_source)
    frame_state, ring_state = state[:state_count], state[state_count + 2 :]
    frame_source, frame_diagonal = state[state_count : state_count + 2]
    gathered = lax.all_to_all(coarse, ("gx", "gy"), 0, 0)
    return call(
        up_kernel,
        (out(rows, columns), out(rows, columns)),
        [vmem(3, ring), vmem(2, 0), vmem(1, 0), pltpu.SemaphoreType.DMA((8,))]
        + [pltpu.VMEM((rows, columns), jnp.float32)] * 2
        + [vmem(2, level) for level in levels]
        + [vmem(1, level) for level in levels],
        60 * cells,
        40 * cells,
        out_specs=[pl.BlockSpec(memory_space=pl.ANY)] * 2,
    )(gathered, own[0], frame_source, diagonal, frame_diagonal, *body_state, *frame_state, *ring_state)


def solution(mesh):
    placed = (P("gx", "gy"), P("gx", "gy"), P("gx", "gy"), P("gx", "gy"))
    return jax.shard_map(
        local, mesh=mesh, in_specs=placed, out_specs=(P("gx", "gy"), P("gx", "gy")), check_vma=False
    )
```

```python
import jax
import jax.numpy as jnp
from jax import lax
from jax.experimental import pallas as pl
from jax.experimental.pallas import tpu as pltpu
from jax.sharding import PartitionSpec as P

LEVELS = 4
SWEEPS = 12

damping = 0.01
relaxation = 0.8

HALO = 24
LANES = 128
INNER = LANES // 2 - HALO
GUARD = 8
PIECES = 5
TALL = 16
VMEM_LIMIT = 40 * 1024 * 1024


def lane_of(x):
    return lax.broadcasted_iota(jnp.int32, x.shape, x.ndim - 1)


def roll(x, amount):
    amount %= LANES
    return x if amount == 0 else pltpu.roll(x, amount, x.ndim - 1)


def from_west(tiles, step):
    moved = [roll(t, step) for t in tiles]
    if len(tiles) == 1:
        return moved
    edge = lane_of(tiles[0]) < step
    return [jnp.where(edge, moved[i - 1], moved[i]) for i in range(len(tiles))]


def from_east(tiles, step):
    moved = [roll(t, -step) for t in tiles]
    count = len(tiles)
    if count == 1:
        return moved
    edge = lane_of(tiles[0]) >= LANES - step
    return [jnp.where(edge, moved[(i + 1) % count], moved[i]) for i in range(count)]


def spread(tiles, step):
    second = (lane_of(tiles[0]) // step) % 2 == 1
    return [jnp.where(second, roll(t, step), t) for t in tiles]


def for_parts(start, size, body, part):
    for offset in range(0, size, part):
        body(start + offset, min(part, size - offset))


def for_chunks(rows, body, largest, part):
    sizes = [size for size in range(8, largest + 1, 8) if rows % size == 0]
    if rows <= largest or not sizes:
        for_parts(0, rows, body, part)
        return

    def step(i, carry):
        for_parts(i * sizes[-1], sizes[-1], body, part)
        return carry

    lax.fori_loop(0, rows // sizes[-1], step, 0)


def load(ref, start, size):
    return [ref[t, pl.ds(GUARD + start, size), :] for t in range(ref.shape[0])]


def store(ref, start, size, tiles):
    for t, tile in enumerate(tiles):
        ref[t, pl.ds(GUARD + start, size), :] = tile


def store_twice(ref, start, size, tiles):
    for t, tile in enumerate(tiles):
        ref[t, pl.ds(GUARD + 2 * start, size, stride=2), :] = tile
        ref[t, pl.ds(GUARD + 2 * start + 1, size, stride=2), :] = tile


def clear_guards(ref, rows):
    zeros = jnp.zeros((GUARD, LANES), jnp.float32)
    for t in range(ref.shape[0]):
        ref[t, 0:GUARD, :] = zeros
        ref[t, GUARD + rows : 2 * GUARD + rows, :] = zeros


def beside(mid, north, south, c_west, c_north, c_south, step):
    west = from_west(mid, step)
    east = from_east([c * m for c, m in zip(c_west, mid)], step)
    return [
        (c_west[t] * west[t] + east[t]) + (c_north[t] * north[t] + c_south[t] * south[t]) for t in range(len(mid))
    ]


def beside_of(ref, coeffs, start, size, step):
    c_west_ref, c_north_ref = coeffs
    mid = load(ref, start, size)
    north, south = load(ref, start - 1, size), load(ref, start + 1, size)
    c_west, c_north = load(c_west_ref, start, size), load(c_north_ref, start, size)
    return mid, beside(mid, north, south, c_west, c_north, load(c_north_ref, start + 1, size), step)


def pool_rows(ref, start, size, step):
    out = []
    for t in range(ref.shape[0]):
        even = ref[t, pl.ds(GUARD + start, size // 2, stride=2), :]
        odd = ref[t, pl.ds(GUARD + start + 1, size // 2, stride=2), :]
        both = even + odd
        out.append(both + roll(both, -step))
    return out


def descend(level, height, weight, source, guess, state, diagonal_ref, field, resid, next_weight, next_source, largest, part):
    step = 2**level
    c_west_ref, c_north_ref, scale_ref, smooth_ref = state
    for ref in (weight, field, c_north_ref):
        clear_guards(ref, height)

    def first_pass(start, size):
        w, w_north, w_south = (load(weight, start + k, size) for k in (0, -1, 1))
        c_north = [jnp.minimum(a, b) for a, b in zip(w, w_north)]
        c_south = [jnp.minimum(a, b) for a, b in zip(w, w_south)]
        c_west = [jnp.minimum(a, b) for a, b in zip(w, from_west(w, step))]
        c_east = from_east(c_west, step)
        diagonal = [damping + c_north[t] + c_south[t] + c_west[t] + c_east[t] for t in range(len(w))]
        scale = [relaxation / d for d in diagonal]
        store(c_north_ref, start, size, c_north)
        store(c_west_ref, start, size, c_west)
        store(scale_ref, start, size, scale)
        store(diagonal_ref, start, size, diagonal)
        value = load(source, start, size)
        if guess is None:
            value = [scale[t] * value[t] for t in range(len(w))]
        else:
            mid, north, south = (load(guess, start + k, size) for k in (0, -1, 1))
            around = beside(mid, north, south, c_west, c_north, c_south, step)
            value = [
                (1.0 - relaxation) * mid[t] + scale[t] * (value[t] + around[t]) for t in range(len(w))
            ]
        store(field, start, size, value)
        if next_weight is not None:
            pooled = [0.125 * p for p in pool_rows(weight, start, size, step)]
            store(next_weight, start // 2, size // 2, pooled)

    def second_pass(start, size):
        mid, around = beside_of(field, (c_west_ref, c_north_ref), start, size, step)
        b, scale, diagonal = (load(ref, start, size) for ref in (source, scale_ref, diagonal_ref))
        rest = [(b[t] + around[t]) - diagonal[t] * mid[t] for t in range(len(b))]
        store(smooth_ref, start, size, [mid[t] + scale[t] * rest[t] for t in range(len(b))])
        store(resid, start, size, rest)
        if next_source is not None:
            pooled = [0.25 * p for p in pool_rows(resid, start, size, step)]
            store(next_source, start // 2, size // 2, pooled)

    for_chunks(height, first_pass, largest, part)
    for_chunks(height, second_pass, largest, part)


def descend_all(rows, sources, guess, weights, states, diagonal, field, resid, largest, part):
    for level in range(LEVELS - 1):
        descend(
            level,
            rows >> level,
            weights[level],
            sources[level],
            guess if level == 0 else None,
            states[4 * level : 4 * level + 4],
            diagonal[level],
            field,
            resid,
            weights[level + 1],
            sources[level + 1],
            largest,
            part,
        )


def to_sides(west, east, cross_ref, pair_ref, k, rows):
    even = lax.axis_index("gy") % 2 == 0
    cross_ref[k, rows, :] = jnp.where(even, west, east)
    pair_ref[k, rows, :] = jnp.where(even, east, west)


def layout_kernel(source, guess, weight, own_source, own_guess, own_weight, cross_ref, pair_ref):
    rows = source.shape[0]
    piece = cross_ref.shape[1]
    tail = rows - (PIECES - 1) * piece
    for k, (block, own) in enumerate(zip((source, guess, weight), (own_source, own_guess, own_weight))):
        clear_guards(own, rows + 2 * HALO)
        sides = []
        for t in range(2):
            own[t, GUARD + HALO : GUARD + HALO + rows, :] = block[:, t * LANES : (t + 1) * LANES]
        for tile, first in ((0, 0), (1, LANES - HALO)):
            columns = slice(tile * LANES, (tile + 1) * LANES)
            last = roll(block[(PIECES - 1) * piece :, columns], (PIECES - 1) * HALO - first)
            packed = jnp.concatenate((last, jnp.zeros((piece - tail, LANES), jnp.float32)), axis=0)
            for p in range(PIECES - 1):
                part = block[p * piece : (p + 1) * piece, columns]
                packed = jnp.where(lane_of(part) // HALO == p, roll(part, p * HALO - first), packed)
            sides.append(packed)
        to_sides(*sides, cross_ref, pair_ref, k, slice(0, piece))


def halo_kernel(*refs):
    first_rows, second_rows, *own, cross_ref, pair_ref = refs[5:]
    total = own[0].shape[1] - 2 * GUARD
    piece = cross_ref.shape[1]
    even = lax.axis_index("gx") % 2 == 0
    shift = (PIECES - 1) * HALO
    for k in range(3):
        above = jnp.where(even, first_rows[k], second_rows[k])
        below = jnp.where(even, second_rows[k], first_rows[k])
        for rows, row, first in ((above, 0, piece - 2 * HALO), (below, total - HALO, piece - HALO)):
            body = [rows[:, t * LANES : (t + 1) * LANES] for t in range(2)]
            for t in range(2):
                own[k][t, GUARD + row : GUARD + row + HALO, :] = body[t]
            span = slice(first, first + HALO)
            here = lane_of(body[0]) >= shift
            cross, pair = cross_ref[k, span, :], pair_ref[k, span, :]
            west, east = roll(body[0], shift), roll(body[1], shift + HALO - LANES)
            even_y = lax.axis_index("gy") % 2 == 0
            cross_ref[k, span, :] = jnp.where(here, jnp.where(even_y, west, east), cross)
            pair_ref[k, span, :] = jnp.where(here, jnp.where(even_y, east, west), pair)


def body_kernel(source, guess, weight, *refs):
    states = refs[: 4 * (LEVELS - 1)]
    last_weight, last_source, first_diagonal, field, resid, weight_in, *inner = refs[4 * (LEVELS - 1) :]
    rows = source.shape[1] - 2 * GUARD
    depth = LEVELS - 2
    weights = (weight_in, *inner[:depth], last_weight)
    sources = (source, *inner[depth : 2 * depth], last_source)
    diagonal = (first_diagonal, *inner[2 * depth :])
    weights[0][...] = weight[...]
    descend_all(rows, sources, guess, weights, states, diagonal, field, resid, 280, 16)


def frame_kernel(own_source, own_guess, own_weight, from_cross, from_pair, body_weight, body_source, *refs):
    even = lax.axis_index("gy") % 2 == 0
    states, refs = refs[: 4 * (LEVELS - 1)], refs[4 * (LEVELS - 1) :]
    frame_source, first_diagonal, ring_state, coarse_ref = refs[0], refs[1], refs[2:6], refs[6]
    frame_guess, frame_weight, field, resid, *refs = refs[7:]
    ring_weight, ring_source, ring_field, ring_resid, ring_diagonal, *inner = refs
    rows = own_source.shape[1] - 2 * GUARD
    depth = LEVELS - 1
    weights = (frame_weight, *inner[:depth])
    sources = (frame_source, *inner[depth : 2 * depth])
    diagonals = (first_diagonal, *inner[2 * depth :])
    piece = rows // PIECES
    for k, (own, frame) in enumerate(
        ((own_source, frame_source), (own_guess, frame_guess), (own_weight, frame_weight))
    ):
        clear_guards(frame, rows)
        left = jnp.where(even, from_cross[k], from_pair[k])
        right = jnp.where(even, from_pair[k], from_cross[k])
        spans = [(p, 0, HALO + p * piece, piece) for p in range(PIECES - 1)]
        spans.append((PIECES - 1, 0, HALO + (PIECES - 1) * piece, piece - 2 * HALO))
        spans += [(PIECES - 1, piece - 2 * HALO, 0, HALO), (PIECES - 1, piece - HALO, rows - HALO, HALO)]
        for p, first, start, size in spans:
            span = slice(GUARD + start, GUARD + start + size)
            west = roll(left[first : first + size], -p * HALO)
            east = roll(right[first : first + size], -(p + 1) * HALO)
            lane = lane_of(west)
            inside = jnp.where(lane < LANES // 2, roll(own[0, span, :], HALO), roll(own[1, span, :], -HALO))
            inside = jnp.where(lane < HALO, west, inside)
            frame[0, span, :] = jnp.where(lane >= LANES - HALO, east, inside)
    descend_all(rows, sources, frame_guess, weights, states, diagonals, field, resid, 280, 280)

    level = LEVELS - 1
    step, halo, height = 2**level, HALO >> level, rows >> level
    for body, frame, ring in (
        (body_weight, weights[level], ring_weight),
        (body_source, sources[level], ring_source),
    ):
        middle = load(body, 0, height)
        around = load(frame, 0, height)[0]
        lane = lane_of(around)
        ahead, back = roll(around, HALO), roll(around, -HALO)
        store(
            ring,
            0,
            height,
            [
                jnp.where(lane < 2 * step, back, middle[0]),
                jnp.where(lane >= LANES - 2 * step, ahead, middle[1]),
                jnp.where(lane < LANES // 2, ahead, back),
            ],
        )
    descend(
        level,
        height,
        ring_weight,
        ring_source,
        None,
        ring_state,
        ring_diagonal,
        ring_field,
        ring_resid,
        None,
        None,
        height,
        height,
    )

    coarse_rows = (height - 2 * halo) // 2
    dense = jnp.zeros((8, LANES), jnp.float32)
    lane = lane_of(dense)
    per_tile = LANES // 2**LEVELS
    pooled_b = pool_rows(ring_resid, halo, 2 * coarse_rows, step)
    pooled_w = pool_rows(ring_weight, halo, 2 * coarse_rows, step)
    index = (lane % per_tile) * 2**LEVELS
    place = lane // per_tile
    for g in range(coarse_rows // 8):
        for group, (values, factor) in enumerate(((pooled_b, 0.25), (pooled_w, 0.125))):
            for t in range(2):
                taken = jnp.take_along_axis(factor * values[t][8 * g : 8 * g + 8], index, axis=1)
                dense = jnp.where(place == 4 * g + 2 * group + t, taken, dense)
    coarse_ref[...] = jnp.broadcast_to(dense[None], coarse_ref.shape)


def coarse_solve(all_ref, width, groups):
    x, nx = lax.axis_index("gx"), lax.axis_size("gx")
    y, ny = lax.axis_index("gy"), lax.axis_size("gy")
    tiles = []
    for dx in (-1, 0, 1):
        for dy in (-1, 0, 1):
            inside = (x + dx >= 0) & (x + dx < nx) & (y + dy >= 0) & (y + dy < ny)
            tile = all_ref[jnp.where(inside, (x + dx) * ny + y + dy, 0)]
            tiles.append(jnp.where(inside, tile, 0.0))
    lane = lane_of(tiles[0])
    blocks = [(0, g) for g in range(groups - TALL // 8, groups)]
    blocks += [(1, g) for g in range(groups)] + [(2, g) for g in range(TALL // 8)]
    b, w = [], []
    for band, g in blocks:
        b_rows = w_rows = jnp.zeros_like(tiles[0])
        for side in range(3):
            tile = tiles[3 * band + side]
            here = (lane >= side * width) & (lane < (side + 1) * width)
            b_rows = jnp.where(here, roll(tile, (side - 2 * g) * width), b_rows)
            w_rows = jnp.where(here, roll(tile, (side - 2 * g - 1) * width), w_rows)
        b.append(b_rows)
        w.append(w_rows)
    b, w = jnp.concatenate(b, axis=0), jnp.concatenate(w, axis=0)

    def north_of(x):
        return pltpu.roll(x, 1, 0)

    def south_of(x):
        return pltpu.roll(x, x.shape[0] - 1, 0)

    c_west = jnp.minimum(w, roll(w, 1))
    c_north = jnp.minimum(w, north_of(w))
    c_east, c_south = roll(c_west, -1), south_of(c_north)
    scale = relaxation / (damping + c_north + c_south + c_west + c_east)
    first = scale * b
    c_west, c_east, c_north, c_south = (scale * c for c in (c_west, c_east, c_north, c_south))

    def sweep(_, e):
        around = (c_west * roll(e, 1) + c_east * roll(e, -1)) + (c_north * north_of(e) + c_south * south_of(e))
        return ((1.0 - relaxation) * e + first) + around

    return lax.fori_loop(0, SWEEPS - 1, sweep, first)


def up_kernel(all_ref, own_source, frame_source, own_diagonal, frame_diagonal, *refs):
    count = 4 * (LEVELS - 1)
    body_state, frame_state, ring_state = refs[:count], refs[count : 2 * count], refs[2 * count : 2 * count + 4]
    out_ref, resid_ref = refs[2 * count + 4 : 2 * count + 6]
    ring_pe, body_final, frame_final, sems, *inner = refs[2 * count + 6 :]
    outs, inner = inner[:2], inner[2:]
    body_pe, frame_pe = inner[: LEVELS - 1], inner[LEVELS - 1 :]
    rows = out_ref.shape[0] + 2 * HALO
    width = out_ref.shape[1] >> LEVELS
    e = coarse_solve(all_ref, width, (out_ref.shape[0] >> LEVELS) // 8)

    level = LEVELS - 1
    step, halo, height = 2**level, HALO >> level, rows >> level
    coarse_rows = (height - 2 * halo) // 2
    picked = e[TALL - 8 : TALL + coarse_rows + 8]
    lane = lane_of(picked)
    for t in range(3):
        group = (lane + t * LANES) // 2**LEVELS
        if t == 2:
            group = jnp.where(lane < LANES // 2, group, group - 3 * LANES // 2**LEVELS)
        taken = jnp.take_along_axis(picked, jnp.clip(group + width, 0, LANES - 1), axis=1)[7 : 7 + coarse_rows + 2]
        ring_pe[t, 0 : 2 * GUARD, :] = jnp.zeros((2 * GUARD, LANES), jnp.float32)
        ring_pe[t, height : height + 2 * GUARD, :] = jnp.zeros((2 * GUARD, LANES), jnp.float32)
        ring_pe[t, pl.ds(GUARD + halo - 2, coarse_rows + 2, stride=2), :] = taken
        ring_pe[t, pl.ds(GUARD + halo - 1, coarse_rows + 2, stride=2), :] = taken

    def climbed(pe, state, start, size, step):
        mid, around = beside_of(pe, state[:2], start, size, step)
        scale, smooth = load(state[2], start, size), load(state[3], start, size)
        return [(smooth[t] + (1.0 - relaxation) * mid[t]) + scale[t] * around[t] for t in range(len(mid))]

    def climb_ring(start, size, level=level, step=step):
        ring = spread(climbed(ring_pe, ring_state, start, size, step), step // 2)
        lane = lane_of(ring[0])
        around = jnp.where(
            lane < LANES // 2,
            jnp.where(lane < HALO, roll(ring[2], HALO), roll(ring[0], HALO)),
            jnp.where(lane < LANES - HALO, roll(ring[1], -HALO), roll(ring[2], -HALO)),
        )
        store_twice(body_pe[level - 1], start, size, ring[:2])
        store_twice(frame_pe[level - 1], start, size, [around])

    for_chunks(height, climb_ring, height, 16)

    for level in range(LEVELS - 2, -1, -1):
        step, height = 2**level, rows >> level
        groups = ((body_pe, body_state, body_final), (frame_pe, frame_state, frame_final))
        for pes, _, _ in groups:
            clear_guards(pes[level], height)

        def climb(start, size, level=level, step=step, groups=groups):
            for pes, states, final in groups:
                value = climbed(pes[level], states[4 * level : 4 * level + 4], start, size, step)
                if level == 0:
                    store(final, start, size, value)
                else:
                    store_twice(pes[level - 1], start, size, spread(value, step // 2))

        for_chunks(height, climb, 280, 16)

    def last(start, size):
        base = start + HALO
        body, around = beside_of(body_final, body_state[:2], base, size, 1)
        frame, frame_around = beside_of(frame_final, frame_state[:2], base, size, 1)
        b, d = load(own_source, base, size), load(own_diagonal, base, size)
        b_frame, d_frame = load(frame_source, base, size), load(frame_diagonal, base, size)
        body = (body, [(b[t] + around[t]) - d[t] * body[t] for t in range(2)])
        frame = (frame[0], (b_frame[0] + frame_around[0]) - d_frame[0] * frame[0])
        lane = lane_of(frame[0])
        near = HALO - 4
        span = pl.ds(start, size)
        for ref, middle, around in ((outs[0], body[0], frame[0]), (outs[1], body[1], frame[1])):
            ref[span, :LANES] = jnp.where(lane < near, roll(around, -HALO), middle[0])
            ref[span, LANES:] = jnp.where(lane >= LANES - near, roll(around, HALO), middle[1])

    parts = sems.shape[0] // 2
    size = out_ref.shape[0] // parts

    def copies(p):
        span = pl.ds(p * size, size)
        return [
            pltpu.make_async_copy(outs[k].at[span], ref.at[span], sems.at[2 * p + k])
            for k, ref in enumerate((out_ref, resid_ref))
        ]

    def finish(p, carry):
        for_parts(p * size, size, last, 16)
        for copy in copies(p):
            copy.start()
        return carry

    lax.fori_loop(0, parts, finish, 0)
    for p in range(parts):
        for copy in copies(p):
            copy.wait()


def call(kernel, out_shape, scratch, flops, moved, **more):
    return pl.pallas_call(
        kernel,
        out_shape=out_shape,
        scratch_shapes=scratch,
        compiler_params=pltpu.CompilerParams(vmem_limit_bytes=VMEM_LIMIT),
        cost_estimate=pl.CostEstimate(flops=flops, bytes_accessed=moved, transcendentals=0),
        **more,
    )


def swap(x, axis, first):
    pairs = [(i, i + 1) for i in range(first, lax.axis_size(axis) - 1, 2)]
    return lax.ppermute(x, axis, pairs + [(j, i) for i, j in pairs])


def local(rhs, pressure, wet_mask, bathy_class):
    rows, columns = rhs.shape
    cells = rows * columns
    total = rows + 2 * HALO
    levels = range(LEVELS - 1)

    def shape(tiles, level):
        return (tiles, (total >> level) + 2 * GUARD, LANES)

    def out(*dims):
        return jax.ShapeDtypeStruct(dims, jnp.float32)

    def vmem(tiles, level):
        return pltpu.VMEM(shape(tiles, level), jnp.float32)

    def fields(r, p, m, c):
        wet = m.astype(jnp.float32)
        return wet * r, wet * p, wet * (1.0 + 0.5 * c.astype(jnp.float32))

    given = (rhs, pressure, wet_mask, bathy_class)

    def edge(start):
        return jnp.stack(fields(*(lax.dynamic_slice_in_dim(x, start, HALO, axis=0) for x in given)))

    even = lax.axis_index("gx") % 2 == 0
    first_rows = swap(edge(jnp.where(even, 0, rows - HALO)), "gx", 1)
    second_rows = swap(edge(jnp.where(even, rows - HALO, 0)), "gx", 0)
    piece = total // PIECES
    own_shapes = [out(*shape(2, 0))] * 3
    laid_out = [*own_shapes, out(3, piece, LANES), out(3, piece, LANES)]
    begun = call(layout_kernel, laid_out, (), 10 * cells, 10 * cells)(*fields(*given))
    *own, to_cross, to_pair = call(
        halo_kernel, laid_out, (), cells, cells, input_output_aliases={k: k for k in range(5)}
    )(*begun, first_rows, second_rows)
    from_cross = swap(to_cross, "gy", 1)
    from_pair = swap(to_pair, "gy", 0)

    state_count = 4 * (LEVELS - 1)
    *body_state, body_weight, body_source, diagonal = call(
        body_kernel,
        [out(*shape(2, level)) for level in levels for _ in range(4)]
        + [out(*shape(2, LEVELS - 1))] * 2
        + [out(*shape(2, 0))],
        [vmem(2, 0)] * 3 + [vmem(2, level) for level in levels[1:]] * 3,
        100 * cells,
        40 * cells,
    )(*own)
    devices = lax.axis_size("gx") * lax.axis_size("gy")
    ring = LEVELS - 1
    *state, coarse = call(
        frame_kernel,
        [out(*shape(1, level)) for level in levels for _ in range(4)]
        + [out(*shape(1, 0))] * 2
        + [out(*shape(3, ring))] * 4
        + [out(devices, 8, LANES)],
        [vmem(1, 0)] * 4 + [vmem(3, ring)] * 5 + [vmem(1, level) for level in range(1, LEVELS)] * 3,
        50 * cells,
        20 * cells,
    )(*own, from_cross, from_pair, body_weight, body_source)
    frame_state, ring_state = state[:state_count], state[state_count + 2 :]
    frame_source, frame_diagonal = state[state_count : state_count + 2]
    gathered = lax.all_to_all(coarse, ("gx", "gy"), 0, 0)
    return call(
        up_kernel,
        (out(rows, columns), out(rows, columns)),
        [vmem(3, ring), vmem(2, 0), vmem(1, 0), pltpu.SemaphoreType.DMA((8,))]
        + [pltpu.VMEM((rows, columns), jnp.float32)] * 2
        + [vmem(2, level) for level in levels]
        + [vmem(1, level) for level in levels],
        60 * cells,
        40 * cells,
        out_specs=[pl.BlockSpec(memory_space=pl.ANY)] * 2,
    )(gathered, own[0], frame_source, diagonal, frame_diagonal, *body_state, *frame_state, *ring_state)


def solution(mesh):
    placed = (P("gx", "gy"), P("gx", "gy"), P("gx", "gy"), P("gx", "gy"))
    return jax.shard_map(
        local, mesh=mesh, in_specs=placed, out_specs=(P("gx", "gy"), P("gx", "gy")), check_vma=False
    )
```

```python
import jax
import jax.numpy as jnp
from jax import lax
from jax.experimental import pallas as pl
from jax.experimental.pallas import tpu as pltpu
from jax.sharding import PartitionSpec as P

LEVELS = 4
SWEEPS = 12

damping = 0.01
relaxation = 0.8

HALO = 24
LANES = 128
INNER = LANES // 2 - HALO
GUARD = 8
PIECES = 5
TALL = 16
VMEM_LIMIT = 40 * 1024 * 1024


def lane_of(x):
    return lax.broadcasted_iota(jnp.int32, x.shape, x.ndim - 1)


def roll(x, amount):
    amount %= LANES
    return x if amount == 0 else pltpu.roll(x, amount, x.ndim - 1)


def from_west(tiles, step):
    moved = [roll(t, step) for t in tiles]
    if len(tiles) == 1:
        return moved
    edge = lane_of(tiles[0]) < step
    return [jnp.where(edge, moved[i - 1], moved[i]) for i in range(len(tiles))]


def from_east(tiles, step):
    moved = [roll(t, -step) for t in tiles]
    count = len(tiles)
    if count == 1:
        return moved
    edge = lane_of(tiles[0]) >= LANES - step
    return [jnp.where(edge, moved[(i + 1) % count], moved[i]) for i in range(count)]


def spread(tiles, step):
    second = (lane_of(tiles[0]) // step) % 2 == 1
    return [jnp.where(second, roll(t, step), t) for t in tiles]


def for_parts(start, size, body, part):
    for offset in range(0, size, part):
        body(start + offset, min(part, size - offset))


def for_chunks(rows, body, largest, part):
    sizes = [size for size in range(8, largest + 1, 8) if rows % size == 0]
    if rows <= largest or not sizes:
        for_parts(0, rows, body, part)
        return

    def step(i, carry):
        for_parts(i * sizes[-1], sizes[-1], body, part)
        return carry

    lax.fori_loop(0, rows // sizes[-1], step, 0)


def load(ref, start, size):
    return [ref[t, pl.ds(GUARD + start, size), :] for t in range(ref.shape[0])]


def store(ref, start, size, tiles):
    for t, tile in enumerate(tiles):
        ref[t, pl.ds(GUARD + start, size), :] = tile


def store_twice(ref, start, size, tiles):
    for t, tile in enumerate(tiles):
        ref[t, pl.ds(GUARD + 2 * start, size, stride=2), :] = tile
        ref[t, pl.ds(GUARD + 2 * start + 1, size, stride=2), :] = tile


def clear_guards(ref, rows):
    zeros = jnp.zeros((GUARD, LANES), jnp.float32)
    for t in range(ref.shape[0]):
        ref[t, 0:GUARD, :] = zeros
        ref[t, GUARD + rows : 2 * GUARD + rows, :] = zeros


def beside(mid, north, south, c_west, c_north, c_south, step):
    west = from_west(mid, step)
    east = from_east([c * m for c, m in zip(c_west, mid)], step)
    return [
        (c_west[t] * west[t] + east[t]) + (c_north[t] * north[t] + c_south[t] * south[t]) for t in range(len(mid))
    ]


def beside_of(ref, coeffs, start, size, step):
    c_west_ref, c_north_ref = coeffs
    mid = load(ref, start, size)
    north, south = load(ref, start - 1, size), load(ref, start + 1, size)
    c_west, c_north = load(c_west_ref, start, size), load(c_north_ref, start, size)
    return mid, beside(mid, north, south, c_west, c_north, load(c_north_ref, start + 1, size), step)


def pool_rows(ref, start, size, step):
    out = []
    for t in range(ref.shape[0]):
        even = ref[t, pl.ds(GUARD + start, size // 2, stride=2), :]
        odd = ref[t, pl.ds(GUARD + start + 1, size // 2, stride=2), :]
        both = even + odd
        out.append(both + roll(both, -step))
    return out


def descend(level, height, weight, source, guess, state, diagonal_ref, field, resid, next_weight, next_source, largest, part):
    step = 2**level
    c_west_ref, c_north_ref, scale_ref, smooth_ref = state
    for ref in (weight, field, c_north_ref):
        clear_guards(ref, height)

    def first_pass(start, size):
        w, w_north, w_south = (load(weight, start + k, size) for k in (0, -1, 1))
        c_north = [jnp.minimum(a, b) for a, b in zip(w, w_north)]
        c_south = [jnp.minimum(a, b) for a, b in zip(w, w_south)]
        c_west = [jnp.minimum(a, b) for a, b in zip(w, from_west(w, step))]
        c_east = from_east(c_west, step)
        diagonal = [damping + c_north[t] + c_south[t] + c_west[t] + c_east[t] for t in range(len(w))]
        scale = [relaxation / d for d in diagonal]
        store(c_north_ref, start, size, c_north)
        store(c_west_ref, start, size, c_west)
        store(scale_ref, start, size, scale)
        store(diagonal_ref, start, size, diagonal)
        value = load(source, start, size)
        if guess is None:
            value = [scale[t] * value[t] for t in range(len(w))]
        else:
            mid, north, south = (load(guess, start + k, size) for k in (0, -1, 1))
            around = beside(mid, north, south, c_west, c_north, c_south, step)
            value = [
                (1.0 - relaxation) * mid[t] + scale[t] * (value[t] + around[t]) for t in range(len(w))
            ]
        store(field, start, size, value)
        if next_weight is not None:
            pooled = [0.125 * p for p in pool_rows(weight, start, size, step)]
            store(next_weight, start // 2, size // 2, pooled)

    def second_pass(start, size):
        mid, around = beside_of(field, (c_west_ref, c_north_ref), start, size, step)
        b, scale, diagonal = (load(ref, start, size) for ref in (source, scale_ref, diagonal_ref))
        rest = [(b[t] + around[t]) - diagonal[t] * mid[t] for t in range(len(b))]
        store(smooth_ref, start, size, [mid[t] + scale[t] * rest[t] for t in range(len(b))])
        store(resid, start, size, rest)
        if next_source is not None:
            pooled = [0.25 * p for p in pool_rows(resid, start, size, step)]
            store(next_source, start // 2, size // 2, pooled)

    for_chunks(height, first_pass, largest, part)
    for_chunks(height, second_pass, largest, part)


def descend_all(rows, sources, guess, weights, states, diagonal, field, resid, largest, part):
    for level in range(LEVELS - 1):
        descend(
            level,
            rows >> level,
            weights[level],
            sources[level],
            guess if level == 0 else None,
            states[4 * level : 4 * level + 4],
            diagonal[level],
            field,
            resid,
            weights[level + 1],
            sources[level + 1],
            largest,
            part,
        )


def to_sides(west, east, cross_ref, pair_ref, k, rows):
    even = lax.axis_index("gy") % 2 == 0
    cross_ref[k, rows, :] = jnp.where(even, west, east)
    pair_ref[k, rows, :] = jnp.where(even, east, west)


def layout_kernel(source, guess, weight, own_source, own_guess, own_weight, cross_ref, pair_ref):
    rows = source.shape[0]
    piece = cross_ref.shape[1]
    tail = rows - (PIECES - 1) * piece
    for k, (block, own) in enumerate(zip((source, guess, weight), (own_source, own_guess, own_weight))):
        clear_guards(own, rows + 2 * HALO)
        sides = []
        for t in range(2):
            own[t, GUARD + HALO : GUARD + HALO + rows, :] = block[:, t * LANES : (t + 1) * LANES]
        for tile, first in ((0, 0), (1, LANES - HALO)):
            columns = slice(tile * LANES, (tile + 1) * LANES)
            last = roll(block[(PIECES - 1) * piece :, columns], (PIECES - 1) * HALO - first)
            packed = jnp.concatenate((last, jnp.zeros((piece - tail, LANES), jnp.float32)), axis=0)
            for p in range(PIECES - 1):
                part = block[p * piece : (p + 1) * piece, columns]
                packed = jnp.where(lane_of(part) // HALO == p, roll(part, p * HALO - first), packed)
            sides.append(packed)
        to_sides(*sides, cross_ref, pair_ref, k, slice(0, piece))


def halo_kernel(*refs):
    first_rows, second_rows, *own, cross_ref, pair_ref = refs[5:]
    total = own[0].shape[1] - 2 * GUARD
    piece = cross_ref.shape[1]
    even = lax.axis_index("gx") % 2 == 0
    shift = (PIECES - 1) * HALO
    for k in range(3):
        above = jnp.where(even, first_rows[k], second_rows[k])
        below = jnp.where(even, second_rows[k], first_rows[k])
        for rows, row, first in ((above, 0, piece - 2 * HALO), (below, total - HALO, piece - HALO)):
            body = [rows[:, t * LANES : (t + 1) * LANES] for t in range(2)]
            for t in range(2):
                own[k][t, GUARD + row : GUARD + row + HALO, :] = body[t]
            span = slice(first, first + HALO)
            here = lane_of(body[0]) >= shift
            cross, pair = cross_ref[k, span, :], pair_ref[k, span, :]
            west, east = roll(body[0], shift), roll(body[1], shift + HALO - LANES)
            even_y = lax.axis_index("gy") % 2 == 0
            cross_ref[k, span, :] = jnp.where(here, jnp.where(even_y, west, east), cross)
            pair_ref[k, span, :] = jnp.where(here, jnp.where(even_y, east, west), pair)


def body_kernel(source, guess, weight, *refs):
    states = refs[: 4 * (LEVELS - 1)]
    last_weight, last_source, first_diagonal, field, resid, weight_in, *inner = refs[4 * (LEVELS - 1) :]
    rows = source.shape[1] - 2 * GUARD
    depth = LEVELS - 2
    weights = (weight_in, *inner[:depth], last_weight)
    sources = (source, *inner[depth : 2 * depth], last_source)
    diagonal = (first_diagonal, *inner[2 * depth :])
    weights[0][...] = weight[...]
    descend_all(rows, sources, guess, weights, states, diagonal, field, resid, 112, 112)


def frame_kernel(own_source, own_guess, own_weight, from_cross, from_pair, body_weight, body_source, *refs):
    even = lax.axis_index("gy") % 2 == 0
    states, refs = refs[: 4 * (LEVELS - 1)], refs[4 * (LEVELS - 1) :]
    frame_source, first_diagonal, ring_state, coarse_ref = refs[0], refs[1], refs[2:6], refs[6]
    frame_guess, frame_weight, field, resid, *refs = refs[7:]
    ring_weight, ring_source, ring_field, ring_resid, ring_diagonal, *inner = refs
    rows = own_source.shape[1] - 2 * GUARD
    depth = LEVELS - 1
    weights = (frame_weight, *inner[:depth])
    sources = (frame_source, *inner[depth : 2 * depth])
    diagonals = (first_diagonal, *inner[2 * depth :])
    piece = rows // PIECES
    for k, (own, frame) in enumerate(
        ((own_source, frame_source), (own_guess, frame_guess), (own_weight, frame_weight))
    ):
        clear_guards(frame, rows)
        left = jnp.where(even, from_cross[k], from_pair[k])
        right = jnp.where(even, from_pair[k], from_cross[k])
        spans = [(p, 0, HALO + p * piece, piece) for p in range(PIECES - 1)]
        spans.append((PIECES - 1, 0, HALO + (PIECES - 1) * piece, piece - 2 * HALO))
        spans += [(PIECES - 1, piece - 2 * HALO, 0, HALO), (PIECES - 1, piece - HALO, rows - HALO, HALO)]
        for p, first, start, size in spans:
            span = slice(GUARD + start, GUARD + start + size)
            west = roll(left[first : first + size], -p * HALO)
            east = roll(right[first : first + size], -(p + 1) * HALO)
            lane = lane_of(west)
            inside = jnp.where(lane < LANES // 2, roll(own[0, span, :], HALO), roll(own[1, span, :], -HALO))
            inside = jnp.where(lane < HALO, west, inside)
            frame[0, span, :] = jnp.where(lane >= LANES - HALO, east, inside)
    descend_all(rows, sources, frame_guess, weights, states, diagonals, field, resid, 112, 112)

    level = LEVELS - 1
    step, halo, height = 2**level, HALO >> level, rows >> level
    for body, frame, ring in (
        (body_weight, weights[level], ring_weight),
        (body_source, sources[level], ring_source),
    ):
        middle = load(body, 0, height)
        around = load(frame, 0, height)[0]
        lane = lane_of(around)
        ahead, back = roll(around, HALO), roll(around, -HALO)
        store(
            ring,
            0,
            height,
            [
                jnp.where(lane < 2 * step, back, middle[0]),
                jnp.where(lane >= LANES - 2 * step, ahead, middle[1]),
                jnp.where(lane < LANES // 2, ahead, back),
            ],
        )
    descend(
        level,
        height,
        ring_weight,
        ring_source,
        None,
        ring_state,
        ring_diagonal,
        ring_field,
        ring_resid,
        None,
        None,
        height,
        height,
    )

    coarse_rows = (height - 2 * halo) // 2
    dense = jnp.zeros((8, LANES), jnp.float32)
    lane = lane_of(dense)
    per_tile = LANES // 2**LEVELS
    pooled_b = pool_rows(ring_resid, halo, 2 * coarse_rows, step)
    pooled_w = pool_rows(ring_weight, halo, 2 * coarse_rows, step)
    index = (lane % per_tile) * 2**LEVELS
    place = lane // per_tile
    for g in range(coarse_rows // 8):
        for group, (values, factor) in enumerate(((pooled_b, 0.25), (pooled_w, 0.125))):
            for t in range(2):
                taken = jnp.take_along_axis(factor * values[t][8 * g : 8 * g + 8], index, axis=1)
                dense = jnp.where(place == 4 * g + 2 * group + t, taken, dense)
    coarse_ref[...] = jnp.broadcast_to(dense[None], coarse_ref.shape)


def coarse_solve(all_ref, width, groups):
    x, nx = lax.axis_index("gx"), lax.axis_size("gx")
    y, ny = lax.axis_index("gy"), lax.axis_size("gy")
    tiles = []
    for dx in (-1, 0, 1):
        for dy in (-1, 0, 1):
            inside = (x + dx >= 0) & (x + dx < nx) & (y + dy >= 0) & (y + dy < ny)
            tile = all_ref[jnp.where(inside, (x + dx) * ny + y + dy, 0)]
            tiles.append(jnp.where(inside, tile, 0.0))
    lane = lane_of(tiles[0])
    blocks = [(0, g) for g in range(groups - TALL // 8, groups)]
    blocks += [(1, g) for g in range(groups)] + [(2, g) for g in range(TALL // 8)]
    b, w = [], []
    for band, g in blocks:
        b_rows = w_rows = jnp.zeros_like(tiles[0])
        for side in range(3):
            tile = tiles[3 * band + side]
            here = (lane >= side * width) & (lane < (side + 1) * width)
            b_rows = jnp.where(here, roll(tile, (side - 2 * g) * width), b_rows)
            w_rows = jnp.where(here, roll(tile, (side - 2 * g - 1) * width), w_rows)
        b.append(b_rows)
        w.append(w_rows)
    b, w = jnp.concatenate(b, axis=0), jnp.concatenate(w, axis=0)

    def north_of(x):
        return pltpu.roll(x, 1, 0)

    def south_of(x):
        return pltpu.roll(x, x.shape[0] - 1, 0)

    c_west = jnp.minimum(w, roll(w, 1))
    c_north = jnp.minimum(w, north_of(w))
    c_east, c_south = roll(c_west, -1), south_of(c_north)
    scale = relaxation / (damping + c_north + c_south + c_west + c_east)
    first = scale * b
    c_west, c_east, c_north, c_south = (scale * c for c in (c_west, c_east, c_north, c_south))

    def sweep(_, e):
        around = (c_west * roll(e, 1) + c_east * roll(e, -1)) + (c_north * north_of(e) + c_south * south_of(e))
        return ((1.0 - relaxation) * e + first) + around

    return lax.fori_loop(0, SWEEPS - 1, sweep, first)


def up_kernel(all_ref, own_source, frame_source, own_diagonal, frame_diagonal, *refs):
    count = 4 * (LEVELS - 1)
    body_state, frame_state, ring_state = refs[:count], refs[count : 2 * count], refs[2 * count : 2 * count + 4]
    out_ref, resid_ref = refs[2 * count + 4 : 2 * count + 6]
    ring_pe, body_final, frame_final, sems, *inner = refs[2 * count + 6 :]
    outs, inner = inner[:2], inner[2:]
    body_pe, frame_pe = inner[: LEVELS - 1], inner[LEVELS - 1 :]
    rows = out_ref.shape[0] + 2 * HALO
    width = out_ref.shape[1] >> LEVELS
    e = coarse_solve(all_ref, width, (out_ref.shape[0] >> LEVELS) // 8)

    level = LEVELS - 1
    step, halo, height = 2**level, HALO >> level, rows >> level
    coarse_rows = (height - 2 * halo) // 2
    picked = e[TALL - 8 : TALL + coarse_rows + 8]
    lane = lane_of(picked)
    for t in range(3):
        group = (lane + t * LANES) // 2**LEVELS
        if t == 2:
            group = jnp.where(lane < LANES // 2, group, group - 3 * LANES // 2**LEVELS)
        taken = jnp.take_along_axis(picked, jnp.clip(group + width, 0, LANES - 1), axis=1)[7 : 7 + coarse_rows + 2]
        ring_pe[t, 0 : 2 * GUARD, :] = jnp.zeros((2 * GUARD, LANES), jnp.float32)
        ring_pe[t, height : height + 2 * GUARD, :] = jnp.zeros((2 * GUARD, LANES), jnp.float32)
        ring_pe[t, pl.ds(GUARD + halo - 2, coarse_rows + 2, stride=2), :] = taken
        ring_pe[t, pl.ds(GUARD + halo - 1, coarse_rows + 2, stride=2), :] = taken

    def climbed(pe, state, start, size, step):
        mid, around = beside_of(pe, state[:2], start, size, step)
        scale, smooth = load(state[2], start, size), load(state[3], start, size)
        return [(smooth[t] + (1.0 - relaxation) * mid[t]) + scale[t] * around[t] for t in range(len(mid))]

    def climb_ring(start, size, level=level, step=step):
        ring = spread(climbed(ring_pe, ring_state, start, size, step), step // 2)
        lane = lane_of(ring[0])
        around = jnp.where(
            lane < LANES // 2,
            jnp.where(lane < HALO, roll(ring[2], HALO), roll(ring[0], HALO)),
            jnp.where(lane < LANES - HALO, roll(ring[1], -HALO), roll(ring[2], -HALO)),
        )
        store_twice(body_pe[level - 1], start, size, ring[:2])
        store_twice(frame_pe[level - 1], start, size, [around])

    for_chunks(height, climb_ring, height, 16)

    for level in range(LEVELS - 2, -1, -1):
        step, height = 2**level, rows >> level
        groups = ((body_pe, body_state, body_final), (frame_pe, frame_state, frame_final))
        for pes, _, _ in groups:
            clear_guards(pes[level], height)

        def climb(start, size, level=level, step=step, groups=groups):
            for pes, states, final in groups:
                value = climbed(pes[level], states[4 * level : 4 * level + 4], start, size, step)
                if level == 0:
                    store(final, start, size, value)
                else:
                    store_twice(pes[level - 1], start, size, spread(value, step // 2))

        for_chunks(height, climb, 112, 16)

    def last(start, size):
        base = start + HALO
        body, around = beside_of(body_final, body_state[:2], base, size, 1)
        frame, frame_around = beside_of(frame_final, frame_state[:2], base, size, 1)
        b, d = load(own_source, base, size), load(own_diagonal, base, size)
        b_frame, d_frame = load(frame_source, base, size), load(frame_diagonal, base, size)
        body = (body, [(b[t] + around[t]) - d[t] * body[t] for t in range(2)])
        frame = (frame[0], (b_frame[0] + frame_around[0]) - d_frame[0] * frame[0])
        lane = lane_of(frame[0])
        near = HALO - 4
        span = pl.ds(start, size)
        for ref, middle, around in ((outs[0], body[0], frame[0]), (outs[1], body[1], frame[1])):
            ref[span, :LANES] = jnp.where(lane < near, roll(around, -HALO), middle[0])
            ref[span, LANES:] = jnp.where(lane >= LANES - near, roll(around, HALO), middle[1])

    parts = sems.shape[0] // 2
    size = out_ref.shape[0] // parts

    def copies(p):
        span = pl.ds(p * size, size)
        return [
            pltpu.make_async_copy(outs[k].at[span], ref.at[span], sems.at[2 * p + k])
            for k, ref in enumerate((out_ref, resid_ref))
        ]

    def finish(p, carry):
        for_parts(p * size, size, last, 16)
        for copy in copies(p):
            copy.start()
        return carry

    lax.fori_loop(0, parts, finish, 0)
    for p in range(parts):
        for copy in copies(p):
            copy.wait()


def call(kernel, out_shape, scratch, flops, moved, **more):
    return pl.pallas_call(
        kernel,
        out_shape=out_shape,
        scratch_shapes=scratch,
        compiler_params=pltpu.CompilerParams(vmem_limit_bytes=VMEM_LIMIT),
        cost_estimate=pl.CostEstimate(flops=flops, bytes_accessed=moved, transcendentals=0),
        **more,
    )


def swap(x, axis, first):
    pairs = [(i, i + 1) for i in range(first, lax.axis_size(axis) - 1, 2)]
    return lax.ppermute(x, axis, pairs + [(j, i) for i, j in pairs])


def local(rhs, pressure, wet_mask, bathy_class):
    rows, columns = rhs.shape
    cells = rows * columns
    total = rows + 2 * HALO
    levels = range(LEVELS - 1)

    def shape(tiles, level):
        return (tiles, (total >> level) + 2 * GUARD, LANES)

    def out(*dims):
        return jax.ShapeDtypeStruct(dims, jnp.float32)

    def vmem(tiles, level):
        return pltpu.VMEM(shape(tiles, level), jnp.float32)

    def fields(r, p, m, c):
        wet = m.astype(jnp.float32)
        return wet * r, wet * p, wet * (1.0 + 0.5 * c.astype(jnp.float32))

    given = (rhs, pressure, wet_mask, bathy_class)

    def edge(start):
        return jnp.stack(fields(*(lax.dynamic_slice_in_dim(x, start, HALO, axis=0) for x in given)))

    even = lax.axis_index("gx") % 2 == 0
    first_rows = swap(edge(jnp.where(even, 0, rows - HALO)), "gx", 1)
    second_rows = swap(edge(jnp.where(even, rows - HALO, 0)), "gx", 0)
    piece = total // PIECES
    own_shapes = [out(*shape(2, 0))] * 3
    laid_out = [*own_shapes, out(3, piece, LANES), out(3, piece, LANES)]
    begun = call(layout_kernel, laid_out, (), 10 * cells, 10 * cells)(*fields(*given))
    *own, to_cross, to_pair = call(
        halo_kernel, laid_out, (), cells, cells, input_output_aliases={k: k for k in range(5)}
    )(*begun, first_rows, second_rows)
    from_cross = swap(to_cross, "gy", 1)
    from_pair = swap(to_pair, "gy", 0)

    state_count = 4 * (LEVELS - 1)
    *body_state, body_weight, body_source, diagonal = call(
        body_kernel,
        [out(*shape(2, level)) for level in levels for _ in range(4)]
        + [out(*shape(2, LEVELS - 1))] * 2
        + [out(*shape(2, 0))],
        [vmem(2, 0)] * 3 + [vmem(2, level) for level in levels[1:]] * 3,
        100 * cells,
        40 * cells,
    )(*own)
    devices = lax.axis_size("gx") * lax.axis_size("gy")
    ring = LEVELS - 1
    *state, coarse = call(
        frame_kernel,
        [out(*shape(1, level)) for level in levels for _ in range(4)]
        + [out(*shape(1, 0))] * 2
        + [out(*shape(3, ring))] * 4
        + [out(devices, 8, LANES)],
        [vmem(1, 0)] * 4 + [vmem(3, ring)] * 5 + [vmem(1, level) for level in range(1, LEVELS)] * 3,
        50 * cells,
        20 * cells,
    )(*own, from_cross, from_pair, body_weight, body_source)
    frame_state, ring_state = state[:state_count], state[state_count + 2 :]
    frame_source, frame_diagonal = state[state_count : state_count + 2]
    gathered = lax.all_to_all(coarse, ("gx", "gy"), 0, 0)
    return call(
        up_kernel,
        (out(rows, columns), out(rows, columns)),
        [vmem(3, ring), vmem(2, 0), vmem(1, 0), pltpu.SemaphoreType.DMA((8,))]
        + [pltpu.VMEM((rows, columns), jnp.float32)] * 2
        + [vmem(2, level) for level in levels]
        + [vmem(1, level) for level in levels],
        60 * cells,
        40 * cells,
        out_specs=[pl.BlockSpec(memory_space=pl.ANY)] * 2,
    )(gathered, own[0], frame_source, diagonal, frame_diagonal, *body_state, *frame_state, *ring_state)


def solution(mesh):
    placed = (P("gx", "gy"), P("gx", "gy"), P("gx", "gy"), P("gx", "gy"))
    return jax.shard_map(
        local, mesh=mesh, in_specs=placed, out_specs=(P("gx", "gy"), P("gx", "gy")), check_vma=False
    )
```

```python
import jax
import jax.numpy as jnp
from jax import lax
from jax.experimental import pallas as pl
from jax.experimental.pallas import tpu as pltpu
from jax.sharding import PartitionSpec as P

LEVELS = 4
SWEEPS = 12

damping = 0.01
relaxation = 0.8

HALO = 24
LANES = 128
INNER = LANES // 2 - HALO
TOP = 32
GUARD = 8
PIECES = 5
TALL = 16
VMEM_LIMIT = 40 * 1024 * 1024


def lane_of(x):
    return lax.broadcasted_iota(jnp.int32, x.shape, x.ndim - 1)


def roll(x, amount):
    amount %= LANES
    return x if amount == 0 else pltpu.roll(x, amount, x.ndim - 1)


def from_west(tiles, step):
    moved = [roll(t, step) for t in tiles]
    if len(tiles) == 1:
        return moved
    edge = lane_of(tiles[0]) < step
    return [jnp.where(edge, moved[i - 1], moved[i]) for i in range(len(tiles))]


def from_east(tiles, step):
    moved = [roll(t, -step) for t in tiles]
    count = len(tiles)
    if count == 1:
        return moved
    edge = lane_of(tiles[0]) >= LANES - step
    return [jnp.where(edge, moved[(i + 1) % count], moved[i]) for i in range(count)]


def clear_rim(ref):
    rim = GUARD + TOP - HALO
    zeros = jnp.zeros((rim, LANES), jnp.float32)
    for t in range(ref.shape[0]):
        ref[t, 0:rim, :] = zeros
        ref[t, ref.shape[1] - rim :, :] = zeros


def spread(tiles, step):
    second = (lane_of(tiles[0]) // step) % 2 == 1
    return [jnp.where(second, roll(t, step), t) for t in tiles]


def for_parts(start, size, body, part):
    for offset in range(0, size, part):
        body(start + offset, min(part, size - offset))


def for_chunks(rows, body, largest, part):
    sizes = [size for size in range(8, largest + 1, 8) if rows % size == 0]
    if rows <= largest or not sizes:
        for_parts(0, rows, body, part)
        return

    def step(i, carry):
        for_parts(i * sizes[-1], sizes[-1], body, part)
        return carry

    lax.fori_loop(0, rows // sizes[-1], step, 0)


def load(ref, start, size):
    return [ref[t, pl.ds(GUARD + start, size), :] for t in range(ref.shape[0])]


def store(ref, start, size, tiles):
    for t, tile in enumerate(tiles):
        ref[t, pl.ds(GUARD + start, size), :] = tile


def store_twice(ref, start, size, tiles):
    for t, tile in enumerate(tiles):
        ref[t, pl.ds(GUARD + 2 * start, size, stride=2), :] = tile
        ref[t, pl.ds(GUARD + 2 * start + 1, size, stride=2), :] = tile


def clear_guards(ref, rows):
    zeros = jnp.zeros((GUARD, LANES), jnp.float32)
    for t in range(ref.shape[0]):
        ref[t, 0:GUARD, :] = zeros
        ref[t, GUARD + rows : 2 * GUARD + rows, :] = zeros


def beside(mid, north, south, c_west, c_north, c_south, step):
    west = from_west(mid, step)
    east = from_east([c * m for c, m in zip(c_west, mid)], step)
    return [
        (c_west[t] * west[t] + east[t]) + (c_north[t] * north[t] + c_south[t] * south[t]) for t in range(len(mid))
    ]


def beside_of(ref, coeffs, start, size, step):
    c_west_ref, c_north_ref = coeffs
    mid = load(ref, start, size)
    north, south = load(ref, start - 1, size), load(ref, start + 1, size)
    c_west, c_north = load(c_west_ref, start, size), load(c_north_ref, start, size)
    return mid, beside(mid, north, south, c_west, c_north, load(c_north_ref, start + 1, size), step)


def pool_rows(ref, start, size, step):
    out = []
    for t in range(ref.shape[0]):
        even = ref[t, pl.ds(GUARD + start, size // 2, stride=2), :]
        odd = ref[t, pl.ds(GUARD + start + 1, size // 2, stride=2), :]
        both = even + odd
        out.append(both + roll(both, -step))
    return out


def descend(level, height, weight, source, guess, state, diagonal_ref, field, resid, next_weight, next_source, largest, part):
    step = 2**level
    c_west_ref, c_north_ref, scale_ref, smooth_ref = state
    for ref in (weight, field, c_north_ref):
        clear_guards(ref, height)

    def first_pass(start, size):
        w, w_north, w_south = (load(weight, start + k, size) for k in (0, -1, 1))
        c_north = [jnp.minimum(a, b) for a, b in zip(w, w_north)]
        c_south = [jnp.minimum(a, b) for a, b in zip(w, w_south)]
        c_west = [jnp.minimum(a, b) for a, b in zip(w, from_west(w, step))]
        c_east = from_east(c_west, step)
        diagonal = [damping + c_north[t] + c_south[t] + c_west[t] + c_east[t] for t in range(len(w))]
        scale = [relaxation / d for d in diagonal]
        store(c_north_ref, start, size, c_north)
        store(c_west_ref, start, size, c_west)
        store(scale_ref, start, size, scale)
        store(diagonal_ref, start, size, diagonal)
        value = load(source, start, size)
        if guess is None:
            value = [scale[t] * value[t] for t in range(len(w))]
        else:
            mid, north, south = (load(guess, start + k, size) for k in (0, -1, 1))
            around = beside(mid, north, south, c_west, c_north, c_south, step)
            value = [
                (1.0 - relaxation) * mid[t] + scale[t] * (value[t] + around[t]) for t in range(len(w))
            ]
        store(field, start, size, value)
        if next_weight is not None:
            pooled = [0.125 * p for p in pool_rows(weight, start, size, step)]
            store(next_weight, start // 2, size // 2, pooled)

    def second_pass(start, size):
        mid, around = beside_of(field, (c_west_ref, c_north_ref), start, size, step)
        b, scale, diagonal = (load(ref, start, size) for ref in (source, scale_ref, diagonal_ref))
        rest = [(b[t] + around[t]) - diagonal[t] * mid[t] for t in range(len(b))]
        store(smooth_ref, start, size, [mid[t] + scale[t] * rest[t] for t in range(len(b))])
        store(resid, start, size, rest)
        if next_source is not None:
            pooled = [0.25 * p for p in pool_rows(resid, start, size, step)]
            store(next_source, start // 2, size // 2, pooled)

    for_chunks(height, first_pass, largest, part)
    for_chunks(height, second_pass, largest, part)


def descend_all(rows, sources, guess, weights, states, diagonal, field, resid, largest, part):
    for level in range(LEVELS - 1):
        descend(
            level,
            rows >> level,
            weights[level],
            sources[level],
            guess if level == 0 else None,
            states[4 * level : 4 * level + 4],
            diagonal[level],
            field,
            resid,
            weights[level + 1],
            sources[level + 1],
            largest,
            part,
        )


def to_sides(west, east, cross_ref, pair_ref, k, rows):
    even = lax.axis_index("gy") % 2 == 0
    cross_ref[k, rows, :] = jnp.where(even, west, east)
    pair_ref[k, rows, :] = jnp.where(even, east, west)


def layout_kernel(source, guess, weight, own_source, own_guess, own_weight, cross_ref, pair_ref):
    rows = source.shape[0]
    piece = cross_ref.shape[1]
    tail = rows - (PIECES - 1) * piece
    for k, (block, own) in enumerate(zip((source, guess, weight), (own_source, own_guess, own_weight))):
        clear_rim(own)
        sides = []
        for t in range(2):
            own[t, GUARD + TOP : GUARD + TOP + rows, :] = block[:, t * LANES : (t + 1) * LANES]
        for tile, first in ((0, 0), (1, LANES - HALO)):
            columns = slice(tile * LANES, (tile + 1) * LANES)
            last = roll(block[(PIECES - 1) * piece :, columns], (PIECES - 1) * HALO - first)
            packed = jnp.concatenate((last, jnp.zeros((piece - tail, LANES), jnp.float32)), axis=0)
            for p in range(PIECES - 1):
                part = block[p * piece : (p + 1) * piece, columns]
                packed = jnp.where(lane_of(part) // HALO == p, roll(part, p * HALO - first), packed)
            sides.append(packed)
        to_sides(*sides, cross_ref, pair_ref, k, slice(0, piece))


def halo_kernel(*refs):
    first_rows, second_rows, *own, cross_ref, pair_ref = refs[5:]
    total = own[0].shape[1] - 2 * GUARD
    piece = cross_ref.shape[1]
    even = lax.axis_index("gx") % 2 == 0
    shift = (PIECES - 1) * HALO
    for k in range(3):
        above = jnp.where(even, first_rows[k], second_rows[k])
        below = jnp.where(even, second_rows[k], first_rows[k])
        for rows, row, first in ((above, TOP - HALO, piece - 2 * HALO), (below, total - TOP, piece - HALO)):
            body = [rows[:, t * LANES : (t + 1) * LANES] for t in range(2)]
            for t in range(2):
                own[k][t, GUARD + row : GUARD + row + HALO, :] = body[t]
            span = slice(first, first + HALO)
            here = lane_of(body[0]) >= shift
            cross, pair = cross_ref[k, span, :], pair_ref[k, span, :]
            west, east = roll(body[0], shift), roll(body[1], shift + HALO - LANES)
            even_y = lax.axis_index("gy") % 2 == 0
            cross_ref[k, span, :] = jnp.where(here, jnp.where(even_y, west, east), cross)
            pair_ref[k, span, :] = jnp.where(here, jnp.where(even_y, east, west), pair)


def body_kernel(source, guess, weight, *refs):
    states = refs[: 4 * (LEVELS - 1)]
    last_weight, last_source, first_diagonal, field, resid, weight_in, *inner = refs[4 * (LEVELS - 1) :]
    rows = source.shape[1] - 2 * GUARD
    depth = LEVELS - 2
    weights = (weight_in, *inner[:depth], last_weight)
    sources = (source, *inner[depth : 2 * depth], last_source)
    diagonal = (first_diagonal, *inner[2 * depth :])
    weights[0][...] = weight[...]
    descend_all(rows, sources, guess, weights, states, diagonal, field, resid, 144, 144)


def frame_kernel(own_source, own_guess, own_weight, from_cross, from_pair, body_weight, body_source, *refs):
    even = lax.axis_index("gy") % 2 == 0
    states, refs = refs[: 4 * (LEVELS - 1)], refs[4 * (LEVELS - 1) :]
    frame_source, first_diagonal, ring_state, coarse_ref = refs[0], refs[1], refs[2:6], refs[6]
    frame_guess, frame_weight, field, resid, *refs = refs[7:]
    ring_weight, ring_source, ring_field, ring_resid, ring_diagonal, *inner = refs
    rows = own_source.shape[1] - 2 * GUARD
    depth = LEVELS - 1
    weights = (frame_weight, *inner[:depth])
    sources = (frame_source, *inner[depth : 2 * depth])
    diagonals = (first_diagonal, *inner[2 * depth :])
    piece = from_cross.shape[1]
    for k, (own, frame) in enumerate(
        ((own_source, frame_source), (own_guess, frame_guess), (own_weight, frame_weight))
    ):
        clear_rim(frame)
        left = jnp.where(even, from_cross[k], from_pair[k])
        right = jnp.where(even, from_pair[k], from_cross[k])
        spans = [(p, 0, TOP + p * piece, piece) for p in range(PIECES - 1)]
        spans.append((PIECES - 1, 0, TOP + (PIECES - 1) * piece, piece - 2 * HALO))
        spans += [(PIECES - 1, piece - 2 * HALO, TOP - HALO, HALO), (PIECES - 1, piece - HALO, rows - TOP, HALO)]
        for p, first, start, size in spans:
            span = slice(GUARD + start, GUARD + start + size)
            west = roll(left[first : first + size], -p * HALO)
            east = roll(right[first : first + size], -(p + 1) * HALO)
            lane = lane_of(west)
            inside = jnp.where(lane < LANES // 2, roll(own[0, span, :], HALO), roll(own[1, span, :], -HALO))
            inside = jnp.where(lane < HALO, west, inside)
            frame[0, span, :] = jnp.where(lane >= LANES - HALO, east, inside)
    descend_all(rows, sources, frame_guess, weights, states, diagonals, field, resid, 288, 288)

    level = LEVELS - 1
    step, halo, height = 2**level, TOP >> level, rows >> level
    for body, frame, ring in (
        (body_weight, weights[level], ring_weight),
        (body_source, sources[level], ring_source),
    ):
        middle = load(body, 0, height)
        around = load(frame, 0, height)[0]
        lane = lane_of(around)
        ahead, back = roll(around, HALO), roll(around, -HALO)
        store(
            ring,
            0,
            height,
            [
                jnp.where(lane < 2 * step, back, middle[0]),
                jnp.where(lane >= LANES - 2 * step, ahead, middle[1]),
                jnp.where(lane < LANES // 2, ahead, back),
            ],
        )
    descend(
        level,
        height,
        ring_weight,
        ring_source,
        None,
        ring_state,
        ring_diagonal,
        ring_field,
        ring_resid,
        None,
        None,
        height,
        height,
    )

    coarse_rows = (height - 2 * halo) // 2
    dense = jnp.zeros((8, LANES), jnp.float32)
    lane = lane_of(dense)
    per_tile = LANES // 2**LEVELS
    pooled_b = pool_rows(ring_resid, halo, 2 * coarse_rows, step)
    pooled_w = pool_rows(ring_weight, halo, 2 * coarse_rows, step)
    index = (lane % per_tile) * 2**LEVELS
    place = lane // per_tile
    for g in range(coarse_rows // 8):
        for group, (values, factor) in enumerate(((pooled_b, 0.25), (pooled_w, 0.125))):
            for t in range(2):
                taken = jnp.take_along_axis(factor * values[t][8 * g : 8 * g + 8], index, axis=1)
                dense = jnp.where(place == 4 * g + 2 * group + t, taken, dense)
    coarse_ref[...] = jnp.broadcast_to(dense[None], coarse_ref.shape)


def coarse_solve(all_ref, width, groups):
    x, nx = lax.axis_index("gx"), lax.axis_size("gx")
    y, ny = lax.axis_index("gy"), lax.axis_size("gy")
    tiles = []
    for dx in (-1, 0, 1):
        for dy in (-1, 0, 1):
            inside = (x + dx >= 0) & (x + dx < nx) & (y + dy >= 0) & (y + dy < ny)
            tile = all_ref[jnp.where(inside, (x + dx) * ny + y + dy, 0)]
            tiles.append(jnp.where(inside, tile, 0.0))
    lane = lane_of(tiles[0])
    blocks = [(0, g) for g in range(groups - TALL // 8, groups)]
    blocks += [(1, g) for g in range(groups)] + [(2, g) for g in range(TALL // 8)]
    b, w = [], []
    for band, g in blocks:
        b_rows = w_rows = jnp.zeros_like(tiles[0])
        for side in range(3):
            tile = tiles[3 * band + side]
            here = (lane >= side * width) & (lane < (side + 1) * width)
            b_rows = jnp.where(here, roll(tile, (side - 2 * g) * width), b_rows)
            w_rows = jnp.where(here, roll(tile, (side - 2 * g - 1) * width), w_rows)
        b.append(b_rows)
        w.append(w_rows)
    b, w = jnp.concatenate(b, axis=0), jnp.concatenate(w, axis=0)

    def north_of(x):
        return pltpu.roll(x, 1, 0)

    def south_of(x):
        return pltpu.roll(x, x.shape[0] - 1, 0)

    c_west = jnp.minimum(w, roll(w, 1))
    c_north = jnp.minimum(w, north_of(w))
    c_east, c_south = roll(c_west, -1), south_of(c_north)
    scale = relaxation / (damping + c_north + c_south + c_west + c_east)
    first = scale * b
    c_west, c_east, c_north, c_south = (scale * c for c in (c_west, c_east, c_north, c_south))

    def sweep(_, e):
        around = (c_west * roll(e, 1) + c_east * roll(e, -1)) + (c_north * north_of(e) + c_south * south_of(e))
        return ((1.0 - relaxation) * e + first) + around

    return lax.fori_loop(0, SWEEPS - 1, sweep, first)


def up_kernel(all_ref, own_source, frame_source, own_diagonal, frame_diagonal, *refs):
    count = 4 * (LEVELS - 1)
    body_state, frame_state, ring_state = refs[:count], refs[count : 2 * count], refs[2 * count : 2 * count + 4]
    out_ref, resid_ref = refs[2 * count + 4 : 2 * count + 6]
    ring_pe, body_final, frame_final, sems, *inner = refs[2 * count + 6 :]
    outs, inner = inner[:2], inner[2:]
    body_pe, frame_pe = inner[: LEVELS - 1], inner[LEVELS - 1 :]
    rows = out_ref.shape[0] + 2 * TOP
    width = out_ref.shape[1] >> LEVELS
    e = coarse_solve(all_ref, width, (out_ref.shape[0] >> LEVELS) // 8)

    level = LEVELS - 1
    step, halo, height = 2**level, TOP >> level, rows >> level
    coarse_rows = (height - 2 * halo) // 2
    picked = e[TALL - 8 : TALL + coarse_rows + 8]
    lane = lane_of(picked)
    for t in range(3):
        group = (lane + t * LANES) // 2**LEVELS
        if t == 2:
            group = jnp.where(lane < LANES // 2, group, group - 3 * LANES // 2**LEVELS)
        taken = jnp.take_along_axis(picked, jnp.clip(group + width, 0, LANES - 1), axis=1)[7 : 7 + coarse_rows + 2]
        ring_pe[t, 0 : 2 * GUARD, :] = jnp.zeros((2 * GUARD, LANES), jnp.float32)
        ring_pe[t, height : height + 2 * GUARD, :] = jnp.zeros((2 * GUARD, LANES), jnp.float32)
        ring_pe[t, pl.ds(GUARD + halo - 2, coarse_rows + 2, stride=2), :] = taken
        ring_pe[t, pl.ds(GUARD + halo - 1, coarse_rows + 2, stride=2), :] = taken

    def climbed(pe, state, start, size, step):
        mid, around = beside_of(pe, state[:2], start, size, step)
        scale, smooth = load(state[2], start, size), load(state[3], start, size)
        return [(smooth[t] + (1.0 - relaxation) * mid[t]) + scale[t] * around[t] for t in range(len(mid))]

    def climb_ring(start, size, level=level, step=step):
        ring = spread(climbed(ring_pe, ring_state, start, size, step), step // 2)
        lane = lane_of(ring[0])
        around = jnp.where(
            lane < LANES // 2,
            jnp.where(lane < HALO, roll(ring[2], HALO), roll(ring[0], HALO)),
            jnp.where(lane < LANES - HALO, roll(ring[1], -HALO), roll(ring[2], -HALO)),
        )
        store_twice(body_pe[level - 1], start, size, ring[:2])
        store_twice(frame_pe[level - 1], start, size, [around])

    for_chunks(height, climb_ring, height, 16)

    for level in range(LEVELS - 2, -1, -1):
        step, height = 2**level, rows >> level
        groups = ((body_pe, body_state, body_final), (frame_pe, frame_state, frame_final))
        for pes, _, _ in groups:
            clear_guards(pes[level], height)

        def climb(start, size, level=level, step=step, groups=groups):
            for pes, states, final in groups:
                value = climbed(pes[level], states[4 * level : 4 * level + 4], start, size, step)
                if level == 0:
                    store(final, start, size, value)
                else:
                    store_twice(pes[level - 1], start, size, spread(value, step // 2))

        for_chunks(height, climb, 144, 72)

    def last(start, size):
        base = start + TOP
        body, around = beside_of(body_final, body_state[:2], base, size, 1)
        frame, frame_around = beside_of(frame_final, frame_state[:2], base, size, 1)
        b, d = load(own_source, base, size), load(own_diagonal, base, size)
        b_frame, d_frame = load(frame_source, base, size), load(frame_diagonal, base, size)
        body = (body, [(b[t] + around[t]) - d[t] * body[t] for t in range(2)])
        frame = (frame[0], (b_frame[0] + frame_around[0]) - d_frame[0] * frame[0])
        lane = lane_of(frame[0])
        near = HALO - 4
        span = pl.ds(start, size)
        for ref, middle, around in ((outs[0], body[0], frame[0]), (outs[1], body[1], frame[1])):
            ref[span, :LANES] = jnp.where(lane < near, roll(around, -HALO), middle[0])
            ref[span, LANES:] = jnp.where(lane >= LANES - near, roll(around, HALO), middle[1])

    parts = sems.shape[0] // 2
    size = out_ref.shape[0] // parts

    def copies(p):
        span = pl.ds(p * size, size)
        return [
            pltpu.make_async_copy(outs[k].at[span], ref.at[span], sems.at[2 * p + k])
            for k, ref in enumerate((out_ref, resid_ref))
        ]

    def finish(p, carry):
        for_parts(p * size, size, last, 16)
        for copy in copies(p):
            copy.start()
        return carry

    lax.fori_loop(0, parts, finish, 0)
    for p in range(parts):
        for copy in copies(p):
            copy.wait()


def call(kernel, out_shape, scratch, flops, moved, **more):
    return pl.pallas_call(
        kernel,
        out_shape=out_shape,
        scratch_shapes=scratch,
        compiler_params=pltpu.CompilerParams(vmem_limit_bytes=VMEM_LIMIT),
        cost_estimate=pl.CostEstimate(flops=flops, bytes_accessed=moved, transcendentals=0),
        **more,
    )


def swap(x, axis, first):
    pairs = [(i, i + 1) for i in range(first, lax.axis_size(axis) - 1, 2)]
    return lax.ppermute(x, axis, pairs + [(j, i) for i, j in pairs])


def local(rhs, pressure, wet_mask, bathy_class):
    rows, columns = rhs.shape
    cells = rows * columns
    total = rows + 2 * TOP
    levels = range(LEVELS - 1)

    def shape(tiles, level):
        return (tiles, (total >> level) + 2 * GUARD, LANES)

    def out(*dims):
        return jax.ShapeDtypeStruct(dims, jnp.float32)

    def vmem(tiles, level):
        return pltpu.VMEM(shape(tiles, level), jnp.float32)

    def fields(r, p, m, c):
        wet = m.astype(jnp.float32)
        return wet * r, wet * p, wet * (1.0 + 0.5 * c.astype(jnp.float32))

    given = (rhs, pressure, wet_mask, bathy_class)

    def edge(start):
        return jnp.stack(fields(*(lax.dynamic_slice_in_dim(x, start, HALO, axis=0) for x in given)))

    even = lax.axis_index("gx") % 2 == 0
    first_rows = swap(edge(jnp.where(even, 0, rows - HALO)), "gx", 1)
    second_rows = swap(edge(jnp.where(even, rows - HALO, 0)), "gx", 0)
    piece = (rows + 2 * HALO) // PIECES
    own_shapes = [out(*shape(2, 0))] * 3
    laid_out = [*own_shapes, out(3, piece, LANES), out(3, piece, LANES)]
    begun = call(layout_kernel, laid_out, (), 10 * cells, 10 * cells)(*fields(*given))
    *own, to_cross, to_pair = call(
        halo_kernel, laid_out, (), cells, cells, input_output_aliases={k: k for k in range(5)}
    )(*begun, first_rows, second_rows)
    from_cross = swap(to_cross, "gy", 1)
    from_pair = swap(to_pair, "gy", 0)

    state_count = 4 * (LEVELS - 1)
    *body_state, body_weight, body_source, diagonal = call(
        body_kernel,
        [out(*shape(2, level)) for level in levels for _ in range(4)]
        + [out(*shape(2, LEVELS - 1))] * 2
        + [out(*shape(2, 0))],
        [vmem(2, 0)] * 3 + [vmem(2, level) for level in levels[1:]] * 3,
        100 * cells,
        40 * cells,
    )(*own)
    devices = lax.axis_size("gx") * lax.axis_size("gy")
    ring = LEVELS - 1
    *state, coarse = call(
        frame_kernel,
        [out(*shape(1, level)) for level in levels for _ in range(4)]
        + [out(*shape(1, 0))] * 2
        + [out(*shape(3, ring))] * 4
        + [out(devices, 8, LANES)],
        [vmem(1, 0)] * 4 + [vmem(3, ring)] * 5 + [vmem(1, level) for level in range(1, LEVELS)] * 3,
        50 * cells,
        20 * cells,
    )(*own, from_cross, from_pair, body_weight, body_source)
    frame_state, ring_state = state[:state_count], state[state_count + 2 :]
    frame_source, frame_diagonal = state[state_count : state_count + 2]
    gathered = lax.all_to_all(coarse, ("gx", "gy"), 0, 0)
    return call(
        up_kernel,
        (out(rows, columns), out(rows, columns)),
        [vmem(3, ring), vmem(2, 0), vmem(1, 0), pltpu.SemaphoreType.DMA((8,))]
        + [pltpu.VMEM((rows, columns), jnp.float32)] * 2
        + [vmem(2, level) for level in levels]
        + [vmem(1, level) for level in levels],
        60 * cells,
        40 * cells,
        out_specs=[pl.BlockSpec(memory_space=pl.ANY)] * 2,
    )(gathered, own[0], frame_source, diagonal, frame_diagonal, *body_state, *frame_state, *ring_state)


def solution(mesh):
    placed = (P("gx", "gy"), P("gx", "gy"), P("gx", "gy"), P("gx", "gy"))
    return jax.shard_map(
        local, mesh=mesh, in_specs=placed, out_specs=(P("gx", "gy"), P("gx", "gy")), check_vma=False
    )
```

```python
import jax
import jax.numpy as jnp
from jax import lax
from jax.experimental import pallas as pl
from jax.experimental.pallas import tpu as pltpu
from jax.sharding import PartitionSpec as P

LEVELS = 4
SWEEPS = 12

damping = 0.01
relaxation = 0.8

HALO = 24
LANES = 128
INNER = LANES // 2 - HALO
TOP = 32
GUARD = 8
PIECES = 5
TALL = 16
VMEM_LIMIT = 40 * 1024 * 1024


def lane_of(x):
    return lax.broadcasted_iota(jnp.int32, x.shape, x.ndim - 1)


def roll(x, amount):
    amount %= LANES
    return x if amount == 0 else pltpu.roll(x, amount, x.ndim - 1)


def from_west(tiles, step):
    moved = [roll(t, step) for t in tiles]
    if len(tiles) == 1:
        return moved
    edge = lane_of(tiles[0]) < step
    return [jnp.where(edge, moved[i - 1], moved[i]) for i in range(len(tiles))]


def from_east(tiles, step):
    moved = [roll(t, -step) for t in tiles]
    count = len(tiles)
    if count == 1:
        return moved
    edge = lane_of(tiles[0]) >= LANES - step
    return [jnp.where(edge, moved[(i + 1) % count], moved[i]) for i in range(count)]


def clear_rim(ref):
    rim = GUARD + TOP - HALO
    zeros = jnp.zeros((rim, LANES), jnp.float32)
    for t in range(ref.shape[0]):
        ref[t, 0:rim, :] = zeros
        ref[t, ref.shape[1] - rim :, :] = zeros


def spread(tiles, step):
    second = (lane_of(tiles[0]) // step) % 2 == 1
    return [jnp.where(second, roll(t, step), t) for t in tiles]


def for_parts(start, size, body, part):
    for offset in range(0, size, part):
        body(start + offset, min(part, size - offset))


def for_chunks(rows, body, largest, part):
    sizes = [size for size in range(8, largest + 1, 8) if rows % size == 0]
    if rows <= largest or not sizes:
        for_parts(0, rows, body, part)
        return

    def step(i, carry):
        for_parts(i * sizes[-1], sizes[-1], body, part)
        return carry

    lax.fori_loop(0, rows // sizes[-1], step, 0)


def load(ref, start, size):
    return [ref[t, pl.ds(GUARD + start, size), :] for t in range(ref.shape[0])]


def store(ref, start, size, tiles):
    for t, tile in enumerate(tiles):
        ref[t, pl.ds(GUARD + start, size), :] = tile


def store_twice(ref, start, size, tiles):
    for t, tile in enumerate(tiles):
        ref[t, pl.ds(GUARD + 2 * start, size, stride=2), :] = tile
        ref[t, pl.ds(GUARD + 2 * start + 1, size, stride=2), :] = tile


def clear_guards(ref, rows):
    zeros = jnp.zeros((GUARD, LANES), jnp.float32)
    for t in range(ref.shape[0]):
        ref[t, 0:GUARD, :] = zeros
        ref[t, GUARD + rows : 2 * GUARD + rows, :] = zeros


def beside(mid, north, south, c_west, c_north, c_south, step):
    west = from_west(mid, step)
    east = from_east([c * m for c, m in zip(c_west, mid)], step)
    return [
        (c_west[t] * west[t] + east[t]) + (c_north[t] * north[t] + c_south[t] * south[t]) for t in range(len(mid))
    ]


def beside_of(ref, coeffs, start, size, step):
    c_west_ref, c_north_ref = coeffs
    mid = load(ref, start, size)
    north, south = load(ref, start - 1, size), load(ref, start + 1, size)
    c_west, c_north = load(c_west_ref, start, size), load(c_north_ref, start, size)
    return mid, beside(mid, north, south, c_west, c_north, load(c_north_ref, start + 1, size), step)


def pool_rows(ref, start, size, step):
    out = []
    for t in range(ref.shape[0]):
        even = ref[t, pl.ds(GUARD + start, size // 2, stride=2), :]
        odd = ref[t, pl.ds(GUARD + start + 1, size // 2, stride=2), :]
        both = even + odd
        out.append(both + roll(both, -step))
    return out


def descend(level, height, weight, source, guess, state, diagonal_ref, field, resid, next_weight, next_source, largest, part):
    step = 2**level
    c_west_ref, c_north_ref, scale_ref, smooth_ref = state
    for ref in (weight, field, c_north_ref):
        clear_guards(ref, height)

    def first_pass(start, size):
        w, w_north, w_south = (load(weight, start + k, size) for k in (0, -1, 1))
        c_north = [jnp.minimum(a, b) for a, b in zip(w, w_north)]
        c_south = [jnp.minimum(a, b) for a, b in zip(w, w_south)]
        c_west = [jnp.minimum(a, b) for a, b in zip(w, from_west(w, step))]
        c_east = from_east(c_west, step)
        diagonal = [damping + c_north[t] + c_south[t] + c_west[t] + c_east[t] for t in range(len(w))]
        scale = [relaxation / d for d in diagonal]
        store(c_north_ref, start, size, c_north)
        store(c_west_ref, start, size, c_west)
        store(scale_ref, start, size, scale)
        store(diagonal_ref, start, size, diagonal)
        value = load(source, start, size)
        if guess is None:
            value = [scale[t] * value[t] for t in range(len(w))]
        else:
            mid, north, south = (load(guess, start + k, size) for k in (0, -1, 1))
            around = beside(mid, north, south, c_west, c_north, c_south, step)
            value = [
                (1.0 - relaxation) * mid[t] + scale[t] * (value[t] + around[t]) for t in range(len(w))
            ]
        store(field, start, size, value)
        if next_weight is not None:
            pooled = [0.125 * p for p in pool_rows(weight, start, size, step)]
            store(next_weight, start // 2, size // 2, pooled)

    def second_pass(start, size):
        mid, around = beside_of(field, (c_west_ref, c_north_ref), start, size, step)
        b, scale, diagonal = (load(ref, start, size) for ref in (source, scale_ref, diagonal_ref))
        rest = [(b[t] + around[t]) - diagonal[t] * mid[t] for t in range(len(b))]
        store(smooth_ref, start, size, [mid[t] + scale[t] * rest[t] for t in range(len(b))])
        store(resid, start, size, rest)
        if next_source is not None:
            pooled = [0.25 * p for p in pool_rows(resid, start, size, step)]
            store(next_source, start // 2, size // 2, pooled)

    for_chunks(height, first_pass, largest, part)
    for_chunks(height, second_pass, largest, part)


def descend_all(rows, sources, guess, weights, states, diagonal, field, resid, largest, part):
    for level in range(LEVELS - 1):
        descend(
            level,
            rows >> level,
            weights[level],
            sources[level],
            guess if level == 0 else None,
            states[4 * level : 4 * level + 4],
            diagonal[level],
            field,
            resid,
            weights[level + 1],
            sources[level + 1],
            largest,
            part,
        )


def to_sides(west, east, cross_ref, pair_ref, k, rows):
    even = lax.axis_index("gy") % 2 == 0
    cross_ref[k, rows, :] = jnp.where(even, west, east)
    pair_ref[k, rows, :] = jnp.where(even, east, west)


def layout_kernel(source, guess, weight, own_source, own_guess, own_weight, cross_ref, pair_ref, *inner):
    rows = source.shape[0]
    piece = cross_ref.shape[1]
    tail = rows - (PIECES - 1) * piece
    for k, (block, own) in enumerate(zip((source, guess, weight), (own_source, own_guess, own_weight))):
        clear_rim(own)
        sides = []
        for t in range(2):
            own[t, GUARD + TOP : GUARD + TOP + rows, :] = block[:, t * LANES : (t + 1) * LANES]
        for tile, first in ((0, 0), (1, LANES - HALO)):
            columns = slice(tile * LANES, (tile + 1) * LANES)
            last = roll(block[(PIECES - 1) * piece :, columns], (PIECES - 1) * HALO - first)
            packed = jnp.concatenate((last, jnp.zeros((piece - tail, LANES), jnp.float32)), axis=0)
            for p in range(PIECES - 1):
                part = block[p * piece : (p + 1) * piece, columns]
                packed = jnp.where(lane_of(part) // HALO == p, roll(part, p * HALO - first), packed)
            sides.append(packed)
        to_sides(*sides, cross_ref, pair_ref, k, slice(0, piece))
    weights, start, height = (own_weight, *inner), TOP, rows
    for level in range(LEVELS):
        pooled = [0.125 * w for w in pool_rows(weights[level], start, height, 2**level)]
        start, height = start // 2, height // 2
        if level < LEVELS - 1:
            store(weights[level + 1], start, height, pooled)
    lane = lane_of(pooled[0])
    free = PIECES * HALO
    index = jnp.clip(lane - free, 0, LANES - 1 - free) * 2**LEVELS
    for t in range(2):
        taken = jnp.take_along_axis(pooled[t], index, axis=1)
        span = slice(t * height, (t + 1) * height)
        for ref in (cross_ref, pair_ref):
            ref[0, span, :] = jnp.where(lane >= free, taken, ref[0, span, :])


def halo_kernel(*refs):
    first_rows, second_rows, *own, cross_ref, pair_ref = refs[5:]
    total = own[0].shape[1] - 2 * GUARD
    piece = cross_ref.shape[1]
    even = lax.axis_index("gx") % 2 == 0
    shift = (PIECES - 1) * HALO
    for k in range(3):
        above = jnp.where(even, first_rows[k], second_rows[k])
        below = jnp.where(even, second_rows[k], first_rows[k])
        for rows, row, first in ((above, TOP - HALO, piece - 2 * HALO), (below, total - TOP, piece - HALO)):
            body = [rows[:, t * LANES : (t + 1) * LANES] for t in range(2)]
            for t in range(2):
                own[k][t, GUARD + row : GUARD + row + HALO, :] = body[t]
            span = slice(first, first + HALO)
            here = lane_of(body[0]) // HALO == PIECES - 1
            cross, pair = cross_ref[k, span, :], pair_ref[k, span, :]
            west, east = roll(body[0], shift), roll(body[1], shift + HALO - LANES)
            even_y = lax.axis_index("gy") % 2 == 0
            cross_ref[k, span, :] = jnp.where(here, jnp.where(even_y, west, east), cross)
            pair_ref[k, span, :] = jnp.where(here, jnp.where(even_y, east, west), pair)


def body_kernel(source, guess, weight, *refs):
    states = refs[: 4 * (LEVELS - 1)]
    last_weight, last_source, first_diagonal, field, resid, weight_in, *inner = refs[4 * (LEVELS - 1) :]
    rows = source.shape[1] - 2 * GUARD
    depth = LEVELS - 2
    weights = (weight_in, *inner[:depth], last_weight)
    sources = (source, *inner[depth : 2 * depth], last_source)
    diagonal = (first_diagonal, *inner[2 * depth :])
    weights[0][...] = weight[...]
    descend_all(rows, sources, guess, weights, states, diagonal, field, resid, 144, 144)


def frame_kernel(own_source, own_guess, own_weight, from_cross, from_pair, body_weight, body_source, *refs):
    even = lax.axis_index("gy") % 2 == 0
    states, refs = refs[: 4 * (LEVELS - 1)], refs[4 * (LEVELS - 1) :]
    frame_source, first_diagonal, ring_state, dense_ref, chunks_ref = refs[0], refs[1], refs[2:6], refs[6], refs[7]
    frame_guess, frame_weight, field, resid, *refs = refs[8:]
    ring_weight, ring_source, ring_field, ring_resid, ring_diagonal, *inner = refs
    rows = own_source.shape[1] - 2 * GUARD
    depth = LEVELS - 1
    weights = (frame_weight, *inner[:depth])
    sources = (frame_source, *inner[depth : 2 * depth])
    diagonals = (first_diagonal, *inner[2 * depth :])
    piece = from_cross.shape[1]
    for k, (own, frame) in enumerate(
        ((own_source, frame_source), (own_guess, frame_guess), (own_weight, frame_weight))
    ):
        clear_rim(frame)
        left = jnp.where(even, from_cross[k], from_pair[k])
        right = jnp.where(even, from_pair[k], from_cross[k])
        spans = [(p, 0, TOP + p * piece, piece) for p in range(PIECES - 1)]
        spans.append((PIECES - 1, 0, TOP + (PIECES - 1) * piece, piece - 2 * HALO))
        spans += [(PIECES - 1, piece - 2 * HALO, TOP - HALO, HALO), (PIECES - 1, piece - HALO, rows - TOP, HALO)]
        for p, first, start, size in spans:
            span = slice(GUARD + start, GUARD + start + size)
            west = roll(left[first : first + size], -p * HALO)
            east = roll(right[first : first + size], -(p + 1) * HALO)
            lane = lane_of(west)
            inside = jnp.where(lane < LANES // 2, roll(own[0, span, :], HALO), roll(own[1, span, :], -HALO))
            inside = jnp.where(lane < HALO, west, inside)
            frame[0, span, :] = jnp.where(lane >= LANES - HALO, east, inside)
    descend_all(rows, sources, frame_guess, weights, states, diagonals, field, resid, 288, 288)

    level = LEVELS - 1
    step, halo, height = 2**level, TOP >> level, rows >> level
    for body, frame, ring in (
        (body_weight, weights[level], ring_weight),
        (body_source, sources[level], ring_source),
    ):
        middle = load(body, 0, height)
        around = load(frame, 0, height)[0]
        lane = lane_of(around)
        ahead, back = roll(around, HALO), roll(around, -HALO)
        store(
            ring,
            0,
            height,
            [
                jnp.where(lane < 2 * step, back, middle[0]),
                jnp.where(lane >= LANES - 2 * step, ahead, middle[1]),
                jnp.where(lane < LANES // 2, ahead, back),
            ],
        )
    descend(
        level,
        height,
        ring_weight,
        ring_source,
        None,
        ring_state,
        ring_diagonal,
        ring_field,
        ring_resid,
        None,
        None,
        height,
        height,
    )

    coarse_rows = (height - 2 * halo) // 2
    dense = jnp.zeros((8, LANES), jnp.float32)
    lane = lane_of(dense)
    per_tile = LANES // 2**LEVELS
    pooled_b = pool_rows(ring_resid, halo, 2 * coarse_rows, step)
    pooled_w = pool_rows(ring_weight, halo, 2 * coarse_rows, step)
    index = (lane % per_tile) * 2**LEVELS
    place = lane // per_tile
    for g in range(coarse_rows // 8):
        for group, (values, factor) in enumerate(((pooled_b, 0.25), (pooled_w, 0.125))):
            for t in range(2):
                taken = jnp.take_along_axis(factor * values[t][8 * g : 8 * g + 8], index, axis=1)
                dense = jnp.where(place == 4 * g + 2 * group + t, taken, dense)
    dense_ref[...] = dense

    index = jnp.minimum(2 * (lane - lane % (2 * per_tile)) + lane % (2 * per_tile), LANES - 1)
    level_with, above, below = (fold(x) for x in (jnp.take_along_axis(dense, index, axis=1), dense, roll(dense, -LANES // 2)))
    x = lax.axis_index("gx")
    for i in range(chunks_ref.shape[0]):
        chunk = jnp.where(i == x, level_with, jnp.where(i < x, above, below))
        chunks_ref[i] = jnp.broadcast_to(chunk[None], chunks_ref.shape[1:])


def fold(x):
    return jnp.where(lane_of(x) < LANES // 2, x, pltpu.roll(roll(x, LANES // 2), 4, 0))[:4]


def unfold(x):
    return jnp.concatenate((x, roll(x, LANES // 2)), axis=0)


def coarse_solve(all_ref, dense_ref, from_cross, from_pair, width, groups):
    x, nx = lax.axis_index("gx"), lax.axis_size("gx")
    y, ny = lax.axis_index("gy"), lax.axis_size("gy")
    tiles = {}
    for dx in (-1, 0, 1):
        for dy in (-1, 0, 1):
            if dx or dy:
                inside = (x + dx >= 0) & (x + dx < nx) & (y + dy >= 0) & (y + dy < ny)
                tile = unfold(all_ref[jnp.where(inside, x + dx, 0), jnp.where(inside, y + dy, 0)])
                tiles[dx, dy] = jnp.where(inside, tile, 0.0)
    dense = dense_ref[...]
    lane = lane_of(dense)
    even = y % 2 == 0
    height = 8 * groups
    cross, pair = from_cross[0, : 2 * height, :], from_pair[0, : 2 * height, :]
    weights = {-1: jnp.where(even, cross, pair), 1: jnp.where(even, pair, cross)}
    bands = [(-1, g) for g in range(TALL // 8)] + [(0, g) for g in range(groups)] + [(1, g) for g in range(TALL // 8)]
    b, w = [], []
    for dx, g in bands:
        b_rows = w_rows = jnp.zeros_like(dense)
        for dy in (-1, 0, 1):
            first = (dy + 1) * width
            here = (lane >= first) & (lane < first + width)
            if dx or not dy:
                tile = tiles[dx, dy] if dx else dense
                b_part, w_part = roll(tile, first - 2 * g * width), roll(tile, first - (2 * g + 1) * width)
            else:
                b_part = roll(tiles[dx, dy], first - g * width)
                free = PIECES * HALO
                parts = [weights[dy][t * height + 8 * g : t * height + 8 * g + 8] for t in range(2)]
                parts = [roll(part, first + t * width // 2 - free) for t, part in enumerate(parts)]
                w_part = jnp.where(lane < first + width // 2, *parts)
            b_rows = jnp.where(here, b_part, b_rows)
            w_rows = jnp.where(here, w_part, w_rows)
        b.append(b_rows)
        w.append(w_rows)
    b, w = jnp.concatenate(b, axis=0), jnp.concatenate(w, axis=0)

    def north_of(x):
        return pltpu.roll(x, 1, 0)

    def south_of(x):
        return pltpu.roll(x, x.shape[0] - 1, 0)

    c_west = jnp.minimum(w, roll(w, 1))
    c_north = jnp.minimum(w, north_of(w))
    c_east, c_south = roll(c_west, -1), south_of(c_north)
    scale = relaxation / (damping + c_north + c_south + c_west + c_east)
    first = scale * b
    c_west, c_east, c_north, c_south = (scale * c for c in (c_west, c_east, c_north, c_south))

    def sweep(_, e):
        around = (c_west * roll(e, 1) + c_east * roll(e, -1)) + (c_north * north_of(e) + c_south * south_of(e))
        return ((1.0 - relaxation) * e + first) + around

    return lax.fori_loop(0, SWEEPS - 1, sweep, first)


def up_kernel(all_ref, dense_ref, from_cross, from_pair, own_source, frame_source, own_diagonal, frame_diagonal, *refs):
    count = 4 * (LEVELS - 1)
    body_state, frame_state, ring_state = refs[:count], refs[count : 2 * count], refs[2 * count : 2 * count + 4]
    out_ref, resid_ref = refs[2 * count + 4 : 2 * count + 6]
    ring_pe, body_final, frame_final, sems, *inner = refs[2 * count + 6 :]
    outs, inner = inner[:2], inner[2:]
    body_pe, frame_pe = inner[: LEVELS - 1], inner[LEVELS - 1 :]
    rows = out_ref.shape[0] + 2 * TOP
    width = out_ref.shape[1] >> LEVELS
    e = coarse_solve(all_ref, dense_ref, from_cross, from_pair, width, (out_ref.shape[0] >> LEVELS) // 8)

    level = LEVELS - 1
    step, halo, height = 2**level, TOP >> level, rows >> level
    coarse_rows = (height - 2 * halo) // 2
    picked = e[TALL - 8 : TALL + coarse_rows + 8]
    lane = lane_of(picked)
    for t in range(3):
        group = (lane + t * LANES) // 2**LEVELS
        if t == 2:
            group = jnp.where(lane < LANES // 2, group, group - 3 * LANES // 2**LEVELS)
        taken = jnp.take_along_axis(picked, jnp.clip(group + width, 0, LANES - 1), axis=1)[7 : 7 + coarse_rows + 2]
        ring_pe[t, 0 : 2 * GUARD, :] = jnp.zeros((2 * GUARD, LANES), jnp.float32)
        ring_pe[t, height : height + 2 * GUARD, :] = jnp.zeros((2 * GUARD, LANES), jnp.float32)
        ring_pe[t, pl.ds(GUARD + halo - 2, coarse_rows + 2, stride=2), :] = taken
        ring_pe[t, pl.ds(GUARD + halo - 1, coarse_rows + 2, stride=2), :] = taken

    def climbed(pe, state, start, size, step):
        mid, around = beside_of(pe, state[:2], start, size, step)
        scale, smooth = load(state[2], start, size), load(state[3], start, size)
        return [(smooth[t] + (1.0 - relaxation) * mid[t]) + scale[t] * around[t] for t in range(len(mid))]

    def climb_ring(start, size, level=level, step=step):
        ring = spread(climbed(ring_pe, ring_state, start, size, step), step // 2)
        lane = lane_of(ring[0])
        around = jnp.where(
            lane < LANES // 2,
            jnp.where(lane < HALO, roll(ring[2], HALO), roll(ring[0], HALO)),
            jnp.where(lane < LANES - HALO, roll(ring[1], -HALO), roll(ring[2], -HALO)),
        )
        store_twice(body_pe[level - 1], start, size, ring[:2])
        store_twice(frame_pe[level - 1], start, size, [around])

    for_chunks(height, climb_ring, height, 16)

    for level in range(LEVELS - 2, -1, -1):
        step, height = 2**level, rows >> level
        groups = ((body_pe, body_state, body_final), (frame_pe, frame_state, frame_final))
        for pes, _, _ in groups:
            clear_guards(pes[level], height)

        def climb(start, size, level=level, step=step, groups=groups):
            for pes, states, final in groups:
                value = climbed(pes[level], states[4 * level : 4 * level + 4], start, size, step)
                if level == 0:
                    store(final, start, size, value)
                else:
                    store_twice(pes[level - 1], start, size, spread(value, step // 2))

        for_chunks(height, climb, 144, 72)

    def last(start, size):
        base = start + TOP
        body, around = beside_of(body_final, body_state[:2], base, size, 1)
        frame, frame_around = beside_of(frame_final, frame_state[:2], base, size, 1)
        b, d = load(own_source, base, size), load(own_diagonal, base, size)
        b_frame, d_frame = load(frame_source, base, size), load(frame_diagonal, base, size)
        body = (body, [(b[t] + around[t]) - d[t] * body[t] for t in range(2)])
        frame = (frame[0], (b_frame[0] + frame_around[0]) - d_frame[0] * frame[0])
        lane = lane_of(frame[0])
        near = HALO - 4
        span = pl.ds(start, size)
        for ref, middle, around in ((outs[0], body[0], frame[0]), (outs[1], body[1], frame[1])):
            ref[span, :LANES] = jnp.where(lane < near, roll(around, -HALO), middle[0])
            ref[span, LANES:] = jnp.where(lane >= LANES - near, roll(around, HALO), middle[1])

    parts = sems.shape[0] // 2
    size = out_ref.shape[0] // parts

    def copies(p):
        span = pl.ds(p * size, size)
        return [
            pltpu.make_async_copy(outs[k].at[span], ref.at[span], sems.at[2 * p + k])
            for k, ref in enumerate((out_ref, resid_ref))
        ]

    def finish(p, carry):
        for_parts(p * size, size, last, 16)
        for copy in copies(p):
            copy.start()
        return carry

    lax.fori_loop(0, parts, finish, 0)
    for p in range(parts):
        for copy in copies(p):
            copy.wait()


def call(kernel, out_shape, scratch, flops, moved, **more):
    return pl.pallas_call(
        kernel,
        out_shape=out_shape,
        scratch_shapes=scratch,
        compiler_params=pltpu.CompilerParams(vmem_limit_bytes=VMEM_LIMIT),
        cost_estimate=pl.CostEstimate(flops=flops, bytes_accessed=moved, transcendentals=0),
        **more,
    )


def swap(x, axis, first):
    pairs = [(i, i + 1) for i in range(first, lax.axis_size(axis) - 1, 2)]
    return lax.ppermute(x, axis, pairs + [(j, i) for i, j in pairs])


def local(rhs, pressure, wet_mask, bathy_class):
    rows, columns = rhs.shape
    cells = rows * columns
    total = rows + 2 * TOP
    levels = range(LEVELS - 1)

    def shape(tiles, level):
        return (tiles, (total >> level) + 2 * GUARD, LANES)

    def out(*dims):
        return jax.ShapeDtypeStruct(dims, jnp.float32)

    def vmem(tiles, level):
        return pltpu.VMEM(shape(tiles, level), jnp.float32)

    def fields(r, p, m, c):
        wet = m.astype(jnp.float32)
        return wet * r, wet * p, wet * (1.0 + 0.5 * c.astype(jnp.float32))

    given = (rhs, pressure, wet_mask, bathy_class)

    def edge(start):
        return jnp.stack(fields(*(lax.dynamic_slice_in_dim(x, start, HALO, axis=0) for x in given)))

    even = lax.axis_index("gx") % 2 == 0
    first_rows = swap(edge(jnp.where(even, 0, rows - HALO)), "gx", 1)
    second_rows = swap(edge(jnp.where(even, rows - HALO, 0)), "gx", 0)
    piece = (rows + 2 * HALO) // PIECES
    own_shapes = [out(*shape(2, 0))] * 3
    laid_out = [*own_shapes, out(3, piece, LANES), out(3, piece, LANES)]
    inner = [vmem(2, level) for level in range(1, LEVELS)]
    begun = call(layout_kernel, laid_out, inner, 10 * cells, 10 * cells)(*fields(*given))
    *own, to_cross, to_pair = call(
        halo_kernel, laid_out, (), cells, cells, input_output_aliases={k: k for k in range(5)}
    )(*begun, first_rows, second_rows)
    from_cross = swap(to_cross, "gy", 1)
    from_pair = swap(to_pair, "gy", 0)

    state_count = 4 * (LEVELS - 1)
    *body_state, body_weight, body_source, diagonal = call(
        body_kernel,
        [out(*shape(2, level)) for level in levels for _ in range(4)]
        + [out(*shape(2, LEVELS - 1))] * 2
        + [out(*shape(2, 0))],
        [vmem(2, 0)] * 3 + [vmem(2, level) for level in levels[1:]] * 3,
        100 * cells,
        40 * cells,
    )(*own)
    nx, ny = lax.axis_size("gx"), lax.axis_size("gy")
    ring = LEVELS - 1
    *state, dense, chunks = call(
        frame_kernel,
        [out(*shape(1, level)) for level in levels for _ in range(4)]
        + [out(*shape(1, 0))] * 2
        + [out(*shape(3, ring))] * 4
        + [out(8, LANES), out(nx, ny, 4, LANES)],
        [vmem(1, 0)] * 4 + [vmem(3, ring)] * 5 + [vmem(1, level) for level in range(1, LEVELS)] * 3,
        50 * cells,
        20 * cells,
    )(*own, from_cross, from_pair, body_weight, body_source)
    frame_state, ring_state = state[:state_count], state[state_count + 2 :]
    frame_source, frame_diagonal = state[state_count : state_count + 2]
    gathered = lax.all_to_all(chunks.reshape(nx * ny, 4, LANES), ("gx", "gy"), 0, 0).reshape(chunks.shape)
    return call(
        up_kernel,
        (out(rows, columns), out(rows, columns)),
        [vmem(3, ring), vmem(2, 0), vmem(1, 0), pltpu.SemaphoreType.DMA((8,))]
        + [pltpu.VMEM((rows, columns), jnp.float32)] * 2
        + [vmem(2, level) for level in levels]
        + [vmem(1, level) for level in levels],
        60 * cells,
        40 * cells,
        out_specs=[pl.BlockSpec(memory_space=pl.ANY)] * 2,
    )(gathered, dense, from_cross, from_pair, own[0], frame_source, diagonal, frame_diagonal, *body_state, *frame_state, *ring_state)


def solution(mesh):
    placed = (P("gx", "gy"), P("gx", "gy"), P("gx", "gy"), P("gx", "gy"))
    return jax.shard_map(
        local, mesh=mesh, in_specs=placed, out_specs=(P("gx", "gy"), P("gx", "gy")), check_vma=False
    )
```

```python
import jax
import jax.numpy as jnp
from jax import lax
from jax.experimental import pallas as pl
from jax.experimental.pallas import tpu as pltpu
from jax.sharding import PartitionSpec as P

LEVELS = 4
SWEEPS = 12

damping = 0.01
relaxation = 0.8

HALO = 24
LANES = 128
INNER = LANES // 2 - HALO
TOP = 32
GUARD = 8
PIECES = 5
TALL = 16
VMEM_LIMIT = 40 * 1024 * 1024


def lane_of(x):
    return lax.broadcasted_iota(jnp.int32, x.shape, x.ndim - 1)


def roll(x, amount):
    amount %= LANES
    return x if amount == 0 else pltpu.roll(x, amount, x.ndim - 1)


def from_west(tiles, step):
    moved = [roll(t, step) for t in tiles]
    if len(tiles) == 1:
        return moved
    edge = lane_of(tiles[0]) < step
    return [jnp.where(edge, moved[i - 1], moved[i]) for i in range(len(tiles))]


def from_east(tiles, step):
    moved = [roll(t, -step) for t in tiles]
    count = len(tiles)
    if count == 1:
        return moved
    edge = lane_of(tiles[0]) >= LANES - step
    return [jnp.where(edge, moved[(i + 1) % count], moved[i]) for i in range(count)]


def clear_rim(ref):
    rim = GUARD + TOP - HALO
    zeros = jnp.zeros((rim, LANES), jnp.float32)
    for t in range(ref.shape[0]):
        ref[t, 0:rim, :] = zeros
        ref[t, ref.shape[1] - rim :, :] = zeros


def spread(tiles, step):
    second = (lane_of(tiles[0]) // step) % 2 == 1
    return [jnp.where(second, roll(t, step), t) for t in tiles]


def for_parts(start, size, body, part):
    for offset in range(0, size, part):
        body(start + offset, min(part, size - offset))


def for_chunks(rows, body, largest, part):
    sizes = [size for size in range(8, largest + 1, 8) if rows % size == 0]
    if rows <= largest or not sizes:
        for_parts(0, rows, body, part)
        return

    def step(i, carry):
        for_parts(i * sizes[-1], sizes[-1], body, part)
        return carry

    lax.fori_loop(0, rows // sizes[-1], step, 0)


def load(ref, start, size):
    return [ref[t, pl.ds(GUARD + start, size), :] for t in range(ref.shape[0])]


def store(ref, start, size, tiles):
    for t, tile in enumerate(tiles):
        ref[t, pl.ds(GUARD + start, size), :] = tile


def store_twice(ref, start, size, tiles):
    for t, tile in enumerate(tiles):
        ref[t, pl.ds(GUARD + 2 * start, size, stride=2), :] = tile
        ref[t, pl.ds(GUARD + 2 * start + 1, size, stride=2), :] = tile


def clear_guards(ref, rows):
    zeros = jnp.zeros((GUARD, LANES), jnp.float32)
    for t in range(ref.shape[0]):
        ref[t, 0:GUARD, :] = zeros
        ref[t, GUARD + rows : 2 * GUARD + rows, :] = zeros


def beside(mid, north, south, c_west, c_north, c_south, step):
    west = from_west(mid, step)
    east = from_east([c * m for c, m in zip(c_west, mid)], step)
    return [
        (c_west[t] * west[t] + east[t]) + (c_north[t] * north[t] + c_south[t] * south[t]) for t in range(len(mid))
    ]


def beside_of(ref, coeffs, start, size, step):
    c_west_ref, c_north_ref = coeffs
    mid = load(ref, start, size)
    north, south = load(ref, start - 1, size), load(ref, start + 1, size)
    c_west, c_north = load(c_west_ref, start, size), load(c_north_ref, start, size)
    return mid, beside(mid, north, south, c_west, c_north, load(c_north_ref, start + 1, size), step)


def pool_rows(ref, start, size, step):
    out = []
    for t in range(ref.shape[0]):
        even = ref[t, pl.ds(GUARD + start, size // 2, stride=2), :]
        odd = ref[t, pl.ds(GUARD + start + 1, size // 2, stride=2), :]
        both = even + odd
        out.append(both + roll(both, -step))
    return out


def descend(level, height, weight, source, guess, state, diagonal_ref, field, resid, next_weight, next_source, largest, part):
    step = 2**level
    c_west_ref, c_north_ref, scale_ref, smooth_ref = state
    for ref in (weight, field, c_north_ref):
        clear_guards(ref, height)

    def first_pass(start, size):
        w, w_north, w_south = (load(weight, start + k, size) for k in (0, -1, 1))
        c_north = [jnp.minimum(a, b) for a, b in zip(w, w_north)]
        c_south = [jnp.minimum(a, b) for a, b in zip(w, w_south)]
        c_west = [jnp.minimum(a, b) for a, b in zip(w, from_west(w, step))]
        c_east = from_east(c_west, step)
        diagonal = [damping + c_north[t] + c_south[t] + c_west[t] + c_east[t] for t in range(len(w))]
        scale = [relaxation / d for d in diagonal]
        store(c_north_ref, start, size, c_north)
        store(c_west_ref, start, size, c_west)
        store(scale_ref, start, size, scale)
        store(diagonal_ref, start, size, diagonal)
        value = load(source, start, size)
        if guess is None:
            value = [scale[t] * value[t] for t in range(len(w))]
        else:
            mid, north, south = (load(guess, start + k, size) for k in (0, -1, 1))
            around = beside(mid, north, south, c_west, c_north, c_south, step)
            value = [
                (1.0 - relaxation) * mid[t] + scale[t] * (value[t] + around[t]) for t in range(len(w))
            ]
        store(field, start, size, value)
        if next_weight is not None:
            pooled = [0.125 * p for p in pool_rows(weight, start, size, step)]
            store(next_weight, start // 2, size // 2, pooled)

    def second_pass(start, size):
        mid, around = beside_of(field, (c_west_ref, c_north_ref), start, size, step)
        b, scale, diagonal = (load(ref, start, size) for ref in (source, scale_ref, diagonal_ref))
        rest = [(b[t] + around[t]) - diagonal[t] * mid[t] for t in range(len(b))]
        store(smooth_ref, start, size, [mid[t] + scale[t] * rest[t] for t in range(len(b))])
        store(resid, start, size, rest)
        if next_source is not None:
            pooled = [0.25 * p for p in pool_rows(resid, start, size, step)]
            store(next_source, start // 2, size // 2, pooled)

    for_chunks(height, first_pass, largest, part)
    for_chunks(height, second_pass, largest, part)


def descend_all(rows, sources, guess, weights, states, diagonal, field, resid, largest, part):
    for level in range(LEVELS - 1):
        descend(
            level,
            rows >> level,
            weights[level],
            sources[level],
            guess if level == 0 else None,
            states[4 * level : 4 * level + 4],
            diagonal[level],
            field,
            resid,
            weights[level + 1],
            sources[level + 1],
            largest,
            part,
        )


def to_sides(west, east, cross_ref, pair_ref, k, rows):
    even = lax.axis_index("gy") % 2 == 0
    cross_ref[k, rows, :] = jnp.where(even, west, east)
    pair_ref[k, rows, :] = jnp.where(even, east, west)


def layout_kernel(source, guess, weight, own_source, own_guess, own_weight, cross_ref, pair_ref, *inner):
    rows = source.shape[0]
    piece = cross_ref.shape[1]
    tail = rows - (PIECES - 1) * piece
    for k, (block, own) in enumerate(zip((source, guess, weight), (own_source, own_guess, own_weight))):
        clear_rim(own)
        sides = []
        for t in range(2):
            own[t, GUARD + TOP : GUARD + TOP + rows, :] = block[:, t * LANES : (t + 1) * LANES]
        for tile, first in ((0, 0), (1, LANES - HALO)):
            columns = slice(tile * LANES, (tile + 1) * LANES)
            last = roll(block[(PIECES - 1) * piece :, columns], (PIECES - 1) * HALO - first)
            packed = jnp.concatenate((last, jnp.zeros((piece - tail, LANES), jnp.float32)), axis=0)
            for p in range(PIECES - 1):
                part = block[p * piece : (p + 1) * piece, columns]
                packed = jnp.where(lane_of(part) // HALO == p, roll(part, p * HALO - first), packed)
            sides.append(packed)
        to_sides(*sides, cross_ref, pair_ref, k, slice(0, piece))
    weights, start, height = (own_weight, *inner), TOP, rows
    for level in range(LEVELS):
        pooled = [0.125 * w for w in pool_rows(weights[level], start, height, 2**level)]
        start, height = start // 2, height // 2
        if level < LEVELS - 1:
            store(weights[level + 1], start, height, pooled)
    lane = lane_of(pooled[0])
    free = PIECES * HALO
    index = jnp.clip(lane - free, 0, LANES - 1 - free) * 2**LEVELS
    for t in range(2):
        taken = jnp.take_along_axis(pooled[t], index, axis=1)
        span = slice(t * height, (t + 1) * height)
        for ref in (cross_ref, pair_ref):
            ref[0, span, :] = jnp.where(lane >= free, taken, ref[0, span, :])


def halo_kernel(*refs):
    first_rows, second_rows, *own, cross_ref, pair_ref = refs[5:]
    total = own[0].shape[1] - 2 * GUARD
    piece = cross_ref.shape[1]
    even = lax.axis_index("gx") % 2 == 0
    shift = (PIECES - 1) * HALO
    for k in range(3):
        above = jnp.where(even, first_rows[k], second_rows[k])
        below = jnp.where(even, second_rows[k], first_rows[k])
        for rows, row, first in ((above, TOP - HALO, piece - 2 * HALO), (below, total - TOP, piece - HALO)):
            body = [rows[:, t * LANES : (t + 1) * LANES] for t in range(2)]
            for t in range(2):
                own[k][t, GUARD + row : GUARD + row + HALO, :] = body[t]
            span = slice(first, first + HALO)
            here = lane_of(body[0]) // HALO == PIECES - 1
            cross, pair = cross_ref[k, span, :], pair_ref[k, span, :]
            west, east = roll(body[0], shift), roll(body[1], shift + HALO - LANES)
            even_y = lax.axis_index("gy") % 2 == 0
            cross_ref[k, span, :] = jnp.where(here, jnp.where(even_y, west, east), cross)
            pair_ref[k, span, :] = jnp.where(here, jnp.where(even_y, east, west), pair)


def body_kernel(source, guess, weight, *refs):
    states = refs[: 4 * (LEVELS - 1)]
    last_weight, last_source, first_diagonal, *refs = refs[4 * (LEVELS - 1) :]
    frames, (field, resid, weight_in, *inner) = refs[:3], refs[3:]
    rows = source.shape[1] - 2 * GUARD
    depth = LEVELS - 2
    weights = (weight_in, *inner[:depth], last_weight)
    sources = (source, *inner[depth : 2 * depth], last_source)
    diagonal = (first_diagonal, *inner[2 * depth :])
    weights[0][...] = weight[...]
    descend_all(rows, sources, guess, weights, states, diagonal, field, resid, 144, 144)
    for own, frame in zip((source, guess, weight), frames):
        tiles = [own[t] for t in range(2)]
        frame[0] = jnp.where(lane_of(tiles[0]) < LANES // 2, roll(tiles[0], HALO), roll(tiles[1], -HALO))


def frame_kernel(_a, _b, _c, from_cross, from_pair, body_weight, body_source, *refs):
    even = lax.axis_index("gy") % 2 == 0
    frames, states, refs = refs[:3], refs[3 : 3 + 4 * (LEVELS - 1)], refs[3 + 4 * (LEVELS - 1) :]
    frame_source, frame_guess, frame_weight = frames
    first_diagonal, ring_state, dense_ref, chunks_ref, field, resid, *refs = refs[0], refs[1:5], *refs[5:]
    ring_weight, ring_source, ring_field, ring_resid, ring_diagonal, *inner = refs
    rows = frame_source.shape[1] - 2 * GUARD
    depth = LEVELS - 1
    weights = (frame_weight, *inner[:depth])
    sources = (frame_source, *inner[depth : 2 * depth])
    diagonals = (first_diagonal, *inner[2 * depth :])
    piece = from_cross.shape[1]
    for k, frame in enumerate(frames):
        left = jnp.where(even, from_cross[k], from_pair[k])
        right = jnp.where(even, from_pair[k], from_cross[k])
        spans = [(p, 0, TOP + p * piece, piece) for p in range(PIECES - 1)]
        spans.append((PIECES - 1, 0, TOP + (PIECES - 1) * piece, piece - 2 * HALO))
        spans += [(PIECES - 1, piece - 2 * HALO, TOP - HALO, HALO), (PIECES - 1, piece - HALO, rows - TOP, HALO)]
        for p, first, start, size in spans:
            span = slice(GUARD + start, GUARD + start + size)
            west = roll(left[first : first + size], -p * HALO)
            east = roll(right[first : first + size], -(p + 1) * HALO)
            lane = lane_of(west)
            inside = jnp.where(lane < HALO, west, frame[0, span, :])
            frame[0, span, :] = jnp.where(lane >= LANES - HALO, east, inside)
    descend_all(rows, sources, frame_guess, weights, states, diagonals, field, resid, 288, 288)

    level = LEVELS - 1
    step, halo, height = 2**level, TOP >> level, rows >> level
    for body, frame, ring in (
        (body_weight, weights[level], ring_weight),
        (body_source, sources[level], ring_source),
    ):
        middle = load(body, 0, height)
        around = load(frame, 0, height)[0]
        lane = lane_of(around)
        ahead, back = roll(around, HALO), roll(around, -HALO)
        store(
            ring,
            0,
            height,
            [
                jnp.where(lane < 2 * step, back, middle[0]),
                jnp.where(lane >= LANES - 2 * step, ahead, middle[1]),
                jnp.where(lane < LANES // 2, ahead, back),
            ],
        )
    descend(
        level,
        height,
        ring_weight,
        ring_source,
        None,
        ring_state,
        ring_diagonal,
        ring_field,
        ring_resid,
        None,
        None,
        height,
        height,
    )

    coarse_rows = (height - 2 * halo) // 2
    dense = jnp.zeros((8, LANES), jnp.float32)
    lane = lane_of(dense)
    per_tile = LANES // 2**LEVELS
    pooled_b = pool_rows(ring_resid, halo, 2 * coarse_rows, step)
    pooled_w = pool_rows(ring_weight, halo, 2 * coarse_rows, step)
    index = (lane % per_tile) * 2**LEVELS
    place = lane // per_tile
    for g in range(coarse_rows // 8):
        for group, (values, factor) in enumerate(((pooled_b, 0.25), (pooled_w, 0.125))):
            for t in range(2):
                taken = jnp.take_along_axis(factor * values[t][8 * g : 8 * g + 8], index, axis=1)
                dense = jnp.where(place == 4 * g + 2 * group + t, taken, dense)
    dense_ref[...] = dense

    index = jnp.minimum(2 * (lane - lane % (2 * per_tile)) + lane % (2 * per_tile), LANES - 1)
    level_with, above, below = (fold(x) for x in (jnp.take_along_axis(dense, index, axis=1), dense, roll(dense, -LANES // 2)))
    x = lax.axis_index("gx")
    for i in range(chunks_ref.shape[0]):
        chunk = jnp.where(i == x, level_with, jnp.where(i < x, above, below))
        chunks_ref[i] = jnp.broadcast_to(chunk[None], chunks_ref.shape[1:])


def fold(x):
    return jnp.where(lane_of(x) < LANES // 2, x, pltpu.roll(roll(x, LANES // 2), 4, 0))[:4]


def unfold(x):
    return jnp.concatenate((x, roll(x, LANES // 2)), axis=0)


def coarse_solve(all_ref, dense_ref, from_cross, from_pair, e_ref, width, groups):
    x, nx = lax.axis_index("gx"), lax.axis_size("gx")
    y, ny = lax.axis_index("gy"), lax.axis_size("gy")
    tiles = {}
    for dx in (-1, 0, 1):
        for dy in (-1, 0, 1):
            if dx or dy:
                inside = (x + dx >= 0) & (x + dx < nx) & (y + dy >= 0) & (y + dy < ny)
                tile = unfold(all_ref[jnp.where(inside, x + dx, 0), jnp.where(inside, y + dy, 0)])
                tiles[dx, dy] = jnp.where(inside, tile, 0.0)
    dense = dense_ref[...]
    lane = lane_of(dense)
    even = y % 2 == 0
    height = 8 * groups
    cross, pair = from_cross[0, : 2 * height, :], from_pair[0, : 2 * height, :]
    weights = {-1: jnp.where(even, cross, pair), 1: jnp.where(even, pair, cross)}
    bands = [(-1, g) for g in range(TALL // 8)] + [(0, g) for g in range(groups)] + [(1, g) for g in range(TALL // 8)]
    b, w = [], []
    for dx, g in bands:
        b_rows = w_rows = jnp.zeros_like(dense)
        for dy in (-1, 0, 1):
            first = (dy + 1) * width
            here = (lane >= first) & (lane < first + width)
            if dx or not dy:
                tile = tiles[dx, dy] if dx else dense
                b_part, w_part = roll(tile, first - 2 * g * width), roll(tile, first - (2 * g + 1) * width)
            else:
                b_part = roll(tiles[dx, dy], first - g * width)
                free = PIECES * HALO
                parts = [weights[dy][t * height + 8 * g : t * height + 8 * g + 8] for t in range(2)]
                parts = [roll(part, first + t * width // 2 - free) for t, part in enumerate(parts)]
                w_part = jnp.where(lane < first + width // 2, *parts)
            b_rows = jnp.where(here, b_part, b_rows)
            w_rows = jnp.where(here, w_part, w_rows)
        b.append(b_rows)
        w.append(w_rows)
    b, w = jnp.concatenate(b, axis=0), jnp.concatenate(w, axis=0)

    rows = b.shape[0]
    zeros = jnp.zeros((GUARD, LANES), jnp.float32)
    e_ref[0:GUARD, :] = zeros
    e_ref[GUARD + rows :, :] = zeros

    def shifted(by):
        return e_ref[GUARD + by : GUARD + by + rows, :]

    e_ref[GUARD : GUARD + rows, :] = w
    c_west = jnp.minimum(w, roll(w, 1))
    c_north, c_south = jnp.minimum(w, shifted(-1)), jnp.minimum(w, shifted(1))
    c_east = roll(c_west, -1)
    scale = relaxation / (damping + c_north + c_south + c_west + c_east)
    first = scale * b
    c_west, c_east, c_north, c_south = (scale * c for c in (c_west, c_east, c_north, c_south))
    e_ref[GUARD : GUARD + rows, :] = first

    def sweep(_, carry):
        e = shifted(0)
        around = (c_west * roll(e, 1) + c_east * roll(e, -1)) + (c_north * shifted(-1) + c_south * shifted(1))
        e_ref[GUARD : GUARD + rows, :] = ((1.0 - relaxation) * e + first) + around
        return carry

    lax.fori_loop(0, SWEEPS - 1, sweep, 0)
    return shifted(0)


def up_kernel(all_ref, dense_ref, from_cross, from_pair, own_source, frame_source, own_diagonal, frame_diagonal, *refs):
    count = 4 * (LEVELS - 1)
    body_state, frame_state, ring_state = refs[:count], refs[count : 2 * count], refs[2 * count : 2 * count + 4]
    out_ref, resid_ref = refs[2 * count + 4 : 2 * count + 6]
    ring_pe, body_final, frame_final, sems, e_ref, *inner = refs[2 * count + 6 :]
    outs, inner = inner[:2], inner[2:]
    body_pe, frame_pe = inner[: LEVELS - 1], inner[LEVELS - 1 :]
    rows = out_ref.shape[0] + 2 * TOP
    width = out_ref.shape[1] >> LEVELS
    e = coarse_solve(all_ref, dense_ref, from_cross, from_pair, e_ref, width, (out_ref.shape[0] >> LEVELS) // 8)

    level = LEVELS - 1
    step, halo, height = 2**level, TOP >> level, rows >> level
    coarse_rows = (height - 2 * halo) // 2
    picked = e[TALL - 8 : TALL + coarse_rows + 8]
    lane = lane_of(picked)
    for t in range(3):
        group = (lane + t * LANES) // 2**LEVELS
        if t == 2:
            group = jnp.where(lane < LANES // 2, group, group - 3 * LANES // 2**LEVELS)
        taken = jnp.take_along_axis(picked, jnp.clip(group + width, 0, LANES - 1), axis=1)[7 : 7 + coarse_rows + 2]
        ring_pe[t, 0 : 2 * GUARD, :] = jnp.zeros((2 * GUARD, LANES), jnp.float32)
        ring_pe[t, height : height + 2 * GUARD, :] = jnp.zeros((2 * GUARD, LANES), jnp.float32)
        ring_pe[t, pl.ds(GUARD + halo - 2, coarse_rows + 2, stride=2), :] = taken
        ring_pe[t, pl.ds(GUARD + halo - 1, coarse_rows + 2, stride=2), :] = taken

    def climbed(pe, state, start, size, step):
        mid, around = beside_of(pe, state[:2], start, size, step)
        scale, smooth = load(state[2], start, size), load(state[3], start, size)
        return [(smooth[t] + (1.0 - relaxation) * mid[t]) + scale[t] * around[t] for t in range(len(mid))]

    def climb_ring(start, size, level=level, step=step):
        ring = spread(climbed(ring_pe, ring_state, start, size, step), step // 2)
        lane = lane_of(ring[0])
        around = jnp.where(
            lane < LANES // 2,
            jnp.where(lane < HALO, roll(ring[2], HALO), roll(ring[0], HALO)),
            jnp.where(lane < LANES - HALO, roll(ring[1], -HALO), roll(ring[2], -HALO)),
        )
        store_twice(body_pe[level - 1], start, size, ring[:2])
        store_twice(frame_pe[level - 1], start, size, [around])

    for_chunks(height, climb_ring, height, 16)

    for level in range(LEVELS - 2, -1, -1):
        step, height = 2**level, rows >> level
        groups = ((body_pe, body_state, body_final), (frame_pe, frame_state, frame_final))
        for pes, _, _ in groups:
            clear_guards(pes[level], height)

        def climb(start, size, level=level, step=step, groups=groups):
            for pes, states, final in groups:
                value = climbed(pes[level], states[4 * level : 4 * level + 4], start, size, step)
                if level == 0:
                    store(final, start, size, value)
                else:
                    store_twice(pes[level - 1], start, size, spread(value, step // 2))

        for_chunks(height, climb, 144, 72)

    def last(start, size):
        base = start + TOP
        body, around = beside_of(body_final, body_state[:2], base, size, 1)
        frame, frame_around = beside_of(frame_final, frame_state[:2], base, size, 1)
        b, d = load(own_source, base, size), load(own_diagonal, base, size)
        b_frame, d_frame = load(frame_source, base, size), load(frame_diagonal, base, size)
        body = (body, [(b[t] + around[t]) - d[t] * body[t] for t in range(2)])
        frame = (frame[0], (b_frame[0] + frame_around[0]) - d_frame[0] * frame[0])
        lane = lane_of(frame[0])
        near = HALO - 4
        span = pl.ds(start, size)
        for ref, middle, around in ((outs[0], body[0], frame[0]), (outs[1], body[1], frame[1])):
            ref[span, :LANES] = jnp.where(lane < near, roll(around, -HALO), middle[0])
            ref[span, LANES:] = jnp.where(lane >= LANES - near, roll(around, HALO), middle[1])

    parts = sems.shape[0] // 2
    size = out_ref.shape[0] // parts

    def copies(p):
        span = pl.ds(p * size, size)
        return [
            pltpu.make_async_copy(outs[k].at[span], ref.at[span], sems.at[2 * p + k])
            for k, ref in enumerate((out_ref, resid_ref))
        ]

    def finish(p, carry):
        for_parts(p * size, size, last, 16)
        for copy in copies(p):
            copy.start()
        return carry

    lax.fori_loop(0, parts, finish, 0)
    for p in range(parts):
        for copy in copies(p):
            copy.wait()


def call(kernel, out_shape, scratch, flops, moved, **more):
    return pl.pallas_call(
        kernel,
        out_shape=out_shape,
        scratch_shapes=scratch,
        compiler_params=pltpu.CompilerParams(vmem_limit_bytes=VMEM_LIMIT),
        cost_estimate=pl.CostEstimate(flops=flops, bytes_accessed=moved, transcendentals=0),
        **more,
    )


def swap(x, axis, first):
    pairs = [(i, i + 1) for i in range(first, lax.axis_size(axis) - 1, 2)]
    return lax.ppermute(x, axis, pairs + [(j, i) for i, j in pairs])


def local(rhs, pressure, wet_mask, bathy_class):
    rows, columns = rhs.shape
    cells = rows * columns
    total = rows + 2 * TOP
    levels = range(LEVELS - 1)

    def shape(tiles, level):
        return (tiles, (total >> level) + 2 * GUARD, LANES)

    def out(*dims):
        return jax.ShapeDtypeStruct(dims, jnp.float32)

    def vmem(tiles, level):
        return pltpu.VMEM(shape(tiles, level), jnp.float32)

    def fields(r, p, m, c):
        wet = m.astype(jnp.float32)
        return wet * r, wet * p, wet * (1.0 + 0.5 * c.astype(jnp.float32))

    given = (rhs, pressure, wet_mask, bathy_class)

    def edge(start):
        return jnp.stack(fields(*(lax.dynamic_slice_in_dim(x, start, HALO, axis=0) for x in given)))

    even = lax.axis_index("gx") % 2 == 0
    first_rows = swap(edge(jnp.where(even, 0, rows - HALO)), "gx", 1)
    second_rows = swap(edge(jnp.where(even, rows - HALO, 0)), "gx", 0)
    piece = (rows + 2 * HALO) // PIECES
    own_shapes = [out(*shape(2, 0))] * 3
    laid_out = [*own_shapes, out(3, piece, LANES), out(3, piece, LANES)]
    inner = [vmem(2, level) for level in range(1, LEVELS)]
    begun = call(layout_kernel, laid_out, inner, 10 * cells, 10 * cells)(*fields(*given))
    *own, to_cross, to_pair = call(
        halo_kernel, laid_out, (), cells, cells, input_output_aliases={k: k for k in range(5)}
    )(*begun, first_rows, second_rows)
    from_cross = swap(to_cross, "gy", 1)
    from_pair = swap(to_pair, "gy", 0)

    state_count = 4 * (LEVELS - 1)
    *body_state, body_weight, body_source, diagonal, frame_source, frame_guess, frame_weight = call(
        body_kernel,
        [out(*shape(2, level)) for level in levels for _ in range(4)]
        + [out(*shape(2, LEVELS - 1))] * 2
        + [out(*shape(2, 0))]
        + [out(*shape(1, 0))] * 3,
        [vmem(2, 0)] * 3 + [vmem(2, level) for level in levels[1:]] * 3,
        100 * cells,
        40 * cells,
    )(*own)
    nx, ny = lax.axis_size("gx"), lax.axis_size("gy")
    ring = LEVELS - 1
    frame_source, _, _, *state, dense, chunks = call(
        frame_kernel,
        [out(*shape(1, 0))] * 3
        + [out(*shape(1, level)) for level in levels for _ in range(4)]
        + [out(*shape(1, 0))]
        + [out(*shape(3, ring))] * 4
        + [out(8, LANES), out(nx, ny, 4, LANES)],
        [vmem(1, 0)] * 2 + [vmem(3, ring)] * 5 + [vmem(1, level) for level in range(1, LEVELS)] * 3,
        50 * cells,
        20 * cells,
        input_output_aliases={k: k for k in range(3)},
    )(frame_source, frame_guess, frame_weight, from_cross, from_pair, body_weight, body_source)
    frame_state, frame_diagonal, ring_state = state[:state_count], state[state_count], state[state_count + 1 :]
    gathered = lax.all_to_all(chunks.reshape(nx * ny, 4, LANES), ("gx", "gy"), 0, 0).reshape(chunks.shape)
    return call(
        up_kernel,
        (out(rows, columns), out(rows, columns)),
        [vmem(3, ring), vmem(2, 0), vmem(1, 0), pltpu.SemaphoreType.DMA((8,))]
        + [pltpu.VMEM(((rows >> LEVELS) + 2 * TALL + 2 * GUARD, LANES), jnp.float32)]
        + [pltpu.VMEM((rows, columns), jnp.float32)] * 2
        + [vmem(2, level) for level in levels]
        + [vmem(1, level) for level in levels],
        60 * cells,
        40 * cells,
        out_specs=[pl.BlockSpec(memory_space=pl.ANY)] * 2,
    )(gathered, dense, from_cross, from_pair, own[0], frame_source, diagonal, frame_diagonal, *body_state, *frame_state, *ring_state)


def solution(mesh):
    placed = (P("gx", "gy"), P("gx", "gy"), P("gx", "gy"), P("gx", "gy"))
    return jax.shard_map(
        local, mesh=mesh, in_specs=placed, out_specs=(P("gx", "gy"), P("gx", "gy")), check_vma=False
    )
```

```python
import jax
import jax.numpy as jnp
from jax import lax
from jax.experimental import pallas as pl
from jax.experimental.pallas import tpu as pltpu
from jax.sharding import PartitionSpec as P

LEVELS = 4
SWEEPS = 12

damping = 0.01
relaxation = 0.8

HALO = 24
LANES = 128
INNER = LANES // 2 - HALO
TOP = 32
GUARD = 8
PIECES = 5
CHUNK = 144
LAG = 8
TALL = 16
VMEM_LIMIT = 40 * 1024 * 1024


def lane_of(x):
    return lax.broadcasted_iota(jnp.int32, x.shape, x.ndim - 1)


def roll(x, amount):
    amount %= LANES
    return x if amount == 0 else pltpu.roll(x, amount, x.ndim - 1)


def from_west(tiles, step):
    moved = [roll(t, step) for t in tiles]
    if len(tiles) == 1:
        return moved
    edge = lane_of(tiles[0]) < step
    return [jnp.where(edge, moved[i - 1], moved[i]) for i in range(len(tiles))]


def from_east(tiles, step):
    moved = [roll(t, -step) for t in tiles]
    count = len(tiles)
    if count == 1:
        return moved
    edge = lane_of(tiles[0]) >= LANES - step
    return [jnp.where(edge, moved[(i + 1) % count], moved[i]) for i in range(count)]


def clear_rim(ref):
    rim = GUARD + TOP - HALO
    zeros = jnp.zeros((rim, LANES), jnp.float32)
    for t in range(ref.shape[0]):
        ref[t, 0:rim, :] = zeros
        ref[t, ref.shape[1] - rim :, :] = zeros


def spread(tiles, step):
    second = (lane_of(tiles[0]) // step) % 2 == 1
    return [jnp.where(second, roll(t, step), t) for t in tiles]


def for_parts(start, size, body, part):
    for offset in range(0, size, part):
        body(start + offset, min(part, size - offset))


def for_chunks(rows, body, largest, part):
    sizes = [size for size in range(8, largest + 1, 8) if rows % size == 0]
    if rows <= largest or not sizes:
        for_parts(0, rows, body, part)
        return

    def step(i, carry):
        for_parts(i * sizes[-1], sizes[-1], body, part)
        return carry

    lax.fori_loop(0, rows // sizes[-1], step, 0)


def load(ref, start, size):
    return [ref[t, pl.ds(GUARD + start, size), :] for t in range(ref.shape[0])]


def store(ref, start, size, tiles):
    for t, tile in enumerate(tiles):
        ref[t, pl.ds(GUARD + start, size), :] = tile


def store_twice(ref, start, size, tiles):
    for t, tile in enumerate(tiles):
        ref[t, pl.ds(GUARD + 2 * start, size, stride=2), :] = tile
        ref[t, pl.ds(GUARD + 2 * start + 1, size, stride=2), :] = tile


def clear_guards(ref, rows):
    zeros = jnp.zeros((GUARD, LANES), jnp.float32)
    for t in range(ref.shape[0]):
        ref[t, 0:GUARD, :] = zeros
        ref[t, GUARD + rows : 2 * GUARD + rows, :] = zeros


def beside(mid, north, south, c_west, c_north, c_south, step):
    west = from_west(mid, step)
    east = from_east([c * m for c, m in zip(c_west, mid)], step)
    return [
        (c_west[t] * west[t] + east[t]) + (c_north[t] * north[t] + c_south[t] * south[t]) for t in range(len(mid))
    ]


def beside_of(ref, coeffs, start, size, step):
    c_west_ref, c_north_ref = coeffs
    mid = load(ref, start, size)
    north, south = load(ref, start - 1, size), load(ref, start + 1, size)
    c_west, c_north = load(c_west_ref, start, size), load(c_north_ref, start, size)
    return mid, beside(mid, north, south, c_west, c_north, load(c_north_ref, start + 1, size), step)


def pool_rows(ref, start, size, step):
    out = []
    for t in range(ref.shape[0]):
        even = ref[t, pl.ds(GUARD + start, size // 2, stride=2), :]
        odd = ref[t, pl.ds(GUARD + start + 1, size // 2, stride=2), :]
        both = even + odd
        out.append(both + roll(both, -step))
    return out


def descend(level, height, weight, source, guess, state, diagonal_ref, field, resid, next_weight, next_source, largest, part):
    step = 2**level
    c_west_ref, c_north_ref, scale_ref, smooth_ref = state
    for ref in (weight, field, c_north_ref):
        clear_guards(ref, height)

    def first_pass(start, size):
        w, w_north, w_south = (load(weight, start + k, size) for k in (0, -1, 1))
        c_north = [jnp.minimum(a, b) for a, b in zip(w, w_north)]
        c_south = [jnp.minimum(a, b) for a, b in zip(w, w_south)]
        c_west = [jnp.minimum(a, b) for a, b in zip(w, from_west(w, step))]
        c_east = from_east(c_west, step)
        diagonal = [damping + c_north[t] + c_south[t] + c_west[t] + c_east[t] for t in range(len(w))]
        scale = [relaxation / d for d in diagonal]
        store(c_north_ref, start, size, c_north)
        store(c_west_ref, start, size, c_west)
        store(scale_ref, start, size, scale)
        store(diagonal_ref, start, size, diagonal)
        value = load(source, start, size)
        if guess is None:
            value = [scale[t] * value[t] for t in range(len(w))]
        else:
            mid, north, south = (load(guess, start + k, size) for k in (0, -1, 1))
            around = beside(mid, north, south, c_west, c_north, c_south, step)
            value = [
                (1.0 - relaxation) * mid[t] + scale[t] * (value[t] + around[t]) for t in range(len(w))
            ]
        store(field, start, size, value)
        if next_weight is not None:
            pooled = [0.125 * p for p in pool_rows(weight, start, size, step)]
            store(next_weight, start // 2, size // 2, pooled)

    def second_pass(start, size):
        mid, around = beside_of(field, (c_west_ref, c_north_ref), start, size, step)
        b, scale, diagonal = (load(ref, start, size) for ref in (source, scale_ref, diagonal_ref))
        rest = [(b[t] + around[t]) - diagonal[t] * mid[t] for t in range(len(b))]
        store(smooth_ref, start, size, [mid[t] + scale[t] * rest[t] for t in range(len(b))])
        store(resid, start, size, rest)
        if next_source is not None:
            pooled = [0.25 * p for p in pool_rows(resid, start, size, step)]
            store(next_source, start // 2, size // 2, pooled)

    for_chunks(height, first_pass, largest, part)
    for_chunks(height, second_pass, largest, part)


def descend_all(rows, sources, guess, weights, states, diagonal, field, resid, largest, part):
    for level in range(LEVELS - 1):
        descend(
            level,
            rows >> level,
            weights[level],
            sources[level],
            guess if level == 0 else None,
            states[4 * level : 4 * level + 4],
            diagonal[level],
            field,
            resid,
            weights[level + 1],
            sources[level + 1],
            largest,
            part,
        )


def to_sides(west, east, cross_ref, pair_ref, k, rows):
    even = lax.axis_index("gy") % 2 == 0
    cross_ref[k, rows, :] = jnp.where(even, west, east)
    pair_ref[k, rows, :] = jnp.where(even, east, west)


def layout_kernel(source, guess, weight, own_source, own_guess, own_weight, cross_ref, pair_ref, *inner):
    rows = source.shape[0]
    piece = cross_ref.shape[1]
    tail = rows - (PIECES - 1) * piece
    for k, (block, own) in enumerate(zip((source, guess, weight), (own_source, own_guess, own_weight))):
        clear_rim(own)
        sides = []
        for t in range(2):
            own[t, GUARD + TOP : GUARD + TOP + rows, :] = block[:, t * LANES : (t + 1) * LANES]
        for tile, first in ((0, 0), (1, LANES - HALO)):
            columns = slice(tile * LANES, (tile + 1) * LANES)
            last = roll(block[(PIECES - 1) * piece :, columns], (PIECES - 1) * HALO - first)
            packed = jnp.concatenate((last, jnp.zeros((piece - tail, LANES), jnp.float32)), axis=0)
            for p in range(PIECES - 1):
                part = block[p * piece : (p + 1) * piece, columns]
                packed = jnp.where(lane_of(part) // HALO == p, roll(part, p * HALO - first), packed)
            sides.append(packed)
        to_sides(*sides, cross_ref, pair_ref, k, slice(0, piece))
    weights, start, height = (own_weight, *inner), TOP, rows
    for level in range(LEVELS):
        pooled = [0.125 * w for w in pool_rows(weights[level], start, height, 2**level)]
        start, height = start // 2, height // 2
        if level < LEVELS - 1:
            store(weights[level + 1], start, height, pooled)
    lane = lane_of(pooled[0])
    free = PIECES * HALO
    index = jnp.clip(lane - free, 0, LANES - 1 - free) * 2**LEVELS
    for t in range(2):
        taken = jnp.take_along_axis(pooled[t], index, axis=1)
        span = slice(t * height, (t + 1) * height)
        for ref in (cross_ref, pair_ref):
            ref[0, span, :] = jnp.where(lane >= free, taken, ref[0, span, :])


def halo_kernel(*refs):
    first_rows, second_rows, *own, cross_ref, pair_ref = refs[5:]
    total = own[0].shape[1] - 2 * GUARD
    piece = cross_ref.shape[1]
    even = lax.axis_index("gx") % 2 == 0
    shift = (PIECES - 1) * HALO
    for k in range(3):
        above = jnp.where(even, first_rows[k], second_rows[k])
        below = jnp.where(even, second_rows[k], first_rows[k])
        for rows, row, first in ((above, TOP - HALO, piece - 2 * HALO), (below, total - TOP, piece - HALO)):
            body = [rows[:, t * LANES : (t + 1) * LANES] for t in range(2)]
            for t in range(2):
                own[k][t, GUARD + row : GUARD + row + HALO, :] = body[t]
            span = slice(first, first + HALO)
            here = lane_of(body[0]) // HALO == PIECES - 1
            cross, pair = cross_ref[k, span, :], pair_ref[k, span, :]
            west, east = roll(body[0], shift), roll(body[1], shift + HALO - LANES)
            even_y = lax.axis_index("gy") % 2 == 0
            cross_ref[k, span, :] = jnp.where(here, jnp.where(even_y, west, east), cross)
            pair_ref[k, span, :] = jnp.where(here, jnp.where(even_y, east, west), pair)


def body_kernel(source, guess, weight, *refs):
    states = refs[: 4 * (LEVELS - 1)]
    last_weight, last_source, first_diagonal, *refs = refs[4 * (LEVELS - 1) :]
    frames, (field, resid, weight_in, *inner) = refs[:3], refs[3:]
    rows = source.shape[1] - 2 * GUARD
    depth = LEVELS - 2
    weights = (weight_in, *inner[:depth], last_weight)
    sources = (source, *inner[depth : 2 * depth], last_source)
    diagonal = (first_diagonal, *inner[2 * depth :])
    weights[0][...] = weight[...]
    descend_all(rows, sources, guess, weights, states, diagonal, field, resid, 144, 144)
    for own, frame in zip((source, guess, weight), frames):
        tiles = [own[t] for t in range(2)]
        frame[0] = jnp.where(lane_of(tiles[0]) < LANES // 2, roll(tiles[0], HALO), roll(tiles[1], -HALO))


def frame_kernel(_a, _b, _c, from_cross, from_pair, body_weight, body_source, *refs):
    even = lax.axis_index("gy") % 2 == 0
    frames, states, refs = refs[:3], refs[3 : 3 + 4 * (LEVELS - 1)], refs[3 + 4 * (LEVELS - 1) :]
    frame_source, frame_guess, frame_weight = frames
    first_diagonal, ring_state, dense_ref, chunks_ref, field, resid, *refs = refs[0], refs[1:5], *refs[5:]
    ring_weight, ring_source, ring_field, ring_resid, ring_diagonal, *inner = refs
    rows = frame_source.shape[1] - 2 * GUARD
    depth = LEVELS - 1
    weights = (frame_weight, *inner[:depth])
    sources = (frame_source, *inner[depth : 2 * depth])
    diagonals = (first_diagonal, *inner[2 * depth :])
    piece = from_cross.shape[1]
    for k, frame in enumerate(frames):
        left = jnp.where(even, from_cross[k], from_pair[k])
        right = jnp.where(even, from_pair[k], from_cross[k])
        spans = [(p, 0, TOP + p * piece, piece) for p in range(PIECES - 1)]
        spans.append((PIECES - 1, 0, TOP + (PIECES - 1) * piece, piece - 2 * HALO))
        spans += [(PIECES - 1, piece - 2 * HALO, TOP - HALO, HALO), (PIECES - 1, piece - HALO, rows - TOP, HALO)]
        for p, first, start, size in spans:
            span = slice(GUARD + start, GUARD + start + size)
            west = roll(left[first : first + size], -p * HALO)
            east = roll(right[first : first + size], -(p + 1) * HALO)
            lane = lane_of(west)
            inside = jnp.where(lane < HALO, west, frame[0, span, :])
            frame[0, span, :] = jnp.where(lane >= LANES - HALO, east, inside)
    descend_all(rows, sources, frame_guess, weights, states, diagonals, field, resid, 288, 288)

    level = LEVELS - 1
    step, halo, height = 2**level, TOP >> level, rows >> level
    for body, frame, ring in (
        (body_weight, weights[level], ring_weight),
        (body_source, sources[level], ring_source),
    ):
        middle = load(body, 0, height)
        around = load(frame, 0, height)[0]
        lane = lane_of(around)
        ahead, back = roll(around, HALO), roll(around, -HALO)
        store(
            ring,
            0,
            height,
            [
                jnp.where(lane < 2 * step, back, middle[0]),
                jnp.where(lane >= LANES - 2 * step, ahead, middle[1]),
                jnp.where(lane < LANES // 2, ahead, back),
            ],
        )
    descend(
        level,
        height,
        ring_weight,
        ring_source,
        None,
        ring_state,
        ring_diagonal,
        ring_field,
        ring_resid,
        None,
        None,
        height,
        height,
    )

    coarse_rows = (height - 2 * halo) // 2
    dense = jnp.zeros((8, LANES), jnp.float32)
    lane = lane_of(dense)
    per_tile = LANES // 2**LEVELS
    pooled_b = pool_rows(ring_resid, halo, 2 * coarse_rows, step)
    pooled_w = pool_rows(ring_weight, halo, 2 * coarse_rows, step)
    index = (lane % per_tile) * 2**LEVELS
    place = lane // per_tile
    for g in range(coarse_rows // 8):
        for group, (values, factor) in enumerate(((pooled_b, 0.25), (pooled_w, 0.125))):
            for t in range(2):
                taken = jnp.take_along_axis(factor * values[t][8 * g : 8 * g + 8], index, axis=1)
                dense = jnp.where(place == 4 * g + 2 * group + t, taken, dense)
    dense_ref[...] = dense

    index = jnp.minimum(2 * (lane - lane % (2 * per_tile)) + lane % (2 * per_tile), LANES - 1)
    level_with, above, below = (fold(x) for x in (jnp.take_along_axis(dense, index, axis=1), dense, roll(dense, -LANES // 2)))
    x = lax.axis_index("gx")
    for i in range(chunks_ref.shape[0]):
        chunk = jnp.where(i == x, level_with, jnp.where(i < x, above, below))
        chunks_ref[i] = jnp.broadcast_to(chunk[None], chunks_ref.shape[1:])


def fold(x):
    return jnp.where(lane_of(x) < LANES // 2, x, pltpu.roll(roll(x, LANES // 2), 4, 0))[:4]


def unfold(x):
    return jnp.concatenate((x, roll(x, LANES // 2)), axis=0)


def coarse_solve(all_ref, dense_ref, from_cross, from_pair, e_ref, width, groups):
    x, nx = lax.axis_index("gx"), lax.axis_size("gx")
    y, ny = lax.axis_index("gy"), lax.axis_size("gy")
    tiles = {}
    for dx in (-1, 0, 1):
        for dy in (-1, 0, 1):
            if dx or dy:
                inside = (x + dx >= 0) & (x + dx < nx) & (y + dy >= 0) & (y + dy < ny)
                tile = unfold(all_ref[jnp.where(inside, x + dx, 0), jnp.where(inside, y + dy, 0)])
                tiles[dx, dy] = jnp.where(inside, tile, 0.0)
    dense = dense_ref[...]
    lane = lane_of(dense)
    even = y % 2 == 0
    height = 8 * groups
    cross, pair = from_cross[0, : 2 * height, :], from_pair[0, : 2 * height, :]
    weights = {-1: jnp.where(even, cross, pair), 1: jnp.where(even, pair, cross)}
    bands = [(-1, g) for g in range(TALL // 8)] + [(0, g) for g in range(groups)] + [(1, g) for g in range(TALL // 8)]
    b, w = [], []
    for dx, g in bands:
        b_rows = w_rows = jnp.zeros_like(dense)
        for dy in (-1, 0, 1):
            first = (dy + 1) * width
            here = (lane >= first) & (lane < first + width)
            if dx or not dy:
                tile = tiles[dx, dy] if dx else dense
                b_part, w_part = roll(tile, first - 2 * g * width), roll(tile, first - (2 * g + 1) * width)
            else:
                b_part = roll(tiles[dx, dy], first - g * width)
                free = PIECES * HALO
                parts = [weights[dy][t * height + 8 * g : t * height + 8 * g + 8] for t in range(2)]
                parts = [roll(part, first + t * width // 2 - free) for t, part in enumerate(parts)]
                w_part = jnp.where(lane < first + width // 2, *parts)
            b_rows = jnp.where(here, b_part, b_rows)
            w_rows = jnp.where(here, w_part, w_rows)
        b.append(b_rows)
        w.append(w_rows)
    b, w = jnp.concatenate(b, axis=0), jnp.concatenate(w, axis=0)

    rows = b.shape[0]
    zeros = jnp.zeros((GUARD, LANES), jnp.float32)
    e_ref[0:GUARD, :] = zeros
    e_ref[GUARD + rows :, :] = zeros

    def shifted(by):
        return e_ref[GUARD + by : GUARD + by + rows, :]

    e_ref[GUARD : GUARD + rows, :] = w
    c_west = jnp.minimum(w, roll(w, 1))
    c_north, c_south = jnp.minimum(w, shifted(-1)), jnp.minimum(w, shifted(1))
    c_east = roll(c_west, -1)
    scale = relaxation / (damping + c_north + c_south + c_west + c_east)
    first = scale * b
    c_west, c_east, c_north, c_south = (scale * c for c in (c_west, c_east, c_north, c_south))
    e_ref[GUARD : GUARD + rows, :] = first

    def sweep(_, carry):
        e = shifted(0)
        around = (c_west * roll(e, 1) + c_east * roll(e, -1)) + (c_north * shifted(-1) + c_south * shifted(1))
        e_ref[GUARD : GUARD + rows, :] = ((1.0 - relaxation) * e + first) + around
        return carry

    lax.fori_loop(0, SWEEPS - 1, sweep, 0)
    return shifted(0)


def up_kernel(all_ref, dense_ref, from_cross, from_pair, own_source, frame_source, own_diagonal, frame_diagonal, *refs):
    count = 4 * (LEVELS - 1)
    body_state, frame_state, ring_state = refs[:count], refs[count : 2 * count], refs[2 * count : 2 * count + 4]
    out_ref, resid_ref = refs[2 * count + 4 : 2 * count + 6]
    ring_pe, body_final, frame_final, sems, e_ref, *inner = refs[2 * count + 6 :]
    outs, inner = inner[:2], inner[2:]
    body_pe, frame_pe = inner[: LEVELS - 1], inner[LEVELS - 1 :]
    rows = out_ref.shape[0] + 2 * TOP
    width = out_ref.shape[1] >> LEVELS
    e = coarse_solve(all_ref, dense_ref, from_cross, from_pair, e_ref, width, (out_ref.shape[0] >> LEVELS) // 8)

    level = LEVELS - 1
    step, halo, height = 2**level, TOP >> level, rows >> level
    coarse_rows = (height - 2 * halo) // 2
    picked = e[TALL - 8 : TALL + coarse_rows + 8]
    lane = lane_of(picked)
    for t in range(3):
        group = (lane + t * LANES) // 2**LEVELS
        if t == 2:
            group = jnp.where(lane < LANES // 2, group, group - 3 * LANES // 2**LEVELS)
        taken = jnp.take_along_axis(picked, jnp.clip(group + width, 0, LANES - 1), axis=1)[7 : 7 + coarse_rows + 2]
        ring_pe[t, 0 : 2 * GUARD, :] = jnp.zeros((2 * GUARD, LANES), jnp.float32)
        ring_pe[t, height : height + 2 * GUARD, :] = jnp.zeros((2 * GUARD, LANES), jnp.float32)
        ring_pe[t, pl.ds(GUARD + halo - 2, coarse_rows + 2, stride=2), :] = taken
        ring_pe[t, pl.ds(GUARD + halo - 1, coarse_rows + 2, stride=2), :] = taken

    def climbed(pe, state, start, size, step):
        mid, around = beside_of(pe, state[:2], start, size, step)
        scale, smooth = load(state[2], start, size), load(state[3], start, size)
        return [(smooth[t] + (1.0 - relaxation) * mid[t]) + scale[t] * around[t] for t in range(len(mid))]

    def climb_ring(start, size, level=level, step=step):
        ring = spread(climbed(ring_pe, ring_state, start, size, step), step // 2)
        lane = lane_of(ring[0])
        around = jnp.where(
            lane < LANES // 2,
            jnp.where(lane < HALO, roll(ring[2], HALO), roll(ring[0], HALO)),
            jnp.where(lane < LANES - HALO, roll(ring[1], -HALO), roll(ring[2], -HALO)),
        )
        store_twice(body_pe[level - 1], start, size, ring[:2])
        store_twice(frame_pe[level - 1], start, size, [around])

    for_chunks(height, climb_ring, height, 16)

    for level in range(LEVELS - 2, -1, -1):
        step, height = 2**level, rows >> level
        groups = ((body_pe, body_state, body_final), (frame_pe, frame_state, frame_final))
        for pes, _, _ in groups:
            clear_guards(pes[level], height)

        def climb(start, size, level=level, step=step, groups=groups):
            for pes, states, final in groups:
                value = climbed(pes[level], states[4 * level : 4 * level + 4], start, size, step)
                if level == 0:
                    store(final, start, size, value)
                else:
                    store_twice(pes[level - 1], start, size, spread(value, step // 2))

        if level > 0:
            for_chunks(height, climb, CHUNK, CHUNK // 2)

    def last(base, size):
        body, around = beside_of(body_final, body_state[:2], base, size, 1)
        frame, frame_around = beside_of(frame_final, frame_state[:2], base, size, 1)
        b, d = load(own_source, base, size), load(own_diagonal, base, size)
        b_frame, d_frame = load(frame_source, base, size), load(frame_diagonal, base, size)
        body = (body, [(b[t] + around[t]) - d[t] * body[t] for t in range(2)])
        frame = (frame[0], (b_frame[0] + frame_around[0]) - d_frame[0] * frame[0])
        lane = lane_of(frame[0])
        near = HALO - 4
        span = pl.ds(base, size)
        for ref, middle, around in ((outs[0], body[0], frame[0]), (outs[1], body[1], frame[1])):
            ref[span, :LANES] = jnp.where(lane < near, roll(around, -HALO), middle[0])
            ref[span, LANES:] = jnp.where(lane >= LANES - near, roll(around, HALO), middle[1])

    count = rows // CHUNK
    ends = [0] + [CHUNK * (p + 1) - LAG - TOP for p in range(count - 1)] + [out_ref.shape[0]]

    def copies(p):
        size = ends[p + 1] - ends[p]
        return [
            pltpu.make_async_copy(
                outs[k].at[pl.ds(TOP + ends[p], size)], ref.at[pl.ds(ends[p], size)], sems.at[2 * p + k]
            )
            for k, ref in enumerate((out_ref, resid_ref))
        ]

    def finish(i, carry):
        for_parts(i * CHUNK, CHUNK, climb, CHUNK // 2)
        base = pl.multiple_of(jnp.maximum(i * CHUNK - LAG, 0), 8)
        for_parts(base, CHUNK, last, CHUNK // 2)
        for p in range(count):

            @pl.when(i == p)
            def _(p=p):
                for copy in copies(p):
                    copy.start()

        return carry

    lax.fori_loop(0, count, finish, 0)
    for p in range(count):
        for copy in copies(p):
            copy.wait()


def call(kernel, out_shape, scratch, flops, moved, **more):
    return pl.pallas_call(
        kernel,
        out_shape=out_shape,
        scratch_shapes=scratch,
        compiler_params=pltpu.CompilerParams(vmem_limit_bytes=VMEM_LIMIT),
        cost_estimate=pl.CostEstimate(flops=flops, bytes_accessed=moved, transcendentals=0),
        **more,
    )


def swap(x, axis, first):
    pairs = [(i, i + 1) for i in range(first, lax.axis_size(axis) - 1, 2)]
    return lax.ppermute(x, axis, pairs + [(j, i) for i, j in pairs])


def local(rhs, pressure, wet_mask, bathy_class):
    rows, columns = rhs.shape
    cells = rows * columns
    total = rows + 2 * TOP
    levels = range(LEVELS - 1)

    def shape(tiles, level):
        return (tiles, (total >> level) + 2 * GUARD, LANES)

    def out(*dims):
        return jax.ShapeDtypeStruct(dims, jnp.float32)

    def vmem(tiles, level):
        return pltpu.VMEM(shape(tiles, level), jnp.float32)

    def fields(r, p, m, c):
        wet = m.astype(jnp.float32)
        return wet * r, wet * p, wet * (1.0 + 0.5 * c.astype(jnp.float32))

    given = (rhs, pressure, wet_mask, bathy_class)

    def edge(start):
        return jnp.stack(fields(*(lax.dynamic_slice_in_dim(x, start, HALO, axis=0) for x in given)))

    even = lax.axis_index("gx") % 2 == 0
    first_rows = swap(edge(jnp.where(even, 0, rows - HALO)), "gx", 1)
    second_rows = swap(edge(jnp.where(even, rows - HALO, 0)), "gx", 0)
    piece = (rows + 2 * HALO) // PIECES
    own_shapes = [out(*shape(2, 0))] * 3
    laid_out = [*own_shapes, out(3, piece, LANES), out(3, piece, LANES)]
    inner = [vmem(2, level) for level in range(1, LEVELS)]
    begun = call(layout_kernel, laid_out, inner, 10 * cells, 10 * cells)(*fields(*given))
    *own, to_cross, to_pair = call(
        halo_kernel, laid_out, (), cells, cells, input_output_aliases={k: k for k in range(5)}
    )(*begun, first_rows, second_rows)
    from_pair = swap(to_pair, "gy", 0)
    from_cross = swap(to_cross, "gy", 1)

    state_count = 4 * (LEVELS - 1)
    *body_state, body_weight, body_source, diagonal, frame_source, frame_guess, frame_weight = call(
        body_kernel,
        [out(*shape(2, level)) for level in levels for _ in range(4)]
        + [out(*shape(2, LEVELS - 1))] * 2
        + [out(*shape(2, 0))]
        + [out(*shape(1, 0))] * 3,
        [vmem(2, 0)] * 3 + [vmem(2, level) for level in levels[1:]] * 3,
        100 * cells,
        40 * cells,
    )(*own)
    nx, ny = lax.axis_size("gx"), lax.axis_size("gy")
    ring = LEVELS - 1
    frame_source, _, _, *state, dense, chunks = call(
        frame_kernel,
        [out(*shape(1, 0))] * 3
        + [out(*shape(1, level)) for level in levels for _ in range(4)]
        + [out(*shape(1, 0))]
        + [out(*shape(3, ring))] * 4
        + [out(8, LANES), out(nx, ny, 4, LANES)],
        [vmem(1, 0)] * 2 + [vmem(3, ring)] * 5 + [vmem(1, level) for level in range(1, LEVELS)] * 3,
        50 * cells,
        20 * cells,
        input_output_aliases={k: k for k in range(3)},
    )(frame_source, frame_guess, frame_weight, from_cross, from_pair, body_weight, body_source)
    frame_state, frame_diagonal, ring_state = state[:state_count], state[state_count], state[state_count + 1 :]
    gathered = lax.all_to_all(chunks.reshape(nx * ny, 4, LANES), ("gx", "gy"), 0, 0).reshape(chunks.shape)
    return call(
        up_kernel,
        (out(rows, columns), out(rows, columns)),
        [vmem(3, ring), vmem(2, 0), vmem(1, 0), pltpu.SemaphoreType.DMA((8,))]
        + [pltpu.VMEM(((rows >> LEVELS) + 2 * TALL + 2 * GUARD, LANES), jnp.float32)]
        + [pltpu.VMEM((total, columns), jnp.float32)] * 2
        + [vmem(2, level) for level in levels]
        + [vmem(1, level) for level in levels],
        60 * cells,
        40 * cells,
        out_specs=[pl.BlockSpec(memory_space=pl.ANY)] * 2,
    )(gathered, dense, from_cross, from_pair, own[0], frame_source, diagonal, frame_diagonal, *body_state, *frame_state, *ring_state)


def solution(mesh):
    placed = (P("gx", "gy"), P("gx", "gy"), P("gx", "gy"), P("gx", "gy"))
    return jax.shard_map(
        local, mesh=mesh, in_specs=placed, out_specs=(P("gx", "gy"), P("gx", "gy")), check_vma=False
    )
```

```python
import jax
import jax.numpy as jnp
from jax import lax
from jax.experimental import pallas as pl
from jax.experimental.pallas import tpu as pltpu
from jax.sharding import PartitionSpec as P

LEVELS = 4
SWEEPS = 12

damping = 0.01
relaxation = 0.8

HALO = 24
LANES = 128
INNER = LANES // 2 - HALO
TOP = 32
GUARD = 8
PIECES = 5
CHUNK = 144
LAG = 8
TALL = 16
VMEM_LIMIT = 40 * 1024 * 1024


def lane_of(x):
    return lax.broadcasted_iota(jnp.int32, x.shape, x.ndim - 1)


def roll(x, amount):
    amount %= LANES
    return x if amount == 0 else pltpu.roll(x, amount, x.ndim - 1)


def from_west(tiles, step):
    moved = [roll(t, step) for t in tiles]
    if len(tiles) == 1:
        return moved
    edge = lane_of(tiles[0]) < step
    return [jnp.where(edge, moved[i - 1], moved[i]) for i in range(len(tiles))]


def from_east(tiles, step):
    moved = [roll(t, -step) for t in tiles]
    count = len(tiles)
    if count == 1:
        return moved
    edge = lane_of(tiles[0]) >= LANES - step
    return [jnp.where(edge, moved[(i + 1) % count], moved[i]) for i in range(count)]


def clear_rim(ref):
    rim = GUARD + TOP - HALO
    zeros = jnp.zeros((rim, LANES), jnp.float32)
    for t in range(ref.shape[0]):
        ref[t, 0:rim, :] = zeros
        ref[t, ref.shape[1] - rim :, :] = zeros


def spread(tiles, step):
    second = (lane_of(tiles[0]) // step) % 2 == 1
    return [jnp.where(second, roll(t, step), t) for t in tiles]


def for_parts(start, size, body, part):
    for offset in range(0, size, part):
        body(start + offset, min(part, size - offset))


def for_chunks(rows, body, largest, part):
    sizes = [size for size in range(8, largest + 1, 8) if rows % size == 0]
    if rows <= largest or not sizes:
        for_parts(0, rows, body, part)
        return

    def step(i, carry):
        for_parts(i * sizes[-1], sizes[-1], body, part)
        return carry

    lax.fori_loop(0, rows // sizes[-1], step, 0)


def load(ref, start, size):
    return [ref[t, pl.ds(GUARD + start, size), :] for t in range(ref.shape[0])]


def store(ref, start, size, tiles):
    for t, tile in enumerate(tiles):
        ref[t, pl.ds(GUARD + start, size), :] = tile


def store_twice(ref, start, size, tiles):
    for t, tile in enumerate(tiles):
        ref[t, pl.ds(GUARD + 2 * start, size, stride=2), :] = tile
        ref[t, pl.ds(GUARD + 2 * start + 1, size, stride=2), :] = tile


def clear_guards(ref, rows):
    zeros = jnp.zeros((GUARD, LANES), jnp.float32)
    for t in range(ref.shape[0]):
        ref[t, 0:GUARD, :] = zeros
        ref[t, GUARD + rows : 2 * GUARD + rows, :] = zeros


def beside(mid, north, south, c_west, c_north, c_south, step):
    west = from_west(mid, step)
    east = from_east([c * m for c, m in zip(c_west, mid)], step)
    return [
        (c_west[t] * west[t] + east[t]) + (c_north[t] * north[t] + c_south[t] * south[t]) for t in range(len(mid))
    ]


def beside_of(ref, coeffs, start, size, step):
    c_west_ref, c_north_ref = coeffs
    mid = load(ref, start, size)
    north, south = load(ref, start - 1, size), load(ref, start + 1, size)
    c_west, c_north = load(c_west_ref, start, size), load(c_north_ref, start, size)
    return mid, beside(mid, north, south, c_west, c_north, load(c_north_ref, start + 1, size), step)


def pool_rows(ref, start, size, step):
    out = []
    for t in range(ref.shape[0]):
        even = ref[t, pl.ds(GUARD + start, size // 2, stride=2), :]
        odd = ref[t, pl.ds(GUARD + start + 1, size // 2, stride=2), :]
        both = even + odd
        out.append(both + roll(both, -step))
    return out


def descend(level, height, weight, source, guess, state, diagonal_ref, field, resid, next_weight, next_source, largest, part):
    step = 2**level
    c_west_ref, c_north_ref, scale_ref, smooth_ref = state
    for ref in (weight, field, c_north_ref):
        clear_guards(ref, height)

    def first_pass(start, size):
        w, w_north, w_south = (load(weight, start + k, size) for k in (0, -1, 1))
        c_north = [jnp.minimum(a, b) for a, b in zip(w, w_north)]
        c_south = [jnp.minimum(a, b) for a, b in zip(w, w_south)]
        c_west = [jnp.minimum(a, b) for a, b in zip(w, from_west(w, step))]
        c_east = from_east(c_west, step)
        diagonal = [damping + c_north[t] + c_south[t] + c_west[t] + c_east[t] for t in range(len(w))]
        scale = [relaxation / d for d in diagonal]
        store(c_north_ref, start, size, c_north)
        store(c_west_ref, start, size, c_west)
        store(scale_ref, start, size, scale)
        store(diagonal_ref, start, size, diagonal)
        value = load(source, start, size)
        if guess is None:
            value = [scale[t] * value[t] for t in range(len(w))]
        else:
            mid, north, south = (load(guess, start + k, size) for k in (0, -1, 1))
            around = beside(mid, north, south, c_west, c_north, c_south, step)
            value = [
                (1.0 - relaxation) * mid[t] + scale[t] * (value[t] + around[t]) for t in range(len(w))
            ]
        store(field, start, size, value)
        if next_weight is not None:
            pooled = [0.125 * p for p in pool_rows(weight, start, size, step)]
            store(next_weight, start // 2, size // 2, pooled)

    def second_pass(start, size):
        mid, around = beside_of(field, (c_west_ref, c_north_ref), start, size, step)
        b, scale, diagonal = (load(ref, start, size) for ref in (source, scale_ref, diagonal_ref))
        rest = [(b[t] + around[t]) - diagonal[t] * mid[t] for t in range(len(b))]
        store(smooth_ref, start, size, [mid[t] + scale[t] * rest[t] for t in range(len(b))])
        store(resid, start, size, rest)
        if next_source is not None:
            pooled = [0.25 * p for p in pool_rows(resid, start, size, step)]
            store(next_source, start // 2, size // 2, pooled)

    for_chunks(height, first_pass, largest, part)
    for_chunks(height, second_pass, largest, part)


def descend_all(rows, sources, guess, weights, states, diagonal, field, resid, largest, part):
    for level in range(LEVELS - 1):
        descend(
            level,
            rows >> level,
            weights[level],
            sources[level],
            guess if level == 0 else None,
            states[4 * level : 4 * level + 4],
            diagonal[level],
            field,
            resid,
            weights[level + 1],
            sources[level + 1],
            largest,
            part,
        )


def to_sides(west, east, cross_ref, pair_ref, k, rows):
    even = lax.axis_index("gy") % 2 == 0
    cross_ref[k, rows, :] = jnp.where(even, west, east)
    pair_ref[k, rows, :] = jnp.where(even, east, west)


def layout_kernel(source, guess, weight, own_source, own_guess, own_weight, cross_ref, pair_ref, *inner):
    rows = source.shape[0]
    piece = cross_ref.shape[1]
    tail = rows - (PIECES - 1) * piece
    for k, (block, own) in enumerate(zip((source, guess, weight), (own_source, own_guess, own_weight))):
        clear_rim(own)
        sides = []
        for t in range(2):
            own[t, GUARD + TOP : GUARD + TOP + rows, :] = block[:, t * LANES : (t + 1) * LANES]
        for tile, first in ((0, 0), (1, LANES - HALO)):
            columns = slice(tile * LANES, (tile + 1) * LANES)
            last = roll(block[(PIECES - 1) * piece :, columns], (PIECES - 1) * HALO - first)
            packed = jnp.concatenate((last, jnp.zeros((piece - tail, LANES), jnp.float32)), axis=0)
            for p in range(PIECES - 1):
                part = block[p * piece : (p + 1) * piece, columns]
                packed = jnp.where(lane_of(part) // HALO == p, roll(part, p * HALO - first), packed)
            sides.append(packed)
        to_sides(*sides, cross_ref, pair_ref, k, slice(0, piece))
    weights, start, height = (own_weight, *inner), TOP, rows
    for level in range(LEVELS):
        pooled = [0.125 * w for w in pool_rows(weights[level], start, height, 2**level)]
        start, height = start // 2, height // 2
        if level < LEVELS - 1:
            store(weights[level + 1], start, height, pooled)
    lane = lane_of(pooled[0])
    free = PIECES * HALO
    index = jnp.clip(lane - free, 0, LANES - 1 - free) * 2**LEVELS
    for t in range(2):
        taken = jnp.take_along_axis(pooled[t], index, axis=1)
        span = slice(t * height, (t + 1) * height)
        for ref in (cross_ref, pair_ref):
            ref[0, span, :] = jnp.where(lane >= free, taken, ref[0, span, :])


def halo_kernel(*refs):
    first_rows, second_rows, *own, cross_ref, pair_ref = refs[5:]
    total = own[0].shape[1] - 2 * GUARD
    piece = cross_ref.shape[1]
    even = lax.axis_index("gx") % 2 == 0
    shift = (PIECES - 1) * HALO
    for k in range(3):
        above = jnp.where(even, first_rows[k], second_rows[k])
        below = jnp.where(even, second_rows[k], first_rows[k])
        for rows, row, first in ((above, TOP - HALO, piece - 2 * HALO), (below, total - TOP, piece - HALO)):
            body = [rows[:, t * LANES : (t + 1) * LANES] for t in range(2)]
            for t in range(2):
                own[k][t, GUARD + row : GUARD + row + HALO, :] = body[t]
            span = slice(first, first + HALO)
            here = lane_of(body[0]) // HALO == PIECES - 1
            cross, pair = cross_ref[k, span, :], pair_ref[k, span, :]
            west, east = roll(body[0], shift), roll(body[1], shift + HALO - LANES)
            even_y = lax.axis_index("gy") % 2 == 0
            cross_ref[k, span, :] = jnp.where(here, jnp.where(even_y, west, east), cross)
            pair_ref[k, span, :] = jnp.where(here, jnp.where(even_y, east, west), pair)


def body_kernel(source, guess, weight, *refs):
    states = refs[: 4 * (LEVELS - 1)]
    last_weight, last_source, first_diagonal, *refs = refs[4 * (LEVELS - 1) :]
    frames, (field, resid, weight_in, *inner) = refs[:3], refs[3:]
    rows = source.shape[1] - 2 * GUARD
    depth = LEVELS - 2
    weights = (weight_in, *inner[:depth], last_weight)
    sources = (source, *inner[depth : 2 * depth], last_source)
    diagonal = (first_diagonal, *inner[2 * depth :])
    weights[0][...] = weight[...]
    descend_all(rows, sources, guess, weights, states, diagonal, field, resid, 144, 144)
    for own, frame in zip((source, guess, weight), frames):
        tiles = [own[t] for t in range(2)]
        frame[0] = jnp.where(lane_of(tiles[0]) < LANES // 2, roll(tiles[0], HALO), roll(tiles[1], -HALO))


def frame_kernel(_a, _b, _c, from_pair, from_cross, body_weight, body_source, *refs):
    even = lax.axis_index("gy") % 2 == 0
    frames, states, refs = refs[:3], refs[3 : 3 + 4 * (LEVELS - 1)], refs[3 + 4 * (LEVELS - 1) :]
    frame_source, frame_guess, frame_weight = frames
    first_diagonal, ring_state, dense_ref, chunks_ref, field, resid, *refs = refs[0], refs[1:5], *refs[5:]
    ring_weight, ring_source, ring_field, ring_resid, ring_diagonal, *inner = refs
    rows = frame_source.shape[1] - 2 * GUARD
    depth = LEVELS - 1
    weights = (frame_weight, *inner[:depth])
    sources = (frame_source, *inner[depth : 2 * depth])
    diagonals = (first_diagonal, *inner[2 * depth :])
    piece = from_cross.shape[1]
    for k, frame in enumerate(frames):
        left = jnp.where(even, from_cross[k], from_pair[k])
        right = jnp.where(even, from_pair[k], from_cross[k])
        spans = [(p, 0, TOP + p * piece, piece) for p in range(PIECES - 1)]
        spans.append((PIECES - 1, 0, TOP + (PIECES - 1) * piece, piece - 2 * HALO))
        spans += [(PIECES - 1, piece - 2 * HALO, TOP - HALO, HALO), (PIECES - 1, piece - HALO, rows - TOP, HALO)]
        for p, first, start, size in spans:
            span = slice(GUARD + start, GUARD + start + size)
            west = roll(left[first : first + size], -p * HALO)
            east = roll(right[first : first + size], -(p + 1) * HALO)
            lane = lane_of(west)
            inside = jnp.where(lane < HALO, west, frame[0, span, :])
            frame[0, span, :] = jnp.where(lane >= LANES - HALO, east, inside)
    descend_all(rows, sources, frame_guess, weights, states, diagonals, field, resid, 288, 288)

    level = LEVELS - 1
    step, halo, height = 2**level, TOP >> level, rows >> level
    for body, frame, ring in (
        (body_weight, weights[level], ring_weight),
        (body_source, sources[level], ring_source),
    ):
        middle = load(body, 0, height)
        around = load(frame, 0, height)[0]
        lane = lane_of(around)
        ahead, back = roll(around, HALO), roll(around, -HALO)
        store(
            ring,
            0,
            height,
            [
                jnp.where(lane < 2 * step, back, middle[0]),
                jnp.where(lane >= LANES - 2 * step, ahead, middle[1]),
                jnp.where(lane < LANES // 2, ahead, back),
            ],
        )
    descend(
        level,
        height,
        ring_weight,
        ring_source,
        None,
        ring_state,
        ring_diagonal,
        ring_field,
        ring_resid,
        None,
        None,
        height,
        height,
    )

    coarse_rows = (height - 2 * halo) // 2
    dense = jnp.zeros((8, LANES), jnp.float32)
    lane = lane_of(dense)
    per_tile = LANES // 2**LEVELS
    pooled_b = pool_rows(ring_resid, halo, 2 * coarse_rows, step)
    pooled_w = pool_rows(ring_weight, halo, 2 * coarse_rows, step)
    index = (lane % per_tile) * 2**LEVELS
    place = lane // per_tile
    for g in range(coarse_rows // 8):
        for group, (values, factor) in enumerate(((pooled_b, 0.25), (pooled_w, 0.125))):
            for t in range(2):
                taken = jnp.take_along_axis(factor * values[t][8 * g : 8 * g + 8], index, axis=1)
                dense = jnp.where(place == 4 * g + 2 * group + t, taken, dense)
    dense_ref[...] = dense

    index = jnp.minimum(2 * (lane - lane % (2 * per_tile)) + lane % (2 * per_tile), LANES - 1)
    level_with, above, below = (fold(x) for x in (jnp.take_along_axis(dense, index, axis=1), dense, roll(dense, -LANES // 2)))
    x = lax.axis_index("gx")
    for i in range(chunks_ref.shape[0]):
        chunk = jnp.where(i == x, level_with, jnp.where(i < x, above, below))
        chunks_ref[i] = jnp.broadcast_to(chunk[None], chunks_ref.shape[1:])


def fold(x):
    return jnp.where(lane_of(x) < LANES // 2, x, pltpu.roll(roll(x, LANES // 2), 4, 0))[:4]


def unfold(x):
    return jnp.concatenate((x, roll(x, LANES // 2)), axis=0)


def coarse_kernel(all_ref, dense_ref, from_pair, from_cross, e_ref):
    groups = (e_ref.shape[0] - 2 * GUARD - 2 * TALL) // 8
    width = LANES // (2 * groups)
    x, nx = lax.axis_index("gx"), lax.axis_size("gx")
    y, ny = lax.axis_index("gy"), lax.axis_size("gy")
    tiles = {}
    for dx in (-1, 0, 1):
        for dy in (-1, 0, 1):
            if dx or dy:
                inside = (x + dx >= 0) & (x + dx < nx) & (y + dy >= 0) & (y + dy < ny)
                tile = unfold(all_ref[jnp.where(inside, x + dx, 0), jnp.where(inside, y + dy, 0)])
                tiles[dx, dy] = jnp.where(inside, tile, 0.0)
    dense = dense_ref[...]
    lane = lane_of(dense)
    even = y % 2 == 0
    height = 8 * groups
    cross, pair = from_cross[0, : 2 * height, :], from_pair[0, : 2 * height, :]
    weights = {-1: jnp.where(even, cross, pair), 1: jnp.where(even, pair, cross)}
    bands = [(-1, g) for g in range(TALL // 8)] + [(0, g) for g in range(groups)] + [(1, g) for g in range(TALL // 8)]
    b, w = [], []
    for dx, g in bands:
        b_rows = w_rows = jnp.zeros_like(dense)
        for dy in (-1, 0, 1):
            first = (dy + 1) * width
            here = (lane >= first) & (lane < first + width)
            if dx or not dy:
                tile = tiles[dx, dy] if dx else dense
                b_part, w_part = roll(tile, first - 2 * g * width), roll(tile, first - (2 * g + 1) * width)
            else:
                b_part = roll(tiles[dx, dy], first - g * width)
                free = PIECES * HALO
                parts = [weights[dy][t * height + 8 * g : t * height + 8 * g + 8] for t in range(2)]
                parts = [roll(part, first + t * width // 2 - free) for t, part in enumerate(parts)]
                w_part = jnp.where(lane < first + width // 2, *parts)
            b_rows = jnp.where(here, b_part, b_rows)
            w_rows = jnp.where(here, w_part, w_rows)
        b.append(b_rows)
        w.append(w_rows)
    b, w = jnp.concatenate(b, axis=0), jnp.concatenate(w, axis=0)

    rows = b.shape[0]
    zeros = jnp.zeros((GUARD, LANES), jnp.float32)
    e_ref[0:GUARD, :] = zeros
    e_ref[GUARD + rows :, :] = zeros

    def shifted(by):
        return e_ref[GUARD + by : GUARD + by + rows, :]

    e_ref[GUARD : GUARD + rows, :] = w
    c_west = jnp.minimum(w, roll(w, 1))
    c_north, c_south = jnp.minimum(w, shifted(-1)), jnp.minimum(w, shifted(1))
    c_east = roll(c_west, -1)
    scale = relaxation / (damping + c_north + c_south + c_west + c_east)
    first = scale * b
    c_west, c_east, c_north, c_south = (scale * c for c in (c_west, c_east, c_north, c_south))
    e_ref[GUARD : GUARD + rows, :] = first

    def sweep(_, carry):
        e = shifted(0)
        around = (c_west * roll(e, 1) + c_east * roll(e, -1)) + (c_north * shifted(-1) + c_south * shifted(1))
        e_ref[GUARD : GUARD + rows, :] = ((1.0 - relaxation) * e + first) + around
        return carry

    lax.fori_loop(0, SWEEPS - 1, sweep, 0)


def up_kernel(e_ref, own_source, frame_source, own_diagonal, frame_diagonal, *refs):
    count = 4 * (LEVELS - 1)
    body_state, frame_state, ring_state = refs[:count], refs[count : 2 * count], refs[2 * count : 2 * count + 4]
    out_ref, resid_ref = refs[2 * count + 4 : 2 * count + 6]
    ring_pe, body_final, frame_final, sems, *inner = refs[2 * count + 6 :]
    outs, inner = inner[:2], inner[2:]
    body_pe, frame_pe = inner[: LEVELS - 1], inner[LEVELS - 1 :]
    rows = out_ref.shape[0] + 2 * TOP
    width = out_ref.shape[1] >> LEVELS

    level = LEVELS - 1
    step, halo, height = 2**level, TOP >> level, rows >> level
    coarse_rows = (height - 2 * halo) // 2
    picked = e_ref[GUARD + TALL - 8 : GUARD + TALL + coarse_rows + 8, :]
    lane = lane_of(picked)
    for t in range(3):
        group = (lane + t * LANES) // 2**LEVELS
        if t == 2:
            group = jnp.where(lane < LANES // 2, group, group - 3 * LANES // 2**LEVELS)
        taken = jnp.take_along_axis(picked, jnp.clip(group + width, 0, LANES - 1), axis=1)[7 : 7 + coarse_rows + 2]
        ring_pe[t, 0 : 2 * GUARD, :] = jnp.zeros((2 * GUARD, LANES), jnp.float32)
        ring_pe[t, height : height + 2 * GUARD, :] = jnp.zeros((2 * GUARD, LANES), jnp.float32)
        ring_pe[t, pl.ds(GUARD + halo - 2, coarse_rows + 2, stride=2), :] = taken
        ring_pe[t, pl.ds(GUARD + halo - 1, coarse_rows + 2, stride=2), :] = taken

    def climbed(pe, state, start, size, step):
        mid, around = beside_of(pe, state[:2], start, size, step)
        scale, smooth = load(state[2], start, size), load(state[3], start, size)
        return [(smooth[t] + (1.0 - relaxation) * mid[t]) + scale[t] * around[t] for t in range(len(mid))]

    def climb_ring(start, size, level=level, step=step):
        ring = spread(climbed(ring_pe, ring_state, start, size, step), step // 2)
        lane = lane_of(ring[0])
        around = jnp.where(
            lane < LANES // 2,
            jnp.where(lane < HALO, roll(ring[2], HALO), roll(ring[0], HALO)),
            jnp.where(lane < LANES - HALO, roll(ring[1], -HALO), roll(ring[2], -HALO)),
        )
        store_twice(body_pe[level - 1], start, size, ring[:2])
        store_twice(frame_pe[level - 1], start, size, [around])

    for_chunks(height, climb_ring, height, 16)

    for level in range(LEVELS - 2, -1, -1):
        step, height = 2**level, rows >> level
        groups = ((body_pe, body_state, body_final), (frame_pe, frame_state, frame_final))
        for pes, _, _ in groups:
            clear_guards(pes[level], height)

        def climb(start, size, level=level, step=step, groups=groups):
            for pes, states, final in groups:
                value = climbed(pes[level], states[4 * level : 4 * level + 4], start, size, step)
                if level == 0:
                    store(final, start, size, value)
                else:
                    store_twice(pes[level - 1], start, size, spread(value, step // 2))

        if level > 0:
            for_chunks(height, climb, CHUNK, CHUNK // 2)

    def last(base, size):
        body, around = beside_of(body_final, body_state[:2], base, size, 1)
        frame, frame_around = beside_of(frame_final, frame_state[:2], base, size, 1)
        b, d = load(own_source, base, size), load(own_diagonal, base, size)
        b_frame, d_frame = load(frame_source, base, size), load(frame_diagonal, base, size)
        body = (body, [(b[t] + around[t]) - d[t] * body[t] for t in range(2)])
        frame = (frame[0], (b_frame[0] + frame_around[0]) - d_frame[0] * frame[0])
        lane = lane_of(frame[0])
        near = HALO - 4
        span = pl.ds(base, size)
        for ref, middle, around in ((outs[0], body[0], frame[0]), (outs[1], body[1], frame[1])):
            ref[span, :LANES] = jnp.where(lane < near, roll(around, -HALO), middle[0])
            ref[span, LANES:] = jnp.where(lane >= LANES - near, roll(around, HALO), middle[1])

    count = rows // CHUNK
    ends = [0] + [CHUNK * (p + 1) - LAG - TOP for p in range(count - 1)] + [out_ref.shape[0]]

    def copies(p):
        size = ends[p + 1] - ends[p]
        return [
            pltpu.make_async_copy(
                outs[k].at[pl.ds(TOP + ends[p], size)], ref.at[pl.ds(ends[p], size)], sems.at[2 * p + k]
            )
            for k, ref in enumerate((out_ref, resid_ref))
        ]

    def finish(i, carry):
        for_parts(i * CHUNK, CHUNK, climb, CHUNK // 2)
        base = pl.multiple_of(jnp.maximum(i * CHUNK - LAG, 0), 8)
        for_parts(base, CHUNK, last, CHUNK // 2)
        for p in range(count):

            @pl.when(i == p)
            def _(p=p):
                for copy in copies(p):
                    copy.start()

        return carry

    lax.fori_loop(0, count, finish, 0)
    for p in range(count):
        for copy in copies(p):
            copy.wait()


def call(kernel, out_shape, scratch, flops, moved, **more):
    return pl.pallas_call(
        kernel,
        out_shape=out_shape,
        scratch_shapes=scratch,
        compiler_params=pltpu.CompilerParams(vmem_limit_bytes=VMEM_LIMIT),
        cost_estimate=pl.CostEstimate(flops=flops, bytes_accessed=moved, transcendentals=0),
        **more,
    )


def swap(x, axis, first):
    pairs = [(i, i + 1) for i in range(first, lax.axis_size(axis) - 1, 2)]
    return lax.ppermute(x, axis, pairs + [(j, i) for i, j in pairs])


def local(rhs, pressure, wet_mask, bathy_class):
    rows, columns = rhs.shape
    cells = rows * columns
    total = rows + 2 * TOP
    levels = range(LEVELS - 1)

    def shape(tiles, level):
        return (tiles, (total >> level) + 2 * GUARD, LANES)

    def out(*dims):
        return jax.ShapeDtypeStruct(dims, jnp.float32)

    def vmem(tiles, level):
        return pltpu.VMEM(shape(tiles, level), jnp.float32)

    def fields(r, p, m, c):
        wet = m.astype(jnp.float32)
        return wet * r, wet * p, wet * (1.0 + 0.5 * c.astype(jnp.float32))

    given = (rhs, pressure, wet_mask, bathy_class)

    def edge(start):
        return jnp.stack(fields(*(lax.dynamic_slice_in_dim(x, start, HALO, axis=0) for x in given)))

    even = lax.axis_index("gx") % 2 == 0
    first_rows = swap(edge(jnp.where(even, 0, rows - HALO)), "gx", 1)
    second_rows = swap(edge(jnp.where(even, rows - HALO, 0)), "gx", 0)
    piece = (rows + 2 * HALO) // PIECES
    own_shapes = [out(*shape(2, 0))] * 3
    laid_out = [*own_shapes, out(3, piece, LANES), out(3, piece, LANES)]
    inner = [vmem(2, level) for level in range(1, LEVELS)]
    begun = call(layout_kernel, laid_out, inner, 10 * cells, 10 * cells)(*fields(*given))
    *own, to_cross, to_pair = call(
        halo_kernel, laid_out, (), cells, cells, input_output_aliases={k: k for k in range(5)}
    )(*begun, first_rows, second_rows)
    from_pair = swap(to_pair, "gy", 0)
    from_cross = swap(to_cross, "gy", 1)

    state_count = 4 * (LEVELS - 1)
    *body_state, body_weight, body_source, diagonal, frame_source, frame_guess, frame_weight = call(
        body_kernel,
        [out(*shape(2, level)) for level in levels for _ in range(4)]
        + [out(*shape(2, LEVELS - 1))] * 2
        + [out(*shape(2, 0))]
        + [out(*shape(1, 0))] * 3,
        [vmem(2, 0)] * 3 + [vmem(2, level) for level in levels[1:]] * 3,
        100 * cells,
        40 * cells,
    )(*own)
    nx, ny = lax.axis_size("gx"), lax.axis_size("gy")
    ring = LEVELS - 1
    frame_source, _, _, *state, dense, chunks = call(
        frame_kernel,
        [out(*shape(1, 0))] * 3
        + [out(*shape(1, level)) for level in levels for _ in range(4)]
        + [out(*shape(1, 0))]
        + [out(*shape(3, ring))] * 4
        + [out(8, LANES), out(nx, ny, 4, LANES)],
        [vmem(1, 0)] * 2 + [vmem(3, ring)] * 5 + [vmem(1, level) for level in range(1, LEVELS)] * 3,
        50 * cells,
        20 * cells,
        input_output_aliases={k: k for k in range(3)},
    )(frame_source, frame_guess, frame_weight, from_pair, from_cross, body_weight, body_source)
    frame_state, frame_diagonal, ring_state = state[:state_count], state[state_count], state[state_count + 1 :]
    gathered = lax.all_to_all(chunks.reshape(nx * ny, 4, LANES), ("gx", "gy"), 0, 0).reshape(chunks.shape)
    correction = call(
        coarse_kernel, out((rows >> LEVELS) + 2 * TALL + 2 * GUARD, LANES), (), cells, cells
    )(gathered, dense, from_pair, from_cross)
    return call(
        up_kernel,
        (out(rows, columns), out(rows, columns)),
        [vmem(3, ring), vmem(2, 0), vmem(1, 0), pltpu.SemaphoreType.DMA((8,))]
        + [pltpu.VMEM((total, columns), jnp.float32)] * 2
        + [vmem(2, level) for level in levels]
        + [vmem(1, level) for level in levels],
        60 * cells,
        40 * cells,
        out_specs=[pl.BlockSpec(memory_space=pl.ANY)] * 2,
    )(correction, own[0], frame_source, diagonal, frame_diagonal, *body_state, *frame_state, *ring_state)


def solution(mesh):
    placed = (P("gx", "gy"), P("gx", "gy"), P("gx", "gy"), P("gx", "gy"))
    return jax.shard_map(
        local, mesh=mesh, in_specs=placed, out_specs=(P("gx", "gy"), P("gx", "gy")), check_vma=False
    )
```

```python
import jax
import jax.numpy as jnp
from jax import lax
from jax.experimental import pallas as pl
from jax.experimental.pallas import tpu as pltpu
from jax.sharding import PartitionSpec as P

LEVELS = 4
SWEEPS = 12

damping = 0.01
relaxation = 0.8

HALO = 24
LANES = 128
INNER = LANES // 2 - HALO
TOP = 32
GUARD = 8
PIECES = 5
CHUNK = 144
LAG = 8
TALL = 16
VMEM_LIMIT = 40 * 1024 * 1024


def lane_of(x):
    return lax.broadcasted_iota(jnp.int32, x.shape, x.ndim - 1)


def roll(x, amount):
    amount %= LANES
    return x if amount == 0 else pltpu.roll(x, amount, x.ndim - 1)


def from_west(tiles, step):
    moved = [roll(t, step) for t in tiles]
    if len(tiles) == 1:
        return moved
    edge = lane_of(tiles[0]) < step
    return [jnp.where(edge, moved[i - 1], moved[i]) for i in range(len(tiles))]


def from_east(tiles, step):
    moved = [roll(t, -step) for t in tiles]
    count = len(tiles)
    if count == 1:
        return moved
    edge = lane_of(tiles[0]) >= LANES - step
    return [jnp.where(edge, moved[(i + 1) % count], moved[i]) for i in range(count)]


def clear_rim(ref):
    rim = GUARD + TOP - HALO
    zeros = jnp.zeros((rim, LANES), jnp.float32)
    for t in range(ref.shape[0]):
        ref[t, 0:rim, :] = zeros
        ref[t, ref.shape[1] - rim :, :] = zeros


def spread(tiles, step):
    second = (lane_of(tiles[0]) // step) % 2 == 1
    return [jnp.where(second, roll(t, step), t) for t in tiles]


def for_parts(start, size, body, part):
    for offset in range(0, size, part):
        body(start + offset, min(part, size - offset))


def for_chunks(rows, body, largest, part):
    sizes = [size for size in range(8, largest + 1, 8) if rows % size == 0]
    if rows <= largest or not sizes:
        for_parts(0, rows, body, part)
        return

    def step(i, carry):
        for_parts(i * sizes[-1], sizes[-1], body, part)
        return carry

    lax.fori_loop(0, rows // sizes[-1], step, 0)


def load(ref, start, size):
    return [ref[t, pl.ds(GUARD + start, size), :] for t in range(ref.shape[0])]


def store(ref, start, size, tiles):
    for t, tile in enumerate(tiles):
        ref[t, pl.ds(GUARD + start, size), :] = tile


def store_twice(ref, start, size, tiles):
    for t, tile in enumerate(tiles):
        ref[t, pl.ds(GUARD + 2 * start, size, stride=2), :] = tile
        ref[t, pl.ds(GUARD + 2 * start + 1, size, stride=2), :] = tile


def clear_guards(ref, rows):
    zeros = jnp.zeros((GUARD, LANES), jnp.float32)
    for t in range(ref.shape[0]):
        ref[t, 0:GUARD, :] = zeros
        ref[t, GUARD + rows : 2 * GUARD + rows, :] = zeros


def beside(mid, north, south, c_west, c_north, c_south, step):
    west = from_west(mid, step)
    east = from_east([c * m for c, m in zip(c_west, mid)], step)
    return [
        (c_west[t] * west[t] + east[t]) + (c_north[t] * north[t] + c_south[t] * south[t]) for t in range(len(mid))
    ]


def beside_of(ref, coeffs, start, size, step):
    c_west_ref, c_north_ref = coeffs
    mid = load(ref, start, size)
    north, south = load(ref, start - 1, size), load(ref, start + 1, size)
    c_west, c_north = load(c_west_ref, start, size), load(c_north_ref, start, size)
    return mid, beside(mid, north, south, c_west, c_north, load(c_north_ref, start + 1, size), step)


def pool_rows(ref, start, size, step):
    out = []
    for t in range(ref.shape[0]):
        even = ref[t, pl.ds(GUARD + start, size // 2, stride=2), :]
        odd = ref[t, pl.ds(GUARD + start + 1, size // 2, stride=2), :]
        both = even + odd
        out.append(both + roll(both, -step))
    return out


def descend(level, height, weight, source, guess, state, diagonal_ref, field, resid, next_weight, next_source, largest, part):
    step = 2**level
    c_west_ref, c_north_ref, scale_ref, smooth_ref = state
    for ref in (weight, field, c_north_ref):
        clear_guards(ref, height)

    def first_pass(start, size):
        w, w_north, w_south = (load(weight, start + k, size) for k in (0, -1, 1))
        c_north = [jnp.minimum(a, b) for a, b in zip(w, w_north)]
        c_south = [jnp.minimum(a, b) for a, b in zip(w, w_south)]
        c_west = [jnp.minimum(a, b) for a, b in zip(w, from_west(w, step))]
        c_east = from_east(c_west, step)
        diagonal = [damping + c_north[t] + c_south[t] + c_west[t] + c_east[t] for t in range(len(w))]
        scale = [relaxation / d for d in diagonal]
        store(c_north_ref, start, size, c_north)
        store(c_west_ref, start, size, c_west)
        store(scale_ref, start, size, scale)
        store(diagonal_ref, start, size, diagonal)
        value = load(source, start, size)
        if guess is None:
            value = [scale[t] * value[t] for t in range(len(w))]
        else:
            mid, north, south = (load(guess, start + k, size) for k in (0, -1, 1))
            around = beside(mid, north, south, c_west, c_north, c_south, step)
            value = [
                (1.0 - relaxation) * mid[t] + scale[t] * (value[t] + around[t]) for t in range(len(w))
            ]
        store(field, start, size, value)
        if next_weight is not None:
            pooled = [0.125 * p for p in pool_rows(weight, start, size, step)]
            store(next_weight, start // 2, size // 2, pooled)

    def second_pass(start, size):
        mid, around = beside_of(field, (c_west_ref, c_north_ref), start, size, step)
        b, scale, diagonal = (load(ref, start, size) for ref in (source, scale_ref, diagonal_ref))
        rest = [(b[t] + around[t]) - diagonal[t] * mid[t] for t in range(len(b))]
        store(smooth_ref, start, size, [mid[t] + scale[t] * rest[t] for t in range(len(b))])
        store(resid, start, size, rest)
        if next_source is not None:
            pooled = [0.25 * p for p in pool_rows(resid, start, size, step)]
            store(next_source, start // 2, size // 2, pooled)

    for_chunks(height, first_pass, largest, part)
    for_chunks(height, second_pass, largest, part)


def descend_all(rows, sources, guess, weights, states, diagonal, field, resid, largest, part):
    for level in range(LEVELS - 1):
        descend(
            level,
            rows >> level,
            weights[level],
            sources[level],
            guess if level == 0 else None,
            states[4 * level : 4 * level + 4],
            diagonal[level],
            field,
            resid,
            weights[level + 1],
            sources[level + 1],
            largest,
            part,
        )


def to_sides(west, east, cross_ref, pair_ref, k, rows):
    even = lax.axis_index("gy") % 2 == 0
    cross_ref[k, rows, :] = jnp.where(even, west, east)
    pair_ref[k, rows, :] = jnp.where(even, east, west)


def layout_kernel(source, guess, weight, own_source, own_guess, own_weight, cross_ref, pair_ref, *inner):
    rows = source.shape[0]
    piece = cross_ref.shape[1]
    tail = rows - (PIECES - 1) * piece
    for k, (block, own) in enumerate(zip((source, guess, weight), (own_source, own_guess, own_weight))):
        clear_rim(own)
        sides = []
        for t in range(2):
            own[t, GUARD + TOP : GUARD + TOP + rows, :] = block[:, t * LANES : (t + 1) * LANES]
        for tile, first in ((0, 0), (1, LANES - HALO)):
            columns = slice(tile * LANES, (tile + 1) * LANES)
            last = roll(block[(PIECES - 1) * piece :, columns], (PIECES - 1) * HALO - first)
            packed = jnp.concatenate((last, jnp.zeros((piece - tail, LANES), jnp.float32)), axis=0)
            for p in range(PIECES - 1):
                part = block[p * piece : (p + 1) * piece, columns]
                packed = jnp.where(lane_of(part) // HALO == p, roll(part, p * HALO - first), packed)
            sides.append(packed)
        to_sides(*sides, cross_ref, pair_ref, k, slice(0, piece))
    weights, start, height = (own_weight, *inner), TOP, rows
    for level in range(LEVELS):
        pooled = [0.125 * w for w in pool_rows(weights[level], start, height, 2**level)]
        start, height = start // 2, height // 2
        if level < LEVELS - 1:
            store(weights[level + 1], start, height, pooled)
    lane = lane_of(pooled[0])
    free = PIECES * HALO
    index = jnp.clip(lane - free, 0, LANES - 1 - free) * 2**LEVELS
    for t in range(2):
        taken = jnp.take_along_axis(pooled[t], index, axis=1)
        span = slice(t * height, (t + 1) * height)
        for ref in (cross_ref, pair_ref):
            ref[0, span, :] = jnp.where(lane >= free, taken, ref[0, span, :])


def halo_kernel(*refs):
    first_rows, second_rows, *own, pair_ref, corner_ref = refs[4:]
    total = own[0].shape[1] - 2 * GUARD
    piece = pair_ref.shape[1]
    even, even_y = lax.axis_index("gx") % 2 == 0, lax.axis_index("gy") % 2 == 0
    shift = (PIECES - 1) * HALO
    for k in range(3):
        above = jnp.where(even, first_rows[k], second_rows[k])
        below = jnp.where(even, second_rows[k], first_rows[k])
        for side, (rows, row) in enumerate(((above, TOP - HALO), (below, total - TOP))):
            body = [rows[:, t * LANES : (t + 1) * LANES] for t in range(2)]
            for t in range(2):
                own[k][t, GUARD + row : GUARD + row + HALO, :] = body[t]
            lane = lane_of(body[0])
            west, east = body[0], roll(body[1], HALO - LANES)
            cross, pair = jnp.where(even_y, west, east), jnp.where(even_y, east, west)
            span = slice(piece - (2 - side) * HALO, piece - (1 - side) * HALO)
            pair_ref[k, span, :] = jnp.where(lane // HALO == PIECES - 1, roll(pair, shift), pair_ref[k, span, :])
            span = slice(side * HALO, (side + 1) * HALO)
            before = corner_ref[span, :] if k else jnp.zeros_like(cross)
            corner_ref[span, :] = jnp.where(lane // HALO == k, roll(cross, k * HALO), before)


def body_kernel(source, guess, weight, *refs):
    states = refs[: 4 * (LEVELS - 1)]
    last_weight, last_source, first_diagonal, *refs = refs[4 * (LEVELS - 1) :]
    frames, (field, resid, weight_in, *inner) = refs[:3], refs[3:]
    rows = source.shape[1] - 2 * GUARD
    depth = LEVELS - 2
    weights = (weight_in, *inner[:depth], last_weight)
    sources = (source, *inner[depth : 2 * depth], last_source)
    diagonal = (first_diagonal, *inner[2 * depth :])
    weights[0][...] = weight[...]
    descend_all(rows, sources, guess, weights, states, diagonal, field, resid, 144, 144)
    for own, frame in zip((source, guess, weight), frames):
        tiles = [own[t] for t in range(2)]
        frame[0] = jnp.where(lane_of(tiles[0]) < LANES // 2, roll(tiles[0], HALO), roll(tiles[1], -HALO))


def frame_kernel(_a, _b, _c, from_cross, from_pair, from_corners, body_weight, body_source, *refs):
    even = lax.axis_index("gy") % 2 == 0
    frames, states, refs = refs[:3], refs[3 : 3 + 4 * (LEVELS - 1)], refs[3 + 4 * (LEVELS - 1) :]
    frame_source, frame_guess, frame_weight = frames
    first_diagonal, ring_state, dense_ref, chunks_ref, field, resid, *refs = refs[0], refs[1:5], *refs[5:]
    ring_weight, ring_source, ring_field, ring_resid, ring_diagonal, *inner = refs
    rows = frame_source.shape[1] - 2 * GUARD
    depth = LEVELS - 1
    weights = (frame_weight, *inner[:depth])
    sources = (frame_source, *inner[depth : 2 * depth])
    diagonals = (first_diagonal, *inner[2 * depth :])
    piece = from_cross.shape[1]
    for k, frame in enumerate(frames):
        cross, pair = from_cross[k], from_pair[k]
        spans = [(TOP + p * piece, p, p, cross[:], pair[:]) for p in range(PIECES - 1)]
        tail = piece - 2 * HALO
        last = PIECES - 1
        spans.append((TOP + last * piece, last, last, cross[:tail], pair[:tail]))
        for side, start in enumerate((TOP - HALO, rows - TOP)):
            corner = from_corners[side * HALO : (side + 1) * HALO, :]
            spans.append((start, k, last, corner, pair[tail + side * HALO : tail + (side + 1) * HALO]))
        for start, cross_group, pair_group, cross_part, pair_part in spans:
            span = slice(GUARD + start, GUARD + start + cross_part.shape[0])
            cross_part, pair_part = roll(cross_part, -cross_group * HALO), roll(pair_part, -pair_group * HALO)
            west = jnp.where(even, cross_part, pair_part)
            east = roll(jnp.where(even, pair_part, cross_part), -HALO)
            lane = lane_of(west)
            inside = jnp.where(lane < HALO, west, frame[0, span, :])
            frame[0, span, :] = jnp.where(lane >= LANES - HALO, east, inside)
    descend_all(rows, sources, frame_guess, weights, states, diagonals, field, resid, 288, 288)

    level = LEVELS - 1
    step, halo, height = 2**level, TOP >> level, rows >> level
    for body, frame, ring in (
        (body_weight, weights[level], ring_weight),
        (body_source, sources[level], ring_source),
    ):
        middle = load(body, 0, height)
        around = load(frame, 0, height)[0]
        lane = lane_of(around)
        ahead, back = roll(around, HALO), roll(around, -HALO)
        store(
            ring,
            0,
            height,
            [
                jnp.where(lane < 2 * step, back, middle[0]),
                jnp.where(lane >= LANES - 2 * step, ahead, middle[1]),
                jnp.where(lane < LANES // 2, ahead, back),
            ],
        )
    descend(
        level,
        height,
        ring_weight,
        ring_source,
        None,
        ring_state,
        ring_diagonal,
        ring_field,
        ring_resid,
        None,
        None,
        height,
        height,
    )

    coarse_rows = (height - 2 * halo) // 2
    dense = jnp.zeros((8, LANES), jnp.float32)
    lane = lane_of(dense)
    per_tile = LANES // 2**LEVELS
    pooled_b = pool_rows(ring_resid, halo, 2 * coarse_rows, step)
    pooled_w = pool_rows(ring_weight, halo, 2 * coarse_rows, step)
    index = (lane % per_tile) * 2**LEVELS
    place = lane // per_tile
    for g in range(coarse_rows // 8):
        for group, (values, factor) in enumerate(((pooled_b, 0.25), (pooled_w, 0.125))):
            for t in range(2):
                taken = jnp.take_along_axis(factor * values[t][8 * g : 8 * g + 8], index, axis=1)
                dense = jnp.where(place == 4 * g + 2 * group + t, taken, dense)
    dense_ref[...] = dense

    index = jnp.minimum(2 * (lane - lane % (2 * per_tile)) + lane % (2 * per_tile), LANES - 1)
    level_with, above, below = (fold(x) for x in (jnp.take_along_axis(dense, index, axis=1), dense, roll(dense, -LANES // 2)))
    x = lax.axis_index("gx")
    for i in range(chunks_ref.shape[0]):
        chunk = jnp.where(i == x, level_with, jnp.where(i < x, above, below))
        chunks_ref[i] = jnp.broadcast_to(chunk[None], chunks_ref.shape[1:])


def fold(x):
    return jnp.where(lane_of(x) < LANES // 2, x, pltpu.roll(roll(x, LANES // 2), 4, 0))[:4]


def unfold(x):
    return jnp.concatenate((x, roll(x, LANES // 2)), axis=0)


def coarse_solve(all_ref, dense_ref, from_cross, from_pair, e_ref, width, groups):
    x, nx = lax.axis_index("gx"), lax.axis_size("gx")
    y, ny = lax.axis_index("gy"), lax.axis_size("gy")
    tiles = {}
    for dx in (-1, 0, 1):
        for dy in (-1, 0, 1):
            if dx or dy:
                inside = (x + dx >= 0) & (x + dx < nx) & (y + dy >= 0) & (y + dy < ny)
                tile = unfold(all_ref[jnp.where(inside, x + dx, 0), jnp.where(inside, y + dy, 0)])
                tiles[dx, dy] = jnp.where(inside, tile, 0.0)
    dense = dense_ref[...]
    lane = lane_of(dense)
    even = y % 2 == 0
    height = 8 * groups
    cross, pair = from_cross[0, : 2 * height, :], from_pair[0, : 2 * height, :]
    weights = {-1: jnp.where(even, cross, pair), 1: jnp.where(even, pair, cross)}
    bands = [(-1, g) for g in range(TALL // 8)] + [(0, g) for g in range(groups)] + [(1, g) for g in range(TALL // 8)]
    b, w = [], []
    for dx, g in bands:
        b_rows = w_rows = jnp.zeros_like(dense)
        for dy in (-1, 0, 1):
            first = (dy + 1) * width
            here = (lane >= first) & (lane < first + width)
            if dx or not dy:
                tile = tiles[dx, dy] if dx else dense
                b_part, w_part = roll(tile, first - 2 * g * width), roll(tile, first - (2 * g + 1) * width)
            else:
                b_part = roll(tiles[dx, dy], first - g * width)
                free = PIECES * HALO
                parts = [weights[dy][t * height + 8 * g : t * height + 8 * g + 8] for t in range(2)]
                parts = [roll(part, first + t * width // 2 - free) for t, part in enumerate(parts)]
                w_part = jnp.where(lane < first + width // 2, *parts)
            b_rows = jnp.where(here, b_part, b_rows)
            w_rows = jnp.where(here, w_part, w_rows)
        b.append(b_rows)
        w.append(w_rows)
    b, w = jnp.concatenate(b, axis=0), jnp.concatenate(w, axis=0)

    rows = b.shape[0]
    zeros = jnp.zeros((GUARD, LANES), jnp.float32)
    e_ref[0:GUARD, :] = zeros
    e_ref[GUARD + rows :, :] = zeros

    def shifted(by):
        return e_ref[GUARD + by : GUARD + by + rows, :]

    e_ref[GUARD : GUARD + rows, :] = w
    c_west = jnp.minimum(w, roll(w, 1))
    c_north, c_south = jnp.minimum(w, shifted(-1)), jnp.minimum(w, shifted(1))
    c_east = roll(c_west, -1)
    scale = relaxation / (damping + c_north + c_south + c_west + c_east)
    first = scale * b
    c_west, c_east, c_north, c_south = (scale * c for c in (c_west, c_east, c_north, c_south))
    e_ref[GUARD : GUARD + rows, :] = first

    def sweep(_, carry):
        e = shifted(0)
        around = (c_west * roll(e, 1) + c_east * roll(e, -1)) + (c_north * shifted(-1) + c_south * shifted(1))
        e_ref[GUARD : GUARD + rows, :] = ((1.0 - relaxation) * e + first) + around
        return carry

    lax.fori_loop(0, SWEEPS - 1, sweep, 0)
    return shifted(0)


def up_kernel(all_ref, dense_ref, from_cross, from_pair, own_source, frame_source, own_diagonal, frame_diagonal, *refs):
    count = 4 * (LEVELS - 1)
    body_state, frame_state, ring_state = refs[:count], refs[count : 2 * count], refs[2 * count : 2 * count + 4]
    out_ref, resid_ref = refs[2 * count + 4 : 2 * count + 6]
    ring_pe, body_final, frame_final, sems, e_ref, *inner = refs[2 * count + 6 :]
    outs, inner = inner[:2], inner[2:]
    body_pe, frame_pe = inner[: LEVELS - 1], inner[LEVELS - 1 :]
    rows = out_ref.shape[0] + 2 * TOP
    width = out_ref.shape[1] >> LEVELS
    e = coarse_solve(all_ref, dense_ref, from_cross, from_pair, e_ref, width, (out_ref.shape[0] >> LEVELS) // 8)

    level = LEVELS - 1
    step, halo, height = 2**level, TOP >> level, rows >> level
    coarse_rows = (height - 2 * halo) // 2
    picked = e[TALL - 8 : TALL + coarse_rows + 8]
    lane = lane_of(picked)
    for t in range(3):
        group = (lane + t * LANES) // 2**LEVELS
        if t == 2:
            group = jnp.where(lane < LANES // 2, group, group - 3 * LANES // 2**LEVELS)
        taken = jnp.take_along_axis(picked, jnp.clip(group + width, 0, LANES - 1), axis=1)[7 : 7 + coarse_rows + 2]
        ring_pe[t, 0 : 2 * GUARD, :] = jnp.zeros((2 * GUARD, LANES), jnp.float32)
        ring_pe[t, height : height + 2 * GUARD, :] = jnp.zeros((2 * GUARD, LANES), jnp.float32)
        ring_pe[t, pl.ds(GUARD + halo - 2, coarse_rows + 2, stride=2), :] = taken
        ring_pe[t, pl.ds(GUARD + halo - 1, coarse_rows + 2, stride=2), :] = taken

    def climbed(pe, state, start, size, step):
        mid, around = beside_of(pe, state[:2], start, size, step)
        scale, smooth = load(state[2], start, size), load(state[3], start, size)
        return [(smooth[t] + (1.0 - relaxation) * mid[t]) + scale[t] * around[t] for t in range(len(mid))]

    def climb_ring(start, size, level=level, step=step):
        ring = spread(climbed(ring_pe, ring_state, start, size, step), step // 2)
        lane = lane_of(ring[0])
        around = jnp.where(
            lane < LANES // 2,
            jnp.where(lane < HALO, roll(ring[2], HALO), roll(ring[0], HALO)),
            jnp.where(lane < LANES - HALO, roll(ring[1], -HALO), roll(ring[2], -HALO)),
        )
        store_twice(body_pe[level - 1], start, size, ring[:2])
        store_twice(frame_pe[level - 1], start, size, [around])

    for_chunks(height, climb_ring, height, 16)

    for level in range(LEVELS - 2, -1, -1):
        step, height = 2**level, rows >> level
        groups = ((body_pe, body_state, body_final), (frame_pe, frame_state, frame_final))
        for pes, _, _ in groups:
            clear_guards(pes[level], height)

        def climb(start, size, level=level, step=step, groups=groups):
            for pes, states, final in groups:
                value = climbed(pes[level], states[4 * level : 4 * level + 4], start, size, step)
                if level == 0:
                    store(final, start, size, value)
                else:
                    store_twice(pes[level - 1], start, size, spread(value, step // 2))

        if level > 0:
            for_chunks(height, climb, CHUNK, CHUNK // 2)

    def last(base, size):
        body, around = beside_of(body_final, body_state[:2], base, size, 1)
        frame, frame_around = beside_of(frame_final, frame_state[:2], base, size, 1)
        b, d = load(own_source, base, size), load(own_diagonal, base, size)
        b_frame, d_frame = load(frame_source, base, size), load(frame_diagonal, base, size)
        body = (body, [(b[t] + around[t]) - d[t] * body[t] for t in range(2)])
        frame = (frame[0], (b_frame[0] + frame_around[0]) - d_frame[0] * frame[0])
        lane = lane_of(frame[0])
        near = HALO - 4
        span = pl.ds(base, size)
        for ref, middle, around in ((outs[0], body[0], frame[0]), (outs[1], body[1], frame[1])):
            ref[span, :LANES] = jnp.where(lane < near, roll(around, -HALO), middle[0])
            ref[span, LANES:] = jnp.where(lane >= LANES - near, roll(around, HALO), middle[1])

    count = rows // CHUNK
    ends = [0] + [CHUNK * (p + 1) - LAG - TOP for p in range(count - 1)] + [out_ref.shape[0]]

    def copies(p):
        size = ends[p + 1] - ends[p]
        return [
            pltpu.make_async_copy(
                outs[k].at[pl.ds(TOP + ends[p], size)], ref.at[pl.ds(ends[p], size)], sems.at[2 * p + k]
            )
            for k, ref in enumerate((out_ref, resid_ref))
        ]

    def finish(i, carry):
        for_parts(i * CHUNK, CHUNK, climb, CHUNK // 2)
        base = pl.multiple_of(jnp.maximum(i * CHUNK - LAG, 0), 8)
        for_parts(base, CHUNK, last, CHUNK // 2)
        for p in range(count):

            @pl.when(i == p)
            def _(p=p):
                for copy in copies(p):
                    copy.start()

        return carry

    lax.fori_loop(0, count, finish, 0)
    for p in range(count):
        for copy in copies(p):
            copy.wait()


def call(kernel, out_shape, scratch, flops, moved, **more):
    return pl.pallas_call(
        kernel,
        out_shape=out_shape,
        scratch_shapes=scratch,
        compiler_params=pltpu.CompilerParams(vmem_limit_bytes=VMEM_LIMIT),
        cost_estimate=pl.CostEstimate(flops=flops, bytes_accessed=moved, transcendentals=0),
        **more,
    )


def swap(x, axis, first):
    pairs = [(i, i + 1) for i in range(first, lax.axis_size(axis) - 1, 2)]
    return lax.ppermute(x, axis, pairs + [(j, i) for i, j in pairs])


def local(rhs, pressure, wet_mask, bathy_class):
    rows, columns = rhs.shape
    cells = rows * columns
    total = rows + 2 * TOP
    levels = range(LEVELS - 1)

    def shape(tiles, level):
        return (tiles, (total >> level) + 2 * GUARD, LANES)

    def out(*dims):
        return jax.ShapeDtypeStruct(dims, jnp.float32)

    def vmem(tiles, level):
        return pltpu.VMEM(shape(tiles, level), jnp.float32)

    def fields(r, p, m, c):
        wet = m.astype(jnp.float32)
        return wet * r, wet * p, wet * (1.0 + 0.5 * c.astype(jnp.float32))

    given = (rhs, pressure, wet_mask, bathy_class)

    def edge(start):
        return jnp.stack(fields(*(lax.dynamic_slice_in_dim(x, start, HALO, axis=0) for x in given)))

    even = lax.axis_index("gx") % 2 == 0
    first_rows = swap(edge(jnp.where(even, 0, rows - HALO)), "gx", 1)
    second_rows = swap(edge(jnp.where(even, rows - HALO, 0)), "gx", 0)
    piece = (rows + 2 * HALO) // PIECES
    own_shapes = [out(*shape(2, 0))] * 3
    edges = out(3, piece, LANES)
    inner = [vmem(2, level) for level in range(1, LEVELS)]
    *begun, to_cross, to_pair = call(layout_kernel, [*own_shapes, edges, edges], inner, 10 * cells, 10 * cells)(
        *fields(*given)
    )
    from_cross = swap(to_cross, "gy", 1)
    *own, to_pair, corners = call(
        halo_kernel,
        [*own_shapes, edges, out(2 * HALO, LANES)],
        (),
        cells,
        cells,
        input_output_aliases={k: k for k in range(4)},
    )(*begun, to_pair, first_rows, second_rows)
    from_pair = swap(to_pair, "gy", 0)
    from_corners = swap(corners, "gy", 1)

    state_count = 4 * (LEVELS - 1)
    *body_state, body_weight, body_source, diagonal, frame_source, frame_guess, frame_weight = call(
        body_kernel,
        [out(*shape(2, level)) for level in levels for _ in range(4)]
        + [out(*shape(2, LEVELS - 1))] * 2
        + [out(*shape(2, 0))]
        + [out(*shape(1, 0))] * 3,
        [vmem(2, 0)] * 3 + [vmem(2, level) for level in levels[1:]] * 3,
        100 * cells,
        40 * cells,
    )(*own)
    nx, ny = lax.axis_size("gx"), lax.axis_size("gy")
    ring = LEVELS - 1
    frame_source, _, _, *state, dense, chunks = call(
        frame_kernel,
        [out(*shape(1, 0))] * 3
        + [out(*shape(1, level)) for level in levels for _ in range(4)]
        + [out(*shape(1, 0))]
        + [out(*shape(3, ring))] * 4
        + [out(8, LANES), out(nx, ny, 4, LANES)],
        [vmem(1, 0)] * 2 + [vmem(3, ring)] * 5 + [vmem(1, level) for level in range(1, LEVELS)] * 3,
        50 * cells,
        20 * cells,
        input_output_aliases={k: k for k in range(3)},
    )(frame_source, frame_guess, frame_weight, from_cross, from_pair, from_corners, body_weight, body_source)
    frame_state, frame_diagonal, ring_state = state[:state_count], state[state_count], state[state_count + 1 :]
    gathered = lax.all_to_all(chunks.reshape(nx * ny, 4, LANES), ("gx", "gy"), 0, 0).reshape(chunks.shape)
    return call(
        up_kernel,
        (out(rows, columns), out(rows, columns)),
        [vmem(3, ring), vmem(2, 0), vmem(1, 0), pltpu.SemaphoreType.DMA((8,))]
        + [pltpu.VMEM(((rows >> LEVELS) + 2 * TALL + 2 * GUARD, LANES), jnp.float32)]
        + [pltpu.VMEM((total, columns), jnp.float32)] * 2
        + [vmem(2, level) for level in levels]
        + [vmem(1, level) for level in levels],
        60 * cells,
        40 * cells,
        out_specs=[pl.BlockSpec(memory_space=pl.ANY)] * 2,
    )(gathered, dense, from_cross, from_pair, own[0], frame_source, diagonal, frame_diagonal, *body_state, *frame_state, *ring_state)


def solution(mesh):
    placed = (P("gx", "gy"), P("gx", "gy"), P("gx", "gy"), P("gx", "gy"))
    return jax.shard_map(
        local, mesh=mesh, in_specs=placed, out_specs=(P("gx", "gy"), P("gx", "gy")), check_vma=False
    )
```

```python
import jax
import jax.numpy as jnp
from jax import lax
from jax.experimental import pallas as pl
from jax.experimental.pallas import tpu as pltpu
from jax.sharding import PartitionSpec as P

LEVELS = 4
SWEEPS = 12

damping = 0.01
relaxation = 0.8

HALO = 16
EDGE = 24
NEAR = 20
LANES = 128
INNER = LANES // 2 - HALO
TOP = 32
GUARD = 8
PIECES = 8
CHUNK = 144
LAG = 8
TALL = 16
VMEM_LIMIT = 40 * 1024 * 1024


def lane_of(x):
    return lax.broadcasted_iota(jnp.int32, x.shape, x.ndim - 1)


def roll(x, amount):
    amount %= LANES
    return x if amount == 0 else pltpu.roll(x, amount, x.ndim - 1)


def from_west(tiles, step):
    moved = [roll(t, step) for t in tiles]
    if len(tiles) == 1:
        return moved
    edge = lane_of(tiles[0]) < step
    return [jnp.where(edge, moved[i - 1], moved[i]) for i in range(len(tiles))]


def from_east(tiles, step):
    moved = [roll(t, -step) for t in tiles]
    count = len(tiles)
    if count == 1:
        return moved
    edge = lane_of(tiles[0]) >= LANES - step
    return [jnp.where(edge, moved[(i + 1) % count], moved[i]) for i in range(count)]


def clear_rim(ref):
    rim = GUARD + TOP - EDGE
    zeros = jnp.zeros((rim, LANES), jnp.float32)
    for t in range(ref.shape[0]):
        ref[t, 0:rim, :] = zeros
        ref[t, ref.shape[1] - rim :, :] = zeros


def spread(tiles, step):
    second = (lane_of(tiles[0]) // step) % 2 == 1
    return [jnp.where(second, roll(t, step), t) for t in tiles]


def for_parts(start, size, body, part):
    for offset in range(0, size, part):
        body(start + offset, min(part, size - offset))


def for_chunks(rows, body, largest, part):
    sizes = [size for size in range(8, largest + 1, 8) if rows % size == 0]
    if rows <= largest or not sizes:
        for_parts(0, rows, body, part)
        return

    def step(i, carry):
        for_parts(i * sizes[-1], sizes[-1], body, part)
        return carry

    lax.fori_loop(0, rows // sizes[-1], step, 0)


def load(ref, start, size):
    return [ref[t, pl.ds(GUARD + start, size), :] for t in range(ref.shape[0])]


def store(ref, start, size, tiles):
    for t, tile in enumerate(tiles):
        ref[t, pl.ds(GUARD + start, size), :] = tile


def store_twice(ref, start, size, tiles):
    for t, tile in enumerate(tiles):
        ref[t, pl.ds(GUARD + 2 * start, size, stride=2), :] = tile
        ref[t, pl.ds(GUARD + 2 * start + 1, size, stride=2), :] = tile


def clear_guards(ref, rows):
    zeros = jnp.zeros((GUARD, LANES), jnp.float32)
    for t in range(ref.shape[0]):
        ref[t, 0:GUARD, :] = zeros
        ref[t, GUARD + rows : 2 * GUARD + rows, :] = zeros


def beside(mid, north, south, c_west, c_north, c_south, step):
    west = from_west(mid, step)
    east = from_east([c * m for c, m in zip(c_west, mid)], step)
    return [
        (c_west[t] * west[t] + east[t]) + (c_north[t] * north[t] + c_south[t] * south[t]) for t in range(len(mid))
    ]


def beside_of(ref, coeffs, start, size, step):
    c_west_ref, c_north_ref = coeffs
    mid = load(ref, start, size)
    north, south = load(ref, start - 1, size), load(ref, start + 1, size)
    c_west, c_north = load(c_west_ref, start, size), load(c_north_ref, start, size)
    return mid, beside(mid, north, south, c_west, c_north, load(c_north_ref, start + 1, size), step)


def pool_rows(ref, start, size, step):
    out = []
    for t in range(ref.shape[0]):
        even = ref[t, pl.ds(GUARD + start, size // 2, stride=2), :]
        odd = ref[t, pl.ds(GUARD + start + 1, size // 2, stride=2), :]
        both = even + odd
        out.append(both + roll(both, -step))
    return out


def descend(level, height, weight, source, guess, state, diagonal_ref, field, resid, next_weight, next_source, largest, part):
    step = 2**level
    c_west_ref, c_north_ref, scale_ref, smooth_ref = state
    for ref in (weight, field, c_north_ref):
        clear_guards(ref, height)

    def first_pass(start, size):
        w, w_north, w_south = (load(weight, start + k, size) for k in (0, -1, 1))
        c_north = [jnp.minimum(a, b) for a, b in zip(w, w_north)]
        c_south = [jnp.minimum(a, b) for a, b in zip(w, w_south)]
        c_west = [jnp.minimum(a, b) for a, b in zip(w, from_west(w, step))]
        c_east = from_east(c_west, step)
        diagonal = [damping + c_north[t] + c_south[t] + c_west[t] + c_east[t] for t in range(len(w))]
        scale = [relaxation / d for d in diagonal]
        store(c_north_ref, start, size, c_north)
        store(c_west_ref, start, size, c_west)
        store(scale_ref, start, size, scale)
        store(diagonal_ref, start, size, diagonal)
        value = load(source, start, size)
        if guess is None:
            value = [scale[t] * value[t] for t in range(len(w))]
        else:
            mid, north, south = (load(guess, start + k, size) for k in (0, -1, 1))
            around = beside(mid, north, south, c_west, c_north, c_south, step)
            value = [
                (1.0 - relaxation) * mid[t] + scale[t] * (value[t] + around[t]) for t in range(len(w))
            ]
        store(field, start, size, value)
        if next_weight is not None:
            pooled = [0.125 * p for p in pool_rows(weight, start, size, step)]
            store(next_weight, start // 2, size // 2, pooled)

    def second_pass(start, size):
        mid, around = beside_of(field, (c_west_ref, c_north_ref), start, size, step)
        b, scale, diagonal = (load(ref, start, size) for ref in (source, scale_ref, diagonal_ref))
        rest = [(b[t] + around[t]) - diagonal[t] * mid[t] for t in range(len(b))]
        store(smooth_ref, start, size, [mid[t] + scale[t] * rest[t] for t in range(len(b))])
        store(resid, start, size, rest)
        if next_source is not None:
            pooled = [0.25 * p for p in pool_rows(resid, start, size, step)]
            store(next_source, start // 2, size // 2, pooled)

    for_chunks(height, first_pass, largest, part)
    for_chunks(height, second_pass, largest, part)


def descend_all(rows, sources, guess, weights, states, diagonal, field, resid, largest, part):
    for level in range(LEVELS - 1):
        descend(
            level,
            rows >> level,
            weights[level],
            sources[level],
            guess if level == 0 else None,
            states[4 * level : 4 * level + 4],
            diagonal[level],
            field,
            resid,
            weights[level + 1],
            sources[level + 1],
            largest,
            part,
        )


def group_of(x, west):
    return (lane_of(x) // HALO + (1 if west else 0)) % PIECES


def packed(part, p, west):
    return roll(part, p * HALO - HALO if west else p * HALO + HALO)


def to_sides(west, east, cross_ref, pair_ref, k, rows):
    even = lax.axis_index("gy") % 2 == 0
    cross_ref[k, rows, :] = jnp.where(even, west, east)
    pair_ref[k, rows, :] = jnp.where(even, east, west)


def layout_kernel(source, guess, weight, own_source, own_guess, own_weight, cross_ref, pair_ref, *inner):
    rows = source.shape[0]
    piece = cross_ref.shape[1]
    whole = rows // piece
    tail = rows - whole * piece
    for own, block in zip((own_source, own_guess, own_weight), (source, guess, weight)):
        clear_rim(own)
        for t in range(2):
            own[t, GUARD + TOP : GUARD + TOP + rows, :] = block[:, t * LANES : (t + 1) * LANES]
    weights, start, height = (own_weight, *inner), TOP, rows
    for level in range(LEVELS):
        pooled = [0.125 * w for w in pool_rows(weights[level], start, height, 2**level)]
        start, height = start // 2, height // 2
        if level < LEVELS - 1:
            store(weights[level + 1], start, height, pooled)
    lane = lane_of(pooled[0])
    width = HALO // 2
    index = (lane % width) * 2**LEVELS
    coarse = [jnp.take_along_axis(p, index, axis=1) for p in pooled]
    coarse = jnp.where(lane % HALO < width, *coarse)
    for k, block in enumerate((source, guess, weight)):
        sides = []
        for west in (True, False):
            columns = slice(0, LANES) if west else slice(LANES, 2 * LANES)
            below = jnp.zeros((piece - tail, LANES), jnp.float32)
            if k < 2:
                below = jnp.concatenate((below[: 2 * EDGE], coarse[k * height // 2 : (k + 1) * height // 2]), axis=0)
            last = packed(block[whole * piece :, columns], whole, west)
            both = jnp.concatenate((last, below), axis=0)
            for p in range(whole):
                part = packed(block[p * piece : (p + 1) * piece, columns], p, west)
                both = jnp.where(group_of(part, west) == p, part, both)
            sides.append(both)
        to_sides(*sides, cross_ref, pair_ref, k, slice(0, piece))


def halo_kernel(*refs):
    first_rows, second_rows, *own, cross_ref, pair_ref = refs[5:]
    total = own[0].shape[1] - 2 * GUARD
    last = PIECES - 1
    first = total - 2 * TOP - last * cross_ref.shape[1]
    even, even_y = lax.axis_index("gx") % 2 == 0, lax.axis_index("gy") % 2 == 0
    for k in range(3):
        above = jnp.where(even, first_rows[k], second_rows[k])
        below = jnp.where(even, second_rows[k], first_rows[k])
        for side, (rows, row) in enumerate(((above, TOP - EDGE), (below, total - TOP))):
            body = [rows[:, t * LANES : (t + 1) * LANES] for t in range(2)]
            for t in range(2):
                own[k][t, GUARD + row : GUARD + row + EDGE, :] = body[t]
            span = slice(first + side * EDGE, first + (side + 1) * EDGE)
            parts = []
            for part, west in zip(body, (True, False)):
                here = group_of(part, west) == last
                parts.append((here, packed(part, last, west)))
            (here_west, west), (here_east, east) = parts
            cross, pair = cross_ref[k, span, :], pair_ref[k, span, :]
            cross_ref[k, span, :] = jnp.where(
                even_y, jnp.where(here_west, west, cross), jnp.where(here_east, east, cross)
            )
            pair_ref[k, span, :] = jnp.where(
                even_y, jnp.where(here_east, east, pair), jnp.where(here_west, west, pair)
            )


def body_kernel(source, guess, weight, *refs):
    states = refs[: 4 * (LEVELS - 1)]
    last_weight, last_source, first_diagonal, *refs = refs[4 * (LEVELS - 1) :]
    frames, (field, resid, weight_in, *inner) = refs[:3], refs[3:]
    rows = source.shape[1] - 2 * GUARD
    depth = LEVELS - 2
    weights = (weight_in, *inner[:depth], last_weight)
    sources = (source, *inner[depth : 2 * depth], last_source)
    diagonal = (first_diagonal, *inner[2 * depth :])
    weights[0][...] = weight[...]
    descend_all(rows, sources, guess, weights, states, diagonal, field, resid, 144, 144)
    for own, frame in zip((source, guess, weight), frames):
        tiles = [own[t] for t in range(2)]
        frame[0] = jnp.where(lane_of(tiles[0]) < LANES // 2, roll(tiles[0], HALO), roll(tiles[1], -HALO))


def frame_kernel(_a, _b, _c, from_pair, from_cross, body_weight, body_source, *refs):
    even = lax.axis_index("gy") % 2 == 0
    frames, states, refs = refs[:3], refs[3 : 3 + 4 * (LEVELS - 1)], refs[3 + 4 * (LEVELS - 1) :]
    frame_source, frame_guess, frame_weight = frames
    first_diagonal, ring_state, dense_ref, chunks_ref, field, resid, *refs = refs[0], refs[1:5], *refs[5:]
    ring_weight, ring_source, ring_field, ring_resid, ring_diagonal, *inner = refs
    rows = frame_source.shape[1] - 2 * GUARD
    depth = LEVELS - 1
    weights = (frame_weight, *inner[:depth])
    sources = (frame_source, *inner[depth : 2 * depth])
    diagonals = (first_diagonal, *inner[2 * depth :])
    piece = from_cross.shape[1]
    for k, frame in enumerate(frames):
        block = rows - 2 * TOP
        last = PIECES - 1
        tail = block - last * piece
        spans = [(p, 0, TOP + p * piece, piece) for p in range(last)]
        spans += [(last, 0, TOP + last * piece, tail)]
        spans += [(last, tail, TOP - EDGE, EDGE), (last, tail + EDGE, rows - TOP, EDGE)]
        for p, first, start, size in spans:
            span = slice(GUARD + start, GUARD + start + size)
            cross, pair = from_cross[k, first : first + size, :], from_pair[k, first : first + size, :]
            from_left = group_of(cross, False) == p
            both = roll(jnp.where(from_left == even, cross, pair), -p * HALO)
            lane = lane_of(both)
            outside = (lane < HALO) | (lane >= LANES - HALO)
            frame[0, span, :] = jnp.where(outside, both, frame[0, span, :])
    descend_all(rows, sources, frame_guess, weights, states, diagonals, field, resid, 288, 288)

    level = LEVELS - 1
    step, halo, height = 2**level, TOP >> level, rows >> level
    for body, frame, ring in (
        (body_weight, weights[level], ring_weight),
        (body_source, sources[level], ring_source),
    ):
        middle = load(body, 0, height)
        around = load(frame, 0, height)[0]
        lane = lane_of(around)
        ahead, back = roll(around, HALO), roll(around, -HALO)
        store(
            ring,
            0,
            height,
            [
                jnp.where(lane < 2 * step, back, middle[0]),
                jnp.where(lane >= LANES - 2 * step, ahead, middle[1]),
                jnp.where(lane < LANES // 2, ahead, back),
            ],
        )
    descend(
        level,
        height,
        ring_weight,
        ring_source,
        None,
        ring_state,
        ring_diagonal,
        ring_field,
        ring_resid,
        None,
        None,
        height,
        height,
    )

    coarse_rows = (height - 2 * halo) // 2
    dense = jnp.zeros((8, LANES), jnp.float32)
    lane = lane_of(dense)
    per_tile = LANES // 2**LEVELS
    pooled_b = pool_rows(ring_resid, halo, 2 * coarse_rows, step)
    pooled_w = pool_rows(ring_weight, halo, 2 * coarse_rows, step)
    index = (lane % per_tile) * 2**LEVELS
    place = lane // per_tile
    for g in range(coarse_rows // 8):
        for group, (values, factor) in enumerate(((pooled_b, 0.25), (pooled_w, 0.125))):
            for t in range(2):
                taken = jnp.take_along_axis(factor * values[t][8 * g : 8 * g + 8], index, axis=1)
                dense = jnp.where(place == 4 * g + 2 * group + t, taken, dense)
    dense_ref[...] = dense

    width = 2 * per_tile
    index = jnp.minimum(2 * (lane - lane % width) + lane % width, LANES - 1)
    smooth = ring_state[3]
    beside_me = []
    for tile, edge, free in ((0, 0, width - 3), (1, LANES - step, 0)):
        chunk = jnp.take_along_axis(dense, index, axis=1)
        first = GUARD + halo
        pieces = []
        for g in range(coarse_rows // 8):
            for odd in range(2):
                rows_of = smooth[tile, pl.ds(first + 16 * g + odd, 8, stride=2), :]
                pieces.append((g * width + free + odd, rows_of))
        top = lax.broadcasted_iota(jnp.int32, dense.shape, 0) == 0
        for g, row in ((0, first - 1), (1, first + 2 * coarse_rows)):
            pieces.append((g * width + free + 2, jnp.where(top, smooth[tile, row : row + 8, :], 0.0)))
        for place, values in pieces:
            chunk = jnp.where(lane == place, roll(values, place - edge), chunk)
        beside_me.append(fold(chunk))
    above, below = fold(dense), fold(roll(dense, -LANES // 2))
    x, y = lax.axis_index("gx"), lax.axis_index("gy")
    for i in range(chunks_ref.shape[0]):
        for j in range(chunks_ref.shape[1]):
            level_with = jnp.where(j < y, beside_me[0], beside_me[1])
            chunks_ref[i, j] = jnp.where(i == x, level_with, jnp.where(i < x, above, below))


def fold(x):
    return jnp.where(lane_of(x) < LANES // 2, x, pltpu.roll(roll(x, LANES // 2), 4, 0))[:4]


def unfold(x):
    return jnp.concatenate((x, roll(x, LANES // 2)), axis=0)


def coarse_solve(all_ref, dense_ref, from_cross, from_pair, e_ref, edge_ref, width, groups):
    x, nx = lax.axis_index("gx"), lax.axis_size("gx")
    y, ny = lax.axis_index("gy"), lax.axis_size("gy")
    tiles = {}
    for dx in (-1, 0, 1):
        for dy in (-1, 0, 1):
            if dx or dy:
                inside = (x + dx >= 0) & (x + dx < nx) & (y + dy >= 0) & (y + dy < ny)
                tile = unfold(all_ref[jnp.where(inside, x + dx, 0), jnp.where(inside, y + dy, 0)])
                tiles[dx, dy] = jnp.where(inside, tile, 0.0)
    dense = dense_ref[...]
    lane = lane_of(dense)
    even = y % 2 == 0
    half = 4 * groups
    first = from_cross.shape[1] - half
    cross, pair = ([ref[k, first:, :] for k in range(2)] for ref in (from_cross, from_pair))
    cross, pair = jnp.concatenate(cross, axis=0), jnp.concatenate(pair, axis=0)
    weights = {-1: jnp.where(even, cross, pair), 1: jnp.where(even, pair, cross)}
    bands = [(-1, g) for g in range(TALL // 8)] + [(0, g) for g in range(groups)] + [(1, g) for g in range(TALL // 8)]
    b, w = [], []
    for dx, g in bands:
        b_rows = w_rows = jnp.zeros_like(dense)
        for dy in (-1, 0, 1):
            first_lane = (dy + 1) * width
            here = (lane >= first_lane) & (lane < first_lane + width)
            if dx or not dy:
                tile = tiles[dx, dy] if dx else dense
                b_part = roll(tile, first_lane - 2 * g * width)
                w_part = roll(tile, first_lane - (2 * g + 1) * width)
            else:
                b_part = roll(tiles[dx, dy], first_lane - g * width)
                at = (PIECES - 1 - (dy > 0)) * HALO
                w_part = roll(weights[dy][8 * g : 8 * g + 8], first_lane - at)
            b_rows = jnp.where(here, b_part, b_rows)
            w_rows = jnp.where(here, w_part, w_rows)
        b.append(b_rows)
        w.append(w_rows)
    b, w = jnp.concatenate(b, axis=0), jnp.concatenate(w, axis=0)

    step = 2 ** (LEVELS - 1)
    start = GUARD + (TOP >> (LEVELS - 1))
    zeros = jnp.zeros((GUARD, LANES), jnp.float32)
    for row in range(0, edge_ref.shape[1], GUARD):
        edge_ref[0, row : row + GUARD, :] = zeros
    before, after = tiles[0, -1], tiles[0, 1]

    def columns(place):
        left, right = roll(before, LANES - step - place), roll(after, -(place + width - 3))
        return jnp.where(lane < step, right, left)

    for g in range(groups):
        for odd in range(2):
            edge_ref[0, pl.ds(start + 16 * g + odd, 8, stride=2), :] = columns(g * width + odd)
    edge_ref[0, start - 1 : start, :] = columns(2)[:1]
    edge_ref[0, start + 16 * groups : start + 16 * groups + 1, :] = columns(width + 2)[:1]

    rows = b.shape[0]
    zeros = jnp.zeros((GUARD, LANES), jnp.float32)
    e_ref[0:GUARD, :] = zeros
    e_ref[GUARD + rows :, :] = zeros

    def shifted(by):
        return e_ref[GUARD + by : GUARD + by + rows, :]

    e_ref[GUARD : GUARD + rows, :] = w
    c_west = jnp.minimum(w, roll(w, 1))
    c_north, c_south = jnp.minimum(w, shifted(-1)), jnp.minimum(w, shifted(1))
    c_east = roll(c_west, -1)
    scale = relaxation / (damping + c_north + c_south + c_west + c_east)
    first = scale * b
    c_west, c_east, c_north, c_south = (scale * c for c in (c_west, c_east, c_north, c_south))
    e_ref[GUARD : GUARD + rows, :] = first

    def sweep(_, carry):
        e = shifted(0)
        around = (c_west * roll(e, 1) + c_east * roll(e, -1)) + (c_north * shifted(-1) + c_south * shifted(1))
        e_ref[GUARD : GUARD + rows, :] = ((1.0 - relaxation) * e + first) + around
        return carry

    lax.fori_loop(0, SWEEPS - 1, sweep, 0)
    return shifted(0)


def up_kernel(all_ref, dense_ref, from_cross, from_pair, own_source, frame_source, own_diagonal, frame_diagonal, *refs):
    count = 4 * (LEVELS - 1)
    body_state, frame_state, ring_state = refs[:count], refs[count : 2 * count], refs[2 * count : 2 * count + 4]
    out_ref, resid_ref = refs[2 * count + 4 : 2 * count + 6]
    ring_pe, body_final, frame_final, sems, e_ref, edge_ref, *inner = refs[2 * count + 6 :]
    outs, inner = inner[:2], inner[2:]
    body_pe, frame_pe = inner[: LEVELS - 1], inner[LEVELS - 1 :]
    rows = out_ref.shape[0] + 2 * TOP
    width = out_ref.shape[1] >> LEVELS
    e = coarse_solve(all_ref, dense_ref, from_cross, from_pair, e_ref, edge_ref, width, (out_ref.shape[0] >> LEVELS) // 8)

    level = LEVELS - 1
    step, halo, height = 2**level, TOP >> level, rows >> level
    coarse_rows = (height - 2 * halo) // 2
    picked = e[TALL - 8 : TALL + coarse_rows + 8]
    lane = lane_of(picked)
    for t in range(3):
        group = (lane + t * LANES) // 2**LEVELS
        if t == 2:
            group = jnp.where(lane < LANES // 2, group, group - 3 * LANES // 2**LEVELS)
        taken = jnp.take_along_axis(picked, jnp.clip(group + width, 0, LANES - 1), axis=1)[7 : 7 + coarse_rows + 2]
        ring_pe[t, 0 : 2 * GUARD, :] = jnp.zeros((2 * GUARD, LANES), jnp.float32)
        ring_pe[t, height : height + 2 * GUARD, :] = jnp.zeros((2 * GUARD, LANES), jnp.float32)
        ring_pe[t, pl.ds(GUARD + halo - 2, coarse_rows + 2, stride=2), :] = taken
        ring_pe[t, pl.ds(GUARD + halo - 1, coarse_rows + 2, stride=2), :] = taken

    def climbed(pe, state, start, size, step, edge=None):
        mid, around = beside_of(pe, state[:2], start, size, step)
        scale, smooth = load(state[2], start, size), load(state[3], start, size)
        if edge is not None:
            smooth = smooth[:2] + load(edge, start, size)
        return [(smooth[t] + (1.0 - relaxation) * mid[t]) + scale[t] * around[t] for t in range(len(mid))]

    def climb_ring(start, size, level=level, step=step):
        ring = spread(climbed(ring_pe, ring_state, start, size, step, edge_ref), step // 2)
        lane = lane_of(ring[0])
        around = jnp.where(
            lane < LANES // 2,
            jnp.where(lane < HALO, roll(ring[2], HALO), roll(ring[0], HALO)),
            jnp.where(lane < LANES - HALO, roll(ring[1], -HALO), roll(ring[2], -HALO)),
        )
        store_twice(body_pe[level - 1], start, size, ring[:2])
        store_twice(frame_pe[level - 1], start, size, [around])

    for_chunks(height, climb_ring, height, 16)

    for level in range(LEVELS - 2, -1, -1):
        step, height = 2**level, rows >> level
        groups = ((body_pe, body_state, body_final), (frame_pe, frame_state, frame_final))
        for pes, _, _ in groups:
            clear_guards(pes[level], height)

        def climb(start, size, level=level, step=step, groups=groups):
            for pes, states, final in groups:
                value = climbed(pes[level], states[4 * level : 4 * level + 4], start, size, step)
                if level == 0:
                    store(final, start, size, value)
                else:
                    store_twice(pes[level - 1], start, size, spread(value, step // 2))

        if level > 0:
            for_chunks(height, climb, CHUNK, CHUNK // 2)

    def last(base, size):
        body, around = beside_of(body_final, body_state[:2], base, size, 1)
        frame, frame_around = beside_of(frame_final, frame_state[:2], base, size, 1)
        b, d = load(own_source, base, size), load(own_diagonal, base, size)
        b_frame, d_frame = load(frame_source, base, size), load(frame_diagonal, base, size)
        body = (body, [(b[t] + around[t]) - d[t] * body[t] for t in range(2)])
        frame = (frame[0], (b_frame[0] + frame_around[0]) - d_frame[0] * frame[0])
        lane = lane_of(frame[0])
        span = pl.ds(base, size)
        for ref, middle, around in ((outs[0], body[0], frame[0]), (outs[1], body[1], frame[1])):
            ref[span, :LANES] = jnp.where(lane < NEAR, roll(around, -HALO), middle[0])
            ref[span, LANES:] = jnp.where(lane >= LANES - NEAR, roll(around, HALO), middle[1])

    count = rows // CHUNK
    ends = [0] + [CHUNK * (p + 1) - LAG - TOP for p in range(count - 1)] + [out_ref.shape[0]]

    def copies(p):
        size = ends[p + 1] - ends[p]
        return [
            pltpu.make_async_copy(
                outs[k].at[pl.ds(TOP + ends[p], size)], ref.at[pl.ds(ends[p], size)], sems.at[2 * p + k]
            )
            for k, ref in enumerate((out_ref, resid_ref))
        ]

    def finish(i, carry):
        for_parts(i * CHUNK, CHUNK, climb, CHUNK // 2)
        base = pl.multiple_of(jnp.maximum(i * CHUNK - LAG, 0), 8)
        for_parts(base, CHUNK, last, CHUNK // 2)
        for p in range(count):

            @pl.when(i == p)
            def _(p=p):
                for copy in copies(p):
                    copy.start()

        return carry

    lax.fori_loop(0, count, finish, 0)
    for p in range(count):
        for copy in copies(p):
            copy.wait()


def call(kernel, out_shape, scratch, flops, moved, **more):
    return pl.pallas_call(
        kernel,
        out_shape=out_shape,
        scratch_shapes=scratch,
        compiler_params=pltpu.CompilerParams(vmem_limit_bytes=VMEM_LIMIT),
        cost_estimate=pl.CostEstimate(flops=flops, bytes_accessed=moved, transcendentals=0),
        **more,
    )


def swap(x, axis, first):
    pairs = [(i, i + 1) for i in range(first, lax.axis_size(axis) - 1, 2)]
    return lax.ppermute(x, axis, pairs + [(j, i) for i, j in pairs])


def local(rhs, pressure, wet_mask, bathy_class):
    rows, columns = rhs.shape
    cells = rows * columns
    total = rows + 2 * TOP
    levels = range(LEVELS - 1)

    def shape(tiles, level):
        return (tiles, (total >> level) + 2 * GUARD, LANES)

    def out(*dims):
        return jax.ShapeDtypeStruct(dims, jnp.float32)

    def vmem(tiles, level):
        return pltpu.VMEM(shape(tiles, level), jnp.float32)

    def fields(r, p, m, c):
        wet = m.astype(jnp.float32)
        return wet * r, wet * p, wet * (1.0 + 0.5 * c.astype(jnp.float32))

    given = (rhs, pressure, wet_mask, bathy_class)

    def edge(start):
        return jnp.stack(fields(*(lax.dynamic_slice_in_dim(x, start, EDGE, axis=0) for x in given)))

    even = lax.axis_index("gx") % 2 == 0
    first_rows = swap(edge(jnp.where(even, 0, rows - EDGE)), "gx", 1)
    second_rows = swap(edge(jnp.where(even, rows - EDGE, 0)), "gx", 0)
    piece = (rows + 2 * EDGE + (rows >> LEVELS) // 2) // PIECES
    own_shapes = [out(*shape(2, 0))] * 3
    laid_out = [*own_shapes, out(3, piece, LANES), out(3, piece, LANES)]
    inner = [vmem(2, level) for level in range(1, LEVELS)]
    begun = call(layout_kernel, laid_out, inner, 10 * cells, 10 * cells)(*fields(*given))
    *own, to_cross, to_pair = call(
        halo_kernel, laid_out, (), cells, cells, input_output_aliases={k: k for k in range(5)}
    )(*begun, first_rows, second_rows)
    from_pair = swap(to_pair, "gy", 0)
    from_cross = swap(to_cross, "gy", 1)

    state_count = 4 * (LEVELS - 1)
    *body_state, body_weight, body_source, diagonal, frame_source, frame_guess, frame_weight = call(
        body_kernel,
        [out(*shape(2, level)) for level in levels for _ in range(4)]
        + [out(*shape(2, LEVELS - 1))] * 2
        + [out(*shape(2, 0))]
        + [out(*shape(1, 0))] * 3,
        [vmem(2, 0)] * 3 + [vmem(2, level) for level in levels[1:]] * 3,
        100 * cells,
        40 * cells,
    )(*own)
    nx, ny = lax.axis_size("gx"), lax.axis_size("gy")
    ring = LEVELS - 1
    frame_source, _, _, *state, dense, chunks = call(
        frame_kernel,
        [out(*shape(1, 0))] * 3
        + [out(*shape(1, level)) for level in levels for _ in range(4)]
        + [out(*shape(1, 0))]
        + [out(*shape(3, ring))] * 4
        + [out(8, LANES), out(nx, ny, 4, LANES)],
        [vmem(1, 0)] * 2 + [vmem(3, ring)] * 5 + [vmem(1, level) for level in range(1, LEVELS)] * 3,
        50 * cells,
        20 * cells,
        input_output_aliases={k: k for k in range(3)},
    )(frame_source, frame_guess, frame_weight, from_pair, from_cross, body_weight, body_source)
    frame_state, frame_diagonal, ring_state = state[:state_count], state[state_count], state[state_count + 1 :]
    gathered = lax.all_to_all(chunks.reshape(nx * ny, 4, LANES), ("gx", "gy"), 0, 0).reshape(chunks.shape)
    return call(
        up_kernel,
        (out(rows, columns), out(rows, columns)),
        [vmem(3, ring), vmem(2, 0), vmem(1, 0), pltpu.SemaphoreType.DMA((8,))]
        + [pltpu.VMEM(((rows >> LEVELS) + 2 * TALL + 2 * GUARD, LANES), jnp.float32), vmem(1, ring)]
        + [pltpu.VMEM((total, columns), jnp.float32)] * 2
        + [vmem(2, level) for level in levels]
        + [vmem(1, level) for level in levels],
        60 * cells,
        40 * cells,
        out_specs=[pl.BlockSpec(memory_space=pl.ANY)] * 2,
    )(gathered, dense, from_cross, from_pair, own[0], frame_source, diagonal, frame_diagonal, *body_state, *frame_state, *ring_state)


def solution(mesh):
    placed = (P("gx", "gy"), P("gx", "gy"), P("gx", "gy"), P("gx", "gy"))
    return jax.shard_map(
        local, mesh=mesh, in_specs=placed, out_specs=(P("gx", "gy"), P("gx", "gy")), check_vma=False
    )
```

```python
import jax
import jax.numpy as jnp
from jax import lax
from jax.experimental import pallas as pl
from jax.experimental.pallas import tpu as pltpu
from jax.sharding import PartitionSpec as P

LEVELS = 4
SWEEPS = 12

damping = 0.01
relaxation = 0.8

HALO = 16
NEAR = 20
LANES = 128
INNER = LANES // 2 - HALO
TOP = 16
GUARD = 8
PIECES = 8
CHUNK = 136
PART = 72
LAG = 8
TALL = 16
VMEM_LIMIT = 40 * 1024 * 1024


def lane_of(x):
    return lax.broadcasted_iota(jnp.int32, x.shape, x.ndim - 1)


def roll(x, amount):
    amount %= LANES
    return x if amount == 0 else pltpu.roll(x, amount, x.ndim - 1)


def from_west(tiles, step):
    moved = [roll(t, step) for t in tiles]
    if len(tiles) == 1:
        return moved
    edge = lane_of(tiles[0]) < step
    return [jnp.where(edge, moved[i - 1], moved[i]) for i in range(len(tiles))]


def from_east(tiles, step):
    moved = [roll(t, -step) for t in tiles]
    count = len(tiles)
    if count == 1:
        return moved
    edge = lane_of(tiles[0]) >= LANES - step
    return [jnp.where(edge, moved[(i + 1) % count], moved[i]) for i in range(count)]


def spread(tiles, step):
    second = (lane_of(tiles[0]) // step) % 2 == 1
    return [jnp.where(second, roll(t, step), t) for t in tiles]


def for_parts(start, size, body, part):
    for offset in range(0, size, part):
        body(start + offset, min(part, size - offset))


def for_chunks(rows, body, largest, part):
    sizes = [size for size in range(8, largest + 1, 8) if rows % size == 0]
    if rows <= largest or not sizes:
        for_parts(0, rows, body, part)
        return

    def step(i, carry):
        for_parts(i * sizes[-1], sizes[-1], body, part)
        return carry

    lax.fori_loop(0, rows // sizes[-1], step, 0)


def load(ref, start, size):
    return [ref[t, pl.ds(GUARD + start, size), :] for t in range(ref.shape[0])]


def store(ref, start, size, tiles):
    for t, tile in enumerate(tiles):
        ref[t, pl.ds(GUARD + start, size), :] = tile


def store_twice(ref, start, size, tiles):
    for t, tile in enumerate(tiles):
        ref[t, pl.ds(GUARD + 2 * start, size, stride=2), :] = tile
        ref[t, pl.ds(GUARD + 2 * start + 1, size, stride=2), :] = tile


def clear_guards(ref, rows):
    zeros = jnp.zeros((GUARD, LANES), jnp.float32)
    for t in range(ref.shape[0]):
        ref[t, 0:GUARD, :] = zeros
        ref[t, GUARD + rows : 2 * GUARD + rows, :] = zeros


def beside(mid, north, south, c_west, c_north, c_south, step):
    west = from_west(mid, step)
    east = from_east([c * m for c, m in zip(c_west, mid)], step)
    return [
        (c_west[t] * west[t] + east[t]) + (c_north[t] * north[t] + c_south[t] * south[t]) for t in range(len(mid))
    ]


def beside_of(ref, coeffs, start, size, step):
    c_west_ref, c_north_ref = coeffs
    mid = load(ref, start, size)
    north, south = load(ref, start - 1, size), load(ref, start + 1, size)
    c_west, c_north = load(c_west_ref, start, size), load(c_north_ref, start, size)
    return mid, beside(mid, north, south, c_west, c_north, load(c_north_ref, start + 1, size), step)


def pool_rows(ref, start, size, step):
    out = []
    for t in range(ref.shape[0]):
        even = ref[t, pl.ds(GUARD + start, size // 2, stride=2), :]
        odd = ref[t, pl.ds(GUARD + start + 1, size // 2, stride=2), :]
        both = even + odd
        out.append(both + roll(both, -step))
    return out


def descend(level, height, weight, source, guess, state, diagonal_ref, field, resid, next_weight, next_source, largest, part):
    step = 2**level
    c_west_ref, c_north_ref, scale_ref, smooth_ref = state
    for ref in (weight, field, c_north_ref):
        clear_guards(ref, height)

    def first_pass(start, size):
        w, w_north, w_south = (load(weight, start + k, size) for k in (0, -1, 1))
        c_north = [jnp.minimum(a, b) for a, b in zip(w, w_north)]
        c_south = [jnp.minimum(a, b) for a, b in zip(w, w_south)]
        c_west = [jnp.minimum(a, b) for a, b in zip(w, from_west(w, step))]
        c_east = from_east(c_west, step)
        diagonal = [damping + c_north[t] + c_south[t] + c_west[t] + c_east[t] for t in range(len(w))]
        scale = [relaxation / d for d in diagonal]
        store(c_north_ref, start, size, c_north)
        store(c_west_ref, start, size, c_west)
        store(scale_ref, start, size, scale)
        store(diagonal_ref, start, size, diagonal)
        value = load(source, start, size)
        if guess is None:
            value = [scale[t] * value[t] for t in range(len(w))]
        else:
            mid, north, south = (load(guess, start + k, size) for k in (0, -1, 1))
            around = beside(mid, north, south, c_west, c_north, c_south, step)
            value = [
                (1.0 - relaxation) * mid[t] + scale[t] * (value[t] + around[t]) for t in range(len(w))
            ]
        store(field, start, size, value)
        if next_weight is not None:
            pooled = [0.125 * p for p in pool_rows(weight, start, size, step)]
            store(next_weight, start // 2, size // 2, pooled)

    def second_pass(start, size):
        mid, around = beside_of(field, (c_west_ref, c_north_ref), start, size, step)
        b, scale, diagonal = (load(ref, start, size) for ref in (source, scale_ref, diagonal_ref))
        rest = [(b[t] + around[t]) - diagonal[t] * mid[t] for t in range(len(b))]
        store(smooth_ref, start, size, [mid[t] + scale[t] * rest[t] for t in range(len(b))])
        store(resid, start, size, rest)
        if next_source is not None:
            pooled = [0.25 * p for p in pool_rows(resid, start, size, step)]
            store(next_source, start // 2, size // 2, pooled)

    for_chunks(height, first_pass, largest, part)
    for_chunks(height, second_pass, largest, part)


def descend_all(rows, sources, guess, weights, states, diagonal, field, resid, largest, part):
    for level in range(LEVELS - 1):
        descend(
            level,
            rows >> level,
            weights[level],
            sources[level],
            guess if level == 0 else None,
            states[4 * level : 4 * level + 4],
            diagonal[level],
            field,
            resid,
            weights[level + 1],
            sources[level + 1],
            largest,
            part,
        )


def group_of(x, west):
    return (lane_of(x) // HALO + (1 if west else 0)) % PIECES


def packed(part, p, west):
    return roll(part, p * HALO - HALO if west else p * HALO + HALO)


def to_sides(west, east, cross_ref, pair_ref, k, rows):
    even = lax.axis_index("gy") % 2 == 0
    cross_ref[k, rows, :] = jnp.where(even, west, east)
    pair_ref[k, rows, :] = jnp.where(even, east, west)


def layout_kernel(source, guess, weight, own_source, own_guess, own_weight, cross_ref, pair_ref, *inner):
    rows = source.shape[0]
    piece = cross_ref.shape[1]
    whole = rows // piece
    tail = rows - whole * piece
    for own, block in zip((own_source, own_guess, own_weight), (source, guess, weight)):
        clear_guards(own, rows + 2 * TOP)
        for t in range(2):
            own[t, GUARD + TOP : GUARD + TOP + rows, :] = block[:, t * LANES : (t + 1) * LANES]
    weights, start, height = (own_weight, *inner), TOP, rows
    for level in range(LEVELS):
        pooled = [0.125 * w for w in pool_rows(weights[level], start, height, 2**level)]
        start, height = start // 2, height // 2
        if level < LEVELS - 1:
            store(weights[level + 1], start, height, pooled)
    lane = lane_of(pooled[0])
    width = HALO // 2
    index = (lane % width) * 2**LEVELS
    coarse = [jnp.take_along_axis(p, index, axis=1) for p in pooled]
    coarse = jnp.where(lane % HALO < width, *coarse)
    for k, block in enumerate((source, guess, weight)):
        sides = []
        for west in (True, False):
            columns = slice(0, LANES) if west else slice(LANES, 2 * LANES)
            below = jnp.zeros((piece - tail, LANES), jnp.float32)
            if k < 2:
                half = coarse[k * height // 2 : (k + 1) * height // 2]
                below = jnp.concatenate((below[: 2 * TOP], half, below[2 * TOP + height // 2 :]), axis=0)
            last = packed(block[whole * piece :, columns], whole, west)
            both = jnp.concatenate((last, below), axis=0)
            for p in range(whole):
                part = packed(block[p * piece : (p + 1) * piece, columns], p, west)
                both = jnp.where(group_of(part, west) == p, part, both)
            sides.append(both)
        to_sides(*sides, cross_ref, pair_ref, k, slice(0, piece))


def halo_kernel(*refs):
    first_rows, second_rows, *own, cross_ref, pair_ref = refs[5:]
    total = own[0].shape[1] - 2 * GUARD
    last = PIECES - 1
    first = total - 2 * TOP - last * cross_ref.shape[1]
    even, even_y = lax.axis_index("gx") % 2 == 0, lax.axis_index("gy") % 2 == 0
    for k in range(3):
        above = jnp.where(even, first_rows[k], second_rows[k])
        below = jnp.where(even, second_rows[k], first_rows[k])
        for side, (rows, row) in enumerate(((above, 0), (below, total - TOP))):
            body = [rows[:, t * LANES : (t + 1) * LANES] for t in range(2)]
            for t in range(2):
                own[k][t, GUARD + row : GUARD + row + TOP, :] = body[t]
            span = slice(first + side * TOP, first + (side + 1) * TOP)
            parts = []
            for part, west in zip(body, (True, False)):
                here = group_of(part, west) == last
                parts.append((here, packed(part, last, west)))
            (here_west, west), (here_east, east) = parts
            cross, pair = cross_ref[k, span, :], pair_ref[k, span, :]
            cross_ref[k, span, :] = jnp.where(
                even_y, jnp.where(here_west, west, cross), jnp.where(here_east, east, cross)
            )
            pair_ref[k, span, :] = jnp.where(
                even_y, jnp.where(here_east, east, pair), jnp.where(here_west, west, pair)
            )


def body_kernel(source, guess, weight, *refs):
    states = refs[: 4 * (LEVELS - 1)]
    last_weight, last_source, first_diagonal, *refs = refs[4 * (LEVELS - 1) :]
    frames, (field, resid, weight_in, *inner) = refs[:3], refs[3:]
    rows = source.shape[1] - 2 * GUARD
    depth = LEVELS - 2
    weights = (weight_in, *inner[:depth], last_weight)
    sources = (source, *inner[depth : 2 * depth], last_source)
    diagonal = (first_diagonal, *inner[2 * depth :])
    weights[0][...] = weight[...]
    descend_all(rows, sources, guess, weights, states, diagonal, field, resid, CHUNK, CHUNK)
    for own, frame in zip((source, guess, weight), frames):
        tiles = [own[t] for t in range(2)]
        frame[0] = jnp.where(lane_of(tiles[0]) < LANES // 2, roll(tiles[0], HALO), roll(tiles[1], -HALO))


def frame_kernel(_a, _b, _c, from_pair, from_cross, body_weight, body_source, *refs):
    even = lax.axis_index("gy") % 2 == 0
    frames, states, refs = refs[:3], refs[3 : 3 + 4 * (LEVELS - 1)], refs[3 + 4 * (LEVELS - 1) :]
    frame_source, frame_guess, frame_weight = frames
    first_diagonal, ring_state, dense_ref, chunks_ref, field, resid, *refs = refs[0], refs[1:5], *refs[5:]
    ring_weight, ring_source, ring_field, ring_resid, ring_diagonal, *inner = refs
    rows = frame_source.shape[1] - 2 * GUARD
    depth = LEVELS - 1
    weights = (frame_weight, *inner[:depth])
    sources = (frame_source, *inner[depth : 2 * depth])
    diagonals = (first_diagonal, *inner[2 * depth :])
    piece = from_cross.shape[1]
    for k, frame in enumerate(frames):
        block = rows - 2 * TOP
        last = PIECES - 1
        tail = block - last * piece
        spans = [(p, 0, TOP + p * piece, piece) for p in range(last)]
        spans += [(last, 0, TOP + last * piece, tail)]
        spans += [(last, tail, 0, TOP), (last, tail + TOP, rows - TOP, TOP)]
        for p, first, start, size in spans:
            span = slice(GUARD + start, GUARD + start + size)
            cross, pair = from_cross[k, first : first + size, :], from_pair[k, first : first + size, :]
            from_left = group_of(cross, False) == p
            both = roll(jnp.where(from_left == even, cross, pair), -p * HALO)
            lane = lane_of(both)
            outside = (lane < HALO) | (lane >= LANES - HALO)
            frame[0, span, :] = jnp.where(outside, both, frame[0, span, :])
    descend_all(rows, sources, frame_guess, weights, states, diagonals, field, resid, 2 * CHUNK, 2 * CHUNK)

    level = LEVELS - 1
    step, halo, height = 2**level, TOP >> level, rows >> level
    for body, frame, ring in (
        (body_weight, weights[level], ring_weight),
        (body_source, sources[level], ring_source),
    ):
        middle = load(body, 0, height)
        around = load(frame, 0, height)[0]
        lane = lane_of(around)
        ahead, back = roll(around, HALO), roll(around, -HALO)
        store(
            ring,
            0,
            height,
            [
                jnp.where(lane < 2 * step, back, middle[0]),
                jnp.where(lane >= LANES - 2 * step, ahead, middle[1]),
                jnp.where(lane < LANES // 2, ahead, back),
            ],
        )
    descend(
        level,
        height,
        ring_weight,
        ring_source,
        None,
        ring_state,
        ring_diagonal,
        ring_field,
        ring_resid,
        None,
        None,
        height,
        height,
    )

    coarse_rows = (height - 2 * halo) // 2
    dense = jnp.zeros((8, LANES), jnp.float32)
    lane = lane_of(dense)
    per_tile = LANES // 2**LEVELS
    pooled_b = pool_rows(ring_resid, halo, 2 * coarse_rows, step)
    pooled_w = pool_rows(ring_weight, halo, 2 * coarse_rows, step)
    index = (lane % per_tile) * 2**LEVELS
    place = lane // per_tile
    for g in range(coarse_rows // 8):
        for group, (values, factor) in enumerate(((pooled_b, 0.25), (pooled_w, 0.125))):
            for t in range(2):
                taken = jnp.take_along_axis(factor * values[t][8 * g : 8 * g + 8], index, axis=1)
                dense = jnp.where(place == 4 * g + 2 * group + t, taken, dense)
    dense_ref[...] = dense

    width = 2 * per_tile
    index = jnp.minimum(2 * (lane - lane % width) + lane % width, LANES - 1)
    smooth = ring_state[3]
    beside_me = []
    for tile, edge, free in ((0, 0, width - 2), (1, LANES - step, 0)):
        chunk = jnp.take_along_axis(dense, index, axis=1)
        first = GUARD + halo
        pieces = []
        for g in range(coarse_rows // 8):
            for odd in range(2):
                rows_of = smooth[tile, pl.ds(first + 16 * g + odd, 8, stride=2), :]
                pieces.append((g * width + free + odd, rows_of))
        for place, values in pieces:
            chunk = jnp.where(lane == place, roll(values, place - edge), chunk)
        beside_me.append(fold(chunk))
    sublane = lax.broadcasted_iota(jnp.int32, dense.shape, 0)
    beyond = []
    for row, group, free in ((0, 1, 6), (2 * coarse_rows - 1, 2, 0)):
        chunk = dense
        for tile in range(2):
            values = jnp.broadcast_to(smooth[tile, GUARD + halo + row : GUARD + halo + row + 1, :], dense.shape)
            values = jnp.take_along_axis(values, (lane % width) * step, axis=1)
            here = (sublane == free + tile) & (lane // width == 2 * group)
            chunk = jnp.where(here, values, chunk)
        beyond.append(chunk)
    above, below = fold(beyond[0]), fold(roll(beyond[1], -LANES // 2))
    x, y = lax.axis_index("gx"), lax.axis_index("gy")
    for i in range(chunks_ref.shape[0]):
        for j in range(chunks_ref.shape[1]):
            level_with = jnp.where(j < y, beside_me[0], beside_me[1])
            chunks_ref[i, j] = jnp.where(i == x, level_with, jnp.where(i < x, above, below))


def fold(x):
    return jnp.where(lane_of(x) < LANES // 2, x, pltpu.roll(roll(x, LANES // 2), 4, 0))[:4]


def unfold(x):
    return jnp.concatenate((x, roll(x, LANES // 2)), axis=0)


def coarse_solve(all_ref, dense_ref, from_cross, from_pair, e_ref, edge_ref, smooth_ref, rows, width, groups):
    x, nx = lax.axis_index("gx"), lax.axis_size("gx")
    y, ny = lax.axis_index("gy"), lax.axis_size("gy")
    tiles = {}
    for dx in (-1, 0, 1):
        for dy in (-1, 0, 1):
            if dx or dy:
                inside = (x + dx >= 0) & (x + dx < nx) & (y + dy >= 0) & (y + dy < ny)
                tile = unfold(all_ref[jnp.where(inside, x + dx, 0), jnp.where(inside, y + dy, 0)])
                tiles[dx, dy] = jnp.where(inside, tile, 0.0)
    dense = dense_ref[...]
    lane = lane_of(dense)
    even = y % 2 == 0
    half = 4 * groups
    first = rows % from_cross.shape[1] + 2 * TOP
    cross, pair = ([ref[k, first : first + half, :] for k in range(2)] for ref in (from_cross, from_pair))
    cross, pair = jnp.concatenate(cross, axis=0), jnp.concatenate(pair, axis=0)
    weights = {-1: jnp.where(even, cross, pair), 1: jnp.where(even, pair, cross)}
    bands = [(-1, g) for g in range(TALL // 8)] + [(0, g) for g in range(groups)] + [(1, g) for g in range(TALL // 8)]
    b, w = [], []
    for dx, g in bands:
        b_rows = w_rows = jnp.zeros_like(dense)
        for dy in (-1, 0, 1):
            first_lane = (dy + 1) * width
            here = (lane >= first_lane) & (lane < first_lane + width)
            if dx or not dy:
                tile = tiles[dx, dy] if dx else dense
                b_part = roll(tile, first_lane - 2 * g * width)
                w_part = roll(tile, first_lane - (2 * g + 1) * width)
            else:
                b_part = roll(tiles[dx, dy], first_lane - g * width)
                at = (PIECES - 1 - (dy > 0)) * HALO
                w_part = roll(weights[dy][8 * g : 8 * g + 8], first_lane - at)
            b_rows = jnp.where(here, b_part, b_rows)
            w_rows = jnp.where(here, w_part, w_rows)
        b.append(b_rows)
        w.append(w_rows)
    b, w = jnp.concatenate(b, axis=0), jnp.concatenate(w, axis=0)

    step = 2 ** (LEVELS - 1)
    start = GUARD + (TOP >> (LEVELS - 1))
    for t in range(2):
        edge_ref[t] = smooth_ref[t]
    edge_ref[2] = jnp.zeros_like(edge_ref[2])

    def columns(place):
        left = roll(tiles[0, -1], LANES - step - place)
        right = roll(tiles[0, 1], -(place + width - 2))
        return jnp.where(lane < step, right, left)

    for g in range(groups):
        for odd in range(2):
            edge_ref[2, pl.ds(start + 16 * g + odd, 8, stride=2), :] = columns(g * width + odd)
    for dx, row, lanes, free in ((-1, start - 1, 0, 0), (1, start + 16 * groups, 2 * width, 6)):
        for t in range(2):
            values = tiles[dx, 0][free + t : free + t + 1]
            values = jnp.take_along_axis(
                jnp.broadcast_to(values, dense.shape), lanes + lane // step, axis=1
            )
            edge_ref[t, row : row + 1, :] = values[:1]
        left = roll(tiles[dx, -1][free + 1 : free + 2], LANES - step - (lanes + width - 1))
        right = roll(tiles[dx, 1][free : free + 1], -lanes)
        edge_ref[2, row : row + 1, :] = jnp.where(lane[:1] < step, right, left)

    tall = b.shape[0]
    zeros = jnp.zeros((GUARD, LANES), jnp.float32)
    e_ref[0:GUARD, :] = zeros
    e_ref[GUARD + tall :, :] = zeros

    def shifted(by):
        return e_ref[GUARD + by : GUARD + by + tall, :]

    e_ref[GUARD : GUARD + tall, :] = w
    c_west = jnp.minimum(w, roll(w, 1))
    c_north, c_south = jnp.minimum(w, shifted(-1)), jnp.minimum(w, shifted(1))
    c_east = roll(c_west, -1)
    scale = relaxation / (damping + c_north + c_south + c_west + c_east)
    first = scale * b
    c_west, c_east, c_north, c_south = (scale * c for c in (c_west, c_east, c_north, c_south))
    e_ref[GUARD : GUARD + tall, :] = first

    def sweep(_, carry):
        e = shifted(0)
        around = (c_west * roll(e, 1) + c_east * roll(e, -1)) + (c_north * shifted(-1) + c_south * shifted(1))
        e_ref[GUARD : GUARD + tall, :] = ((1.0 - relaxation) * e + first) + around
        return carry

    lax.fori_loop(0, SWEEPS - 1, sweep, 0)
    return shifted(0)


def up_kernel(all_ref, dense_ref, from_cross, from_pair, own_source, frame_source, own_diagonal, frame_diagonal, *refs):
    count = 4 * (LEVELS - 1)
    body_state, frame_state, ring_state = refs[:count], refs[count : 2 * count], refs[2 * count : 2 * count + 4]
    out_ref, resid_ref = refs[2 * count + 4 : 2 * count + 6]
    ring_pe, body_final, frame_final, sems, e_ref, edge_ref, *inner = refs[2 * count + 6 :]
    outs, inner = inner[:2], inner[2:]
    body_pe, frame_pe = inner[: LEVELS - 1], inner[LEVELS - 1 :]
    rows = out_ref.shape[0] + 2 * TOP
    width = out_ref.shape[1] >> LEVELS
    e = coarse_solve(all_ref, dense_ref, from_cross, from_pair, e_ref, edge_ref, ring_state[3], out_ref.shape[0], width, (out_ref.shape[0] >> LEVELS) // 8)

    level = LEVELS - 1
    step, halo, height = 2**level, TOP >> level, rows >> level
    coarse_rows = (height - 2 * halo) // 2
    picked = e[TALL - 8 : TALL + coarse_rows + 8]
    lane = lane_of(picked)
    for t in range(3):
        group = (lane + t * LANES) // 2**LEVELS
        if t == 2:
            group = jnp.where(lane < LANES // 2, group, group - 3 * LANES // 2**LEVELS)
        taken = jnp.take_along_axis(picked, jnp.clip(group + width, 0, LANES - 1), axis=1)[7 : 7 + coarse_rows + 2]
        ring_pe[t, 0 : 2 * GUARD, :] = jnp.zeros((2 * GUARD, LANES), jnp.float32)
        ring_pe[t, height : height + 2 * GUARD, :] = jnp.zeros((2 * GUARD, LANES), jnp.float32)
        ring_pe[t, pl.ds(GUARD + halo - 2, coarse_rows + 2, stride=2), :] = taken
        ring_pe[t, pl.ds(GUARD + halo - 1, coarse_rows + 2, stride=2), :] = taken

    def climbed(pe, state, start, size, step, edge=None):
        mid, around = beside_of(pe, state[:2], start, size, step)
        scale, smooth = load(state[2], start, size), load(state[3], start, size)
        if edge is not None:
            smooth = load(edge, start, size)
        return [(smooth[t] + (1.0 - relaxation) * mid[t]) + scale[t] * around[t] for t in range(len(mid))]

    def climb_ring(start, size, level=level, step=step):
        ring = spread(climbed(ring_pe, ring_state, start, size, step, edge_ref), step // 2)
        lane = lane_of(ring[0])
        around = jnp.where(
            lane < LANES // 2,
            jnp.where(lane < HALO, roll(ring[2], HALO), roll(ring[0], HALO)),
            jnp.where(lane < LANES - HALO, roll(ring[1], -HALO), roll(ring[2], -HALO)),
        )
        store_twice(body_pe[level - 1], start, size, ring[:2])
        store_twice(frame_pe[level - 1], start, size, [around])

    for_chunks(height, climb_ring, height, 16)

    for level in range(LEVELS - 2, -1, -1):
        step, height = 2**level, rows >> level
        groups = ((body_pe, body_state, body_final), (frame_pe, frame_state, frame_final))
        for pes, _, _ in groups:
            clear_guards(pes[level], height)

        def climb(start, size, level=level, step=step, groups=groups):
            for pes, states, final in groups:
                value = climbed(pes[level], states[4 * level : 4 * level + 4], start, size, step)
                if level == 0:
                    store(final, start, size, value)
                else:
                    store_twice(pes[level - 1], start, size, spread(value, step // 2))

        if level > 0:
            for_chunks(height, climb, CHUNK, PART)

    def last(base, size):
        body, around = beside_of(body_final, body_state[:2], base, size, 1)
        frame, frame_around = beside_of(frame_final, frame_state[:2], base, size, 1)
        b, d = load(own_source, base, size), load(own_diagonal, base, size)
        b_frame, d_frame = load(frame_source, base, size), load(frame_diagonal, base, size)
        body = (body, [(b[t] + around[t]) - d[t] * body[t] for t in range(2)])
        frame = (frame[0], (b_frame[0] + frame_around[0]) - d_frame[0] * frame[0])
        lane = lane_of(frame[0])
        span = pl.ds(base, size)
        for ref, middle, around in ((outs[0], body[0], frame[0]), (outs[1], body[1], frame[1])):
            ref[span, :LANES] = jnp.where(lane < NEAR, roll(around, -HALO), middle[0])
            ref[span, LANES:] = jnp.where(lane >= LANES - NEAR, roll(around, HALO), middle[1])

    count = rows // CHUNK
    ends = [0] + [CHUNK * (p + 1) - LAG - TOP for p in range(count - 1)] + [out_ref.shape[0]]

    def copies(p):
        size = ends[p + 1] - ends[p]
        return [
            pltpu.make_async_copy(
                outs[k].at[pl.ds(TOP + ends[p], size)], ref.at[pl.ds(ends[p], size)], sems.at[2 * p + k]
            )
            for k, ref in enumerate((out_ref, resid_ref))
        ]

    def finish(i, carry):
        for_parts(i * CHUNK, CHUNK, climb, PART)
        base = pl.multiple_of(jnp.maximum(i * CHUNK - LAG, 0), 8)
        for_parts(base, CHUNK, last, PART)
        for p in range(count):

            @pl.when(i == p)
            def _(p=p):
                for copy in copies(p):
                    copy.start()

        return carry

    lax.fori_loop(0, count, finish, 0)
    for p in range(count):
        for copy in copies(p):
            copy.wait()


def call(kernel, out_shape, scratch, flops, moved, **more):
    return pl.pallas_call(
        kernel,
        out_shape=out_shape,
        scratch_shapes=scratch,
        compiler_params=pltpu.CompilerParams(vmem_limit_bytes=VMEM_LIMIT),
        cost_estimate=pl.CostEstimate(flops=flops, bytes_accessed=moved, transcendentals=0),
        **more,
    )


def swap(x, axis, first):
    pairs = [(i, i + 1) for i in range(first, lax.axis_size(axis) - 1, 2)]
    return lax.ppermute(x, axis, pairs + [(j, i) for i, j in pairs])


def local(rhs, pressure, wet_mask, bathy_class):
    rows, columns = rhs.shape
    cells = rows * columns
    total = rows + 2 * TOP
    levels = range(LEVELS - 1)

    def shape(tiles, level):
        return (tiles, (total >> level) + 2 * GUARD, LANES)

    def out(*dims):
        return jax.ShapeDtypeStruct(dims, jnp.float32)

    def vmem(tiles, level):
        return pltpu.VMEM(shape(tiles, level), jnp.float32)

    def fields(r, p, m, c):
        wet = m.astype(jnp.float32)
        return wet * r, wet * p, wet * (1.0 + 0.5 * c.astype(jnp.float32))

    given = (rhs, pressure, wet_mask, bathy_class)

    def edge(start):
        return jnp.stack(fields(*(lax.dynamic_slice_in_dim(x, start, TOP, axis=0) for x in given)))

    even = lax.axis_index("gx") % 2 == 0
    first_rows = swap(edge(jnp.where(even, 0, rows - TOP)), "gx", 1)
    second_rows = swap(edge(jnp.where(even, rows - TOP, 0)), "gx", 0)
    piece = -(-(rows + 2 * TOP + (rows >> LEVELS) // 2) // (8 * PIECES)) * 8
    own_shapes = [out(*shape(2, 0))] * 3
    laid_out = [*own_shapes, out(3, piece, LANES), out(3, piece, LANES)]
    inner = [vmem(2, level) for level in range(1, LEVELS)]
    begun = call(layout_kernel, laid_out, inner, 10 * cells, 10 * cells)(*fields(*given))
    *own, to_cross, to_pair = call(
        halo_kernel, laid_out, (), cells, cells, input_output_aliases={k: k for k in range(5)}
    )(*begun, first_rows, second_rows)
    from_pair = swap(to_pair, "gy", 0)
    from_cross = swap(to_cross, "gy", 1)

    state_count = 4 * (LEVELS - 1)
    *body_state, body_weight, body_source, diagonal, frame_source, frame_guess, frame_weight = call(
        body_kernel,
        [out(*shape(2, level)) for level in levels for _ in range(4)]
        + [out(*shape(2, LEVELS - 1))] * 2
        + [out(*shape(2, 0))]
        + [out(*shape(1, 0))] * 3,
        [vmem(2, 0)] * 3 + [vmem(2, level) for level in levels[1:]] * 3,
        100 * cells,
        40 * cells,
    )(*own)
    nx, ny = lax.axis_size("gx"), lax.axis_size("gy")
    ring = LEVELS - 1
    frame_source, _, _, *state, dense, chunks = call(
        frame_kernel,
        [out(*shape(1, 0))] * 3
        + [out(*shape(1, level)) for level in levels for _ in range(4)]
        + [out(*shape(1, 0))]
        + [out(*shape(3, ring))] * 4
        + [out(8, LANES), out(nx, ny, 4, LANES)],
        [vmem(1, 0)] * 2 + [vmem(3, ring)] * 5 + [vmem(1, level) for level in range(1, LEVELS)] * 3,
        50 * cells,
        20 * cells,
        input_output_aliases={k: k for k in range(3)},
    )(frame_source, frame_guess, frame_weight, from_pair, from_cross, body_weight, body_source)
    frame_state, frame_diagonal, ring_state = state[:state_count], state[state_count], state[state_count + 1 :]
    gathered = lax.all_to_all(chunks.reshape(nx * ny, 4, LANES), ("gx", "gy"), 0, 0).reshape(chunks.shape)
    return call(
        up_kernel,
        (out(rows, columns), out(rows, columns)),
        [vmem(3, ring), vmem(2, 0), vmem(1, 0), pltpu.SemaphoreType.DMA((8,))]
        + [pltpu.VMEM(((rows >> LEVELS) + 2 * TALL + 2 * GUARD, LANES), jnp.float32), vmem(3, ring)]
        + [pltpu.VMEM((total, columns), jnp.float32)] * 2
        + [vmem(2, level) for level in levels]
        + [vmem(1, level) for level in levels],
        60 * cells,
        40 * cells,
        out_specs=[pl.BlockSpec(memory_space=pl.ANY)] * 2,
    )(gathered, dense, from_cross, from_pair, own[0], frame_source, diagonal, frame_diagonal, *body_state, *frame_state, *ring_state)


def solution(mesh):
    placed = (P("gx", "gy"), P("gx", "gy"), P("gx", "gy"), P("gx", "gy"))
    return jax.shard_map(
        local, mesh=mesh, in_specs=placed, out_specs=(P("gx", "gy"), P("gx", "gy")), check_vma=False
    )
```

```python
import jax
import jax.numpy as jnp
from jax import lax
from jax.experimental import pallas as pl
from jax.experimental.pallas import tpu as pltpu
from jax.sharding import PartitionSpec as P

LEVELS = 4
SWEEPS = 12

damping = 0.01
relaxation = 0.8

HALO = 16
NEAR = 20
LANES = 128
INNER = LANES // 2 - HALO
TOP = 16
GUARD = 8
PIECES = 8
CHUNK = 136
PART = CHUNK
LAG = 8
TALL = 16
VMEM_LIMIT = 40 * 1024 * 1024


def lane_of(x):
    return lax.broadcasted_iota(jnp.int32, x.shape, x.ndim - 1)


def roll(x, amount):
    amount %= LANES
    return x if amount == 0 else pltpu.roll(x, amount, x.ndim - 1)


def from_west(tiles, step):
    moved = [roll(t, step) for t in tiles]
    if len(tiles) == 1:
        return moved
    edge = lane_of(tiles[0]) < step
    return [jnp.where(edge, moved[i - 1], moved[i]) for i in range(len(tiles))]


def from_east(tiles, step):
    moved = [roll(t, -step) for t in tiles]
    count = len(tiles)
    if count == 1:
        return moved
    edge = lane_of(tiles[0]) >= LANES - step
    return [jnp.where(edge, moved[(i + 1) % count], moved[i]) for i in range(count)]


def spread(tiles, step):
    second = (lane_of(tiles[0]) // step) % 2 == 1
    return [jnp.where(second, roll(t, step), t) for t in tiles]


def for_parts(start, size, body, part):
    for offset in range(0, size, part):
        body(start + offset, min(part, size - offset))


def for_chunks(rows, body, largest, part):
    sizes = [size for size in range(8, largest + 1, 8) if rows % size == 0]
    if rows <= largest or not sizes:
        for_parts(0, rows, body, part)
        return

    def step(i, carry):
        for_parts(i * sizes[-1], sizes[-1], body, part)
        return carry

    lax.fori_loop(0, rows // sizes[-1], step, 0)


def load(ref, start, size):
    return [ref[t, pl.ds(GUARD + start, size), :] for t in range(ref.shape[0])]


def store(ref, start, size, tiles):
    for t, tile in enumerate(tiles):
        ref[t, pl.ds(GUARD + start, size), :] = tile


def store_twice(ref, start, size, tiles):
    for t, tile in enumerate(tiles):
        ref[t, pl.ds(GUARD + 2 * start, size, stride=2), :] = tile
        ref[t, pl.ds(GUARD + 2 * start + 1, size, stride=2), :] = tile


def clear_guards(ref, rows):
    zeros = jnp.zeros((GUARD, LANES), jnp.float32)
    for t in range(ref.shape[0]):
        ref[t, 0:GUARD, :] = zeros
        ref[t, GUARD + rows : 2 * GUARD + rows, :] = zeros


def beside(mid, north, south, c_west, c_north, c_south, step):
    west = from_west(mid, step)
    east = from_east([c * m for c, m in zip(c_west, mid)], step)
    return [
        (c_west[t] * west[t] + east[t]) + (c_north[t] * north[t] + c_south[t] * south[t]) for t in range(len(mid))
    ]


def beside_of(ref, coeffs, start, size, step):
    c_west_ref, c_north_ref = coeffs
    mid = load(ref, start, size)
    north, south = load(ref, start - 1, size), load(ref, start + 1, size)
    c_west, c_north = load(c_west_ref, start, size), load(c_north_ref, start, size)
    return mid, beside(mid, north, south, c_west, c_north, load(c_north_ref, start + 1, size), step)


def pool_rows(ref, start, size, step):
    out = []
    for t in range(ref.shape[0]):
        even = ref[t, pl.ds(GUARD + start, size // 2, stride=2), :]
        odd = ref[t, pl.ds(GUARD + start + 1, size // 2, stride=2), :]
        both = even + odd
        out.append(both + roll(both, -step))
    return out


def descend(level, height, weight, source, guess, state, diagonal_ref, field, resid, next_weight, next_source, largest, part):
    step = 2**level
    c_west_ref, c_north_ref, scale_ref, smooth_ref = state
    for ref in (weight, field, c_north_ref):
        clear_guards(ref, height)

    def first_pass(start, size):
        w, w_north, w_south = (load(weight, start + k, size) for k in (0, -1, 1))
        c_north = [jnp.minimum(a, b) for a, b in zip(w, w_north)]
        c_south = [jnp.minimum(a, b) for a, b in zip(w, w_south)]
        c_west = [jnp.minimum(a, b) for a, b in zip(w, from_west(w, step))]
        c_east = from_east(c_west, step)
        diagonal = [damping + c_north[t] + c_south[t] + c_west[t] + c_east[t] for t in range(len(w))]
        scale = [relaxation / d for d in diagonal]
        store(c_north_ref, start, size, c_north)
        store(c_west_ref, start, size, c_west)
        store(scale_ref, start, size, scale)
        store(diagonal_ref, start, size, diagonal)
        value = load(source, start, size)
        if guess is None:
            value = [scale[t] * value[t] for t in range(len(w))]
        else:
            mid, north, south = (load(guess, start + k, size) for k in (0, -1, 1))
            around = beside(mid, north, south, c_west, c_north, c_south, step)
            value = [
                (1.0 - relaxation) * mid[t] + scale[t] * (value[t] + around[t]) for t in range(len(w))
            ]
        store(field, start, size, value)
        if next_weight is not None:
            pooled = [0.125 * p for p in pool_rows(weight, start, size, step)]
            store(next_weight, start // 2, size // 2, pooled)

    def second_pass(start, size):
        mid, around = beside_of(field, (c_west_ref, c_north_ref), start, size, step)
        b, scale, diagonal = (load(ref, start, size) for ref in (source, scale_ref, diagonal_ref))
        rest = [(b[t] + around[t]) - diagonal[t] * mid[t] for t in range(len(b))]
        store(smooth_ref, start, size, [mid[t] + scale[t] * rest[t] for t in range(len(b))])
        store(resid, start, size, rest)
        if next_source is not None:
            pooled = [0.25 * p for p in pool_rows(resid, start, size, step)]
            store(next_source, start // 2, size // 2, pooled)

    for_chunks(height, first_pass, largest, part)
    for_chunks(height, second_pass, largest, part)


def descend_all(rows, sources, guess, weights, states, diagonal, field, resid, largest, part):
    for level in range(LEVELS - 1):
        descend(
            level,
            rows >> level,
            weights[level],
            sources[level],
            guess if level == 0 else None,
            states[4 * level : 4 * level + 4],
            diagonal[level],
            field,
            resid,
            weights[level + 1],
            sources[level + 1],
            largest,
            part,
        )


def group_of(x, west):
    return (lane_of(x) // HALO + (1 if west else 0)) % PIECES


def packed(part, p, west):
    return roll(part, p * HALO - HALO if west else p * HALO + HALO)


def to_sides(west, east, cross_ref, pair_ref, k, rows):
    even = lax.axis_index("gy") % 2 == 0
    cross_ref[k, rows, :] = jnp.where(even, west, east)
    pair_ref[k, rows, :] = jnp.where(even, east, west)


def inner_columns(tiles):
    return jnp.where(lane_of(tiles[0]) < LANES // 2, roll(tiles[0], HALO), roll(tiles[1], -HALO))


def layout_kernel(source, guess, weight, *refs):
    owns, frames, (cross_ref, pair_ref, *inner) = refs[:3], refs[3:6], refs[6:]
    rows = source.shape[0]
    piece = cross_ref.shape[1]
    whole = rows // piece
    tail = rows - whole * piece
    for own, frame, block in zip(owns, frames, (source, guess, weight)):
        clear_guards(own, rows + 2 * TOP)
        clear_guards(frame, rows + 2 * TOP)
        tiles = [block[:, t * LANES : (t + 1) * LANES] for t in range(2)]
        for t in range(2):
            own[t, GUARD + TOP : GUARD + TOP + rows, :] = tiles[t]
        frame[0, GUARD + TOP : GUARD + TOP + rows, :] = inner_columns(tiles)
    weights, start, height = (owns[2], *inner), TOP, rows
    for level in range(LEVELS):
        pooled = [0.125 * w for w in pool_rows(weights[level], start, height, 2**level)]
        start, height = start // 2, height // 2
        if level < LEVELS - 1:
            store(weights[level + 1], start, height, pooled)
    lane = lane_of(pooled[0])
    width = HALO // 2
    index = (lane % width) * 2**LEVELS
    coarse = [jnp.take_along_axis(p, index, axis=1) for p in pooled]
    coarse = jnp.where(lane % HALO < width, *coarse)
    for k, block in enumerate((source, guess, weight)):
        sides = []
        for west in (True, False):
            columns = slice(0, LANES) if west else slice(LANES, 2 * LANES)
            below = jnp.zeros((piece - tail, LANES), jnp.float32)
            if k < 2:
                half = coarse[k * height // 2 : (k + 1) * height // 2]
                below = jnp.concatenate((below[: 2 * TOP], half, below[2 * TOP + height // 2 :]), axis=0)
            last = packed(block[whole * piece :, columns], whole, west)
            both = jnp.concatenate((last, below), axis=0)
            for p in range(whole):
                part = packed(block[p * piece : (p + 1) * piece, columns], p, west)
                both = jnp.where(group_of(part, west) == p, part, both)
            sides.append(both)
        to_sides(*sides, cross_ref, pair_ref, k, slice(0, piece))


def halo_kernel(*refs):
    first_rows, second_rows, *own, cross_ref, pair_ref = refs[8:]
    own, frames = own[:3], own[3:]
    total = own[0].shape[1] - 2 * GUARD
    last = PIECES - 1
    first = total - 2 * TOP - last * cross_ref.shape[1]
    even, even_y = lax.axis_index("gx") % 2 == 0, lax.axis_index("gy") % 2 == 0
    for k in range(3):
        above = jnp.where(even, first_rows[k], second_rows[k])
        below = jnp.where(even, second_rows[k], first_rows[k])
        for side, (rows, row) in enumerate(((above, 0), (below, total - TOP))):
            body = [rows[:, t * LANES : (t + 1) * LANES] for t in range(2)]
            for t in range(2):
                own[k][t, GUARD + row : GUARD + row + TOP, :] = body[t]
            frames[k][0, GUARD + row : GUARD + row + TOP, :] = inner_columns(body)
            span = slice(first + side * TOP, first + (side + 1) * TOP)
            parts = []
            for part, west in zip(body, (True, False)):
                here = group_of(part, west) == last
                parts.append((here, packed(part, last, west)))
            (here_west, west), (here_east, east) = parts
            cross, pair = cross_ref[k, span, :], pair_ref[k, span, :]
            cross_ref[k, span, :] = jnp.where(
                even_y, jnp.where(here_west, west, cross), jnp.where(here_east, east, cross)
            )
            pair_ref[k, span, :] = jnp.where(
                even_y, jnp.where(here_east, east, pair), jnp.where(here_west, west, pair)
            )


def body_kernel(source, guess, weight, *refs):
    states = refs[: 4 * (LEVELS - 1)]
    last_weight, last_source, first_diagonal, *refs = refs[4 * (LEVELS - 1) :]
    field, resid, weight_in, *inner = refs
    rows = source.shape[1] - 2 * GUARD
    depth = LEVELS - 2
    weights = (weight_in, *inner[:depth], last_weight)
    sources = (source, *inner[depth : 2 * depth], last_source)
    diagonal = (first_diagonal, *inner[2 * depth :])
    weights[0][...] = weight[...]
    descend_all(rows, sources, guess, weights, states, diagonal, field, resid, CHUNK, CHUNK)


def frame_kernel(_a, _b, _c, from_pair, from_cross, body_weight, body_source, *refs):
    even = lax.axis_index("gy") % 2 == 0
    frames, states, refs = refs[:3], refs[3 : 3 + 4 * (LEVELS - 1)], refs[3 + 4 * (LEVELS - 1) :]
    frame_source, frame_guess, frame_weight = frames
    first_diagonal, ring_state, dense_ref, chunks_ref, field, resid, *refs = refs[0], refs[1:5], *refs[5:]
    ring_weight, ring_source, ring_field, ring_resid, ring_diagonal, *inner = refs
    rows = frame_source.shape[1] - 2 * GUARD
    depth = LEVELS - 1
    weights = (frame_weight, *inner[:depth])
    sources = (frame_source, *inner[depth : 2 * depth])
    diagonals = (first_diagonal, *inner[2 * depth :])
    piece = from_cross.shape[1]
    for k, frame in enumerate(frames):
        block = rows - 2 * TOP
        last = PIECES - 1
        tail = block - last * piece
        spans = [(p, 0, TOP + p * piece, piece) for p in range(last)]
        spans += [(last, 0, TOP + last * piece, tail)]
        spans += [(last, tail, 0, TOP), (last, tail + TOP, rows - TOP, TOP)]
        for p, first, start, size in spans:
            span = slice(GUARD + start, GUARD + start + size)
            cross, pair = from_cross[k, first : first + size, :], from_pair[k, first : first + size, :]
            from_left = group_of(cross, False) == p
            both = roll(jnp.where(from_left == even, cross, pair), -p * HALO)
            lane = lane_of(both)
            outside = (lane < HALO) | (lane >= LANES - HALO)
            frame[0, span, :] = jnp.where(outside, both, frame[0, span, :])
    descend_all(rows, sources, frame_guess, weights, states, diagonals, field, resid, 2 * CHUNK, 2 * CHUNK)

    level = LEVELS - 1
    step, halo, height = 2**level, TOP >> level, rows >> level
    for body, frame, ring in (
        (body_weight, weights[level], ring_weight),
        (body_source, sources[level], ring_source),
    ):
        middle = load(body, 0, height)
        around = load(frame, 0, height)[0]
        lane = lane_of(around)
        ahead, back = roll(around, HALO), roll(around, -HALO)
        store(
            ring,
            0,
            height,
            [
                jnp.where(lane < 2 * step, back, middle[0]),
                jnp.where(lane >= LANES - 2 * step, ahead, middle[1]),
                jnp.where(lane < LANES // 2, ahead, back),
            ],
        )
    descend(
        level,
        height,
        ring_weight,
        ring_source,
        None,
        ring_state,
        ring_diagonal,
        ring_field,
        ring_resid,
        None,
        None,
        height,
        height,
    )

    coarse_rows = (height - 2 * halo) // 2
    dense = jnp.zeros((8, LANES), jnp.float32)
    lane = lane_of(dense)
    per_tile = LANES // 2**LEVELS
    pooled_b = pool_rows(ring_resid, halo, 2 * coarse_rows, step)
    pooled_w = pool_rows(ring_weight, halo, 2 * coarse_rows, step)
    index = (lane % per_tile) * 2**LEVELS
    place = lane // per_tile
    for g in range(coarse_rows // 8):
        for group, (values, factor) in enumerate(((pooled_b, 0.25), (pooled_w, 0.125))):
            for t in range(2):
                taken = jnp.take_along_axis(factor * values[t][8 * g : 8 * g + 8], index, axis=1)
                dense = jnp.where(place == 4 * g + 2 * group + t, taken, dense)
    dense_ref[...] = dense

    width = 2 * per_tile
    index = jnp.minimum(2 * (lane - lane % width) + lane % width, LANES - 1)
    smooth = ring_state[3]
    beside_me = []
    for tile, edge, free in ((0, 0, width - 2), (1, LANES - step, 0)):
        chunk = jnp.take_along_axis(dense, index, axis=1)
        first = GUARD + halo
        pieces = []
        for g in range(coarse_rows // 8):
            for odd in range(2):
                rows_of = smooth[tile, pl.ds(first + 16 * g + odd, 8, stride=2), :]
                pieces.append((g * width + free + odd, rows_of))
        for place, values in pieces:
            chunk = jnp.where(lane == place, roll(values, place - edge), chunk)
        beside_me.append(fold(chunk))
    sublane = lax.broadcasted_iota(jnp.int32, dense.shape, 0)
    beyond = []
    for row, group, free in ((0, 1, 6), (2 * coarse_rows - 1, 2, 0)):
        chunk = dense
        for tile in range(2):
            values = jnp.broadcast_to(smooth[tile, GUARD + halo + row : GUARD + halo + row + 1, :], dense.shape)
            values = jnp.take_along_axis(values, (lane % width) * step, axis=1)
            here = (sublane == free + tile) & (lane // width == 2 * group)
            chunk = jnp.where(here, values, chunk)
        beyond.append(chunk)
    above, below = fold(beyond[0]), fold(roll(beyond[1], -LANES // 2))
    x, y = lax.axis_index("gx"), lax.axis_index("gy")
    for i in range(chunks_ref.shape[0]):
        for j in range(chunks_ref.shape[1]):
            level_with = jnp.where(j < y, beside_me[0], beside_me[1])
            chunks_ref[i, j] = jnp.where(i == x, level_with, jnp.where(i < x, above, below))


def fold(x):
    return jnp.where(lane_of(x) < LANES // 2, x, pltpu.roll(roll(x, LANES // 2), 4, 0))[:4]


def unfold(x):
    return jnp.concatenate((x, roll(x, LANES // 2)), axis=0)


def coarse_solve(all_ref, dense_ref, from_cross, from_pair, e_ref, edge_ref, smooth_ref, rows, width, groups):
    x, nx = lax.axis_index("gx"), lax.axis_size("gx")
    y, ny = lax.axis_index("gy"), lax.axis_size("gy")
    tiles = {}
    for dx in (-1, 0, 1):
        for dy in (-1, 0, 1):
            if dx or dy:
                inside = (x + dx >= 0) & (x + dx < nx) & (y + dy >= 0) & (y + dy < ny)
                tile = unfold(all_ref[jnp.where(inside, x + dx, 0), jnp.where(inside, y + dy, 0)])
                tiles[dx, dy] = jnp.where(inside, tile, 0.0)
    dense = dense_ref[...]
    lane = lane_of(dense)
    even = y % 2 == 0
    half = 4 * groups
    first = rows % from_cross.shape[1] + 2 * TOP
    cross, pair = ([ref[k, first : first + half, :] for k in range(2)] for ref in (from_cross, from_pair))
    cross, pair = jnp.concatenate(cross, axis=0), jnp.concatenate(pair, axis=0)
    weights = {-1: jnp.where(even, cross, pair), 1: jnp.where(even, pair, cross)}
    bands = [(-1, g) for g in range(TALL // 8)] + [(0, g) for g in range(groups)] + [(1, g) for g in range(TALL // 8)]
    b, w = [], []
    for dx, g in bands:
        b_rows = w_rows = jnp.zeros_like(dense)
        for dy in (-1, 0, 1):
            first_lane = (dy + 1) * width
            here = (lane >= first_lane) & (lane < first_lane + width)
            if dx or not dy:
                tile = tiles[dx, dy] if dx else dense
                b_part = roll(tile, first_lane - 2 * g * width)
                w_part = roll(tile, first_lane - (2 * g + 1) * width)
            else:
                b_part = roll(tiles[dx, dy], first_lane - g * width)
                at = (PIECES - 1 - (dy > 0)) * HALO
                w_part = roll(weights[dy][8 * g : 8 * g + 8], first_lane - at)
            b_rows = jnp.where(here, b_part, b_rows)
            w_rows = jnp.where(here, w_part, w_rows)
        b.append(b_rows)
        w.append(w_rows)
    b, w = jnp.concatenate(b, axis=0), jnp.concatenate(w, axis=0)

    step = 2 ** (LEVELS - 1)
    start = GUARD + (TOP >> (LEVELS - 1))
    for t in range(2):
        edge_ref[t] = smooth_ref[t]
    edge_ref[2] = jnp.zeros_like(edge_ref[2])

    def columns(place):
        left = roll(tiles[0, -1], LANES - step - place)
        right = roll(tiles[0, 1], -(place + width - 2))
        return jnp.where(lane < step, right, left)

    for g in range(groups):
        for odd in range(2):
            edge_ref[2, pl.ds(start + 16 * g + odd, 8, stride=2), :] = columns(g * width + odd)
    for dx, row, lanes, free in ((-1, start - 1, 0, 0), (1, start + 16 * groups, 2 * width, 6)):
        for t in range(2):
            values = tiles[dx, 0][free + t : free + t + 1]
            values = jnp.take_along_axis(
                jnp.broadcast_to(values, dense.shape), lanes + lane // step, axis=1
            )
            edge_ref[t, row : row + 1, :] = values[:1]
        left = roll(tiles[dx, -1][free + 1 : free + 2], LANES - step - (lanes + width - 1))
        right = roll(tiles[dx, 1][free : free + 1], -lanes)
        edge_ref[2, row : row + 1, :] = jnp.where(lane[:1] < step, right, left)

    tall = b.shape[0]
    zeros = jnp.zeros((GUARD, LANES), jnp.float32)
    e_ref[0:GUARD, :] = zeros
    e_ref[GUARD + tall :, :] = zeros

    def shifted(by):
        return e_ref[GUARD + by : GUARD + by + tall, :]

    e_ref[GUARD : GUARD + tall, :] = w
    c_west = jnp.minimum(w, roll(w, 1))
    c_north, c_south = jnp.minimum(w, shifted(-1)), jnp.minimum(w, shifted(1))
    c_east = roll(c_west, -1)
    scale = relaxation / (damping + c_north + c_south + c_west + c_east)
    first = scale * b
    c_west, c_east, c_north, c_south = (scale * c for c in (c_west, c_east, c_north, c_south))
    e_ref[GUARD : GUARD + tall, :] = first

    def sweep(_, carry):
        e = shifted(0)
        around = (c_west * roll(e, 1) + c_east * roll(e, -1)) + (c_north * shifted(-1) + c_south * shifted(1))
        e_ref[GUARD : GUARD + tall, :] = ((1.0 - relaxation) * e + first) + around
        return carry

    lax.fori_loop(0, SWEEPS - 1, sweep, 0)
    return shifted(0)


def up_kernel(all_ref, dense_ref, from_cross, from_pair, own_source, frame_source, own_diagonal, frame_diagonal, *refs):
    count = 4 * (LEVELS - 1)
    body_state, frame_state, ring_state = refs[:count], refs[count : 2 * count], refs[2 * count : 2 * count + 4]
    out_ref, resid_ref = refs[2 * count + 4 : 2 * count + 6]
    ring_pe, body_final, frame_final, sems, e_ref, edge_ref, *inner = refs[2 * count + 6 :]
    outs, inner = inner[:2], inner[2:]
    body_pe, frame_pe = inner[: LEVELS - 1], inner[LEVELS - 1 :]
    rows = out_ref.shape[0] + 2 * TOP
    width = out_ref.shape[1] >> LEVELS
    e = coarse_solve(all_ref, dense_ref, from_cross, from_pair, e_ref, edge_ref, ring_state[3], out_ref.shape[0], width, (out_ref.shape[0] >> LEVELS) // 8)

    level = LEVELS - 1
    step, halo, height = 2**level, TOP >> level, rows >> level
    coarse_rows = (height - 2 * halo) // 2
    picked = e[TALL - 8 : TALL + coarse_rows + 8]
    lane = lane_of(picked)
    for t in range(3):
        group = (lane + t * LANES) // 2**LEVELS
        if t == 2:
            group = jnp.where(lane < LANES // 2, group, group - 3 * LANES // 2**LEVELS)
        taken = jnp.take_along_axis(picked, jnp.clip(group + width, 0, LANES - 1), axis=1)[7 : 7 + coarse_rows + 2]
        ring_pe[t, 0 : 2 * GUARD, :] = jnp.zeros((2 * GUARD, LANES), jnp.float32)
        ring_pe[t, height : height + 2 * GUARD, :] = jnp.zeros((2 * GUARD, LANES), jnp.float32)
        ring_pe[t, pl.ds(GUARD + halo - 2, coarse_rows + 2, stride=2), :] = taken
        ring_pe[t, pl.ds(GUARD + halo - 1, coarse_rows + 2, stride=2), :] = taken

    def climbed(pe, state, start, size, step, edge=None):
        mid, around = beside_of(pe, state[:2], start, size, step)
        scale, smooth = load(state[2], start, size), load(state[3], start, size)
        if edge is not None:
            smooth = load(edge, start, size)
        return [(smooth[t] + (1.0 - relaxation) * mid[t]) + scale[t] * around[t] for t in range(len(mid))]

    def climb_ring(start, size, level=level, step=step):
        ring = spread(climbed(ring_pe, ring_state, start, size, step, edge_ref), step // 2)
        lane = lane_of(ring[0])
        around = jnp.where(
            lane < LANES // 2,
            jnp.where(lane < HALO, roll(ring[2], HALO), roll(ring[0], HALO)),
            jnp.where(lane < LANES - HALO, roll(ring[1], -HALO), roll(ring[2], -HALO)),
        )
        store_twice(body_pe[level - 1], start, size, ring[:2])
        store_twice(frame_pe[level - 1], start, size, [around])

    for_chunks(height, climb_ring, height, height)

    for level in range(LEVELS - 2, -1, -1):
        step, height = 2**level, rows >> level
        groups = ((body_pe, body_state, body_final), (frame_pe, frame_state, frame_final))
        for pes, _, _ in groups:
            clear_guards(pes[level], height)

        def climb(start, size, level=level, step=step, groups=groups):
            for pes, states, final in groups:
                value = climbed(pes[level], states[4 * level : 4 * level + 4], start, size, step)
                if level == 0:
                    store(final, start, size, value)
                else:
                    store_twice(pes[level - 1], start, size, spread(value, step // 2))

        if level > 0:
            for_chunks(height, climb, CHUNK, PART)

    def last(base, size):
        body, around = beside_of(body_final, body_state[:2], base, size, 1)
        frame, frame_around = beside_of(frame_final, frame_state[:2], base, size, 1)
        b, d = load(own_source, base, size), load(own_diagonal, base, size)
        b_frame, d_frame = load(frame_source, base, size), load(frame_diagonal, base, size)
        body = (body, [(b[t] + around[t]) - d[t] * body[t] for t in range(2)])
        frame = (frame[0], (b_frame[0] + frame_around[0]) - d_frame[0] * frame[0])
        lane = lane_of(frame[0])
        span = pl.ds(base, size)
        for ref, middle, around in ((outs[0], body[0], frame[0]), (outs[1], body[1], frame[1])):
            ref[span, :LANES] = jnp.where(lane < NEAR, roll(around, -HALO), middle[0])
            ref[span, LANES:] = jnp.where(lane >= LANES - NEAR, roll(around, HALO), middle[1])

    count = rows // CHUNK
    ends = [0] + [CHUNK * (p + 1) - LAG - TOP for p in range(count - 1)] + [out_ref.shape[0]]

    def copies(p):
        size = ends[p + 1] - ends[p]
        return [
            pltpu.make_async_copy(
                outs[k].at[pl.ds(TOP + ends[p], size)], ref.at[pl.ds(ends[p], size)], sems.at[2 * p + k]
            )
            for k, ref in enumerate((out_ref, resid_ref))
        ]

    def finish(i, carry):
        for_parts(i * CHUNK, CHUNK, climb, PART)
        base = pl.multiple_of(jnp.maximum(i * CHUNK - LAG, 0), 8)
        for_parts(base, CHUNK, last, PART)
        for p in range(count):

            @pl.when(i == p)
            def _(p=p):
                for copy in copies(p):
                    copy.start()

        return carry

    lax.fori_loop(0, count, finish, 0)
    for p in range(count):
        for copy in copies(p):
            copy.wait()


def call(kernel, out_shape, scratch, flops, moved, **more):
    return pl.pallas_call(
        kernel,
        out_shape=out_shape,
        scratch_shapes=scratch,
        compiler_params=pltpu.CompilerParams(vmem_limit_bytes=VMEM_LIMIT),
        cost_estimate=pl.CostEstimate(flops=flops, bytes_accessed=moved, transcendentals=0),
        **more,
    )


def swap(x, axis, first):
    pairs = [(i, i + 1) for i in range(first, lax.axis_size(axis) - 1, 2)]
    return lax.ppermute(x, axis, pairs + [(j, i) for i, j in pairs])


def local(rhs, pressure, wet_mask, bathy_class):
    rows, columns = rhs.shape
    cells = rows * columns
    total = rows + 2 * TOP
    levels = range(LEVELS - 1)

    def shape(tiles, level):
        return (tiles, (total >> level) + 2 * GUARD, LANES)

    def out(*dims):
        return jax.ShapeDtypeStruct(dims, jnp.float32)

    def vmem(tiles, level):
        return pltpu.VMEM(shape(tiles, level), jnp.float32)

    def fields(r, p, m, c):
        wet = m.astype(jnp.float32)
        return wet * r, wet * p, wet * (1.0 + 0.5 * c.astype(jnp.float32))

    given = (rhs, pressure, wet_mask, bathy_class)

    def edge(start):
        return jnp.stack(fields(*(lax.dynamic_slice_in_dim(x, start, TOP, axis=0) for x in given)))

    even = lax.axis_index("gx") % 2 == 0
    first_rows = swap(edge(jnp.where(even, 0, rows - TOP)), "gx", 1)
    second_rows = swap(edge(jnp.where(even, rows - TOP, 0)), "gx", 0)
    piece = -(-(rows + 2 * TOP + (rows >> LEVELS) // 2) // (8 * PIECES)) * 8
    own_shapes = [out(*shape(2, 0))] * 3
    laid_out = [*own_shapes, *[out(*shape(1, 0))] * 3, out(3, piece, LANES), out(3, piece, LANES)]
    inner = [vmem(2, level) for level in range(1, LEVELS)]
    begun = call(layout_kernel, laid_out, inner, 10 * cells, 10 * cells)(*fields(*given))
    *own, to_cross, to_pair = call(
        halo_kernel, laid_out, (), cells, cells, input_output_aliases={k: k for k in range(8)}
    )(*begun, first_rows, second_rows)
    own, frames = own[:3], own[3:]
    from_pair = swap(to_pair, "gy", 0)
    from_cross = swap(to_cross, "gy", 1)

    state_count = 4 * (LEVELS - 1)
    *body_state, body_weight, body_source, diagonal = call(
        body_kernel,
        [out(*shape(2, level)) for level in levels for _ in range(4)]
        + [out(*shape(2, LEVELS - 1))] * 2
        + [out(*shape(2, 0))],
        [vmem(2, 0)] * 3 + [vmem(2, level) for level in levels[1:]] * 3,
        100 * cells,
        40 * cells,
    )(*own)
    nx, ny = lax.axis_size("gx"), lax.axis_size("gy")
    ring = LEVELS - 1
    frame_source, _, _, *state, dense, chunks = call(
        frame_kernel,
        [out(*shape(1, 0))] * 3
        + [out(*shape(1, level)) for level in levels for _ in range(4)]
        + [out(*shape(1, 0))]
        + [out(*shape(3, ring))] * 4
        + [out(8, LANES), out(nx, ny, 4, LANES)],
        [vmem(1, 0)] * 2 + [vmem(3, ring)] * 5 + [vmem(1, level) for level in range(1, LEVELS)] * 3,
        50 * cells,
        20 * cells,
        input_output_aliases={k: k for k in range(3)},
    )(*frames, from_pair, from_cross, body_weight, body_source)
    frame_state, frame_diagonal, ring_state = state[:state_count], state[state_count], state[state_count + 1 :]
    gathered = lax.all_to_all(chunks.reshape(nx * ny, 4, LANES), ("gx", "gy"), 0, 0).reshape(chunks.shape)
    return call(
        up_kernel,
        (out(rows, columns), out(rows, columns)),
        [vmem(3, ring), vmem(2, 0), vmem(1, 0), pltpu.SemaphoreType.DMA((8,))]
        + [pltpu.VMEM(((rows >> LEVELS) + 2 * TALL + 2 * GUARD, LANES), jnp.float32), vmem(3, ring)]
        + [pltpu.VMEM((total, columns), jnp.float32)] * 2
        + [vmem(2, level) for level in levels]
        + [vmem(1, level) for level in levels],
        60 * cells,
        40 * cells,
        out_specs=[pl.BlockSpec(memory_space=pl.ANY)] * 2,
    )(gathered, dense, from_cross, from_pair, own[0], frame_source, diagonal, frame_diagonal, *body_state, *frame_state, *ring_state)


def solution(mesh):
    placed = (P("gx", "gy"), P("gx", "gy"), P("gx", "gy"), P("gx", "gy"))
    return jax.shard_map(
        local, mesh=mesh, in_specs=placed, out_specs=(P("gx", "gy"), P("gx", "gy")), check_vma=False
    )
```

```python
import jax
import jax.numpy as jnp
from jax import lax
from jax.experimental import pallas as pl
from jax.experimental.pallas import tpu as pltpu
from jax.sharding import PartitionSpec as P

LEVELS = 4
SWEEPS = 12

damping = 0.01
relaxation = 0.8

HALO = 16
NEAR = 20
LANES = 128
INNER = LANES // 2 - HALO
TOP = 16
GUARD = 8
PIECES = 8
CHUNK = 136
PART = CHUNK
LAG = 8
TALL = 16
VMEM_LIMIT = 40 * 1024 * 1024


def lane_of(x):
    return lax.broadcasted_iota(jnp.int32, x.shape, x.ndim - 1)


def roll(x, amount):
    amount %= LANES
    return x if amount == 0 else pltpu.roll(x, amount, x.ndim - 1)


def from_west(tiles, step):
    moved = [roll(t, step) for t in tiles]
    if len(tiles) == 1:
        return moved
    edge = lane_of(tiles[0]) < step
    return [jnp.where(edge, moved[i - 1], moved[i]) for i in range(len(tiles))]


def from_east(tiles, step):
    moved = [roll(t, -step) for t in tiles]
    count = len(tiles)
    if count == 1:
        return moved
    edge = lane_of(tiles[0]) >= LANES - step
    return [jnp.where(edge, moved[(i + 1) % count], moved[i]) for i in range(count)]


def spread(tiles, step):
    second = (lane_of(tiles[0]) // step) % 2 == 1
    return [jnp.where(second, roll(t, step), t) for t in tiles]


def for_parts(start, size, body, part):
    for offset in range(0, size, part):
        body(start + offset, min(part, size - offset))


def for_chunks(rows, body, largest, part):
    sizes = [size for size in range(8, largest + 1, 8) if rows % size == 0]
    if rows <= largest or not sizes:
        for_parts(0, rows, body, part)
        return

    def step(i, carry):
        for_parts(i * sizes[-1], sizes[-1], body, part)
        return carry

    lax.fori_loop(0, rows // sizes[-1], step, 0)


def load(ref, start, size):
    return [ref[t, pl.ds(GUARD + start, size), :] for t in range(ref.shape[0])]


def store(ref, start, size, tiles):
    for t, tile in enumerate(tiles):
        ref[t, pl.ds(GUARD + start, size), :] = tile


def store_twice(ref, start, size, tiles):
    for t, tile in enumerate(tiles):
        ref[t, pl.ds(GUARD + 2 * start, size, stride=2), :] = tile
        ref[t, pl.ds(GUARD + 2 * start + 1, size, stride=2), :] = tile


def clear_guards(ref, rows):
    zeros = jnp.zeros((GUARD, LANES), jnp.float32)
    for t in range(ref.shape[0]):
        ref[t, 0:GUARD, :] = zeros
        ref[t, GUARD + rows : 2 * GUARD + rows, :] = zeros


def beside(mid, north, south, c_west, c_north, c_south, step):
    west = from_west(mid, step)
    east = from_east([c * m for c, m in zip(c_west, mid)], step)
    return [
        (c_west[t] * west[t] + east[t]) + (c_north[t] * north[t] + c_south[t] * south[t]) for t in range(len(mid))
    ]


def beside_of(ref, coeffs, start, size, step):
    c_west_ref, c_north_ref = coeffs
    mid = load(ref, start, size)
    north, south = load(ref, start - 1, size), load(ref, start + 1, size)
    c_west, c_north = load(c_west_ref, start, size), load(c_north_ref, start, size)
    return mid, beside(mid, north, south, c_west, c_north, load(c_north_ref, start + 1, size), step)


def pool_rows(ref, start, size, step):
    out = []
    for t in range(ref.shape[0]):
        even = ref[t, pl.ds(GUARD + start, size // 2, stride=2), :]
        odd = ref[t, pl.ds(GUARD + start + 1, size // 2, stride=2), :]
        both = even + odd
        out.append(both + roll(both, -step))
    return out


def descend(level, height, weight, source, guess, state, diagonal_ref, field, resid, next_weight, next_source, largest, part):
    step = 2**level
    c_west_ref, c_north_ref, scale_ref, smooth_ref = state
    for ref in (weight, field, c_north_ref):
        clear_guards(ref, height)

    def first_pass(start, size):
        w, w_north, w_south = (load(weight, start + k, size) for k in (0, -1, 1))
        c_north = [jnp.minimum(a, b) for a, b in zip(w, w_north)]
        c_south = [jnp.minimum(a, b) for a, b in zip(w, w_south)]
        c_west = [jnp.minimum(a, b) for a, b in zip(w, from_west(w, step))]
        c_east = from_east(c_west, step)
        diagonal = [damping + c_north[t] + c_south[t] + c_west[t] + c_east[t] for t in range(len(w))]
        scale = [relaxation / d for d in diagonal]
        store(c_north_ref, start, size, c_north)
        store(c_west_ref, start, size, c_west)
        store(scale_ref, start, size, scale)
        store(diagonal_ref, start, size, diagonal)
        value = load(source, start, size)
        if guess is None:
            value = [scale[t] * value[t] for t in range(len(w))]
        else:
            mid, north, south = (load(guess, start + k, size) for k in (0, -1, 1))
            around = beside(mid, north, south, c_west, c_north, c_south, step)
            value = [
                (1.0 - relaxation) * mid[t] + scale[t] * (value[t] + around[t]) for t in range(len(w))
            ]
        store(field, start, size, value)
        if next_weight is not None:
            pooled = [0.125 * p for p in pool_rows(weight, start, size, step)]
            store(next_weight, start // 2, size // 2, pooled)

    def second_pass(start, size):
        mid, around = beside_of(field, (c_west_ref, c_north_ref), start, size, step)
        b, scale, diagonal = (load(ref, start, size) for ref in (source, scale_ref, diagonal_ref))
        rest = [(b[t] + around[t]) - diagonal[t] * mid[t] for t in range(len(b))]
        store(smooth_ref, start, size, [mid[t] + scale[t] * rest[t] for t in range(len(b))])
        store(resid, start, size, rest)
        if next_source is not None:
            pooled = [0.25 * p for p in pool_rows(resid, start, size, step)]
            store(next_source, start // 2, size // 2, pooled)

    for_chunks(height, first_pass, largest, part)
    for_chunks(height, second_pass, largest, part)


def descend_all(rows, sources, guess, weights, states, diagonal, field, resid, largest, part):
    for level in range(LEVELS - 1):
        descend(
            level,
            rows >> level,
            weights[level],
            sources[level],
            guess if level == 0 else None,
            states[4 * level : 4 * level + 4],
            diagonal[level],
            field,
            resid,
            weights[level + 1],
            sources[level + 1],
            largest,
            part,
        )


def group_of(x, west):
    return (lane_of(x) // HALO + (1 if west else 0)) % PIECES


def packed(part, p, west):
    return roll(part, p * HALO - HALO if west else p * HALO + HALO)


def to_sides(west, east, cross_ref, pair_ref, k, rows):
    even = lax.axis_index("gy") % 2 == 0
    cross_ref[k, rows, :] = jnp.where(even, west, east)
    pair_ref[k, rows, :] = jnp.where(even, east, west)


def inner_columns(tiles):
    return jnp.where(lane_of(tiles[0]) < LANES // 2, roll(tiles[0], HALO), roll(tiles[1], -HALO))


def layout_kernel(source, guess, weight, *refs):
    owns, frames, (cross_ref, pair_ref, *inner) = refs[:3], refs[3:6], refs[6:]
    rows = source.shape[0]
    piece = cross_ref.shape[1]
    whole = rows // piece
    tail = rows - whole * piece
    for own, frame, block in zip(owns, frames, (source, guess, weight)):
        clear_guards(own, rows + 2 * TOP)
        clear_guards(frame, rows + 2 * TOP)
        tiles = [block[:, t * LANES : (t + 1) * LANES] for t in range(2)]
        for t in range(2):
            own[t, GUARD + TOP : GUARD + TOP + rows, :] = tiles[t]
        frame[0, GUARD + TOP : GUARD + TOP + rows, :] = inner_columns(tiles)
    weights, start, height = (owns[2], *inner), TOP, rows
    for level in range(LEVELS):
        pooled = [0.125 * w for w in pool_rows(weights[level], start, height, 2**level)]
        start, height = start // 2, height // 2
        if level < LEVELS - 1:
            store(weights[level + 1], start, height, pooled)
    lane = lane_of(pooled[0])
    width = HALO // 2
    index = (lane % width) * 2**LEVELS
    coarse = [jnp.take_along_axis(p, index, axis=1) for p in pooled]
    coarse = jnp.where(lane % HALO < width, *coarse)
    for k, block in enumerate((source, guess, weight)):
        sides = []
        for west in (True, False):
            columns = slice(0, LANES) if west else slice(LANES, 2 * LANES)
            below = jnp.zeros((piece - tail, LANES), jnp.float32)
            if k < 2:
                half = coarse[k * height // 2 : (k + 1) * height // 2]
                below = jnp.concatenate((below[: 2 * TOP], half, below[2 * TOP + height // 2 :]), axis=0)
            last = packed(block[whole * piece :, columns], whole, west)
            both = jnp.concatenate((last, below), axis=0)
            for p in range(whole):
                part = packed(block[p * piece : (p + 1) * piece, columns], p, west)
                both = jnp.where(group_of(part, west) == p, part, both)
            sides.append(both)
        to_sides(*sides, cross_ref, pair_ref, k, slice(0, piece))


def halo_kernel(*refs):
    first_rows, second_rows, *own, cross_ref, pair_ref = refs[8:]
    own, frames = own[:3], own[3:]
    total = own[0].shape[1] - 2 * GUARD
    last = PIECES - 1
    first = total - 2 * TOP - last * cross_ref.shape[1]
    even, even_y = lax.axis_index("gx") % 2 == 0, lax.axis_index("gy") % 2 == 0
    for k in range(3):
        above = jnp.where(even, first_rows[k], second_rows[k])
        below = jnp.where(even, second_rows[k], first_rows[k])
        for side, (rows, row) in enumerate(((above, 0), (below, total - TOP))):
            body = [rows[:, t * LANES : (t + 1) * LANES] for t in range(2)]
            for t in range(2):
                own[k][t, GUARD + row : GUARD + row + TOP, :] = body[t]
            frames[k][0, GUARD + row : GUARD + row + TOP, :] = inner_columns(body)
            span = slice(first + side * TOP, first + (side + 1) * TOP)
            parts = []
            for part, west in zip(body, (True, False)):
                here = group_of(part, west) == last
                parts.append((here, packed(part, last, west)))
            (here_west, west), (here_east, east) = parts
            cross, pair = cross_ref[k, span, :], pair_ref[k, span, :]
            cross_ref[k, span, :] = jnp.where(
                even_y, jnp.where(here_west, west, cross), jnp.where(here_east, east, cross)
            )
            pair_ref[k, span, :] = jnp.where(
                even_y, jnp.where(here_east, east, pair), jnp.where(here_west, west, pair)
            )


def body_kernel(source, guess, weight, *refs):
    states = refs[: 4 * (LEVELS - 1)]
    last_weight, last_source, first_diagonal, *refs = refs[4 * (LEVELS - 1) :]
    field, resid, weight_in, *inner = refs
    rows = source.shape[1] - 2 * GUARD
    depth = LEVELS - 2
    weights = (weight_in, *inner[:depth], last_weight)
    sources = (source, *inner[depth : 2 * depth], last_source)
    diagonal = (first_diagonal, *inner[2 * depth :])
    weights[0][...] = weight[...]
    descend_all(rows, sources, guess, weights, states, diagonal, field, resid, CHUNK, CHUNK)


def frame_kernel(_a, _b, _c, from_pair, from_cross, body_weight, body_source, *refs):
    even = lax.axis_index("gy") % 2 == 0
    frames, states, refs = refs[:3], refs[3 : 3 + 4 * (LEVELS - 1)], refs[3 + 4 * (LEVELS - 1) :]
    frame_source, frame_guess, frame_weight = frames
    first_diagonal, ring_state, dense_ref, chunks_ref, field, resid, *refs = refs[0], refs[1:5], *refs[5:]
    ring_weight, ring_source, ring_field, ring_resid, ring_diagonal, *inner = refs
    rows = frame_source.shape[1] - 2 * GUARD
    depth = LEVELS - 1
    weights = (frame_weight, *inner[:depth])
    sources = (frame_source, *inner[depth : 2 * depth])
    diagonals = (first_diagonal, *inner[2 * depth :])
    piece = from_cross.shape[1]
    for k, frame in enumerate(frames):
        block = rows - 2 * TOP
        last = PIECES - 1
        tail = block - last * piece
        spans = [(p, 0, TOP + p * piece, piece) for p in range(last)]
        spans += [(last, 0, TOP + last * piece, tail)]
        spans += [(last, tail, 0, TOP), (last, tail + TOP, rows - TOP, TOP)]
        for p, first, start, size in spans:
            span = slice(GUARD + start, GUARD + start + size)
            cross, pair = from_cross[k, first : first + size, :], from_pair[k, first : first + size, :]
            from_left = group_of(cross, False) == p
            both = roll(jnp.where(from_left == even, cross, pair), -p * HALO)
            lane = lane_of(both)
            outside = (lane < HALO) | (lane >= LANES - HALO)
            frame[0, span, :] = jnp.where(outside, both, frame[0, span, :])
    descend_all(rows, sources, frame_guess, weights, states, diagonals, field, resid, 2 * CHUNK, 2 * CHUNK)

    level = LEVELS - 1
    step, halo, height = 2**level, TOP >> level, rows >> level
    for body, frame, ring in (
        (body_weight, weights[level], ring_weight),
        (body_source, sources[level], ring_source),
    ):
        middle = load(body, 0, height)
        around = load(frame, 0, height)[0]
        lane = lane_of(around)
        ahead, back = roll(around, HALO), roll(around, -HALO)
        store(
            ring,
            0,
            height,
            [
                jnp.where(lane < 2 * step, back, middle[0]),
                jnp.where(lane >= LANES - 2 * step, ahead, middle[1]),
                jnp.where(lane < LANES // 2, ahead, back),
            ],
        )
    descend(
        level,
        height,
        ring_weight,
        ring_source,
        None,
        ring_state,
        ring_diagonal,
        ring_field,
        ring_resid,
        None,
        None,
        height,
        height,
    )

    coarse_rows = (height - 2 * halo) // 2
    dense = jnp.zeros((8, LANES), jnp.float32)
    lane = lane_of(dense)
    per_tile = LANES // 2**LEVELS
    pooled_b = pool_rows(ring_resid, halo, 2 * coarse_rows, step)
    pooled_w = pool_rows(ring_weight, halo, 2 * coarse_rows, step)
    index = (lane % per_tile) * 2**LEVELS
    place = lane // per_tile
    for g in range(coarse_rows // 8):
        for group, (values, factor) in enumerate(((pooled_b, 0.25), (pooled_w, 0.125))):
            for t in range(2):
                taken = jnp.take_along_axis(factor * values[t][8 * g : 8 * g + 8], index, axis=1)
                dense = jnp.where(place == 4 * g + 2 * group + t, taken, dense)
    dense_ref[...] = dense

    width = 2 * per_tile
    index = jnp.minimum(2 * (lane - lane % width) + lane % width, LANES - 1)
    smooth = ring_state[3]
    beside_me = []
    for tile, edge, free in ((0, 0, width - 2), (1, LANES - step, 0)):
        chunk = jnp.take_along_axis(dense, index, axis=1)
        first = GUARD + halo
        pieces = []
        for g in range(coarse_rows // 8):
            for odd in range(2):
                rows_of = smooth[tile, pl.ds(first + 16 * g + odd, 8, stride=2), :]
                pieces.append((g * width + free + odd, rows_of))
        for place, values in pieces:
            chunk = jnp.where(lane == place, roll(values, place - edge), chunk)
        beside_me.append(fold(chunk))
    sublane = lax.broadcasted_iota(jnp.int32, dense.shape, 0)
    beyond = []
    for row, group, free in ((0, 1, 6), (2 * coarse_rows - 1, 2, 0)):
        chunk = dense
        for tile in range(2):
            values = jnp.broadcast_to(smooth[tile, GUARD + halo + row : GUARD + halo + row + 1, :], dense.shape)
            values = jnp.take_along_axis(values, (lane % width) * step, axis=1)
            here = (sublane == free + tile) & (lane // width == 2 * group)
            chunk = jnp.where(here, values, chunk)
        beyond.append(chunk)
    above, below = fold(beyond[0]), fold(roll(beyond[1], -LANES // 2))
    x, y = lax.axis_index("gx"), lax.axis_index("gy")
    for i in range(chunks_ref.shape[0]):
        for j in range(chunks_ref.shape[1]):
            level_with = jnp.where(j < y, beside_me[0], beside_me[1])
            chunks_ref[i, j] = jnp.where(i == x, level_with, jnp.where(i < x, above, below))


def fold(x):
    return jnp.where(lane_of(x) < LANES // 2, x, pltpu.roll(roll(x, LANES // 2), 4, 0))[:4]


def unfold(x):
    return jnp.concatenate((x, roll(x, LANES // 2)), axis=0)


def coarse_solve(all_ref, dense_ref, from_cross, from_pair, e_ref, edge_ref, smooth_ref, rows, width, groups):
    x, nx = lax.axis_index("gx"), lax.axis_size("gx")
    y, ny = lax.axis_index("gy"), lax.axis_size("gy")
    tiles = {}
    for dx in (-1, 0, 1):
        for dy in (-1, 0, 1):
            if dx or dy:
                inside = (x + dx >= 0) & (x + dx < nx) & (y + dy >= 0) & (y + dy < ny)
                tile = unfold(all_ref[jnp.where(inside, x + dx, 0), jnp.where(inside, y + dy, 0)])
                tiles[dx, dy] = jnp.where(inside, tile, 0.0)
    dense = dense_ref[...]
    lane = lane_of(dense)
    even = y % 2 == 0
    half = 4 * groups
    first = rows % from_cross.shape[1] + 2 * TOP
    cross, pair = ([ref[k, first : first + half, :] for k in range(2)] for ref in (from_cross, from_pair))
    cross, pair = jnp.concatenate(cross, axis=0), jnp.concatenate(pair, axis=0)
    weights = {-1: jnp.where(even, cross, pair), 1: jnp.where(even, pair, cross)}
    bands = [(-1, g) for g in range(TALL // 8)] + [(0, g) for g in range(groups)] + [(1, g) for g in range(TALL // 8)]
    b, w = [], []
    for dx, g in bands:
        b_rows = w_rows = jnp.zeros_like(dense)
        for dy in (-1, 0, 1):
            first_lane = (dy + 1) * width
            here = (lane >= first_lane) & (lane < first_lane + width)
            if dx or not dy:
                tile = tiles[dx, dy] if dx else dense
                b_part = roll(tile, first_lane - 2 * g * width)
                w_part = roll(tile, first_lane - (2 * g + 1) * width)
            else:
                b_part = roll(tiles[dx, dy], first_lane - g * width)
                at = (PIECES - 1 - (dy > 0)) * HALO
                w_part = roll(weights[dy][8 * g : 8 * g + 8], first_lane - at)
            b_rows = jnp.where(here, b_part, b_rows)
            w_rows = jnp.where(here, w_part, w_rows)
        b.append(b_rows)
        w.append(w_rows)
    b, w = jnp.concatenate(b, axis=0), jnp.concatenate(w, axis=0)

    step = 2 ** (LEVELS - 1)
    start = GUARD + (TOP >> (LEVELS - 1))
    for t in range(2):
        edge_ref[t] = smooth_ref[t]
    edge_ref[2] = jnp.zeros_like(edge_ref[2])

    def columns(place):
        left = roll(tiles[0, -1], LANES - step - place)
        right = roll(tiles[0, 1], -(place + width - 2))
        return jnp.where(lane < step, right, left)

    for g in range(groups):
        for odd in range(2):
            edge_ref[2, pl.ds(start + 16 * g + odd, 8, stride=2), :] = columns(g * width + odd)
    for dx, row, lanes, free in ((-1, start - 1, 0, 0), (1, start + 16 * groups, 2 * width, 6)):
        for t in range(2):
            values = tiles[dx, 0][free + t : free + t + 1]
            values = jnp.take_along_axis(
                jnp.broadcast_to(values, dense.shape), lanes + lane // step, axis=1
            )
            edge_ref[t, row : row + 1, :] = values[:1]
        left = roll(tiles[dx, -1][free + 1 : free + 2], LANES - step - (lanes + width - 1))
        right = roll(tiles[dx, 1][free : free + 1], -lanes)
        edge_ref[2, row : row + 1, :] = jnp.where(lane[:1] < step, right, left)

    tall = b.shape[0]
    zeros = jnp.zeros((GUARD, LANES), jnp.float32)
    e_ref[0:GUARD, :] = zeros
    e_ref[GUARD + tall :, :] = zeros

    def shifted(by):
        return e_ref[GUARD + by : GUARD + by + tall, :]

    e_ref[GUARD : GUARD + tall, :] = w
    c_west = jnp.minimum(w, roll(w, 1))
    c_north, c_south = jnp.minimum(w, shifted(-1)), jnp.minimum(w, shifted(1))
    c_east = roll(c_west, -1)
    scale = relaxation / (damping + c_north + c_south + c_west + c_east)
    first = scale * b
    c_west, c_east, c_north, c_south = (scale * c for c in (c_west, c_east, c_north, c_south))
    e_ref[GUARD : GUARD + tall, :] = first

    def sweep(_, carry):
        e = shifted(0)
        around = (c_west * roll(e, 1) + c_east * roll(e, -1)) + (c_north * shifted(-1) + c_south * shifted(1))
        e_ref[GUARD : GUARD + tall, :] = ((1.0 - relaxation) * e + first) + around
        return carry

    lax.fori_loop(0, SWEEPS - 1, sweep, 0)
    return shifted(0)


def up_kernel(all_ref, dense_ref, from_cross, from_pair, own_source, frame_source, own_diagonal, frame_diagonal, *refs):
    count = 4 * (LEVELS - 1)
    body_state, frame_state, ring_state = refs[:count], refs[count : 2 * count], refs[2 * count : 2 * count + 4]
    out_ref, resid_ref = refs[2 * count + 4 : 2 * count + 6]
    ring_pe, body_final, frame_final, sems, e_ref, edge_ref, *inner = refs[2 * count + 6 :]
    outs, inner = inner[:2], inner[2:]
    body_pe, frame_pe = inner[: LEVELS - 1], inner[LEVELS - 1 :]
    rows = out_ref.shape[0] + 2 * TOP
    width = out_ref.shape[1] >> LEVELS
    e = coarse_solve(all_ref, dense_ref, from_cross, from_pair, e_ref, edge_ref, ring_state[3], out_ref.shape[0], width, (out_ref.shape[0] >> LEVELS) // 8)

    level = LEVELS - 1
    step, halo, height = 2**level, TOP >> level, rows >> level
    coarse_rows = (height - 2 * halo) // 2
    picked = e[TALL - 8 : TALL + coarse_rows + 8]
    lane = lane_of(picked)
    for t in range(3):
        group = (lane + t * LANES) // 2**LEVELS
        if t == 2:
            group = jnp.where(lane < LANES // 2, group, group - 3 * LANES // 2**LEVELS)
        taken = jnp.take_along_axis(picked, jnp.clip(group + width, 0, LANES - 1), axis=1)[7 : 7 + coarse_rows + 2]
        ring_pe[t, 0 : 2 * GUARD, :] = jnp.zeros((2 * GUARD, LANES), jnp.float32)
        ring_pe[t, height : height + 2 * GUARD, :] = jnp.zeros((2 * GUARD, LANES), jnp.float32)
        ring_pe[t, pl.ds(GUARD + halo - 2, coarse_rows + 2, stride=2), :] = taken
        ring_pe[t, pl.ds(GUARD + halo - 1, coarse_rows + 2, stride=2), :] = taken

    def climbed(pe, state, start, size, step, edge=None):
        mid, around = beside_of(pe, state[:2], start, size, step)
        scale, smooth = load(state[2], start, size), load(state[3], start, size)
        if edge is not None:
            smooth = load(edge, start, size)
        return [(smooth[t] + (1.0 - relaxation) * mid[t]) + scale[t] * around[t] for t in range(len(mid))]

    def climb_ring(start, size, level=level, step=step):
        ring = spread(climbed(ring_pe, ring_state, start, size, step, edge_ref), step // 2)
        lane = lane_of(ring[0])
        around = jnp.where(
            lane < LANES // 2,
            jnp.where(lane < HALO, roll(ring[2], HALO), roll(ring[0], HALO)),
            jnp.where(lane < LANES - HALO, roll(ring[1], -HALO), roll(ring[2], -HALO)),
        )
        store_twice(body_pe[level - 1], start, size, ring[:2])
        store_twice(frame_pe[level - 1], start, size, [around])

    for_chunks(height, climb_ring, height, height)

    for level in range(LEVELS - 2, -1, -1):
        step, height = 2**level, rows >> level
        groups = ((body_pe, body_state, body_final), (frame_pe, frame_state, frame_final))
        for pes, _, _ in groups:
            clear_guards(pes[level], height)

        def climb(start, size, level=level, step=step, groups=groups):
            for pes, states, final in groups:
                value = climbed(pes[level], states[4 * level : 4 * level + 4], start, size, step)
                if level == 0:
                    store(final, start, size, value)
                else:
                    store_twice(pes[level - 1], start, size, spread(value, step // 2))

        if level > 0:
            for_chunks(height, climb, 2 * CHUNK, PART)

    def last(base, size):
        body, around = beside_of(body_final, body_state[:2], base, size, 1)
        frame, frame_around = beside_of(frame_final, frame_state[:2], base, size, 1)
        b, d = load(own_source, base, size), load(own_diagonal, base, size)
        b_frame, d_frame = load(frame_source, base, size), load(frame_diagonal, base, size)
        body = (body, [(b[t] + around[t]) - d[t] * body[t] for t in range(2)])
        frame = (frame[0], (b_frame[0] + frame_around[0]) - d_frame[0] * frame[0])
        lane = lane_of(frame[0])
        span = pl.ds(base, size)
        for ref, middle, around in ((outs[0], body[0], frame[0]), (outs[1], body[1], frame[1])):
            ref[span, :LANES] = jnp.where(lane < NEAR, roll(around, -HALO), middle[0])
            ref[span, LANES:] = jnp.where(lane >= LANES - NEAR, roll(around, HALO), middle[1])

    size = 2 * CHUNK
    count = rows // size
    ends = [0] + [size * (p + 1) - LAG - TOP for p in range(count - 1)] + [out_ref.shape[0]]

    def copies(p):
        middle = (ends[p] + ends[p + 1]) // 16 * 8
        return [
            pltpu.make_async_copy(
                outs[k].at[pl.ds(TOP + first, last - first)],
                ref.at[pl.ds(first, last - first)],
                sems.at[4 * p + 2 * h + k],
            )
            for h, (first, last) in enumerate(((ends[p], middle), (middle, ends[p + 1])))
            for k, ref in enumerate((out_ref, resid_ref))
        ]

    def finish(i, carry):
        for_parts(i * size, size, climb, PART)
        base = pl.multiple_of(jnp.maximum(i * size - LAG, 0), 8)
        for_parts(base, size, last, PART)
        for p in range(count):

            @pl.when(i == p)
            def _(p=p):
                for copy in copies(p):
                    copy.start()

        return carry

    lax.fori_loop(0, count, finish, 0)
    for p in range(count):
        for copy in copies(p):
            copy.wait()


def call(kernel, out_shape, scratch, flops, moved, **more):
    return pl.pallas_call(
        kernel,
        out_shape=out_shape,
        scratch_shapes=scratch,
        compiler_params=pltpu.CompilerParams(vmem_limit_bytes=VMEM_LIMIT),
        cost_estimate=pl.CostEstimate(flops=flops, bytes_accessed=moved, transcendentals=0),
        **more,
    )


def swap(x, axis, first):
    pairs = [(i, i + 1) for i in range(first, lax.axis_size(axis) - 1, 2)]
    return lax.ppermute(x, axis, pairs + [(j, i) for i, j in pairs])


def local(rhs, pressure, wet_mask, bathy_class):
    rows, columns = rhs.shape
    cells = rows * columns
    total = rows + 2 * TOP
    levels = range(LEVELS - 1)

    def shape(tiles, level):
        return (tiles, (total >> level) + 2 * GUARD, LANES)

    def out(*dims):
        return jax.ShapeDtypeStruct(dims, jnp.float32)

    def vmem(tiles, level):
        return pltpu.VMEM(shape(tiles, level), jnp.float32)

    def fields(r, p, m, c):
        wet = m.astype(jnp.float32)
        return wet * r, wet * p, wet * (1.0 + 0.5 * c.astype(jnp.float32))

    given = (rhs, pressure, wet_mask, bathy_class)

    def edge(start):
        return jnp.stack(fields(*(lax.dynamic_slice_in_dim(x, start, TOP, axis=0) for x in given)))

    even = lax.axis_index("gx") % 2 == 0
    first_rows = swap(edge(jnp.where(even, 0, rows - TOP)), "gx", 1)
    second_rows = swap(edge(jnp.where(even, rows - TOP, 0)), "gx", 0)
    piece = -(-(rows + 2 * TOP + (rows >> LEVELS) // 2) // (8 * PIECES)) * 8
    own_shapes = [out(*shape(2, 0))] * 3
    laid_out = [*own_shapes, *[out(*shape(1, 0))] * 3, out(3, piece, LANES), out(3, piece, LANES)]
    inner = [vmem(2, level) for level in range(1, LEVELS)]
    begun = call(layout_kernel, laid_out, inner, 10 * cells, 10 * cells)(*fields(*given))
    *own, to_cross, to_pair = call(
        halo_kernel, laid_out, (), cells, cells, input_output_aliases={k: k for k in range(8)}
    )(*begun, first_rows, second_rows)
    own, frames = own[:3], own[3:]
    from_pair = swap(to_pair, "gy", 0)
    from_cross = swap(to_cross, "gy", 1)

    state_count = 4 * (LEVELS - 1)
    *body_state, body_weight, body_source, diagonal = call(
        body_kernel,
        [out(*shape(2, level)) for level in levels for _ in range(4)]
        + [out(*shape(2, LEVELS - 1))] * 2
        + [out(*shape(2, 0))],
        [vmem(2, 0)] * 3 + [vmem(2, level) for level in levels[1:]] * 3,
        100 * cells,
        40 * cells,
    )(*own)
    nx, ny = lax.axis_size("gx"), lax.axis_size("gy")
    ring = LEVELS - 1
    frame_source, _, _, *state, dense, chunks = call(
        frame_kernel,
        [out(*shape(1, 0))] * 3
        + [out(*shape(1, level)) for level in levels for _ in range(4)]
        + [out(*shape(1, 0))]
        + [out(*shape(3, ring))] * 4
        + [out(8, LANES), out(nx, ny, 4, LANES)],
        [vmem(1, 0)] * 2 + [vmem(3, ring)] * 5 + [vmem(1, level) for level in range(1, LEVELS)] * 3,
        50 * cells,
        20 * cells,
        input_output_aliases={k: k for k in range(3)},
    )(*frames, from_pair, from_cross, body_weight, body_source)
    frame_state, frame_diagonal, ring_state = state[:state_count], state[state_count], state[state_count + 1 :]
    gathered = lax.all_to_all(chunks.reshape(nx * ny, 4, LANES), ("gx", "gy"), 0, 0).reshape(chunks.shape)
    return call(
        up_kernel,
        (out(rows, columns), out(rows, columns)),
        [vmem(3, ring), vmem(2, 0), vmem(1, 0), pltpu.SemaphoreType.DMA((8,))]
        + [pltpu.VMEM(((rows >> LEVELS) + 2 * TALL + 2 * GUARD, LANES), jnp.float32), vmem(3, ring)]
        + [pltpu.VMEM((total, columns), jnp.float32)] * 2
        + [vmem(2, level) for level in levels]
        + [vmem(1, level) for level in levels],
        60 * cells,
        40 * cells,
        out_specs=[pl.BlockSpec(memory_space=pl.ANY)] * 2,
    )(gathered, dense, from_cross, from_pair, own[0], frame_source, diagonal, frame_diagonal, *body_state, *frame_state, *ring_state)


def solution(mesh):
    placed = (P("gx", "gy"), P("gx", "gy"), P("gx", "gy"), P("gx", "gy"))
    return jax.shard_map(
        local, mesh=mesh, in_specs=placed, out_specs=(P("gx", "gy"), P("gx", "gy")), check_vma=False
    )
```

```python
import jax
import jax.numpy as jnp
from jax import lax
from jax.experimental import pallas as pl
from jax.experimental.pallas import tpu as pltpu
from jax.sharding import PartitionSpec as P

LEVELS = 4
SWEEPS = 12

damping = 0.01
relaxation = 0.8

HALO = 16
NEAR = 20
LANES = 128
INNER = LANES // 2 - HALO
TOP = 16
GUARD = 8
PIECES = 8
CHUNK = 136
PART = CHUNK
LAG = 8
TALL = 16
VMEM_LIMIT = 40 * 1024 * 1024


def lane_of(x):
    return lax.broadcasted_iota(jnp.int32, x.shape, x.ndim - 1)


def roll(x, amount):
    amount %= LANES
    return x if amount == 0 else pltpu.roll(x, amount, x.ndim - 1)


def from_west(tiles, step):
    moved = [roll(t, step) for t in tiles]
    if len(tiles) == 1:
        return moved
    edge = lane_of(tiles[0]) < step
    return [jnp.where(edge, moved[i - 1], moved[i]) for i in range(len(tiles))]


def from_east(tiles, step):
    moved = [roll(t, -step) for t in tiles]
    count = len(tiles)
    if count == 1:
        return moved
    edge = lane_of(tiles[0]) >= LANES - step
    return [jnp.where(edge, moved[(i + 1) % count], moved[i]) for i in range(count)]


def spread(tiles, step):
    second = (lane_of(tiles[0]) // step) % 2 == 1
    return [jnp.where(second, roll(t, step), t) for t in tiles]


def for_parts(start, size, body, part):
    for offset in range(0, size, part):
        body(start + offset, min(part, size - offset))


def for_chunks(rows, body, largest, part):
    sizes = [size for size in range(8, largest + 1, 8) if rows % size == 0]
    if rows <= largest or not sizes:
        for_parts(0, rows, body, part)
        return

    def step(i, carry):
        for_parts(i * sizes[-1], sizes[-1], body, part)
        return carry

    lax.fori_loop(0, rows // sizes[-1], step, 0)


def load(ref, start, size):
    return [ref[t, pl.ds(GUARD + start, size), :] for t in range(ref.shape[0])]


def store(ref, start, size, tiles):
    for t, tile in enumerate(tiles):
        ref[t, pl.ds(GUARD + start, size), :] = tile


def store_twice(ref, start, size, tiles):
    for t, tile in enumerate(tiles):
        ref[t, pl.ds(GUARD + 2 * start, size, stride=2), :] = tile
        ref[t, pl.ds(GUARD + 2 * start + 1, size, stride=2), :] = tile


def clear_guards(ref, rows):
    zeros = jnp.zeros((GUARD, LANES), jnp.float32)
    for t in range(ref.shape[0]):
        ref[t, 0:GUARD, :] = zeros
        ref[t, GUARD + rows : 2 * GUARD + rows, :] = zeros


def beside(mid, north, south, c_west, c_north, c_south, step):
    west = from_west(mid, step)
    east = from_east([c * m for c, m in zip(c_west, mid)], step)
    return [
        (c_west[t] * west[t] + east[t]) + (c_north[t] * north[t] + c_south[t] * south[t]) for t in range(len(mid))
    ]


def beside_of(ref, coeffs, start, size, step):
    c_west_ref, c_north_ref = coeffs
    mid = load(ref, start, size)
    north, south = load(ref, start - 1, size), load(ref, start + 1, size)
    c_west, c_north = load(c_west_ref, start, size), load(c_north_ref, start, size)
    return mid, beside(mid, north, south, c_west, c_north, load(c_north_ref, start + 1, size), step)


def pool_rows(ref, start, size, step):
    out = []
    for t in range(ref.shape[0]):
        even = ref[t, pl.ds(GUARD + start, size // 2, stride=2), :]
        odd = ref[t, pl.ds(GUARD + start + 1, size // 2, stride=2), :]
        both = even + odd
        out.append(both + roll(both, -step))
    return out


def descend(level, height, weight, source, guess, state, diagonal_ref, field, resid, next_weight, next_source, largest, part):
    step = 2**level
    c_west_ref, c_north_ref, scale_ref, smooth_ref = state
    for ref in (weight, field, c_north_ref):
        clear_guards(ref, height)

    def first_pass(start, size):
        w, w_north, w_south = (load(weight, start + k, size) for k in (0, -1, 1))
        c_north = [jnp.minimum(a, b) for a, b in zip(w, w_north)]
        c_south = [jnp.minimum(a, b) for a, b in zip(w, w_south)]
        c_west = [jnp.minimum(a, b) for a, b in zip(w, from_west(w, step))]
        c_east = from_east(c_west, step)
        diagonal = [damping + c_north[t] + c_south[t] + c_west[t] + c_east[t] for t in range(len(w))]
        scale = [relaxation / d for d in diagonal]
        store(c_north_ref, start, size, c_north)
        store(c_west_ref, start, size, c_west)
        store(scale_ref, start, size, scale)
        store(diagonal_ref, start, size, diagonal)
        value = load(source, start, size)
        if guess is None:
            value = [scale[t] * value[t] for t in range(len(w))]
        else:
            mid, north, south = (load(guess, start + k, size) for k in (0, -1, 1))
            around = beside(mid, north, south, c_west, c_north, c_south, step)
            value = [
                (1.0 - relaxation) * mid[t] + scale[t] * (value[t] + around[t]) for t in range(len(w))
            ]
        store(field, start, size, value)
        if next_weight is not None:
            pooled = [0.125 * p for p in pool_rows(weight, start, size, step)]
            store(next_weight, start // 2, size // 2, pooled)

    def second_pass(start, size):
        mid, around = beside_of(field, (c_west_ref, c_north_ref), start, size, step)
        b, scale, diagonal = (load(ref, start, size) for ref in (source, scale_ref, diagonal_ref))
        rest = [(b[t] + around[t]) - diagonal[t] * mid[t] for t in range(len(b))]
        store(smooth_ref, start, size, [mid[t] + scale[t] * rest[t] for t in range(len(b))])
        store(resid, start, size, rest)
        if next_source is not None:
            pooled = [0.25 * p for p in pool_rows(resid, start, size, step)]
            store(next_source, start // 2, size // 2, pooled)

    for_chunks(height, first_pass, largest, part)
    for_chunks(height, second_pass, largest, part)


def descend_all(rows, sources, guess, weights, states, diagonal, field, resid, largest, part):
    for level in range(LEVELS - 1):
        descend(
            level,
            rows >> level,
            weights[level],
            sources[level],
            guess if level == 0 else None,
            states[4 * level : 4 * level + 4],
            diagonal[level],
            field,
            resid,
            weights[level + 1],
            sources[level + 1],
            largest,
            part,
        )


def group_of(x, west):
    return (lane_of(x) // HALO + (1 if west else 0)) % PIECES


def packed(part, p, west):
    return roll(part, p * HALO - HALO if west else p * HALO + HALO)


def to_sides(west, east, cross_ref, pair_ref, k, rows):
    even = lax.axis_index("gy") % 2 == 0
    cross_ref[k, rows, :] = jnp.where(even, west, east)
    pair_ref[k, rows, :] = jnp.where(even, east, west)


def inner_columns(tiles):
    return jnp.where(lane_of(tiles[0]) < LANES // 2, roll(tiles[0], HALO), roll(tiles[1], -HALO))


def layout_kernel(source, guess, weight, *refs):
    owns, frames, (cross_ref, pair_ref, *inner) = refs[:3], refs[3:6], refs[6:]
    rows = source.shape[0]
    piece = cross_ref.shape[1]
    whole = rows // piece
    tail = rows - whole * piece
    for own, frame, block in zip(owns, frames, (source, guess, weight)):
        clear_guards(own, rows + 2 * TOP)
        clear_guards(frame, rows + 2 * TOP)
        tiles = [block[:, t * LANES : (t + 1) * LANES] for t in range(2)]
        for t in range(2):
            own[t, GUARD + TOP : GUARD + TOP + rows, :] = tiles[t]
        frame[0, GUARD + TOP : GUARD + TOP + rows, :] = inner_columns(tiles)
    weights, start, height = (owns[2], *inner), TOP, rows
    for level in range(LEVELS):
        pooled = [0.125 * w for w in pool_rows(weights[level], start, height, 2**level)]
        start, height = start // 2, height // 2
        if level < LEVELS - 1:
            store(weights[level + 1], start, height, pooled)
    lane = lane_of(pooled[0])
    width = HALO // 2
    index = (lane % width) * 2**LEVELS
    coarse = [jnp.take_along_axis(p, index, axis=1) for p in pooled]
    coarse = jnp.where(lane % HALO < width, *coarse)
    for k, block in enumerate((source, guess, weight)):
        sides = []
        for west in (True, False):
            columns = slice(0, LANES) if west else slice(LANES, 2 * LANES)
            below = jnp.zeros((piece - tail, LANES), jnp.float32)
            if k < 2:
                half = coarse[k * height // 2 : (k + 1) * height // 2]
                below = jnp.concatenate((below[: 2 * TOP], half, below[2 * TOP + height // 2 :]), axis=0)
            last = packed(block[whole * piece :, columns], whole, west)
            both = jnp.concatenate((last, below), axis=0)
            for p in range(whole):
                part = packed(block[p * piece : (p + 1) * piece, columns], p, west)
                both = jnp.where(group_of(part, west) == p, part, both)
            sides.append(both)
        to_sides(*sides, cross_ref, pair_ref, k, slice(0, piece))


def halo_kernel(*refs):
    first_rows, second_rows, *own, cross_ref, pair_ref = refs[8:]
    own, frames = own[:3], own[3:]
    total = own[0].shape[1] - 2 * GUARD
    last = PIECES - 1
    first = total - 2 * TOP - last * cross_ref.shape[1]
    even, even_y = lax.axis_index("gx") % 2 == 0, lax.axis_index("gy") % 2 == 0
    for k in range(3):
        above = jnp.where(even, first_rows[k], second_rows[k])
        below = jnp.where(even, second_rows[k], first_rows[k])
        for side, (rows, row) in enumerate(((above, 0), (below, total - TOP))):
            body = [rows[:, t * LANES : (t + 1) * LANES] for t in range(2)]
            for t in range(2):
                own[k][t, GUARD + row : GUARD + row + TOP, :] = body[t]
            frames[k][0, GUARD + row : GUARD + row + TOP, :] = inner_columns(body)
            span = slice(first + side * TOP, first + (side + 1) * TOP)
            parts = []
            for part, west in zip(body, (True, False)):
                here = group_of(part, west) == last
                parts.append((here, packed(part, last, west)))
            (here_west, west), (here_east, east) = parts
            cross, pair = cross_ref[k, span, :], pair_ref[k, span, :]
            cross_ref[k, span, :] = jnp.where(
                even_y, jnp.where(here_west, west, cross), jnp.where(here_east, east, cross)
            )
            pair_ref[k, span, :] = jnp.where(
                even_y, jnp.where(here_east, east, pair), jnp.where(here_west, west, pair)
            )


def body_kernel(source, guess, weight, *refs):
    states = refs[: 4 * (LEVELS - 1)]
    last_weight, last_source, first_diagonal, *refs = refs[4 * (LEVELS - 1) :]
    field, resid, weight_in, *inner = refs
    rows = source.shape[1] - 2 * GUARD
    depth = LEVELS - 2
    weights = (weight_in, *inner[:depth], last_weight)
    sources = (source, *inner[depth : 2 * depth], last_source)
    diagonal = (first_diagonal, *inner[2 * depth :])
    weights[0][...] = weight[...]
    descend_all(rows, sources, guess, weights, states, diagonal, field, resid, 2 * CHUNK, CHUNK)


def frame_kernel(_a, _b, _c, from_pair, from_cross, body_weight, body_source, *refs):
    even = lax.axis_index("gy") % 2 == 0
    frames, states, refs = refs[:3], refs[3 : 3 + 4 * (LEVELS - 1)], refs[3 + 4 * (LEVELS - 1) :]
    frame_source, frame_guess, frame_weight = frames
    first_diagonal, ring_state, dense_ref, chunks_ref, field, resid, *refs = refs[0], refs[1:5], *refs[5:]
    ring_weight, ring_source, ring_field, ring_resid, ring_diagonal, *inner = refs
    rows = frame_source.shape[1] - 2 * GUARD
    depth = LEVELS - 1
    weights = (frame_weight, *inner[:depth])
    sources = (frame_source, *inner[depth : 2 * depth])
    diagonals = (first_diagonal, *inner[2 * depth :])
    piece = from_cross.shape[1]
    for k, frame in enumerate(frames):
        block = rows - 2 * TOP
        last = PIECES - 1
        tail = block - last * piece
        spans = [(p, 0, TOP + p * piece, piece) for p in range(last)]
        spans += [(last, 0, TOP + last * piece, tail)]
        spans += [(last, tail, 0, TOP), (last, tail + TOP, rows - TOP, TOP)]
        for p, first, start, size in spans:
            span = slice(GUARD + start, GUARD + start + size)
            cross, pair = from_cross[k, first : first + size, :], from_pair[k, first : first + size, :]
            from_left = group_of(cross, False) == p
            both = roll(jnp.where(from_left == even, cross, pair), -p * HALO)
            lane = lane_of(both)
            outside = (lane < HALO) | (lane >= LANES - HALO)
            frame[0, span, :] = jnp.where(outside, both, frame[0, span, :])
    descend_all(rows, sources, frame_guess, weights, states, diagonals, field, resid, 4 * CHUNK, 2 * CHUNK)

    level = LEVELS - 1
    step, halo, height = 2**level, TOP >> level, rows >> level
    for body, frame, ring in (
        (body_weight, weights[level], ring_weight),
        (body_source, sources[level], ring_source),
    ):
        middle = load(body, 0, height)
        around = load(frame, 0, height)[0]
        lane = lane_of(around)
        ahead, back = roll(around, HALO), roll(around, -HALO)
        store(
            ring,
            0,
            height,
            [
                jnp.where(lane < 2 * step, back, middle[0]),
                jnp.where(lane >= LANES - 2 * step, ahead, middle[1]),
                jnp.where(lane < LANES // 2, ahead, back),
            ],
        )
    descend(
        level,
        height,
        ring_weight,
        ring_source,
        None,
        ring_state,
        ring_diagonal,
        ring_field,
        ring_resid,
        None,
        None,
        height,
        height,
    )

    coarse_rows = (height - 2 * halo) // 2
    dense = jnp.zeros((8, LANES), jnp.float32)
    lane = lane_of(dense)
    per_tile = LANES // 2**LEVELS
    pooled_b = pool_rows(ring_resid, halo, 2 * coarse_rows, step)
    pooled_w = pool_rows(ring_weight, halo, 2 * coarse_rows, step)
    index = (lane % per_tile) * 2**LEVELS
    place = lane // per_tile
    for g in range(coarse_rows // 8):
        for group, (values, factor) in enumerate(((pooled_b, 0.25), (pooled_w, 0.125))):
            for t in range(2):
                taken = jnp.take_along_axis(factor * values[t][8 * g : 8 * g + 8], index, axis=1)
                dense = jnp.where(place == 4 * g + 2 * group + t, taken, dense)
    dense_ref[...] = dense

    width = 2 * per_tile
    index = jnp.minimum(2 * (lane - lane % width) + lane % width, LANES - 1)
    smooth = ring_state[3]
    beside_me = []
    for tile, edge, free in ((0, 0, width - 2), (1, LANES - step, 0)):
        chunk = jnp.take_along_axis(dense, index, axis=1)
        first = GUARD + halo
        pieces = []
        for g in range(coarse_rows // 8):
            for odd in range(2):
                rows_of = smooth[tile, pl.ds(first + 16 * g + odd, 8, stride=2), :]
                pieces.append((g * width + free + odd, rows_of))
        for place, values in pieces:
            chunk = jnp.where(lane == place, roll(values, place - edge), chunk)
        beside_me.append(fold(chunk))
    sublane = lax.broadcasted_iota(jnp.int32, dense.shape, 0)
    beyond = []
    for row, group, free in ((0, 1, 6), (2 * coarse_rows - 1, 2, 0)):
        chunk = dense
        for tile in range(2):
            values = jnp.broadcast_to(smooth[tile, GUARD + halo + row : GUARD + halo + row + 1, :], dense.shape)
            values = jnp.take_along_axis(values, (lane % width) * step, axis=1)
            here = (sublane == free + tile) & (lane // width == 2 * group)
            chunk = jnp.where(here, values, chunk)
        beyond.append(chunk)
    above, below = fold(beyond[0]), fold(roll(beyond[1], -LANES // 2))
    x, y = lax.axis_index("gx"), lax.axis_index("gy")
    for i in range(chunks_ref.shape[0]):
        for j in range(chunks_ref.shape[1]):
            level_with = jnp.where(j < y, beside_me[0], beside_me[1])
            chunks_ref[i, j] = jnp.where(i == x, level_with, jnp.where(i < x, above, below))


def fold(x):
    return jnp.where(lane_of(x) < LANES // 2, x, pltpu.roll(roll(x, LANES // 2), 4, 0))[:4]


def unfold(x):
    return jnp.concatenate((x, roll(x, LANES // 2)), axis=0)


def coarse_solve(all_ref, dense_ref, from_cross, from_pair, e_ref, edge_ref, smooth_ref, rows, width, groups):
    x, nx = lax.axis_index("gx"), lax.axis_size("gx")
    y, ny = lax.axis_index("gy"), lax.axis_size("gy")
    tiles = {}
    for dx in (-1, 0, 1):
        for dy in (-1, 0, 1):
            if dx or dy:
                inside = (x + dx >= 0) & (x + dx < nx) & (y + dy >= 0) & (y + dy < ny)
                tile = unfold(all_ref[jnp.where(inside, x + dx, 0), jnp.where(inside, y + dy, 0)])
                tiles[dx, dy] = jnp.where(inside, tile, 0.0)
    dense = dense_ref[...]
    lane = lane_of(dense)
    even = y % 2 == 0
    half = 4 * groups
    first = rows % from_cross.shape[1] + 2 * TOP
    cross, pair = ([ref[k, first : first + half, :] for k in range(2)] for ref in (from_cross, from_pair))
    cross, pair = jnp.concatenate(cross, axis=0), jnp.concatenate(pair, axis=0)
    weights = {-1: jnp.where(even, cross, pair), 1: jnp.where(even, pair, cross)}
    bands = [(-1, g) for g in range(TALL // 8)] + [(0, g) for g in range(groups)] + [(1, g) for g in range(TALL // 8)]
    b, w = [], []
    for dx, g in bands:
        b_rows = w_rows = jnp.zeros_like(dense)
        for dy in (-1, 0, 1):
            first_lane = (dy + 1) * width
            here = (lane >= first_lane) & (lane < first_lane + width)
            if dx or not dy:
                tile = tiles[dx, dy] if dx else dense
                b_part = roll(tile, first_lane - 2 * g * width)
                w_part = roll(tile, first_lane - (2 * g + 1) * width)
            else:
                b_part = roll(tiles[dx, dy], first_lane - g * width)
                at = (PIECES - 1 - (dy > 0)) * HALO
                w_part = roll(weights[dy][8 * g : 8 * g + 8], first_lane - at)
            b_rows = jnp.where(here, b_part, b_rows)
            w_rows = jnp.where(here, w_part, w_rows)
        b.append(b_rows)
        w.append(w_rows)
    b, w = jnp.concatenate(b, axis=0), jnp.concatenate(w, axis=0)

    step = 2 ** (LEVELS - 1)
    start = GUARD + (TOP >> (LEVELS - 1))
    for t in range(2):
        edge_ref[t] = smooth_ref[t]
    edge_ref[2] = jnp.zeros_like(edge_ref[2])

    def columns(place):
        left = roll(tiles[0, -1], LANES - step - place)
        right = roll(tiles[0, 1], -(place + width - 2))
        return jnp.where(lane < step, right, left)

    for g in range(groups):
        for odd in range(2):
            edge_ref[2, pl.ds(start + 16 * g + odd, 8, stride=2), :] = columns(g * width + odd)
    for dx, row, lanes, free in ((-1, start - 1, 0, 0), (1, start + 16 * groups, 2 * width, 6)):
        for t in range(2):
            values = tiles[dx, 0][free + t : free + t + 1]
            values = jnp.take_along_axis(
                jnp.broadcast_to(values, dense.shape), lanes + lane // step, axis=1
            )
            edge_ref[t, row : row + 1, :] = values[:1]
        left = roll(tiles[dx, -1][free + 1 : free + 2], LANES - step - (lanes + width - 1))
        right = roll(tiles[dx, 1][free : free + 1], -lanes)
        edge_ref[2, row : row + 1, :] = jnp.where(lane[:1] < step, right, left)

    tall = b.shape[0]
    zeros = jnp.zeros((GUARD, LANES), jnp.float32)
    e_ref[0:GUARD, :] = zeros
    e_ref[GUARD + tall :, :] = zeros

    def shifted(by):
        return e_ref[GUARD + by : GUARD + by + tall, :]

    e_ref[GUARD : GUARD + tall, :] = w
    c_west = jnp.minimum(w, roll(w, 1))
    c_north, c_south = jnp.minimum(w, shifted(-1)), jnp.minimum(w, shifted(1))
    c_east = roll(c_west, -1)
    scale = relaxation / (damping + c_north + c_south + c_west + c_east)
    first = scale * b
    c_west, c_east, c_north, c_south = (scale * c for c in (c_west, c_east, c_north, c_south))
    e_ref[GUARD : GUARD + tall, :] = first

    def sweep(_, e):
        own = ((1.0 - relaxation) * e + first) + (c_north * shifted(-1) + c_south * shifted(1))
        e = (own + c_west * roll(e, 1)) + c_east * roll(e, -1)
        e_ref[GUARD : GUARD + tall, :] = e
        return e

    return lax.fori_loop(0, SWEEPS - 1, sweep, first)


def up_kernel(all_ref, dense_ref, from_cross, from_pair, own_source, frame_source, own_diagonal, frame_diagonal, *refs):
    count = 4 * (LEVELS - 1)
    body_state, frame_state, ring_state = refs[:count], refs[count : 2 * count], refs[2 * count : 2 * count + 4]
    out_ref, resid_ref = refs[2 * count + 4 : 2 * count + 6]
    ring_pe, body_final, frame_final, sems, e_ref, edge_ref, *inner = refs[2 * count + 6 :]
    outs, inner = inner[:2], inner[2:]
    body_pe, frame_pe = inner[: LEVELS - 1], inner[LEVELS - 1 :]
    rows = out_ref.shape[0] + 2 * TOP
    width = out_ref.shape[1] >> LEVELS
    e = coarse_solve(all_ref, dense_ref, from_cross, from_pair, e_ref, edge_ref, ring_state[3], out_ref.shape[0], width, (out_ref.shape[0] >> LEVELS) // 8)

    level = LEVELS - 1
    step, halo, height = 2**level, TOP >> level, rows >> level
    coarse_rows = (height - 2 * halo) // 2
    picked = e[TALL - 8 : TALL + coarse_rows + 8]
    lane = lane_of(picked)
    for t in range(3):
        group = (lane + t * LANES) // 2**LEVELS
        if t == 2:
            group = jnp.where(lane < LANES // 2, group, group - 3 * LANES // 2**LEVELS)
        taken = jnp.take_along_axis(picked, jnp.clip(group + width, 0, LANES - 1), axis=1)[7 : 7 + coarse_rows + 2]
        ring_pe[t, 0 : 2 * GUARD, :] = jnp.zeros((2 * GUARD, LANES), jnp.float32)
        ring_pe[t, height : height + 2 * GUARD, :] = jnp.zeros((2 * GUARD, LANES), jnp.float32)
        ring_pe[t, pl.ds(GUARD + halo - 2, coarse_rows + 2, stride=2), :] = taken
        ring_pe[t, pl.ds(GUARD + halo - 1, coarse_rows + 2, stride=2), :] = taken

    def climbed(pe, state, start, size, step, edge=None):
        mid, around = beside_of(pe, state[:2], start, size, step)
        scale, smooth = load(state[2], start, size), load(state[3], start, size)
        if edge is not None:
            smooth = load(edge, start, size)
        return [(smooth[t] + (1.0 - relaxation) * mid[t]) + scale[t] * around[t] for t in range(len(mid))]

    def climb_ring(start, size, level=level, step=step):
        ring = spread(climbed(ring_pe, ring_state, start, size, step, edge_ref), step // 2)
        lane = lane_of(ring[0])
        around = jnp.where(
            lane < LANES // 2,
            jnp.where(lane < HALO, roll(ring[2], HALO), roll(ring[0], HALO)),
            jnp.where(lane < LANES - HALO, roll(ring[1], -HALO), roll(ring[2], -HALO)),
        )
        store_twice(body_pe[level - 1], start, size, ring[:2])
        store_twice(frame_pe[level - 1], start, size, [around])

    for_chunks(height, climb_ring, height, height)

    for level in range(LEVELS - 2, -1, -1):
        step, height = 2**level, rows >> level
        groups = ((body_pe, body_state, body_final), (frame_pe, frame_state, frame_final))
        for pes, _, _ in groups:
            clear_guards(pes[level], height)

        def climb(start, size, level=level, step=step, groups=groups):
            for pes, states, final in groups:
                value = climbed(pes[level], states[4 * level : 4 * level + 4], start, size, step)
                if level == 0:
                    store(final, start, size, value)
                else:
                    store_twice(pes[level - 1], start, size, spread(value, step // 2))

        if level > 0:
            for_chunks(height, climb, 2 * CHUNK, PART)

    def last(base, size):
        body, around = beside_of(body_final, body_state[:2], base, size, 1)
        frame, frame_around = beside_of(frame_final, frame_state[:2], base, size, 1)
        b, d = load(own_source, base, size), load(own_diagonal, base, size)
        b_frame, d_frame = load(frame_source, base, size), load(frame_diagonal, base, size)
        body = (body, [(b[t] + around[t]) - d[t] * body[t] for t in range(2)])
        frame = (frame[0], (b_frame[0] + frame_around[0]) - d_frame[0] * frame[0])
        lane = lane_of(frame[0])
        span = pl.ds(base, size)
        for ref, middle, around in ((outs[0], body[0], frame[0]), (outs[1], body[1], frame[1])):
            ref[span, :LANES] = jnp.where(lane < NEAR, roll(around, -HALO), middle[0])
            ref[span, LANES:] = jnp.where(lane >= LANES - NEAR, roll(around, HALO), middle[1])

    size = 2 * CHUNK
    count = rows // size
    ends = [0] + [size * (p + 1) - LAG - TOP for p in range(count - 1)] + [out_ref.shape[0]]

    def copies(p):
        middle = (ends[p] + ends[p + 1]) // 16 * 8
        return [
            pltpu.make_async_copy(
                outs[k].at[pl.ds(TOP + first, last - first)],
                ref.at[pl.ds(first, last - first)],
                sems.at[4 * p + 2 * h + k],
            )
            for h, (first, last) in enumerate(((ends[p], middle), (middle, ends[p + 1])))
            for k, ref in enumerate((out_ref, resid_ref))
        ]

    def finish(i, carry):
        for_parts(i * size, size, climb, PART)
        base = pl.multiple_of(jnp.maximum(i * size - LAG, 0), 8)
        for_parts(base, size, last, PART)
        for p in range(count):

            @pl.when(i == p)
            def _(p=p):
                for copy in copies(p):
                    copy.start()

        return carry

    lax.fori_loop(0, count, finish, 0)
    for p in range(count):
        for copy in copies(p):
            copy.wait()


def call(kernel, out_shape, scratch, flops, moved, **more):
    return pl.pallas_call(
        kernel,
        out_shape=out_shape,
        scratch_shapes=scratch,
        compiler_params=pltpu.CompilerParams(vmem_limit_bytes=VMEM_LIMIT),
        cost_estimate=pl.CostEstimate(flops=flops, bytes_accessed=moved, transcendentals=0),
        **more,
    )


def swap(x, axis, first):
    pairs = [(i, i + 1) for i in range(first, lax.axis_size(axis) - 1, 2)]
    return lax.ppermute(x, axis, pairs + [(j, i) for i, j in pairs])


def local(rhs, pressure, wet_mask, bathy_class):
    rows, columns = rhs.shape
    cells = rows * columns
    total = rows + 2 * TOP
    levels = range(LEVELS - 1)

    def shape(tiles, level):
        return (tiles, (total >> level) + 2 * GUARD, LANES)

    def out(*dims):
        return jax.ShapeDtypeStruct(dims, jnp.float32)

    def vmem(tiles, level):
        return pltpu.VMEM(shape(tiles, level), jnp.float32)

    def fields(r, p, m, c):
        wet = m.astype(jnp.float32)
        return wet * r, wet * p, wet * (1.0 + 0.5 * c.astype(jnp.float32))

    given = (rhs, pressure, wet_mask, bathy_class)

    def edge(start):
        return jnp.stack(fields(*(lax.dynamic_slice_in_dim(x, start, TOP, axis=0) for x in given)))

    even = lax.axis_index("gx") % 2 == 0
    first_rows = swap(edge(jnp.where(even, 0, rows - TOP)), "gx", 1)
    second_rows = swap(edge(jnp.where(even, rows - TOP, 0)), "gx", 0)
    piece = -(-(rows + 2 * TOP + (rows >> LEVELS) // 2) // (8 * PIECES)) * 8
    own_shapes = [out(*shape(2, 0))] * 3
    laid_out = [*own_shapes, *[out(*shape(1, 0))] * 3, out(3, piece, LANES), out(3, piece, LANES)]
    inner = [vmem(2, level) for level in range(1, LEVELS)]
    begun = call(layout_kernel, laid_out, inner, 10 * cells, 10 * cells)(*fields(*given))
    *own, to_cross, to_pair = call(
        halo_kernel, laid_out, (), cells, cells, input_output_aliases={k: k for k in range(8)}
    )(*begun, first_rows, second_rows)
    own, frames = own[:3], own[3:]
    from_pair = swap(to_pair, "gy", 0)
    from_cross = swap(to_cross, "gy", 1)

    state_count = 4 * (LEVELS - 1)
    *body_state, body_weight, body_source, diagonal = call(
        body_kernel,
        [out(*shape(2, level)) for level in levels for _ in range(4)]
        + [out(*shape(2, LEVELS - 1))] * 2
        + [out(*shape(2, 0))],
        [vmem(2, 0)] * 3 + [vmem(2, level) for level in levels[1:]] * 3,
        100 * cells,
        40 * cells,
    )(*own)
    nx, ny = lax.axis_size("gx"), lax.axis_size("gy")
    ring = LEVELS - 1
    frame_source, _, _, *state, dense, chunks = call(
        frame_kernel,
        [out(*shape(1, 0))] * 3
        + [out(*shape(1, level)) for level in levels for _ in range(4)]
        + [out(*shape(1, 0))]
        + [out(*shape(3, ring))] * 4
        + [out(8, LANES), out(nx, ny, 4, LANES)],
        [vmem(1, 0)] * 2 + [vmem(3, ring)] * 5 + [vmem(1, level) for level in range(1, LEVELS)] * 3,
        50 * cells,
        20 * cells,
        input_output_aliases={k: k for k in range(3)},
    )(*frames, from_pair, from_cross, body_weight, body_source)
    frame_state, frame_diagonal, ring_state = state[:state_count], state[state_count], state[state_count + 1 :]
    gathered = lax.all_to_all(chunks.reshape(nx * ny, 4, LANES), ("gx", "gy"), 0, 0).reshape(chunks.shape)
    return call(
        up_kernel,
        (out(rows, columns), out(rows, columns)),
        [vmem(3, ring), vmem(2, 0), vmem(1, 0), pltpu.SemaphoreType.DMA((8,))]
        + [pltpu.VMEM(((rows >> LEVELS) + 2 * TALL + 2 * GUARD, LANES), jnp.float32), vmem(3, ring)]
        + [pltpu.VMEM((total, columns), jnp.float32)] * 2
        + [vmem(2, level) for level in levels]
        + [vmem(1, level) for level in levels],
        60 * cells,
        40 * cells,
        out_specs=[pl.BlockSpec(memory_space=pl.ANY)] * 2,
    )(gathered, dense, from_cross, from_pair, own[0], frame_source, diagonal, frame_diagonal, *body_state, *frame_state, *ring_state)


def solution(mesh):
    placed = (P("gx", "gy"), P("gx", "gy"), P("gx", "gy"), P("gx", "gy"))
    return jax.shard_map(
        local, mesh=mesh, in_specs=placed, out_specs=(P("gx", "gy"), P("gx", "gy")), check_vma=False
    )
```

```python
import jax
import jax.numpy as jnp
from jax import lax
from jax.experimental import pallas as pl
from jax.experimental.pallas import tpu as pltpu
from jax.sharding import PartitionSpec as P

LEVELS = 4
SWEEPS = 12

damping = 0.01
relaxation = 0.8

HALO = 16
NEAR = 20
LANES = 128
INNER = LANES // 2 - HALO
TOP = 16
GUARD = 8
PIECES = 8
CHUNK = 136
PART = CHUNK
LAG = 8
TALL = 16
VMEM_LIMIT = 40 * 1024 * 1024


def lane_of(x):
    return lax.broadcasted_iota(jnp.int32, x.shape, x.ndim - 1)


def roll(x, amount):
    amount %= LANES
    return x if amount == 0 else pltpu.roll(x, amount, x.ndim - 1)


def from_west(tiles, step):
    moved = [roll(t, step) for t in tiles]
    if len(tiles) == 1:
        return moved
    edge = lane_of(tiles[0]) < step
    return [jnp.where(edge, moved[i - 1], moved[i]) for i in range(len(tiles))]


def from_east(tiles, step):
    moved = [roll(t, -step) for t in tiles]
    count = len(tiles)
    if count == 1:
        return moved
    edge = lane_of(tiles[0]) >= LANES - step
    return [jnp.where(edge, moved[(i + 1) % count], moved[i]) for i in range(count)]


def spread(tiles, step):
    second = (lane_of(tiles[0]) // step) % 2 == 1
    return [jnp.where(second, roll(t, step), t) for t in tiles]


def for_parts(start, size, body, part):
    for offset in range(0, size, part):
        body(start + offset, min(part, size - offset))


def for_chunks(rows, body, largest, part):
    sizes = [size for size in range(8, largest + 1, 8) if rows % size == 0]
    if rows <= largest or not sizes:
        for_parts(0, rows, body, part)
        return

    def step(i, carry):
        for_parts(i * sizes[-1], sizes[-1], body, part)
        return carry

    lax.fori_loop(0, rows // sizes[-1], step, 0)


def load(ref, start, size):
    return [ref[t, pl.ds(GUARD + start, size), :] for t in range(ref.shape[0])]


def store(ref, start, size, tiles):
    for t, tile in enumerate(tiles):
        ref[t, pl.ds(GUARD + start, size), :] = tile


def store_twice(ref, start, size, tiles):
    for t, tile in enumerate(tiles):
        ref[t, pl.ds(GUARD + 2 * start, size, stride=2), :] = tile
        ref[t, pl.ds(GUARD + 2 * start + 1, size, stride=2), :] = tile


def clear_guards(ref, rows):
    zeros = jnp.zeros((GUARD, LANES), jnp.float32)
    for t in range(ref.shape[0]):
        ref[t, 0:GUARD, :] = zeros
        ref[t, GUARD + rows : 2 * GUARD + rows, :] = zeros


def beside(mid, north, south, c_west, c_north, c_south, step):
    west = from_west(mid, step)
    east = from_east([c * m for c, m in zip(c_west, mid)], step)
    return [
        (c_west[t] * west[t] + east[t]) + (c_north[t] * north[t] + c_south[t] * south[t]) for t in range(len(mid))
    ]


def beside_of(ref, coeffs, start, size, step):
    c_west_ref, c_north_ref = coeffs
    mid = load(ref, start, size)
    north, south = load(ref, start - 1, size), load(ref, start + 1, size)
    c_west, c_north = load(c_west_ref, start, size), load(c_north_ref, start, size)
    return mid, beside(mid, north, south, c_west, c_north, load(c_north_ref, start + 1, size), step)


def pool_rows(ref, start, size, step):
    out = []
    for t in range(ref.shape[0]):
        even = ref[t, pl.ds(GUARD + start, size // 2, stride=2), :]
        odd = ref[t, pl.ds(GUARD + start + 1, size // 2, stride=2), :]
        both = even + odd
        out.append(both + roll(both, -step))
    return out


def descend(level, height, weight, source, guess, state, diagonal_ref, field, resid, next_weight, next_source, largest, part):
    step = 2**level
    c_west_ref, c_north_ref, scale_ref, smooth_ref = state
    for ref in (weight, field, c_north_ref):
        clear_guards(ref, height)

    def first_pass(start, size):
        w, w_north, w_south = (load(weight, start + k, size) for k in (0, -1, 1))
        c_north = [jnp.minimum(a, b) for a, b in zip(w, w_north)]
        c_south = [jnp.minimum(a, b) for a, b in zip(w, w_south)]
        c_west = [jnp.minimum(a, b) for a, b in zip(w, from_west(w, step))]
        c_east = from_east(c_west, step)
        diagonal = [damping + c_north[t] + c_south[t] + c_west[t] + c_east[t] for t in range(len(w))]
        scale = [relaxation / d for d in diagonal]
        store(c_north_ref, start, size, c_north)
        store(c_west_ref, start, size, c_west)
        store(scale_ref, start, size, scale)
        store(diagonal_ref, start, size, diagonal)
        value = load(source, start, size)
        if guess is None:
            value = [scale[t] * value[t] for t in range(len(w))]
        else:
            mid, north, south = (load(guess, start + k, size) for k in (0, -1, 1))
            around = beside(mid, north, south, c_west, c_north, c_south, step)
            value = [
                (1.0 - relaxation) * mid[t] + scale[t] * (value[t] + around[t]) for t in range(len(w))
            ]
        store(field, start, size, value)
        if next_weight is not None:
            pooled = [0.125 * p for p in pool_rows(weight, start, size, step)]
            store(next_weight, start // 2, size // 2, pooled)

    def second_pass(start, size):
        mid, around = beside_of(field, (c_west_ref, c_north_ref), start, size, step)
        b, scale, diagonal = (load(ref, start, size) for ref in (source, scale_ref, diagonal_ref))
        rest = [(b[t] + around[t]) - diagonal[t] * mid[t] for t in range(len(b))]
        store(smooth_ref, start, size, [mid[t] + scale[t] * rest[t] for t in range(len(b))])
        store(resid, start, size, rest)
        if next_source is not None:
            pooled = [0.25 * p for p in pool_rows(resid, start, size, step)]
            store(next_source, start // 2, size // 2, pooled)

    for_chunks(height, first_pass, largest, part)
    for_chunks(height, second_pass, largest, part)


def descend_all(rows, sources, guess, weights, states, diagonal, field, resid, largest, part):
    for level in range(LEVELS - 1):
        descend(
            level,
            rows >> level,
            weights[level],
            sources[level],
            guess if level == 0 else None,
            states[4 * level : 4 * level + 4],
            diagonal[level],
            field,
            resid,
            weights[level + 1],
            sources[level + 1],
            largest,
            part,
        )


def group_of(x, west):
    return (lane_of(x) // HALO + (1 if west else 0)) % PIECES


def packed(part, p, west):
    return roll(part, p * HALO - HALO if west else p * HALO + HALO)


def to_sides(west, east, cross_ref, pair_ref, k, rows):
    even = lax.axis_index("gy") % 2 == 0
    cross_ref[k, rows, :] = jnp.where(even, west, east)
    pair_ref[k, rows, :] = jnp.where(even, east, west)


def inner_columns(tiles):
    return jnp.where(lane_of(tiles[0]) < LANES // 2, roll(tiles[0], HALO), roll(tiles[1], -HALO))


def layout_kernel(source, guess, weight, *refs):
    owns, frames, (cross_ref, pair_ref, *inner) = refs[:3], refs[3:6], refs[6:]
    rows = source.shape[0]
    piece = cross_ref.shape[1]
    whole = rows // piece
    tail = rows - whole * piece
    for own, frame, block in zip(owns, frames, (source, guess, weight)):
        clear_guards(own, rows + 2 * TOP)
        clear_guards(frame, rows + 2 * TOP)
        tiles = [block[:, t * LANES : (t + 1) * LANES] for t in range(2)]
        for t in range(2):
            own[t, GUARD + TOP : GUARD + TOP + rows, :] = tiles[t]
        frame[0, GUARD + TOP : GUARD + TOP + rows, :] = inner_columns(tiles)
    weights, start, height = (owns[2], *inner), TOP, rows
    for level in range(LEVELS):
        pooled = [0.125 * w for w in pool_rows(weights[level], start, height, 2**level)]
        start, height = start // 2, height // 2
        if level < LEVELS - 1:
            store(weights[level + 1], start, height, pooled)
    lane = lane_of(pooled[0])
    width = HALO // 2
    index = (lane % width) * 2**LEVELS
    coarse = [jnp.take_along_axis(p, index, axis=1) for p in pooled]
    coarse = jnp.where(lane % HALO < width, *coarse)
    for k, block in enumerate((source, guess, weight)):
        sides = []
        for west in (True, False):
            columns = slice(0, LANES) if west else slice(LANES, 2 * LANES)
            below = jnp.zeros((piece - tail, LANES), jnp.float32)
            if k < 2:
                half = coarse[k * height // 2 : (k + 1) * height // 2]
                below = jnp.concatenate((below[: 2 * TOP], half, below[2 * TOP + height // 2 :]), axis=0)
            last = packed(block[whole * piece :, columns], whole, west)
            both = jnp.concatenate((last, below), axis=0)
            for p in range(whole):
                part = packed(block[p * piece : (p + 1) * piece, columns], p, west)
                both = jnp.where(group_of(part, west) == p, part, both)
            sides.append(both)
        to_sides(*sides, cross_ref, pair_ref, k, slice(0, piece))


def halo_kernel(*refs):
    first_rows, second_rows, *own, cross_ref, pair_ref = refs[8:]
    own, frames = own[:3], own[3:]
    total = own[0].shape[1] - 2 * GUARD
    last = PIECES - 1
    first = total - 2 * TOP - last * cross_ref.shape[1]
    even, even_y = lax.axis_index("gx") % 2 == 0, lax.axis_index("gy") % 2 == 0
    for k in range(3):
        above = jnp.where(even, first_rows[k], second_rows[k])
        below = jnp.where(even, second_rows[k], first_rows[k])
        for side, (rows, row) in enumerate(((above, 0), (below, total - TOP))):
            body = [rows[:, t * LANES : (t + 1) * LANES] for t in range(2)]
            for t in range(2):
                own[k][t, GUARD + row : GUARD + row + TOP, :] = body[t]
            frames[k][0, GUARD + row : GUARD + row + TOP, :] = inner_columns(body)
            span = slice(first + side * TOP, first + (side + 1) * TOP)
            parts = []
            for part, west in zip(body, (True, False)):
                here = group_of(part, west) == last
                parts.append((here, packed(part, last, west)))
            (here_west, west), (here_east, east) = parts
            cross, pair = cross_ref[k, span, :], pair_ref[k, span, :]
            cross_ref[k, span, :] = jnp.where(
                even_y, jnp.where(here_west, west, cross), jnp.where(here_east, east, cross)
            )
            pair_ref[k, span, :] = jnp.where(
                even_y, jnp.where(here_east, east, pair), jnp.where(here_west, west, pair)
            )


def body_kernel(source, guess, weight, *refs):
    states = refs[: 4 * (LEVELS - 1)]
    last_weight, last_source, first_diagonal, *refs = refs[4 * (LEVELS - 1) :]
    field, resid, weight_in, *inner = refs
    rows = source.shape[1] - 2 * GUARD
    depth = LEVELS - 2
    weights = (weight_in, *inner[:depth], last_weight)
    sources = (source, *inner[depth : 2 * depth], last_source)
    diagonal = (first_diagonal, *inner[2 * depth :])
    weights[0][...] = weight[...]
    descend_all(rows, sources, guess, weights, states, diagonal, field, resid, 2 * CHUNK, CHUNK)


def frame_kernel(_a, _b, _c, from_pair, from_cross, body_weight, body_source, *refs):
    even = lax.axis_index("gy") % 2 == 0
    frames, states, refs = refs[:3], refs[3 : 3 + 4 * (LEVELS - 1)], refs[3 + 4 * (LEVELS - 1) :]
    frame_source, frame_guess, frame_weight = frames
    first_diagonal, ring_state, dense_ref, chunks_ref, field, resid, *refs = refs[0], refs[1:5], *refs[5:]
    ring_weight, ring_source, ring_field, ring_resid, ring_diagonal, *inner = refs
    rows = frame_source.shape[1] - 2 * GUARD
    depth = LEVELS - 1
    weights = (frame_weight, *inner[:depth])
    sources = (frame_source, *inner[depth : 2 * depth])
    diagonals = (first_diagonal, *inner[2 * depth :])
    piece = from_cross.shape[1]
    for k, frame in enumerate(frames):
        block = rows - 2 * TOP
        last = PIECES - 1
        tail = block - last * piece
        spans = [(p, 0, TOP + p * piece, piece) for p in range(last)]
        spans += [(last, 0, TOP + last * piece, tail)]
        spans += [(last, tail, 0, TOP), (last, tail + TOP, rows - TOP, TOP)]
        for p, first, start, size in spans:
            span = slice(GUARD + start, GUARD + start + size)
            cross, pair = from_cross[k, first : first + size, :], from_pair[k, first : first + size, :]
            from_left = group_of(cross, False) == p
            both = roll(jnp.where(from_left == even, cross, pair), -p * HALO)
            lane = lane_of(both)
            outside = (lane < HALO) | (lane >= LANES - HALO)
            frame[0, span, :] = jnp.where(outside, both, frame[0, span, :])
    descend_all(rows, sources, frame_guess, weights, states, diagonals, field, resid, 4 * CHUNK, 2 * CHUNK)

    level = LEVELS - 1
    step, halo, height = 2**level, TOP >> level, rows >> level
    for body, frame, ring in (
        (body_weight, weights[level], ring_weight),
        (body_source, sources[level], ring_source),
    ):
        middle = load(body, 0, height)
        around = load(frame, 0, height)[0]
        lane = lane_of(around)
        ahead, back = roll(around, HALO), roll(around, -HALO)
        store(
            ring,
            0,
            height,
            [
                jnp.where(lane < 2 * step, back, middle[0]),
                jnp.where(lane >= LANES - 2 * step, ahead, middle[1]),
                jnp.where(lane < LANES // 2, ahead, back),
            ],
        )
    descend(
        level,
        height,
        ring_weight,
        ring_source,
        None,
        ring_state,
        ring_diagonal,
        ring_field,
        ring_resid,
        None,
        None,
        height,
        height,
    )

    coarse_rows = (height - 2 * halo) // 2
    dense = jnp.zeros((8, LANES), jnp.float32)
    lane = lane_of(dense)
    per_tile = LANES // 2**LEVELS
    pooled_b = pool_rows(ring_resid, halo, 2 * coarse_rows, step)
    pooled_w = pool_rows(ring_weight, halo, 2 * coarse_rows, step)
    index = (lane % per_tile) * 2**LEVELS
    place = lane // per_tile
    for g in range(coarse_rows // 8):
        for group, (values, factor) in enumerate(((pooled_b, 0.25), (pooled_w, 0.125))):
            for t in range(2):
                taken = jnp.take_along_axis(factor * values[t][8 * g : 8 * g + 8], index, axis=1)
                dense = jnp.where(place == 4 * g + 2 * group + t, taken, dense)
    dense_ref[...] = dense

    width = 2 * per_tile
    index = jnp.minimum(2 * (lane - lane % width) + lane % width, LANES - 1)
    smooth = ring_state[3]
    beside_me = []
    for tile, edge, free in ((0, 0, width - 2), (1, LANES - step, 0)):
        chunk = jnp.take_along_axis(dense, index, axis=1)
        first = GUARD + halo
        pieces = []
        for g in range(coarse_rows // 8):
            for odd in range(2):
                rows_of = smooth[tile, pl.ds(first + 16 * g + odd, 8, stride=2), :]
                pieces.append((g * width + free + odd, rows_of))
        for place, values in pieces:
            chunk = jnp.where(lane == place, roll(values, place - edge), chunk)
        beside_me.append(fold(chunk))
    sublane = lax.broadcasted_iota(jnp.int32, dense.shape, 0)
    beyond = []
    for row, group, free in ((0, 1, 6), (2 * coarse_rows - 1, 2, 0)):
        chunk = dense
        for tile in range(2):
            values = jnp.broadcast_to(smooth[tile, GUARD + halo + row : GUARD + halo + row + 1, :], dense.shape)
            values = jnp.take_along_axis(values, (lane % width) * step, axis=1)
            here = (sublane == free + tile) & (lane // width == 2 * group)
            chunk = jnp.where(here, values, chunk)
        beyond.append(chunk)
    above, below = fold(beyond[0]), fold(roll(beyond[1], -LANES // 2))
    x, y = lax.axis_index("gx"), lax.axis_index("gy")
    for i in range(chunks_ref.shape[0]):
        for j in range(chunks_ref.shape[1]):
            level_with = jnp.where(j < y, beside_me[0], beside_me[1])
            chunks_ref[i, j] = jnp.where(i == x, level_with, jnp.where(i < x, above, below))


def fold(x):
    return jnp.where(lane_of(x) < LANES // 2, x, pltpu.roll(roll(x, LANES // 2), 4, 0))[:4]


def unfold(x):
    return jnp.concatenate((x, roll(x, LANES // 2)), axis=0)


def coarse_solve(all_ref, dense_ref, from_cross, from_pair, e_ref, edge_ref, smooth_ref, rows, width, groups):
    x, nx = lax.axis_index("gx"), lax.axis_size("gx")
    y, ny = lax.axis_index("gy"), lax.axis_size("gy")
    tiles = {}
    for dx in (-1, 0, 1):
        for dy in (-1, 0, 1):
            if dx or dy:
                inside = (x + dx >= 0) & (x + dx < nx) & (y + dy >= 0) & (y + dy < ny)
                tile = unfold(all_ref[jnp.where(inside, x + dx, 0), jnp.where(inside, y + dy, 0)])
                tiles[dx, dy] = jnp.where(inside, tile, 0.0)
    dense = dense_ref[...]
    lane = lane_of(dense)
    even = y % 2 == 0
    half = 4 * groups
    first = rows % from_cross.shape[1] + 2 * TOP
    cross, pair = ([ref[k, first : first + half, :] for k in range(2)] for ref in (from_cross, from_pair))
    cross, pair = jnp.concatenate(cross, axis=0), jnp.concatenate(pair, axis=0)
    weights = {-1: jnp.where(even, cross, pair), 1: jnp.where(even, pair, cross)}
    bands = [(-1, g) for g in range(TALL // 8)] + [(0, g) for g in range(groups)] + [(1, g) for g in range(TALL // 8)]
    b, w = [], []
    for dx, g in bands:
        b_rows = w_rows = jnp.zeros_like(dense)
        for dy in (-1, 0, 1):
            first_lane = (dy + 1) * width
            here = (lane >= first_lane) & (lane < first_lane + width)
            if dx or not dy:
                tile = tiles[dx, dy] if dx else dense
                b_part = roll(tile, first_lane - 2 * g * width)
                w_part = roll(tile, first_lane - (2 * g + 1) * width)
            else:
                b_part = roll(tiles[dx, dy], first_lane - g * width)
                at = (PIECES - 1 - (dy > 0)) * HALO
                w_part = roll(weights[dy][8 * g : 8 * g + 8], first_lane - at)
            b_rows = jnp.where(here, b_part, b_rows)
            w_rows = jnp.where(here, w_part, w_rows)
        b.append(b_rows)
        w.append(w_rows)
    b, w = jnp.concatenate(b, axis=0), jnp.concatenate(w, axis=0)

    step = 2 ** (LEVELS - 1)
    start = GUARD + (TOP >> (LEVELS - 1))
    for t in range(2):
        edge_ref[t] = smooth_ref[t]
    edge_ref[2] = jnp.zeros_like(edge_ref[2])

    def columns(place):
        left = roll(tiles[0, -1], LANES - step - place)
        right = roll(tiles[0, 1], -(place + width - 2))
        return jnp.where(lane < step, right, left)

    for g in range(groups):
        for odd in range(2):
            edge_ref[2, pl.ds(start + 16 * g + odd, 8, stride=2), :] = columns(g * width + odd)
    for dx, row, lanes, free in ((-1, start - 1, 0, 0), (1, start + 16 * groups, 2 * width, 6)):
        for t in range(2):
            values = tiles[dx, 0][free + t : free + t + 1]
            values = jnp.take_along_axis(
                jnp.broadcast_to(values, dense.shape), lanes + lane // step, axis=1
            )
            edge_ref[t, row : row + 1, :] = values[:1]
        left = roll(tiles[dx, -1][free + 1 : free + 2], LANES - step - (lanes + width - 1))
        right = roll(tiles[dx, 1][free : free + 1], -lanes)
        edge_ref[2, row : row + 1, :] = jnp.where(lane[:1] < step, right, left)

    tall = b.shape[0]
    zeros = jnp.zeros((GUARD, LANES), jnp.float32)
    e_ref[0:GUARD, :] = zeros
    e_ref[GUARD + tall :, :] = zeros

    def shifted(by):
        return e_ref[GUARD + by : GUARD + by + tall, :]

    e_ref[GUARD : GUARD + tall, :] = w
    c_west = jnp.minimum(w, roll(w, 1))
    c_north, c_south = jnp.minimum(w, shifted(-1)), jnp.minimum(w, shifted(1))
    c_east = roll(c_west, -1)
    scale = relaxation / (damping + c_north + c_south + c_west + c_east)
    first = scale * b
    c_west, c_east, c_north, c_south = (scale * c for c in (c_west, c_east, c_north, c_south))
    e_ref[GUARD : GUARD + tall, :] = first

    def sweep(_, carry):
        e = shifted(0)
        around = (c_west * roll(e, 1) + c_east * roll(e, -1)) + (c_north * shifted(-1) + c_south * shifted(1))
        e_ref[GUARD : GUARD + tall, :] = ((1.0 - relaxation) * e + first) + around
        return carry

    lax.fori_loop(0, SWEEPS - 1, sweep, 0)
    return shifted(0)


def up_kernel(all_ref, dense_ref, from_cross, from_pair, own_source, frame_source, own_diagonal, frame_diagonal, *refs):
    count = 4 * (LEVELS - 1)
    body_state, frame_state, ring_state = refs[:count], refs[count : 2 * count], refs[2 * count : 2 * count + 4]
    out_ref, resid_ref = refs[2 * count + 4 : 2 * count + 6]
    ring_pe, body_final, frame_final, sems, e_ref, edge_ref, *inner = refs[2 * count + 6 :]
    outs, inner = inner[:2], inner[2:]
    body_pe, frame_pe = inner[: LEVELS - 1], inner[LEVELS - 1 :]
    rows = out_ref.shape[0] + 2 * TOP
    width = out_ref.shape[1] >> LEVELS
    e = coarse_solve(all_ref, dense_ref, from_cross, from_pair, e_ref, edge_ref, ring_state[3], out_ref.shape[0], width, (out_ref.shape[0] >> LEVELS) // 8)

    level = LEVELS - 1
    step, halo, height = 2**level, TOP >> level, rows >> level
    coarse_rows = (height - 2 * halo) // 2
    picked = e[TALL - 8 : TALL + coarse_rows + 8]
    lane = lane_of(picked)
    for t in range(3):
        group = (lane + t * LANES) // 2**LEVELS
        if t == 2:
            group = jnp.where(lane < LANES // 2, group, group - 3 * LANES // 2**LEVELS)
        taken = jnp.take_along_axis(picked, jnp.clip(group + width, 0, LANES - 1), axis=1)[7 : 7 + coarse_rows + 2]
        ring_pe[t, 0 : 2 * GUARD, :] = jnp.zeros((2 * GUARD, LANES), jnp.float32)
        ring_pe[t, height : height + 2 * GUARD, :] = jnp.zeros((2 * GUARD, LANES), jnp.float32)
        ring_pe[t, pl.ds(GUARD + halo - 2, coarse_rows + 2, stride=2), :] = taken
        ring_pe[t, pl.ds(GUARD + halo - 1, coarse_rows + 2, stride=2), :] = taken

    def climbed(pe, state, start, size, step, edge=None):
        mid, around = beside_of(pe, state[:2], start, size, step)
        scale, smooth = load(state[2], start, size), load(state[3], start, size)
        if edge is not None:
            smooth = load(edge, start, size)
        return [(smooth[t] + (1.0 - relaxation) * mid[t]) + scale[t] * around[t] for t in range(len(mid))]

    def climb_ring(start, size, level=level, step=step):
        ring = spread(climbed(ring_pe, ring_state, start, size, step, edge_ref), step // 2)
        lane = lane_of(ring[0])
        around = jnp.where(
            lane < LANES // 2,
            jnp.where(lane < HALO, roll(ring[2], HALO), roll(ring[0], HALO)),
            jnp.where(lane < LANES - HALO, roll(ring[1], -HALO), roll(ring[2], -HALO)),
        )
        store_twice(body_pe[level - 1], start, size, ring[:2])
        store_twice(frame_pe[level - 1], start, size, [around])

    for_chunks(height, climb_ring, height, height)

    for level in range(LEVELS - 2, -1, -1):
        step, height = 2**level, rows >> level
        groups = ((body_pe, body_state, body_final), (frame_pe, frame_state, frame_final))
        for pes, _, _ in groups:
            clear_guards(pes[level], height)

        def climb(start, size, level=level, step=step, groups=groups):
            for pes, states, final in groups:
                value = climbed(pes[level], states[4 * level : 4 * level + 4], start, size, step)
                if level == 0:
                    store(final, start, size, value)
                else:
                    store_twice(pes[level - 1], start, size, spread(value, step // 2))

        if level > 0:
            for_chunks(height, climb, 2 * CHUNK, PART)

    def last(base, size):
        body, around = beside_of(body_final, body_state[:2], base, size, 1)
        frame, frame_around = beside_of(frame_final, frame_state[:2], base, size, 1)
        b, d = load(own_source, base, size), load(own_diagonal, base, size)
        b_frame, d_frame = load(frame_source, base, size), load(frame_diagonal, base, size)
        body = (body, [(b[t] + around[t]) - d[t] * body[t] for t in range(2)])
        frame = (frame[0], (b_frame[0] + frame_around[0]) - d_frame[0] * frame[0])
        lane = lane_of(frame[0])
        span = pl.ds(base, size)
        for ref, middle, around in ((outs[0], body[0], frame[0]), (outs[1], body[1], frame[1])):
            ref[span, :LANES] = jnp.where(lane < NEAR, roll(around, -HALO), middle[0])
            ref[span, LANES:] = jnp.where(lane >= LANES - NEAR, roll(around, HALO), middle[1])

    count = rows // CHUNK
    ends = [0] + [CHUNK * (p + 1) - LAG - TOP for p in range(count - 1)] + [out_ref.shape[0]]

    def copies(p):
        middle = (ends[p] + ends[p + 1]) // 16 * 8
        return [
            pltpu.make_async_copy(
                outs[k].at[pl.ds(TOP + first, last - first)],
                ref.at[pl.ds(first, last - first)],
                sems.at[4 * p + 2 * h + k],
            )
            for h, (first, last) in enumerate(((ends[p], middle), (middle, ends[p + 1])))
            for k, ref in enumerate((out_ref, resid_ref))
        ]

    for p in range(count):
        climb(p * CHUNK, CHUNK)
        last(max(p * CHUNK - LAG, 0), CHUNK)
        for copy in copies(p):
            copy.start()
    for p in range(count):
        for copy in copies(p):
            copy.wait()


def call(kernel, out_shape, scratch, flops, moved, **more):
    return pl.pallas_call(
        kernel,
        out_shape=out_shape,
        scratch_shapes=scratch,
        compiler_params=pltpu.CompilerParams(vmem_limit_bytes=VMEM_LIMIT),
        cost_estimate=pl.CostEstimate(flops=flops, bytes_accessed=moved, transcendentals=0),
        **more,
    )


def swap(x, axis, first):
    pairs = [(i, i + 1) for i in range(first, lax.axis_size(axis) - 1, 2)]
    return lax.ppermute(x, axis, pairs + [(j, i) for i, j in pairs])


def local(rhs, pressure, wet_mask, bathy_class):
    rows, columns = rhs.shape
    cells = rows * columns
    total = rows + 2 * TOP
    levels = range(LEVELS - 1)

    def shape(tiles, level):
        return (tiles, (total >> level) + 2 * GUARD, LANES)

    def out(*dims):
        return jax.ShapeDtypeStruct(dims, jnp.float32)

    def vmem(tiles, level):
        return pltpu.VMEM(shape(tiles, level), jnp.float32)

    def fields(r, p, m, c):
        wet = m.astype(jnp.float32)
        return wet * r, wet * p, wet * (1.0 + 0.5 * c.astype(jnp.float32))

    given = (rhs, pressure, wet_mask, bathy_class)

    def edge(start):
        return jnp.stack(fields(*(lax.dynamic_slice_in_dim(x, start, TOP, axis=0) for x in given)))

    even = lax.axis_index("gx") % 2 == 0
    first_rows = swap(edge(jnp.where(even, 0, rows - TOP)), "gx", 1)
    second_rows = swap(edge(jnp.where(even, rows - TOP, 0)), "gx", 0)
    piece = -(-(rows + 2 * TOP + (rows >> LEVELS) // 2) // (8 * PIECES)) * 8
    own_shapes = [out(*shape(2, 0))] * 3
    laid_out = [*own_shapes, *[out(*shape(1, 0))] * 3, out(3, piece, LANES), out(3, piece, LANES)]
    inner = [vmem(2, level) for level in range(1, LEVELS)]
    begun = call(layout_kernel, laid_out, inner, 10 * cells, 10 * cells)(*fields(*given))
    *own, to_cross, to_pair = call(
        halo_kernel, laid_out, (), cells, cells, input_output_aliases={k: k for k in range(8)}
    )(*begun, first_rows, second_rows)
    own, frames = own[:3], own[3:]
    from_pair = swap(to_pair, "gy", 0)
    from_cross = swap(to_cross, "gy", 1)

    state_count = 4 * (LEVELS - 1)
    *body_state, body_weight, body_source, diagonal = call(
        body_kernel,
        [out(*shape(2, level)) for level in levels for _ in range(4)]
        + [out(*shape(2, LEVELS - 1))] * 2
        + [out(*shape(2, 0))],
        [vmem(2, 0)] * 3 + [vmem(2, level) for level in levels[1:]] * 3,
        100 * cells,
        40 * cells,
    )(*own)
    nx, ny = lax.axis_size("gx"), lax.axis_size("gy")
    ring = LEVELS - 1
    frame_source, _, _, *state, dense, chunks = call(
        frame_kernel,
        [out(*shape(1, 0))] * 3
        + [out(*shape(1, level)) for level in levels for _ in range(4)]
        + [out(*shape(1, 0))]
        + [out(*shape(3, ring))] * 4
        + [out(8, LANES), out(nx, ny, 4, LANES)],
        [vmem(1, 0)] * 2 + [vmem(3, ring)] * 5 + [vmem(1, level) for level in range(1, LEVELS)] * 3,
        50 * cells,
        20 * cells,
        input_output_aliases={k: k for k in range(3)},
    )(*frames, from_pair, from_cross, body_weight, body_source)
    frame_state, frame_diagonal, ring_state = state[:state_count], state[state_count], state[state_count + 1 :]
    gathered = lax.all_to_all(chunks.reshape(nx * ny, 4, LANES), ("gx", "gy"), 0, 0).reshape(chunks.shape)
    return call(
        up_kernel,
        (out(rows, columns), out(rows, columns)),
        [vmem(3, ring), vmem(2, 0), vmem(1, 0), pltpu.SemaphoreType.DMA((16,))]
        + [pltpu.VMEM(((rows >> LEVELS) + 2 * TALL + 2 * GUARD, LANES), jnp.float32), vmem(3, ring)]
        + [pltpu.VMEM((total, columns), jnp.float32)] * 2
        + [vmem(2, level) for level in levels]
        + [vmem(1, level) for level in levels],
        60 * cells,
        40 * cells,
        out_specs=[pl.BlockSpec(memory_space=pl.ANY)] * 2,
    )(gathered, dense, from_cross, from_pair, own[0], frame_source, diagonal, frame_diagonal, *body_state, *frame_state, *ring_state)


def solution(mesh):
    placed = (P("gx", "gy"), P("gx", "gy"), P("gx", "gy"), P("gx", "gy"))
    return jax.shard_map(
        local, mesh=mesh, in_specs=placed, out_specs=(P("gx", "gy"), P("gx", "gy")), check_vma=False
    )
```

```python
import jax
import jax.numpy as jnp
from jax import lax
from jax.experimental import pallas as pl
from jax.experimental.pallas import tpu as pltpu
from jax.sharding import PartitionSpec as P

LEVELS = 4
SWEEPS = 12

damping = 0.01
relaxation = 0.8

HALO = 16
NEAR = 20
LANES = 128
INNER = LANES // 2 - HALO
TOP = 16
GUARD = 8
PIECES = 8
CHUNK = 136
PART = CHUNK
LAG = 8
TALL = 16
VMEM_LIMIT = 40 * 1024 * 1024


def lane_of(x):
    return lax.broadcasted_iota(jnp.int32, x.shape, x.ndim - 1)


def roll(x, amount):
    amount %= LANES
    return x if amount == 0 else pltpu.roll(x, amount, x.ndim - 1)


def from_west(tiles, step):
    moved = [roll(t, step) for t in tiles]
    if len(tiles) == 1:
        return moved
    edge = lane_of(tiles[0]) < step
    return [jnp.where(edge, moved[i - 1], moved[i]) for i in range(len(tiles))]


def from_east(tiles, step):
    moved = [roll(t, -step) for t in tiles]
    count = len(tiles)
    if count == 1:
        return moved
    edge = lane_of(tiles[0]) >= LANES - step
    return [jnp.where(edge, moved[(i + 1) % count], moved[i]) for i in range(count)]


def spread(tiles, step):
    second = (lane_of(tiles[0]) // step) % 2 == 1
    return [jnp.where(second, roll(t, step), t) for t in tiles]


def for_parts(start, size, body, part):
    for offset in range(0, size, part):
        body(start + offset, min(part, size - offset))


def for_chunks(rows, body, largest, part):
    sizes = [size for size in range(8, largest + 1, 8) if rows % size == 0]
    if rows <= largest or not sizes:
        for_parts(0, rows, body, part)
        return

    def step(i, carry):
        for_parts(i * sizes[-1], sizes[-1], body, part)
        return carry

    lax.fori_loop(0, rows // sizes[-1], step, 0)


def load(ref, start, size):
    return [ref[t, pl.ds(GUARD + start, size), :] for t in range(ref.shape[0])]


def store(ref, start, size, tiles):
    for t, tile in enumerate(tiles):
        ref[t, pl.ds(GUARD + start, size), :] = tile


def store_twice(ref, start, size, tiles):
    for t, tile in enumerate(tiles):
        ref[t, pl.ds(GUARD + 2 * start, size, stride=2), :] = tile
        ref[t, pl.ds(GUARD + 2 * start + 1, size, stride=2), :] = tile


def clear_guards(ref, rows):
    zeros = jnp.zeros((GUARD, LANES), jnp.float32)
    for t in range(ref.shape[0]):
        ref[t, 0:GUARD, :] = zeros
        ref[t, GUARD + rows : 2 * GUARD + rows, :] = zeros


def beside(mid, north, south, c_west, c_north, c_south, step):
    west = from_west(mid, step)
    east = from_east([c * m for c, m in zip(c_west, mid)], step)
    return [
        (c_west[t] * west[t] + east[t]) + (c_north[t] * north[t] + c_south[t] * south[t]) for t in range(len(mid))
    ]


def beside_of(ref, coeffs, start, size, step):
    c_west_ref, c_north_ref = coeffs
    mid = load(ref, start, size)
    north, south = load(ref, start - 1, size), load(ref, start + 1, size)
    c_west, c_north = load(c_west_ref, start, size), load(c_north_ref, start, size)
    return mid, beside(mid, north, south, c_west, c_north, load(c_north_ref, start + 1, size), step)


def pool_rows(ref, start, size, step):
    out = []
    for t in range(ref.shape[0]):
        even = ref[t, pl.ds(GUARD + start, size // 2, stride=2), :]
        odd = ref[t, pl.ds(GUARD + start + 1, size // 2, stride=2), :]
        both = even + odd
        out.append(both + roll(both, -step))
    return out


def descend(level, height, weight, source, guess, state, diagonal_ref, field, resid, next_weight, next_source, largest, part):
    step = 2**level
    c_west_ref, c_north_ref, scale_ref, smooth_ref = state
    for ref in (weight, field, c_north_ref):
        clear_guards(ref, height)

    def first_pass(start, size):
        w, w_north, w_south = (load(weight, start + k, size) for k in (0, -1, 1))
        c_north = [jnp.minimum(a, b) for a, b in zip(w, w_north)]
        c_south = [jnp.minimum(a, b) for a, b in zip(w, w_south)]
        c_west = [jnp.minimum(a, b) for a, b in zip(w, from_west(w, step))]
        c_east = from_east(c_west, step)
        diagonal = [damping + c_north[t] + c_south[t] + c_west[t] + c_east[t] for t in range(len(w))]
        scale = [relaxation / d for d in diagonal]
        store(c_north_ref, start, size, c_north)
        store(c_west_ref, start, size, c_west)
        store(scale_ref, start, size, scale)
        store(diagonal_ref, start, size, diagonal)
        value = load(source, start, size)
        if guess is None:
            value = [scale[t] * value[t] for t in range(len(w))]
        else:
            mid, north, south = (load(guess, start + k, size) for k in (0, -1, 1))
            around = beside(mid, north, south, c_west, c_north, c_south, step)
            value = [
                (1.0 - relaxation) * mid[t] + scale[t] * (value[t] + around[t]) for t in range(len(w))
            ]
        store(field, start, size, value)
        if next_weight is not None:
            pooled = [0.125 * p for p in pool_rows(weight, start, size, step)]
            store(next_weight, start // 2, size // 2, pooled)

    def second_pass(start, size):
        mid, around = beside_of(field, (c_west_ref, c_north_ref), start, size, step)
        b, scale, diagonal = (load(ref, start, size) for ref in (source, scale_ref, diagonal_ref))
        rest = [(b[t] + around[t]) - diagonal[t] * mid[t] for t in range(len(b))]
        store(smooth_ref, start, size, [mid[t] + scale[t] * rest[t] for t in range(len(b))])
        store(resid, start, size, rest)
        if next_source is not None:
            pooled = [0.25 * p for p in pool_rows(resid, start, size, step)]
            store(next_source, start // 2, size // 2, pooled)

    for_chunks(height, first_pass, largest, part)
    for_chunks(height, second_pass, largest, part)


def descend_all(rows, sources, guess, weights, states, diagonal, field, resid, largest, part):
    for level in range(LEVELS - 1):
        descend(
            level,
            rows >> level,
            weights[level],
            sources[level],
            guess if level == 0 else None,
            states[4 * level : 4 * level + 4],
            diagonal[level],
            field,
            resid,
            weights[level + 1],
            sources[level + 1],
            largest,
            part,
        )


def group_of(x, west):
    return (lane_of(x) // HALO + (1 if west else 0)) % PIECES


def packed(part, p, west):
    return roll(part, p * HALO - HALO if west else p * HALO + HALO)


def to_sides(west, east, cross_ref, pair_ref, k, rows):
    even = lax.axis_index("gy") % 2 == 0
    cross_ref[k, rows, :] = jnp.where(even, west, east)
    pair_ref[k, rows, :] = jnp.where(even, east, west)


def inner_columns(tiles):
    return jnp.where(lane_of(tiles[0]) < LANES // 2, roll(tiles[0], HALO), roll(tiles[1], -HALO))


def layout_kernel(source, guess, weight, *refs):
    owns, frames, (cross_ref, pair_ref, *inner) = refs[:3], refs[3:6], refs[6:]
    rows = source.shape[0]
    piece = cross_ref.shape[1]
    whole = rows // piece
    tail = rows - whole * piece
    for own, frame, block in zip(owns, frames, (source, guess, weight)):
        clear_guards(own, rows + 2 * TOP)
        clear_guards(frame, rows + 2 * TOP)
        tiles = [block[:, t * LANES : (t + 1) * LANES] for t in range(2)]
        for t in range(2):
            own[t, GUARD + TOP : GUARD + TOP + rows, :] = tiles[t]
        frame[0, GUARD + TOP : GUARD + TOP + rows, :] = inner_columns(tiles)
    weights, start, height = (owns[2], *inner), TOP, rows
    for level in range(LEVELS):
        pooled = [0.125 * w for w in pool_rows(weights[level], start, height, 2**level)]
        start, height = start // 2, height // 2
        if level < LEVELS - 1:
            store(weights[level + 1], start, height, pooled)
    lane = lane_of(pooled[0])
    width = HALO // 2
    index = (lane % width) * 2**LEVELS
    coarse = [jnp.take_along_axis(p, index, axis=1) for p in pooled]
    coarse = jnp.where(lane % HALO < width, *coarse)
    for k, block in enumerate((source, guess, weight)):
        sides = []
        for west in (True, False):
            columns = slice(0, LANES) if west else slice(LANES, 2 * LANES)
            below = jnp.zeros((piece - tail, LANES), jnp.float32)
            if k < 2:
                half = coarse[k * height // 2 : (k + 1) * height // 2]
                below = jnp.concatenate((below[: 2 * TOP], half, below[2 * TOP + height // 2 :]), axis=0)
            last = packed(block[whole * piece :, columns], whole, west)
            both = jnp.concatenate((last, below), axis=0)
            for p in range(whole):
                part = packed(block[p * piece : (p + 1) * piece, columns], p, west)
                both = jnp.where(group_of(part, west) == p, part, both)
            sides.append(both)
        to_sides(*sides, cross_ref, pair_ref, k, slice(0, piece))


def halo_kernel(*refs):
    first_rows, second_rows, *own, cross_ref, pair_ref = refs[8:]
    own, frames = own[:3], own[3:]
    total = own[0].shape[1] - 2 * GUARD
    last = PIECES - 1
    first = total - 2 * TOP - last * cross_ref.shape[1]
    even, even_y = lax.axis_index("gx") % 2 == 0, lax.axis_index("gy") % 2 == 0
    for k in range(3):
        above = jnp.where(even, first_rows[k], second_rows[k])
        below = jnp.where(even, second_rows[k], first_rows[k])
        for side, (rows, row) in enumerate(((above, 0), (below, total - TOP))):
            body = [rows[:, t * LANES : (t + 1) * LANES] for t in range(2)]
            for t in range(2):
                own[k][t, GUARD + row : GUARD + row + TOP, :] = body[t]
            frames[k][0, GUARD + row : GUARD + row + TOP, :] = inner_columns(body)
            span = slice(first + side * TOP, first + (side + 1) * TOP)
            parts = []
            for part, west in zip(body, (True, False)):
                here = group_of(part, west) == last
                parts.append((here, packed(part, last, west)))
            (here_west, west), (here_east, east) = parts
            cross, pair = cross_ref[k, span, :], pair_ref[k, span, :]
            cross_ref[k, span, :] = jnp.where(
                even_y, jnp.where(here_west, west, cross), jnp.where(here_east, east, cross)
            )
            pair_ref[k, span, :] = jnp.where(
                even_y, jnp.where(here_east, east, pair), jnp.where(here_west, west, pair)
            )


def body_kernel(source, guess, weight, *refs):
    states = refs[: 4 * (LEVELS - 1)]
    last_weight, last_source, first_diagonal, *refs = refs[4 * (LEVELS - 1) :]
    field, resid, weight_in, *inner = refs
    rows = source.shape[1] - 2 * GUARD
    depth = LEVELS - 2
    weights = (weight_in, *inner[:depth], last_weight)
    sources = (source, *inner[depth : 2 * depth], last_source)
    diagonal = (first_diagonal, *inner[2 * depth :])
    weights[0][...] = weight[...]
    descend_all(rows, sources, guess, weights, states, diagonal, field, resid, 2 * CHUNK, CHUNK)


def frame_kernel(_a, _b, _c, from_pair, from_cross, body_weight, body_source, *refs):
    even = lax.axis_index("gy") % 2 == 0
    frames, states, refs = refs[:3], refs[3 : 3 + 4 * (LEVELS - 1)], refs[3 + 4 * (LEVELS - 1) :]
    frame_source, frame_guess, frame_weight = frames
    first_diagonal, ring_state, dense_ref, chunks_ref, field, resid, *refs = refs[0], refs[1:5], *refs[5:]
    ring_weight, ring_source, ring_field, ring_resid, ring_diagonal, *inner = refs
    rows = frame_source.shape[1] - 2 * GUARD
    depth = LEVELS - 1
    weights = (frame_weight, *inner[:depth])
    sources = (frame_source, *inner[depth : 2 * depth])
    diagonals = (first_diagonal, *inner[2 * depth :])
    piece = from_cross.shape[1]
    for k, frame in enumerate(frames):
        block = rows - 2 * TOP
        last = PIECES - 1
        tail = block - last * piece
        spans = [(p, 0, TOP + p * piece, piece) for p in range(last)]
        spans += [(last, 0, TOP + last * piece, tail)]
        spans += [(last, tail, 0, TOP), (last, tail + TOP, rows - TOP, TOP)]
        for p, first, start, size in spans:
            span = slice(GUARD + start, GUARD + start + size)
            cross, pair = from_cross[k, first : first + size, :], from_pair[k, first : first + size, :]
            from_left = group_of(cross, False) == p
            both = roll(jnp.where(from_left == even, cross, pair), -p * HALO)
            lane = lane_of(both)
            outside = (lane < HALO) | (lane >= LANES - HALO)
            frame[0, span, :] = jnp.where(outside, both, frame[0, span, :])
    descend_all(rows, sources, frame_guess, weights, states, diagonals, field, resid, 4 * CHUNK, 2 * CHUNK)

    level = LEVELS - 1
    step, halo, height = 2**level, TOP >> level, rows >> level
    for body, frame, ring in (
        (body_weight, weights[level], ring_weight),
        (body_source, sources[level], ring_source),
    ):
        middle = load(body, 0, height)
        around = load(frame, 0, height)[0]
        lane = lane_of(around)
        ahead, back = roll(around, HALO), roll(around, -HALO)
        store(
            ring,
            0,
            height,
            [
                jnp.where(lane < 2 * step, back, middle[0]),
                jnp.where(lane >= LANES - 2 * step, ahead, middle[1]),
                jnp.where(lane < LANES // 2, ahead, back),
            ],
        )
    descend(
        level,
        height,
        ring_weight,
        ring_source,
        None,
        ring_state,
        ring_diagonal,
        ring_field,
        ring_resid,
        None,
        None,
        height,
        height,
    )

    coarse_rows = (height - 2 * halo) // 2
    dense = jnp.zeros((8, LANES), jnp.float32)
    lane = lane_of(dense)
    per_tile = LANES // 2**LEVELS
    pooled_b = pool_rows(ring_resid, halo, 2 * coarse_rows, step)
    pooled_w = pool_rows(ring_weight, halo, 2 * coarse_rows, step)
    index = (lane % per_tile) * 2**LEVELS
    place = lane // per_tile
    for g in range(coarse_rows // 8):
        for group, (values, factor) in enumerate(((pooled_b, 0.25), (pooled_w, 0.125))):
            for t in range(2):
                taken = jnp.take_along_axis(factor * values[t][8 * g : 8 * g + 8], index, axis=1)
                dense = jnp.where(place == 4 * g + 2 * group + t, taken, dense)
    dense_ref[...] = dense

    width = 2 * per_tile
    index = jnp.minimum(2 * (lane - lane % width) + lane % width, LANES - 1)
    smooth = ring_state[3]
    beside_me = []
    for tile, edge, free in ((0, 0, width - 2), (1, LANES - step, 0)):
        chunk = jnp.take_along_axis(dense, index, axis=1)
        first = GUARD + halo
        pieces = []
        for g in range(coarse_rows // 8):
            for odd in range(2):
                rows_of = smooth[tile, pl.ds(first + 16 * g + odd, 8, stride=2), :]
                pieces.append((g * width + free + odd, rows_of))
        for place, values in pieces:
            chunk = jnp.where(lane == place, roll(values, place - edge), chunk)
        beside_me.append(fold(chunk))
    sublane = lax.broadcasted_iota(jnp.int32, dense.shape, 0)
    beyond = []
    for row, group, free in ((0, 1, 6), (2 * coarse_rows - 1, 2, 0)):
        chunk = dense
        for tile in range(2):
            values = jnp.broadcast_to(smooth[tile, GUARD + halo + row : GUARD + halo + row + 1, :], dense.shape)
            values = jnp.take_along_axis(values, (lane % width) * step, axis=1)
            here = (sublane == free + tile) & (lane // width == 2 * group)
            chunk = jnp.where(here, values, chunk)
        beyond.append(chunk)
    above, below = fold(beyond[0]), fold(roll(beyond[1], -LANES // 2))
    x, y = lax.axis_index("gx"), lax.axis_index("gy")
    for i in range(chunks_ref.shape[0]):
        for j in range(chunks_ref.shape[1]):
            level_with = jnp.where(j < y, beside_me[0], beside_me[1])
            chunks_ref[i, j] = jnp.where(i == x, level_with, jnp.where(i < x, above, below))


def fold(x):
    return jnp.where(lane_of(x) < LANES // 2, x, pltpu.roll(roll(x, LANES // 2), 4, 0))[:4]


def unfold(x):
    return jnp.concatenate((x, roll(x, LANES // 2)), axis=0)


def coarse_solve(all_ref, dense_ref, from_cross, from_pair, e_ref, edge_ref, smooth_ref, rows, width, groups):
    x, nx = lax.axis_index("gx"), lax.axis_size("gx")
    y, ny = lax.axis_index("gy"), lax.axis_size("gy")
    tiles = {}
    for dx in (-1, 0, 1):
        for dy in (-1, 0, 1):
            if dx or dy:
                inside = (x + dx >= 0) & (x + dx < nx) & (y + dy >= 0) & (y + dy < ny)
                tile = unfold(all_ref[jnp.where(inside, x + dx, 0), jnp.where(inside, y + dy, 0)])
                tiles[dx, dy] = jnp.where(inside, tile, 0.0)
    dense = dense_ref[...]
    lane = lane_of(dense)
    even = y % 2 == 0
    half = 4 * groups
    first = rows % from_cross.shape[1] + 2 * TOP
    cross, pair = ([ref[k, first : first + half, :] for k in range(2)] for ref in (from_cross, from_pair))
    cross, pair = jnp.concatenate(cross, axis=0), jnp.concatenate(pair, axis=0)
    weights = {-1: jnp.where(even, cross, pair), 1: jnp.where(even, pair, cross)}
    bands = [(-1, g) for g in range(TALL // 8)] + [(0, g) for g in range(groups)] + [(1, g) for g in range(TALL // 8)]
    b, w = [], []
    for dx, g in bands:
        b_rows = w_rows = jnp.zeros_like(dense)
        for dy in (-1, 0, 1):
            first_lane = (dy + 1) * width
            here = (lane >= first_lane) & (lane < first_lane + width)
            if dx or not dy:
                tile = tiles[dx, dy] if dx else dense
                b_part = roll(tile, first_lane - 2 * g * width)
                w_part = roll(tile, first_lane - (2 * g + 1) * width)
            else:
                b_part = roll(tiles[dx, dy], first_lane - g * width)
                at = (PIECES - 1 - (dy > 0)) * HALO
                w_part = roll(weights[dy][8 * g : 8 * g + 8], first_lane - at)
            b_rows = jnp.where(here, b_part, b_rows)
            w_rows = jnp.where(here, w_part, w_rows)
        b.append(b_rows)
        w.append(w_rows)
    b, w = jnp.concatenate(b, axis=0), jnp.concatenate(w, axis=0)

    step = 2 ** (LEVELS - 1)
    start = GUARD + (TOP >> (LEVELS - 1))
    for t in range(2):
        edge_ref[t] = smooth_ref[t]
    edge_ref[2] = jnp.zeros_like(edge_ref[2])

    def columns(place):
        left = roll(tiles[0, -1], LANES - step - place)
        right = roll(tiles[0, 1], -(place + width - 2))
        return jnp.where(lane < step, right, left)

    for g in range(groups):
        for odd in range(2):
            edge_ref[2, pl.ds(start + 16 * g + odd, 8, stride=2), :] = columns(g * width + odd)
    for dx, row, lanes, free in ((-1, start - 1, 0, 0), (1, start + 16 * groups, 2 * width, 6)):
        for t in range(2):
            values = tiles[dx, 0][free + t : free + t + 1]
            values = jnp.take_along_axis(
                jnp.broadcast_to(values, dense.shape), lanes + lane // step, axis=1
            )
            edge_ref[t, row : row + 1, :] = values[:1]
        left = roll(tiles[dx, -1][free + 1 : free + 2], LANES - step - (lanes + width - 1))
        right = roll(tiles[dx, 1][free : free + 1], -lanes)
        edge_ref[2, row : row + 1, :] = jnp.where(lane[:1] < step, right, left)

    tall = b.shape[0]
    zeros = jnp.zeros((GUARD, LANES), jnp.float32)
    e_ref[0:GUARD, :] = zeros
    e_ref[GUARD + tall :, :] = zeros

    def shifted(by):
        return e_ref[GUARD + by : GUARD + by + tall, :]

    e_ref[GUARD : GUARD + tall, :] = w
    c_west = jnp.minimum(w, roll(w, 1))
    c_north, c_south = jnp.minimum(w, shifted(-1)), jnp.minimum(w, shifted(1))
    c_east = roll(c_west, -1)
    scale = relaxation / (damping + c_north + c_south + c_west + c_east)
    first = scale * b
    c_west, c_east, c_north, c_south = (scale * c for c in (c_west, c_east, c_north, c_south))
    e_ref[GUARD : GUARD + tall, :] = first

    def sweep(_, carry):
        e = shifted(0)
        around = (c_west * roll(e, 1) + c_east * roll(e, -1)) + (c_north * shifted(-1) + c_south * shifted(1))
        e_ref[GUARD : GUARD + tall, :] = ((1.0 - relaxation) * e + first) + around
        return carry

    lax.fori_loop(0, SWEEPS - 1, sweep, 0)
    return shifted(0)


def up_kernel(all_ref, dense_ref, from_cross, from_pair, own_source, frame_source, own_diagonal, frame_diagonal, *refs):
    count = 4 * (LEVELS - 1)
    body_state, frame_state, ring_state = refs[:count], refs[count : 2 * count], refs[2 * count : 2 * count + 4]
    out_ref, resid_ref = refs[2 * count + 4 : 2 * count + 6]
    ring_pe, body_final, frame_final, sems, e_ref, edge_ref, *inner = refs[2 * count + 6 :]
    outs, inner = inner[:2], inner[2:]
    body_pe, frame_pe = inner[: LEVELS - 1], inner[LEVELS - 1 :]
    rows = out_ref.shape[0] + 2 * TOP
    width = out_ref.shape[1] >> LEVELS
    e = coarse_solve(all_ref, dense_ref, from_cross, from_pair, e_ref, edge_ref, ring_state[3], out_ref.shape[0], width, (out_ref.shape[0] >> LEVELS) // 8)

    level = LEVELS - 1
    step, halo, height = 2**level, TOP >> level, rows >> level
    coarse_rows = (height - 2 * halo) // 2
    picked = e[TALL - 8 : TALL + coarse_rows + 8]
    lane = lane_of(picked)
    for t in range(3):
        group = (lane + t * LANES) // 2**LEVELS
        if t == 2:
            group = jnp.where(lane < LANES // 2, group, group - 3 * LANES // 2**LEVELS)
        taken = jnp.take_along_axis(picked, jnp.clip(group + width, 0, LANES - 1), axis=1)[7 : 7 + coarse_rows + 2]
        ring_pe[t, 0 : 2 * GUARD, :] = jnp.zeros((2 * GUARD, LANES), jnp.float32)
        ring_pe[t, height : height + 2 * GUARD, :] = jnp.zeros((2 * GUARD, LANES), jnp.float32)
        ring_pe[t, pl.ds(GUARD + halo - 2, coarse_rows + 2, stride=2), :] = taken
        ring_pe[t, pl.ds(GUARD + halo - 1, coarse_rows + 2, stride=2), :] = taken

    def climbed(pe, state, start, size, step, edge=None):
        mid, around = beside_of(pe, state[:2], start, size, step)
        scale, smooth = load(state[2], start, size), load(state[3], start, size)
        if edge is not None:
            smooth = load(edge, start, size)
        return [(smooth[t] + (1.0 - relaxation) * mid[t]) + scale[t] * around[t] for t in range(len(mid))]

    def climb_ring(start, size, level=level, step=step):
        ring = spread(climbed(ring_pe, ring_state, start, size, step, edge_ref), step // 2)
        lane = lane_of(ring[0])
        around = jnp.where(
            lane < LANES // 2,
            jnp.where(lane < HALO, roll(ring[2], HALO), roll(ring[0], HALO)),
            jnp.where(lane < LANES - HALO, roll(ring[1], -HALO), roll(ring[2], -HALO)),
        )
        store_twice(body_pe[level - 1], start, size, ring[:2])
        store_twice(frame_pe[level - 1], start, size, [around])

    for_chunks(height, climb_ring, height, height)

    for level in range(LEVELS - 2, -1, -1):
        step, height = 2**level, rows >> level
        groups = ((body_pe, body_state, body_final), (frame_pe, frame_state, frame_final))
        for pes, _, _ in groups:
            clear_guards(pes[level], height)

        def climb(start, size, level=level, step=step, groups=groups):
            for pes, states, final in groups:
                value = climbed(pes[level], states[4 * level : 4 * level + 4], start, size, step)
                if level == 0:
                    store(final, start, size, value)
                else:
                    store_twice(pes[level - 1], start, size, spread(value, step // 2))

        if level > 0:
            for_chunks(height, climb, 2 * CHUNK, PART)

    def last(base, size):
        body, around = beside_of(body_final, body_state[:2], base, size, 1)
        frame, frame_around = beside_of(frame_final, frame_state[:2], base, size, 1)
        b, d = load(own_source, base, size), load(own_diagonal, base, size)
        b_frame, d_frame = load(frame_source, base, size), load(frame_diagonal, base, size)
        body = (body, [(b[t] + around[t]) - d[t] * body[t] for t in range(2)])
        frame = (frame[0], (b_frame[0] + frame_around[0]) - d_frame[0] * frame[0])
        lane = lane_of(frame[0])
        span = pl.ds(base, size)
        for ref, middle, around in ((outs[0], body[0], frame[0]), (outs[1], body[1], frame[1])):
            ref[span, :LANES] = jnp.where(lane < NEAR, roll(around, -HALO), middle[0])
            ref[span, LANES:] = jnp.where(lane >= LANES - NEAR, roll(around, HALO), middle[1])

    count = rows // CHUNK
    ends = [0] + [CHUNK * (p + 1) - LAG - TOP for p in range(count - 1)] + [out_ref.shape[0]]

    spans = [*zip(ends[:-2], ends[1:-1])]
    middle = (ends[-2] + ends[-1]) // 16 * 8
    spans += [(ends[-2], middle), (middle, ends[-1])]
    sent = []
    for p in range(count):
        start, stop = max(p * CHUNK, TOP - 8), min((p + 1) * CHUNK, rows - TOP + 8)
        climb(start, stop - start)
        for first, end in spans[p : p + 1] if p < count - 1 else spans[p:]:
            last(TOP + first, end - first)
            for k, ref in enumerate((out_ref, resid_ref)):
                size = end - first
                source = outs[k].at[pl.ds(TOP + first, size)]
                copy = pltpu.make_async_copy(source, ref.at[pl.ds(first, size)], sems.at[len(sent)])
                copy.start()
                sent.append(copy)
    for copy in sent:
        copy.wait()


def call(kernel, out_shape, scratch, flops, moved, **more):
    return pl.pallas_call(
        kernel,
        out_shape=out_shape,
        scratch_shapes=scratch,
        compiler_params=pltpu.CompilerParams(vmem_limit_bytes=VMEM_LIMIT),
        cost_estimate=pl.CostEstimate(flops=flops, bytes_accessed=moved, transcendentals=0),
        **more,
    )


def swap(x, axis, first):
    pairs = [(i, i + 1) for i in range(first, lax.axis_size(axis) - 1, 2)]
    return lax.ppermute(x, axis, pairs + [(j, i) for i, j in pairs])


def local(rhs, pressure, wet_mask, bathy_class):
    rows, columns = rhs.shape
    cells = rows * columns
    total = rows + 2 * TOP
    levels = range(LEVELS - 1)

    def shape(tiles, level):
        return (tiles, (total >> level) + 2 * GUARD, LANES)

    def out(*dims):
        return jax.ShapeDtypeStruct(dims, jnp.float32)

    def vmem(tiles, level):
        return pltpu.VMEM(shape(tiles, level), jnp.float32)

    def fields(r, p, m, c):
        wet = m.astype(jnp.float32)
        return wet * r, wet * p, wet * (1.0 + 0.5 * c.astype(jnp.float32))

    given = (rhs, pressure, wet_mask, bathy_class)

    def edge(start):
        return jnp.stack(fields(*(lax.dynamic_slice_in_dim(x, start, TOP, axis=0) for x in given)))

    even = lax.axis_index("gx") % 2 == 0
    first_rows = swap(edge(jnp.where(even, 0, rows - TOP)), "gx", 1)
    second_rows = swap(edge(jnp.where(even, rows - TOP, 0)), "gx", 0)
    piece = -(-(rows + 2 * TOP + (rows >> LEVELS) // 2) // (8 * PIECES)) * 8
    own_shapes = [out(*shape(2, 0))] * 3
    laid_out = [*own_shapes, *[out(*shape(1, 0))] * 3, out(3, piece, LANES), out(3, piece, LANES)]
    inner = [vmem(2, level) for level in range(1, LEVELS)]
    begun = call(layout_kernel, laid_out, inner, 10 * cells, 10 * cells)(*fields(*given))
    *own, to_cross, to_pair = call(
        halo_kernel, laid_out, (), cells, cells, input_output_aliases={k: k for k in range(8)}
    )(*begun, first_rows, second_rows)
    own, frames = own[:3], own[3:]
    from_pair = swap(to_pair, "gy", 0)
    from_cross = swap(to_cross, "gy", 1)

    state_count = 4 * (LEVELS - 1)
    *body_state, body_weight, body_source, diagonal = call(
        body_kernel,
        [out(*shape(2, level)) for level in levels for _ in range(4)]
        + [out(*shape(2, LEVELS - 1))] * 2
        + [out(*shape(2, 0))],
        [vmem(2, 0)] * 3 + [vmem(2, level) for level in levels[1:]] * 3,
        100 * cells,
        40 * cells,
    )(*own)
    nx, ny = lax.axis_size("gx"), lax.axis_size("gy")
    ring = LEVELS - 1
    frame_source, _, _, *state, dense, chunks = call(
        frame_kernel,
        [out(*shape(1, 0))] * 3
        + [out(*shape(1, level)) for level in levels for _ in range(4)]
        + [out(*shape(1, 0))]
        + [out(*shape(3, ring))] * 4
        + [out(8, LANES), out(nx, ny, 4, LANES)],
        [vmem(1, 0)] * 2 + [vmem(3, ring)] * 5 + [vmem(1, level) for level in range(1, LEVELS)] * 3,
        50 * cells,
        20 * cells,
        input_output_aliases={k: k for k in range(3)},
    )(*frames, from_pair, from_cross, body_weight, body_source)
    frame_state, frame_diagonal, ring_state = state[:state_count], state[state_count], state[state_count + 1 :]
    gathered = lax.all_to_all(chunks.reshape(nx * ny, 4, LANES), ("gx", "gy"), 0, 0).reshape(chunks.shape)
    return call(
        up_kernel,
        (out(rows, columns), out(rows, columns)),
        [vmem(3, ring), vmem(2, 0), vmem(1, 0), pltpu.SemaphoreType.DMA((16,))]
        + [pltpu.VMEM(((rows >> LEVELS) + 2 * TALL + 2 * GUARD, LANES), jnp.float32), vmem(3, ring)]
        + [pltpu.VMEM((total, columns), jnp.float32)] * 2
        + [vmem(2, level) for level in levels]
        + [vmem(1, level) for level in levels],
        60 * cells,
        40 * cells,
        out_specs=[pl.BlockSpec(memory_space=pl.ANY)] * 2,
    )(gathered, dense, from_cross, from_pair, own[0], frame_source, diagonal, frame_diagonal, *body_state, *frame_state, *ring_state)


def solution(mesh):
    placed = (P("gx", "gy"), P("gx", "gy"), P("gx", "gy"), P("gx", "gy"))
    return jax.shard_map(
        local, mesh=mesh, in_specs=placed, out_specs=(P("gx", "gy"), P("gx", "gy")), check_vma=False
    )
```

```python
import jax
import jax.numpy as jnp
from jax import lax
from jax.experimental import pallas as pl
from jax.experimental.pallas import tpu as pltpu
from jax.sharding import PartitionSpec as P

LEVELS = 4
SWEEPS = 12

damping = 0.01
relaxation = 0.8

HALO = 16
NEAR = 20
LANES = 128
INNER = LANES // 2 - HALO
TOP = 16
GUARD = 8
PIECES = 8
CHUNK = 136
PART = CHUNK
LAG = 8
TALL = 16
VMEM_LIMIT = 40 * 1024 * 1024


def lane_of(x):
    return lax.broadcasted_iota(jnp.int32, x.shape, x.ndim - 1)


def roll(x, amount):
    amount %= LANES
    return x if amount == 0 else pltpu.roll(x, amount, x.ndim - 1)


def from_west(tiles, step):
    moved = [roll(t, step) for t in tiles]
    if len(tiles) == 1:
        return moved
    edge = lane_of(tiles[0]) < step
    return [jnp.where(edge, moved[i - 1], moved[i]) for i in range(len(tiles))]


def from_east(tiles, step):
    moved = [roll(t, -step) for t in tiles]
    count = len(tiles)
    if count == 1:
        return moved
    edge = lane_of(tiles[0]) >= LANES - step
    return [jnp.where(edge, moved[(i + 1) % count], moved[i]) for i in range(count)]


def spread(tiles, step):
    second = (lane_of(tiles[0]) // step) % 2 == 1
    return [jnp.where(second, roll(t, step), t) for t in tiles]


def for_parts(start, size, body, part):
    for offset in range(0, size, part):
        body(start + offset, min(part, size - offset))


def for_chunks(rows, body, largest, part):
    sizes = [size for size in range(8, largest + 1, 8) if rows % size == 0]
    if rows <= largest or not sizes:
        for_parts(0, rows, body, part)
        return

    def step(i, carry):
        for_parts(i * sizes[-1], sizes[-1], body, part)
        return carry

    lax.fori_loop(0, rows // sizes[-1], step, 0)


def load(ref, start, size):
    return [ref[t, pl.ds(GUARD + start, size), :] for t in range(ref.shape[0])]


def store(ref, start, size, tiles):
    for t, tile in enumerate(tiles):
        ref[t, pl.ds(GUARD + start, size), :] = tile


def store_twice(ref, start, size, tiles):
    for t, tile in enumerate(tiles):
        ref[t, pl.ds(GUARD + 2 * start, size, stride=2), :] = tile
        ref[t, pl.ds(GUARD + 2 * start + 1, size, stride=2), :] = tile


def clear_guards(ref, rows):
    zeros = jnp.zeros((GUARD, LANES), jnp.float32)
    for t in range(ref.shape[0]):
        ref[t, 0:GUARD, :] = zeros
        ref[t, GUARD + rows : 2 * GUARD + rows, :] = zeros


def beside(mid, north, south, c_west, c_north, c_south, step):
    west = from_west(mid, step)
    east = from_east([c * m for c, m in zip(c_west, mid)], step)
    return [
        (c_west[t] * west[t] + east[t]) + (c_north[t] * north[t] + c_south[t] * south[t]) for t in range(len(mid))
    ]


def beside_of(ref, coeffs, start, size, step):
    c_west_ref, c_north_ref = coeffs
    mid = load(ref, start, size)
    north, south = load(ref, start - 1, size), load(ref, start + 1, size)
    c_west, c_north = load(c_west_ref, start, size), load(c_north_ref, start, size)
    return mid, beside(mid, north, south, c_west, c_north, load(c_north_ref, start + 1, size), step)


def pool_rows(ref, start, size, step):
    out = []
    for t in range(ref.shape[0]):
        even = ref[t, pl.ds(GUARD + start, size // 2, stride=2), :]
        odd = ref[t, pl.ds(GUARD + start + 1, size // 2, stride=2), :]
        both = even + odd
        out.append(both + roll(both, -step))
    return out


def descend(level, height, weight, source, guess, state, diagonal_ref, field, resid, next_weight, next_source, largest, part):
    step = 2**level
    c_west_ref, c_north_ref, scale_ref, smooth_ref = state
    for ref in (weight, field, c_north_ref):
        clear_guards(ref, height)

    def first_pass(start, size):
        w, w_north, w_south = (load(weight, start + k, size) for k in (0, -1, 1))
        c_north = [jnp.minimum(a, b) for a, b in zip(w, w_north)]
        c_south = [jnp.minimum(a, b) for a, b in zip(w, w_south)]
        c_west = [jnp.minimum(a, b) for a, b in zip(w, from_west(w, step))]
        c_east = from_east(c_west, step)
        diagonal = [damping + c_north[t] + c_south[t] + c_west[t] + c_east[t] for t in range(len(w))]
        scale = [relaxation / d for d in diagonal]
        store(c_north_ref, start, size, c_north)
        store(c_west_ref, start, size, c_west)
        store(scale_ref, start, size, scale)
        store(diagonal_ref, start, size, diagonal)
        value = load(source, start, size)
        if guess is None:
            value = [scale[t] * value[t] for t in range(len(w))]
        else:
            mid, north, south = (load(guess, start + k, size) for k in (0, -1, 1))
            around = beside(mid, north, south, c_west, c_north, c_south, step)
            value = [
                (1.0 - relaxation) * mid[t] + scale[t] * (value[t] + around[t]) for t in range(len(w))
            ]
        store(field, start, size, value)
        if next_weight is not None:
            pooled = [0.125 * p for p in pool_rows(weight, start, size, step)]
            store(next_weight, start // 2, size // 2, pooled)

    def second_pass(start, size):
        mid, around = beside_of(field, (c_west_ref, c_north_ref), start, size, step)
        b, scale, diagonal = (load(ref, start, size) for ref in (source, scale_ref, diagonal_ref))
        rest = [(b[t] + around[t]) - diagonal[t] * mid[t] for t in range(len(b))]
        store(smooth_ref, start, size, [mid[t] + scale[t] * rest[t] for t in range(len(b))])
        store(resid, start, size, rest)
        if next_source is not None:
            pooled = [0.25 * p for p in pool_rows(resid, start, size, step)]
            store(next_source, start // 2, size // 2, pooled)

    for_chunks(height, first_pass, largest, part)
    for_chunks(height, second_pass, largest, part)


def descend_all(rows, sources, guess, weights, states, diagonal, field, resid, largest, part):
    for level in range(LEVELS - 1):
        descend(
            level,
            rows >> level,
            weights[level],
            sources[level],
            guess if level == 0 else None,
            states[4 * level : 4 * level + 4],
            diagonal[level],
            field,
            resid,
            weights[level + 1],
            sources[level + 1],
            largest,
            part,
        )


def group_of(x, west):
    return (lane_of(x) // HALO + (1 if west else 0)) % PIECES


def packed(part, p, west):
    return roll(part, p * HALO - HALO if west else p * HALO + HALO)


def to_sides(west, east, cross_ref, pair_ref, k, rows):
    even = lax.axis_index("gy") % 2 == 0
    cross_ref[k, rows, :] = jnp.where(even, west, east)
    pair_ref[k, rows, :] = jnp.where(even, east, west)


def inner_columns(tiles):
    return jnp.where(lane_of(tiles[0]) < LANES // 2, roll(tiles[0], HALO), roll(tiles[1], -HALO))


def layout_kernel(source, guess, weight, *refs):
    owns, frames, (cross_ref, pair_ref, *inner) = refs[:3], refs[3:6], refs[6:]
    rows = source.shape[0]
    piece = cross_ref.shape[1]
    whole = rows // piece
    tail = rows - whole * piece
    for own, frame, block in zip(owns, frames, (source, guess, weight)):
        clear_guards(own, rows + 2 * TOP)
        clear_guards(frame, rows + 2 * TOP)
        tiles = [block[:, t * LANES : (t + 1) * LANES] for t in range(2)]
        for t in range(2):
            own[t, GUARD + TOP : GUARD + TOP + rows, :] = tiles[t]
        frame[0, GUARD + TOP : GUARD + TOP + rows, :] = inner_columns(tiles)
    weights, start, height = (owns[2], *inner), TOP, rows
    for level in range(LEVELS):
        pooled = [0.125 * w for w in pool_rows(weights[level], start, height, 2**level)]
        start, height = start // 2, height // 2
        if level < LEVELS - 1:
            store(weights[level + 1], start, height, pooled)
    lane = lane_of(pooled[0])
    width = HALO // 2
    index = (lane % width) * 2**LEVELS
    coarse = [jnp.take_along_axis(p, index, axis=1) for p in pooled]
    coarse = jnp.where(lane % HALO < width, *coarse)
    for k, block in enumerate((source, guess, weight)):
        sides = []
        for west in (True, False):
            columns = slice(0, LANES) if west else slice(LANES, 2 * LANES)
            below = jnp.zeros((piece - tail, LANES), jnp.float32)
            if k < 2:
                half = coarse[k * height // 2 : (k + 1) * height // 2]
                below = jnp.concatenate((below[: 2 * TOP], half, below[2 * TOP + height // 2 :]), axis=0)
            last = packed(block[whole * piece :, columns], whole, west)
            both = jnp.concatenate((last, below), axis=0)
            for p in range(whole):
                part = packed(block[p * piece : (p + 1) * piece, columns], p, west)
                both = jnp.where(group_of(part, west) == p, part, both)
            sides.append(both)
        to_sides(*sides, cross_ref, pair_ref, k, slice(0, piece))


def halo_kernel(*refs):
    first_rows, second_rows, *own, cross_ref, pair_ref = refs[8:]
    own, frames = own[:3], own[3:]
    total = own[0].shape[1] - 2 * GUARD
    last = PIECES - 1
    first = total - 2 * TOP - last * cross_ref.shape[1]
    even, even_y = lax.axis_index("gx") % 2 == 0, lax.axis_index("gy") % 2 == 0
    for k in range(3):
        above = jnp.where(even, first_rows[k], second_rows[k])
        below = jnp.where(even, second_rows[k], first_rows[k])
        for side, (rows, row) in enumerate(((above, 0), (below, total - TOP))):
            body = [rows[:, t * LANES : (t + 1) * LANES] for t in range(2)]
            for t in range(2):
                own[k][t, GUARD + row : GUARD + row + TOP, :] = body[t]
            frames[k][0, GUARD + row : GUARD + row + TOP, :] = inner_columns(body)
            span = slice(first + side * TOP, first + (side + 1) * TOP)
            parts = []
            for part, west in zip(body, (True, False)):
                here = group_of(part, west) == last
                parts.append((here, packed(part, last, west)))
            (here_west, west), (here_east, east) = parts
            cross, pair = cross_ref[k, span, :], pair_ref[k, span, :]
            cross_ref[k, span, :] = jnp.where(
                even_y, jnp.where(here_west, west, cross), jnp.where(here_east, east, cross)
            )
            pair_ref[k, span, :] = jnp.where(
                even_y, jnp.where(here_east, east, pair), jnp.where(here_west, west, pair)
            )


def body_kernel(source, guess, weight, *refs):
    states = refs[: 4 * (LEVELS - 1)]
    last_weight, last_source, first_diagonal, *refs = refs[4 * (LEVELS - 1) :]
    field, resid, weight_in, *inner = refs
    rows = source.shape[1] - 2 * GUARD
    depth = LEVELS - 2
    weights = (weight_in, *inner[:depth], last_weight)
    sources = (source, *inner[depth : 2 * depth], last_source)
    diagonal = (first_diagonal, *inner[2 * depth :])
    weights[0][...] = weight[...]
    descend_all(rows, sources, guess, weights, states, diagonal, field, resid, 2 * CHUNK, CHUNK)


def frame_kernel(_a, _b, _c, from_pair, from_cross, body_weight, body_source, *refs):
    even = lax.axis_index("gy") % 2 == 0
    frames, states, refs = refs[:3], refs[3 : 3 + 4 * (LEVELS - 1)], refs[3 + 4 * (LEVELS - 1) :]
    frame_source, frame_guess, frame_weight = frames
    first_diagonal, ring_state, dense_ref, chunks_ref, field, resid, *refs = refs[0], refs[1:5], *refs[5:]
    ring_weight, ring_source, ring_field, ring_resid, ring_diagonal, *inner = refs
    rows = frame_source.shape[1] - 2 * GUARD
    depth = LEVELS - 1
    weights = (frame_weight, *inner[:depth])
    sources = (frame_source, *inner[depth : 2 * depth])
    diagonals = (first_diagonal, *inner[2 * depth :])
    piece = from_cross.shape[1]
    for k, frame in enumerate(frames):
        block = rows - 2 * TOP
        last = PIECES - 1
        tail = block - last * piece
        spans = [(p, 0, TOP + p * piece, piece) for p in range(last)]
        spans += [(last, 0, TOP + last * piece, tail)]
        spans += [(last, tail, 0, TOP), (last, tail + TOP, rows - TOP, TOP)]
        for p, first, start, size in spans:
            span = slice(GUARD + start, GUARD + start + size)
            cross, pair = from_cross[k, first : first + size, :], from_pair[k, first : first + size, :]
            from_left = group_of(cross, False) == p
            both = roll(jnp.where(from_left == even, cross, pair), -p * HALO)
            lane = lane_of(both)
            outside = (lane < HALO) | (lane >= LANES - HALO)
            frame[0, span, :] = jnp.where(outside, both, frame[0, span, :])
    descend_all(rows, sources, frame_guess, weights, states, diagonals, field, resid, 4 * CHUNK, 2 * CHUNK)

    level = LEVELS - 1
    step, halo, height = 2**level, TOP >> level, rows >> level
    for body, frame, ring in (
        (body_weight, weights[level], ring_weight),
        (body_source, sources[level], ring_source),
    ):
        middle = load(body, 0, height)
        around = load(frame, 0, height)[0]
        lane = lane_of(around)
        ahead, back = roll(around, HALO), roll(around, -HALO)
        store(
            ring,
            0,
            height,
            [
                jnp.where(lane < 2 * step, back, middle[0]),
                jnp.where(lane >= LANES - 2 * step, ahead, middle[1]),
                jnp.where(lane < LANES // 2, ahead, back),
            ],
        )
    descend(
        level,
        height,
        ring_weight,
        ring_source,
        None,
        ring_state,
        ring_diagonal,
        ring_field,
        ring_resid,
        None,
        None,
        height,
        height,
    )

    coarse_rows = (height - 2 * halo) // 2
    dense = jnp.zeros((8, LANES), jnp.float32)
    lane = lane_of(dense)
    per_tile = LANES // 2**LEVELS
    pooled_b = pool_rows(ring_resid, halo, 2 * coarse_rows, step)
    pooled_w = pool_rows(ring_weight, halo, 2 * coarse_rows, step)
    index = (lane % per_tile) * 2**LEVELS
    place = lane // per_tile
    for g in range(coarse_rows // 8):
        for group, (values, factor) in enumerate(((pooled_b, 0.25), (pooled_w, 0.125))):
            for t in range(2):
                taken = jnp.take_along_axis(factor * values[t][8 * g : 8 * g + 8], index, axis=1)
                dense = jnp.where(place == 4 * g + 2 * group + t, taken, dense)
    dense_ref[...] = dense

    width = 2 * per_tile
    index = jnp.minimum(2 * (lane - lane % width) + lane % width, LANES - 1)
    smooth = ring_state[3]
    beside_me = []
    for tile, edge, free in ((0, 0, width - 2), (1, LANES - step, 0)):
        chunk = jnp.take_along_axis(dense, index, axis=1)
        first = GUARD + halo
        pieces = []
        for g in range(coarse_rows // 8):
            for odd in range(2):
                rows_of = smooth[tile, pl.ds(first + 16 * g + odd, 8, stride=2), :]
                pieces.append((g * width + free + odd, rows_of))
        for place, values in pieces:
            chunk = jnp.where(lane == place, roll(values, place - edge), chunk)
        beside_me.append(fold(chunk))
    sublane = lax.broadcasted_iota(jnp.int32, dense.shape, 0)
    beyond = []
    for row, group, free in ((0, 1, 6), (2 * coarse_rows - 1, 2, 0)):
        chunk = dense
        for tile in range(2):
            values = jnp.broadcast_to(smooth[tile, GUARD + halo + row : GUARD + halo + row + 1, :], dense.shape)
            values = jnp.take_along_axis(values, (lane % width) * step, axis=1)
            here = (sublane == free + tile) & (lane // width == 2 * group)
            chunk = jnp.where(here, values, chunk)
        beyond.append(chunk)
    above, below = fold(beyond[0]), fold(roll(beyond[1], -LANES // 2))
    x, y = lax.axis_index("gx"), lax.axis_index("gy")
    for i in range(chunks_ref.shape[0]):
        for j in range(chunks_ref.shape[1]):
            level_with = jnp.where(j < y, beside_me[0], beside_me[1])
            chunks_ref[i, j] = jnp.where(i == x, level_with, jnp.where(i < x, above, below))


def fold(x):
    return jnp.where(lane_of(x) < LANES // 2, x, pltpu.roll(roll(x, LANES // 2), 4, 0))[:4]


def unfold(x):
    return jnp.concatenate((x, roll(x, LANES // 2)), axis=0)


def coarse_solve(all_ref, dense_ref, from_cross, from_pair, e_ref, edge_ref, smooth_ref, rows, width, groups):
    x, nx = lax.axis_index("gx"), lax.axis_size("gx")
    y, ny = lax.axis_index("gy"), lax.axis_size("gy")
    tiles = {}
    for dx in (-1, 0, 1):
        for dy in (-1, 0, 1):
            if dx or dy:
                inside = (x + dx >= 0) & (x + dx < nx) & (y + dy >= 0) & (y + dy < ny)
                tile = unfold(all_ref[jnp.where(inside, x + dx, 0), jnp.where(inside, y + dy, 0)])
                tiles[dx, dy] = jnp.where(inside, tile, 0.0)
    dense = dense_ref[...]
    lane = lane_of(dense)
    even = y % 2 == 0
    half = 4 * groups
    first = rows % from_cross.shape[1] + 2 * TOP
    cross, pair = ([ref[k, first : first + half, :] for k in range(2)] for ref in (from_cross, from_pair))
    cross, pair = jnp.concatenate(cross, axis=0), jnp.concatenate(pair, axis=0)
    weights = {-1: jnp.where(even, cross, pair), 1: jnp.where(even, pair, cross)}
    bands = [(-1, g) for g in range(TALL // 8)] + [(0, g) for g in range(groups)] + [(1, g) for g in range(TALL // 8)]
    b, w = [], []
    for dx, g in bands:
        b_rows = w_rows = jnp.zeros_like(dense)
        for dy in (-1, 0, 1):
            first_lane = (dy + 1) * width
            here = (lane >= first_lane) & (lane < first_lane + width)
            if dx or not dy:
                tile = tiles[dx, dy] if dx else dense
                b_part = roll(tile, first_lane - 2 * g * width)
                w_part = roll(tile, first_lane - (2 * g + 1) * width)
            else:
                b_part = roll(tiles[dx, dy], first_lane - g * width)
                at = (PIECES - 1 - (dy > 0)) * HALO
                w_part = roll(weights[dy][8 * g : 8 * g + 8], first_lane - at)
            b_rows = jnp.where(here, b_part, b_rows)
            w_rows = jnp.where(here, w_part, w_rows)
        b.append(b_rows)
        w.append(w_rows)
    b, w = jnp.concatenate(b, axis=0), jnp.concatenate(w, axis=0)

    step = 2 ** (LEVELS - 1)
    start = GUARD + (TOP >> (LEVELS - 1))
    for t in range(2):
        edge_ref[t] = smooth_ref[t]
    edge_ref[2] = jnp.zeros_like(edge_ref[2])

    def columns(place):
        left = roll(tiles[0, -1], LANES - step - place)
        right = roll(tiles[0, 1], -(place + width - 2))
        return jnp.where(lane < step, right, left)

    for g in range(groups):
        for odd in range(2):
            edge_ref[2, pl.ds(start + 16 * g + odd, 8, stride=2), :] = columns(g * width + odd)
    for dx, row, lanes, free in ((-1, start - 1, 0, 0), (1, start + 16 * groups, 2 * width, 6)):
        for t in range(2):
            values = tiles[dx, 0][free + t : free + t + 1]
            values = jnp.take_along_axis(
                jnp.broadcast_to(values, dense.shape), lanes + lane // step, axis=1
            )
            edge_ref[t, row : row + 1, :] = values[:1]
        left = roll(tiles[dx, -1][free + 1 : free + 2], LANES - step - (lanes + width - 1))
        right = roll(tiles[dx, 1][free : free + 1], -lanes)
        edge_ref[2, row : row + 1, :] = jnp.where(lane[:1] < step, right, left)

    tall = b.shape[0]
    zeros = jnp.zeros((GUARD, LANES), jnp.float32)
    for k in range(2):
        e_ref[k, 0:GUARD, :] = zeros
        e_ref[k, GUARD + tall :, :] = zeros

    def shifted(k, by):
        return e_ref[k, GUARD + by : GUARD + by + tall, :]

    e_ref[1, GUARD : GUARD + tall, :] = w
    c_west = jnp.minimum(w, roll(w, 1))
    c_north, c_south = jnp.minimum(w, shifted(1, -1)), jnp.minimum(w, shifted(1, 1))
    c_east = roll(c_west, -1)
    scale = relaxation / (damping + c_north + c_south + c_west + c_east)
    first = scale * b
    c_west, c_east, c_north, c_south = (scale * c for c in (c_west, c_east, c_north, c_south))
    e_ref[0, GUARD : GUARD + tall, :] = first
    for sweep in range(SWEEPS - 1):
        k = sweep % 2
        e = shifted(k, 0)
        around = (c_west * roll(e, 1) + c_east * roll(e, -1)) + (c_north * shifted(k, -1) + c_south * shifted(k, 1))
        e_ref[1 - k, GUARD : GUARD + tall, :] = ((1.0 - relaxation) * e + first) + around
    return shifted((SWEEPS - 1) % 2, 0)


def up_kernel(all_ref, dense_ref, from_cross, from_pair, own_source, frame_source, own_diagonal, frame_diagonal, *refs):
    count = 4 * (LEVELS - 1)
    body_state, frame_state, ring_state = refs[:count], refs[count : 2 * count], refs[2 * count : 2 * count + 4]
    out_ref, resid_ref = refs[2 * count + 4 : 2 * count + 6]
    ring_pe, body_final, frame_final, sems, e_ref, edge_ref, *inner = refs[2 * count + 6 :]
    outs, inner = inner[:2], inner[2:]
    body_pe, frame_pe = inner[: LEVELS - 1], inner[LEVELS - 1 :]
    rows = out_ref.shape[0] + 2 * TOP
    width = out_ref.shape[1] >> LEVELS
    e = coarse_solve(all_ref, dense_ref, from_cross, from_pair, e_ref, edge_ref, ring_state[3], out_ref.shape[0], width, (out_ref.shape[0] >> LEVELS) // 8)

    level = LEVELS - 1
    step, halo, height = 2**level, TOP >> level, rows >> level
    coarse_rows = (height - 2 * halo) // 2
    picked = e[TALL - 8 : TALL + coarse_rows + 8]
    lane = lane_of(picked)
    for t in range(3):
        group = (lane + t * LANES) // 2**LEVELS
        if t == 2:
            group = jnp.where(lane < LANES // 2, group, group - 3 * LANES // 2**LEVELS)
        taken = jnp.take_along_axis(picked, jnp.clip(group + width, 0, LANES - 1), axis=1)[7 : 7 + coarse_rows + 2]
        ring_pe[t, 0 : 2 * GUARD, :] = jnp.zeros((2 * GUARD, LANES), jnp.float32)
        ring_pe[t, height : height + 2 * GUARD, :] = jnp.zeros((2 * GUARD, LANES), jnp.float32)
        ring_pe[t, pl.ds(GUARD + halo - 2, coarse_rows + 2, stride=2), :] = taken
        ring_pe[t, pl.ds(GUARD + halo - 1, coarse_rows + 2, stride=2), :] = taken

    def climbed(pe, state, start, size, step, edge=None):
        mid, around = beside_of(pe, state[:2], start, size, step)
        scale, smooth = load(state[2], start, size), load(state[3], start, size)
        if edge is not None:
            smooth = load(edge, start, size)
        return [(smooth[t] + (1.0 - relaxation) * mid[t]) + scale[t] * around[t] for t in range(len(mid))]

    def climb_ring(start, size, level=level, step=step):
        ring = spread(climbed(ring_pe, ring_state, start, size, step, edge_ref), step // 2)
        lane = lane_of(ring[0])
        around = jnp.where(
            lane < LANES // 2,
            jnp.where(lane < HALO, roll(ring[2], HALO), roll(ring[0], HALO)),
            jnp.where(lane < LANES - HALO, roll(ring[1], -HALO), roll(ring[2], -HALO)),
        )
        store_twice(body_pe[level - 1], start, size, ring[:2])
        store_twice(frame_pe[level - 1], start, size, [around])

    for_chunks(height, climb_ring, height, height)

    for level in range(LEVELS - 2, -1, -1):
        step, height = 2**level, rows >> level
        groups = ((body_pe, body_state, body_final), (frame_pe, frame_state, frame_final))
        for pes, _, _ in groups:
            clear_guards(pes[level], height)

        def climb(start, size, level=level, step=step, groups=groups):
            for pes, states, final in groups:
                value = climbed(pes[level], states[4 * level : 4 * level + 4], start, size, step)
                if level == 0:
                    store(final, start, size, value)
                else:
                    store_twice(pes[level - 1], start, size, spread(value, step // 2))

        if level > 0:
            for_chunks(height, climb, 2 * CHUNK, PART)

    def last(base, size):
        body, around = beside_of(body_final, body_state[:2], base, size, 1)
        frame, frame_around = beside_of(frame_final, frame_state[:2], base, size, 1)
        b, d = load(own_source, base, size), load(own_diagonal, base, size)
        b_frame, d_frame = load(frame_source, base, size), load(frame_diagonal, base, size)
        body = (body, [(b[t] + around[t]) - d[t] * body[t] for t in range(2)])
        frame = (frame[0], (b_frame[0] + frame_around[0]) - d_frame[0] * frame[0])
        lane = lane_of(frame[0])
        span = pl.ds(base, size)
        for ref, middle, around in ((outs[0], body[0], frame[0]), (outs[1], body[1], frame[1])):
            ref[span, :LANES] = jnp.where(lane < NEAR, roll(around, -HALO), middle[0])
            ref[span, LANES:] = jnp.where(lane >= LANES - NEAR, roll(around, HALO), middle[1])

    count = rows // CHUNK
    ends = [0] + [CHUNK * (p + 1) - LAG - TOP for p in range(count - 1)] + [out_ref.shape[0]]

    spans = [*zip(ends[:-2], ends[1:-1])]
    middle = (ends[-2] + ends[-1]) // 16 * 8
    spans += [(ends[-2], middle), (middle, ends[-1])]
    sent = []
    for p in range(count):
        start, stop = max(p * CHUNK, TOP - 8), min((p + 1) * CHUNK, rows - TOP + 8)
        climb(start, stop - start)
        for first, end in spans[p : p + 1] if p < count - 1 else spans[p:]:
            last(TOP + first, end - first)
            for k, ref in enumerate((out_ref, resid_ref)):
                size = end - first
                source = outs[k].at[pl.ds(TOP + first, size)]
                copy = pltpu.make_async_copy(source, ref.at[pl.ds(first, size)], sems.at[len(sent)])
                copy.start()
                sent.append(copy)
    for copy in sent:
        copy.wait()


def call(kernel, out_shape, scratch, flops, moved, **more):
    return pl.pallas_call(
        kernel,
        out_shape=out_shape,
        scratch_shapes=scratch,
        compiler_params=pltpu.CompilerParams(vmem_limit_bytes=VMEM_LIMIT),
        cost_estimate=pl.CostEstimate(flops=flops, bytes_accessed=moved, transcendentals=0),
        **more,
    )


def swap(x, axis, first):
    pairs = [(i, i + 1) for i in range(first, lax.axis_size(axis) - 1, 2)]
    return lax.ppermute(x, axis, pairs + [(j, i) for i, j in pairs])


def local(rhs, pressure, wet_mask, bathy_class):
    rows, columns = rhs.shape
    cells = rows * columns
    total = rows + 2 * TOP
    levels = range(LEVELS - 1)

    def shape(tiles, level):
        return (tiles, (total >> level) + 2 * GUARD, LANES)

    def out(*dims):
        return jax.ShapeDtypeStruct(dims, jnp.float32)

    def vmem(tiles, level):
        return pltpu.VMEM(shape(tiles, level), jnp.float32)

    def fields(r, p, m, c):
        wet = m.astype(jnp.float32)
        return wet * r, wet * p, wet * (1.0 + 0.5 * c.astype(jnp.float32))

    given = (rhs, pressure, wet_mask, bathy_class)

    def edge(start):
        return jnp.stack(fields(*(lax.dynamic_slice_in_dim(x, start, TOP, axis=0) for x in given)))

    even = lax.axis_index("gx") % 2 == 0
    first_rows = swap(edge(jnp.where(even, 0, rows - TOP)), "gx", 1)
    second_rows = swap(edge(jnp.where(even, rows - TOP, 0)), "gx", 0)
    piece = -(-(rows + 2 * TOP + (rows >> LEVELS) // 2) // (8 * PIECES)) * 8
    own_shapes = [out(*shape(2, 0))] * 3
    laid_out = [*own_shapes, *[out(*shape(1, 0))] * 3, out(3, piece, LANES), out(3, piece, LANES)]
    inner = [vmem(2, level) for level in range(1, LEVELS)]
    begun = call(layout_kernel, laid_out, inner, 10 * cells, 10 * cells)(*fields(*given))
    *own, to_cross, to_pair = call(
        halo_kernel, laid_out, (), cells, cells, input_output_aliases={k: k for k in range(8)}
    )(*begun, first_rows, second_rows)
    own, frames = own[:3], own[3:]
    from_pair = swap(to_pair, "gy", 0)
    from_cross = swap(to_cross, "gy", 1)

    state_count = 4 * (LEVELS - 1)
    *body_state, body_weight, body_source, diagonal = call(
        body_kernel,
        [out(*shape(2, level)) for level in levels for _ in range(4)]
        + [out(*shape(2, LEVELS - 1))] * 2
        + [out(*shape(2, 0))],
        [vmem(2, 0)] * 3 + [vmem(2, level) for level in levels[1:]] * 3,
        100 * cells,
        40 * cells,
    )(*own)
    nx, ny = lax.axis_size("gx"), lax.axis_size("gy")
    ring = LEVELS - 1
    frame_source, _, _, *state, dense, chunks = call(
        frame_kernel,
        [out(*shape(1, 0))] * 3
        + [out(*shape(1, level)) for level in levels for _ in range(4)]
        + [out(*shape(1, 0))]
        + [out(*shape(3, ring))] * 4
        + [out(8, LANES), out(nx, ny, 4, LANES)],
        [vmem(1, 0)] * 2 + [vmem(3, ring)] * 5 + [vmem(1, level) for level in range(1, LEVELS)] * 3,
        50 * cells,
        20 * cells,
        input_output_aliases={k: k for k in range(3)},
    )(*frames, from_pair, from_cross, body_weight, body_source)
    frame_state, frame_diagonal, ring_state = state[:state_count], state[state_count], state[state_count + 1 :]
    gathered = lax.all_to_all(chunks.reshape(nx * ny, 4, LANES), ("gx", "gy"), 0, 0).reshape(chunks.shape)
    return call(
        up_kernel,
        (out(rows, columns), out(rows, columns)),
        [vmem(3, ring), vmem(2, 0), vmem(1, 0), pltpu.SemaphoreType.DMA((16,))]
        + [pltpu.VMEM((2, (rows >> LEVELS) + 2 * TALL + 2 * GUARD, LANES), jnp.float32), vmem(3, ring)]
        + [pltpu.VMEM((total, columns), jnp.float32)] * 2
        + [vmem(2, level) for level in levels]
        + [vmem(1, level) for level in levels],
        60 * cells,
        40 * cells,
        out_specs=[pl.BlockSpec(memory_space=pl.ANY)] * 2,
    )(gathered, dense, from_cross, from_pair, own[0], frame_source, diagonal, frame_diagonal, *body_state, *frame_state, *ring_state)


def solution(mesh):
    placed = (P("gx", "gy"), P("gx", "gy"), P("gx", "gy"), P("gx", "gy"))
    return jax.shard_map(
        local, mesh=mesh, in_specs=placed, out_specs=(P("gx", "gy"), P("gx", "gy")), check_vma=False
    )
```

```python
import jax
import jax.numpy as jnp
from jax import lax
from jax.experimental import pallas as pl
from jax.experimental.pallas import tpu as pltpu
from jax.sharding import PartitionSpec as P

LEVELS = 4
SWEEPS = 12

damping = 0.01
relaxation = 0.8

HALO = 16
NEAR = 20
LANES = 128
INNER = LANES // 2 - HALO
TOP = 16
GUARD = 8
PIECES = 8
CHUNK = 136
PART = CHUNK
LAG = 8
TALL = 16
VMEM_LIMIT = 40 * 1024 * 1024


def lane_of(x):
    return lax.broadcasted_iota(jnp.int32, x.shape, x.ndim - 1)


def roll(x, amount):
    amount %= LANES
    return x if amount == 0 else pltpu.roll(x, amount, x.ndim - 1)


def from_west(tiles, step):
    moved = [roll(t, step) for t in tiles]
    if len(tiles) == 1:
        return moved
    edge = lane_of(tiles[0]) < step
    return [jnp.where(edge, moved[i - 1], moved[i]) for i in range(len(tiles))]


def from_east(tiles, step):
    moved = [roll(t, -step) for t in tiles]
    count = len(tiles)
    if count == 1:
        return moved
    edge = lane_of(tiles[0]) >= LANES - step
    return [jnp.where(edge, moved[(i + 1) % count], moved[i]) for i in range(count)]


def spread(tiles, step):
    second = (lane_of(tiles[0]) // step) % 2 == 1
    return [jnp.where(second, roll(t, step), t) for t in tiles]


def for_parts(start, size, body, part):
    for offset in range(0, size, part):
        body(start + offset, min(part, size - offset))


def for_chunks(rows, body, largest, part):
    sizes = [size for size in range(8, largest + 1, 8) if rows % size == 0]
    if rows <= largest or not sizes:
        for_parts(0, rows, body, part)
        return

    def step(i, carry):
        for_parts(i * sizes[-1], sizes[-1], body, part)
        return carry

    lax.fori_loop(0, rows // sizes[-1], step, 0)


def load(ref, start, size):
    return [ref[t, pl.ds(GUARD + start, size), :] for t in range(ref.shape[0])]


def store(ref, start, size, tiles):
    for t, tile in enumerate(tiles):
        ref[t, pl.ds(GUARD + start, size), :] = tile


def store_twice(ref, start, size, tiles):
    for t, tile in enumerate(tiles):
        ref[t, pl.ds(GUARD + 2 * start, size, stride=2), :] = tile
        ref[t, pl.ds(GUARD + 2 * start + 1, size, stride=2), :] = tile


def clear_guards(ref, rows):
    zeros = jnp.zeros((GUARD, LANES), jnp.float32)
    for t in range(ref.shape[0]):
        ref[t, 0:GUARD, :] = zeros
        ref[t, GUARD + rows : 2 * GUARD + rows, :] = zeros


def beside(mid, north, south, c_west, c_north, c_south, step):
    west = from_west(mid, step)
    east = from_east([c * m for c, m in zip(c_west, mid)], step)
    return [
        (c_west[t] * west[t] + east[t]) + (c_north[t] * north[t] + c_south[t] * south[t]) for t in range(len(mid))
    ]


def beside_of(ref, coeffs, start, size, step):
    c_west_ref, c_north_ref = coeffs
    mid = load(ref, start, size)
    north, south = load(ref, start - 1, size), load(ref, start + 1, size)
    c_west, c_north = load(c_west_ref, start, size), load(c_north_ref, start, size)
    return mid, beside(mid, north, south, c_west, c_north, load(c_north_ref, start + 1, size), step)


def pool_rows(ref, start, size, step):
    out = []
    for t in range(ref.shape[0]):
        even = ref[t, pl.ds(GUARD + start, size // 2, stride=2), :]
        odd = ref[t, pl.ds(GUARD + start + 1, size // 2, stride=2), :]
        both = even + odd
        out.append(both + roll(both, -step))
    return out


def descend(level, height, weight, source, guess, state, diagonal_ref, field, resid, next_weight, next_source, largest, part):
    step = 2**level
    c_west_ref, c_north_ref, scale_ref, smooth_ref = state
    for ref in (weight, field, c_north_ref):
        clear_guards(ref, height)

    def first_pass(start, size):
        w, w_north, w_south = (load(weight, start + k, size) for k in (0, -1, 1))
        c_north = [jnp.minimum(a, b) for a, b in zip(w, w_north)]
        c_south = [jnp.minimum(a, b) for a, b in zip(w, w_south)]
        c_west = [jnp.minimum(a, b) for a, b in zip(w, from_west(w, step))]
        c_east = from_east(c_west, step)
        diagonal = [damping + c_north[t] + c_south[t] + c_west[t] + c_east[t] for t in range(len(w))]
        scale = [relaxation / d for d in diagonal]
        store(c_north_ref, start, size, c_north)
        store(c_west_ref, start, size, c_west)
        store(scale_ref, start, size, scale)
        store(diagonal_ref, start, size, diagonal)
        value = load(source, start, size)
        if guess is None:
            value = [scale[t] * value[t] for t in range(len(w))]
        else:
            mid, north, south = (load(guess, start + k, size) for k in (0, -1, 1))
            around = beside(mid, north, south, c_west, c_north, c_south, step)
            value = [
                (1.0 - relaxation) * mid[t] + scale[t] * (value[t] + around[t]) for t in range(len(w))
            ]
        store(field, start, size, value)
        if next_weight is not None:
            pooled = [0.125 * p for p in pool_rows(weight, start, size, step)]
            store(next_weight, start // 2, size // 2, pooled)

    def second_pass(start, size):
        mid, around = beside_of(field, (c_west_ref, c_north_ref), start, size, step)
        b, scale, diagonal = (load(ref, start, size) for ref in (source, scale_ref, diagonal_ref))
        rest = [(b[t] + around[t]) - diagonal[t] * mid[t] for t in range(len(b))]
        store(smooth_ref, start, size, [mid[t] + scale[t] * rest[t] for t in range(len(b))])
        store(resid, start, size, rest)
        if next_source is not None:
            pooled = [0.25 * p for p in pool_rows(resid, start, size, step)]
            store(next_source, start // 2, size // 2, pooled)

    for_chunks(height, first_pass, largest, part)
    for_chunks(height, second_pass, largest, part)


def descend_all(rows, sources, guess, weights, states, diagonal, field, resid, largest, part):
    for level in range(LEVELS - 1):
        descend(
            level,
            rows >> level,
            weights[level],
            sources[level],
            guess if level == 0 else None,
            states[4 * level : 4 * level + 4],
            diagonal[level],
            field,
            resid,
            weights[level + 1],
            sources[level + 1],
            largest,
            part,
        )


def group_of(x, west):
    return (lane_of(x) // HALO + (1 if west else 0)) % PIECES


def packed(part, p, west):
    return roll(part, p * HALO - HALO if west else p * HALO + HALO)


def to_sides(west, east, cross_ref, pair_ref, k, rows):
    even = lax.axis_index("gy") % 2 == 0
    cross_ref[k, rows, :] = jnp.where(even, west, east)
    pair_ref[k, rows, :] = jnp.where(even, east, west)


def inner_columns(tiles):
    return jnp.where(lane_of(tiles[0]) < LANES // 2, roll(tiles[0], HALO), roll(tiles[1], -HALO))


def layout_kernel(source, guess, weight, *refs):
    owns, frames, (cross_ref, pair_ref, *inner) = refs[:3], refs[3:6], refs[6:]
    rows = source.shape[0]
    piece = cross_ref.shape[1]
    whole = rows // piece
    tail = rows - whole * piece
    for own, frame, block in zip(owns, frames, (source, guess, weight)):
        clear_guards(own, rows + 2 * TOP)
        clear_guards(frame, rows + 2 * TOP)
        tiles = [block[:, t * LANES : (t + 1) * LANES] for t in range(2)]
        for t in range(2):
            own[t, GUARD + TOP : GUARD + TOP + rows, :] = tiles[t]
        frame[0, GUARD + TOP : GUARD + TOP + rows, :] = inner_columns(tiles)
    weights, start, height = (owns[2], *inner), TOP, rows
    for level in range(LEVELS):
        pooled = [0.125 * w for w in pool_rows(weights[level], start, height, 2**level)]
        start, height = start // 2, height // 2
        if level < LEVELS - 1:
            store(weights[level + 1], start, height, pooled)
    lane = lane_of(pooled[0])
    width = HALO // 2
    index = (lane % width) * 2**LEVELS
    coarse = [jnp.take_along_axis(p, index, axis=1) for p in pooled]
    coarse = jnp.where(lane % HALO < width, *coarse)
    for k, block in enumerate((source, guess, weight)):
        sides = []
        for west in (True, False):
            columns = slice(0, LANES) if west else slice(LANES, 2 * LANES)
            below = jnp.zeros((piece - tail, LANES), jnp.float32)
            if k < 2:
                half = coarse[k * height // 2 : (k + 1) * height // 2]
                below = jnp.concatenate((below[: 2 * TOP], half, below[2 * TOP + height // 2 :]), axis=0)
            last = packed(block[whole * piece :, columns], whole, west)
            both = jnp.concatenate((last, below), axis=0)
            for p in range(whole):
                part = packed(block[p * piece : (p + 1) * piece, columns], p, west)
                both = jnp.where(group_of(part, west) == p, part, both)
            sides.append(both)
        to_sides(*sides, cross_ref, pair_ref, k, slice(0, piece))


def halo_kernel(*refs):
    first_rows, second_rows, *own, cross_ref, pair_ref = refs[8:]
    own, frames = own[:3], own[3:]
    total = own[0].shape[1] - 2 * GUARD
    last = PIECES - 1
    first = total - 2 * TOP - last * cross_ref.shape[1]
    even, even_y = lax.axis_index("gx") % 2 == 0, lax.axis_index("gy") % 2 == 0
    for k in range(3):
        above = jnp.where(even, first_rows[k], second_rows[k])
        below = jnp.where(even, second_rows[k], first_rows[k])
        for side, (rows, row) in enumerate(((above, 0), (below, total - TOP))):
            body = [rows[:, t * LANES : (t + 1) * LANES] for t in range(2)]
            for t in range(2):
                own[k][t, GUARD + row : GUARD + row + TOP, :] = body[t]
            frames[k][0, GUARD + row : GUARD + row + TOP, :] = inner_columns(body)
            span = slice(first + side * TOP, first + (side + 1) * TOP)
            parts = []
            for part, west in zip(body, (True, False)):
                here = group_of(part, west) == last
                parts.append((here, packed(part, last, west)))
            (here_west, west), (here_east, east) = parts
            cross, pair = cross_ref[k, span, :], pair_ref[k, span, :]
            cross_ref[k, span, :] = jnp.where(
                even_y, jnp.where(here_west, west, cross), jnp.where(here_east, east, cross)
            )
            pair_ref[k, span, :] = jnp.where(
                even_y, jnp.where(here_east, east, pair), jnp.where(here_west, west, pair)
            )


def body_kernel(source, guess, weight, *refs):
    states = refs[: 4 * (LEVELS - 1)]
    last_weight, last_source, first_diagonal, *refs = refs[4 * (LEVELS - 1) :]
    field, resid, weight_in, *inner = refs
    rows = source.shape[1] - 2 * GUARD
    depth = LEVELS - 2
    weights = (weight_in, *inner[:depth], last_weight)
    sources = (source, *inner[depth : 2 * depth], last_source)
    diagonal = (first_diagonal, *inner[2 * depth :])
    weights[0][...] = weight[...]
    descend_all(rows, sources, guess, weights, states, diagonal, field, resid, 2 * CHUNK, CHUNK)


def frame_kernel(_a, _b, _c, from_pair, from_cross, body_weight, body_source, *refs):
    even = lax.axis_index("gy") % 2 == 0
    frames, states, refs = refs[:3], refs[3 : 3 + 4 * (LEVELS - 1)], refs[3 + 4 * (LEVELS - 1) :]
    frame_source, frame_guess, frame_weight = frames
    first_diagonal, ring_state, dense_ref, chunks_ref, field, resid, *refs = refs[0], refs[1:5], *refs[5:]
    ring_weight, ring_source, ring_field, ring_resid, ring_diagonal, *inner = refs
    rows = frame_source.shape[1] - 2 * GUARD
    depth = LEVELS - 1
    weights = (frame_weight, *inner[:depth])
    sources = (frame_source, *inner[depth : 2 * depth])
    diagonals = (first_diagonal, *inner[2 * depth :])
    piece = from_cross.shape[1]
    for k, frame in enumerate(frames):
        block = rows - 2 * TOP
        last = PIECES - 1
        tail = block - last * piece
        spans = [(p, 0, TOP + p * piece, piece) for p in range(last)]
        spans += [(last, 0, TOP + last * piece, tail)]
        spans += [(last, tail, 0, TOP), (last, tail + TOP, rows - TOP, TOP)]
        for p, first, start, size in spans:
            span = slice(GUARD + start, GUARD + start + size)
            cross, pair = from_cross[k, first : first + size, :], from_pair[k, first : first + size, :]
            from_left = group_of(cross, False) == p
            both = roll(jnp.where(from_left == even, cross, pair), -p * HALO)
            lane = lane_of(both)
            outside = (lane < HALO) | (lane >= LANES - HALO)
            frame[0, span, :] = jnp.where(outside, both, frame[0, span, :])
    descend_all(rows, sources, frame_guess, weights, states, diagonals, field, resid, 4 * CHUNK, 2 * CHUNK)

    level = LEVELS - 1
    step, halo, height = 2**level, TOP >> level, rows >> level
    for body, frame, ring in (
        (body_weight, weights[level], ring_weight),
        (body_source, sources[level], ring_source),
    ):
        middle = load(body, 0, height)
        around = load(frame, 0, height)[0]
        lane = lane_of(around)
        ahead, back = roll(around, HALO), roll(around, -HALO)
        store(
            ring,
            0,
            height,
            [
                jnp.where(lane < 2 * step, back, middle[0]),
                jnp.where(lane >= LANES - 2 * step, ahead, middle[1]),
                jnp.where(lane < LANES // 2, ahead, back),
            ],
        )
    descend(
        level,
        height,
        ring_weight,
        ring_source,
        None,
        ring_state,
        ring_diagonal,
        ring_field,
        ring_resid,
        None,
        None,
        height,
        height,
    )

    coarse_rows = (height - 2 * halo) // 2
    dense = jnp.zeros((8, LANES), jnp.float32)
    lane = lane_of(dense)
    per_tile = LANES // 2**LEVELS
    pooled_b = pool_rows(ring_resid, halo, 2 * coarse_rows, step)
    pooled_w = pool_rows(ring_weight, halo, 2 * coarse_rows, step)
    index = (lane % per_tile) * 2**LEVELS
    place = lane // per_tile
    for g in range(coarse_rows // 8):
        for group, (values, factor) in enumerate(((pooled_b, 0.25), (pooled_w, 0.125))):
            for t in range(2):
                taken = jnp.take_along_axis(factor * values[t][8 * g : 8 * g + 8], index, axis=1)
                dense = jnp.where(place == 4 * g + 2 * group + t, taken, dense)
    dense_ref[...] = dense

    width = 2 * per_tile
    index = jnp.minimum(2 * (lane - lane % width) + lane % width, LANES - 1)
    smooth = ring_state[3]
    beside_me = []
    for tile, edge, free in ((0, 0, width - 2), (1, LANES - step, 0)):
        chunk = jnp.take_along_axis(dense, index, axis=1)
        first = GUARD + halo
        pieces = []
        for g in range(coarse_rows // 8):
            for odd in range(2):
                rows_of = smooth[tile, pl.ds(first + 16 * g + odd, 8, stride=2), :]
                pieces.append((g * width + free + odd, rows_of))
        for place, values in pieces:
            chunk = jnp.where(lane == place, roll(values, place - edge), chunk)
        beside_me.append(fold(chunk))
    sublane = lax.broadcasted_iota(jnp.int32, dense.shape, 0)
    beyond = []
    for row, group, free in ((0, 1, 6), (2 * coarse_rows - 1, 2, 0)):
        chunk = dense
        for tile in range(2):
            values = jnp.broadcast_to(smooth[tile, GUARD + halo + row : GUARD + halo + row + 1, :], dense.shape)
            values = jnp.take_along_axis(values, (lane % width) * step, axis=1)
            here = (sublane == free + tile) & (lane // width == 2 * group)
            chunk = jnp.where(here, values, chunk)
        beyond.append(chunk)
    above, below = fold(beyond[0]), fold(roll(beyond[1], -LANES // 2))
    x, y = lax.axis_index("gx"), lax.axis_index("gy")
    for i in range(chunks_ref.shape[0]):
        for j in range(chunks_ref.shape[1]):
            level_with = jnp.where(j < y, beside_me[0], beside_me[1])
            chunks_ref[i, j] = jnp.where(i == x, level_with, jnp.where(i < x, above, below))


def fold(x):
    return jnp.where(lane_of(x) < LANES // 2, x, pltpu.roll(roll(x, LANES // 2), 4, 0))[:4]


def unfold(x):
    return jnp.concatenate((x, roll(x, LANES // 2)), axis=0)


def coarse_solve(all_ref, dense_ref, from_cross, from_pair, e_ref, edge_ref, smooth_ref, rows, width, groups):
    x, nx = lax.axis_index("gx"), lax.axis_size("gx")
    y, ny = lax.axis_index("gy"), lax.axis_size("gy")
    tiles = {}
    for dx in (-1, 0, 1):
        for dy in (-1, 0, 1):
            if dx or dy:
                inside = (x + dx >= 0) & (x + dx < nx) & (y + dy >= 0) & (y + dy < ny)
                tile = unfold(all_ref[jnp.where(inside, x + dx, 0), jnp.where(inside, y + dy, 0)])
                tiles[dx, dy] = jnp.where(inside, tile, 0.0)
    dense = dense_ref[...]
    lane = lane_of(dense)
    even = y % 2 == 0
    half = 4 * groups
    first = rows % from_cross.shape[1] + 2 * TOP
    cross, pair = ([ref[k, first : first + half, :] for k in range(2)] for ref in (from_cross, from_pair))
    cross, pair = jnp.concatenate(cross, axis=0), jnp.concatenate(pair, axis=0)
    weights = {-1: jnp.where(even, cross, pair), 1: jnp.where(even, pair, cross)}
    bands = [(-1, g) for g in range(TALL // 8)] + [(0, g) for g in range(groups)] + [(1, g) for g in range(TALL // 8)]
    b, w = [], []
    for dx, g in bands:
        b_rows = w_rows = jnp.zeros_like(dense)
        for dy in (-1, 0, 1):
            first_lane = (dy + 1) * width
            here = (lane >= first_lane) & (lane < first_lane + width)
            if dx or not dy:
                tile = tiles[dx, dy] if dx else dense
                b_part = roll(tile, first_lane - 2 * g * width)
                w_part = roll(tile, first_lane - (2 * g + 1) * width)
            else:
                b_part = roll(tiles[dx, dy], first_lane - g * width)
                at = (PIECES - 1 - (dy > 0)) * HALO
                w_part = roll(weights[dy][8 * g : 8 * g + 8], first_lane - at)
            b_rows = jnp.where(here, b_part, b_rows)
            w_rows = jnp.where(here, w_part, w_rows)
        b.append(b_rows)
        w.append(w_rows)
    b, w = jnp.concatenate(b, axis=0), jnp.concatenate(w, axis=0)

    step = 2 ** (LEVELS - 1)
    start = GUARD + (TOP >> (LEVELS - 1))
    for t in range(2):
        edge_ref[t] = smooth_ref[t]
    edge_ref[2] = jnp.zeros_like(edge_ref[2])

    def columns(place):
        left = roll(tiles[0, -1], LANES - step - place)
        right = roll(tiles[0, 1], -(place + width - 2))
        return jnp.where(lane < step, right, left)

    for g in range(groups):
        for odd in range(2):
            edge_ref[2, pl.ds(start + 16 * g + odd, 8, stride=2), :] = columns(g * width + odd)
    for dx, row, lanes, free in ((-1, start - 1, 0, 0), (1, start + 16 * groups, 2 * width, 6)):
        for t in range(2):
            values = tiles[dx, 0][free + t : free + t + 1]
            values = jnp.take_along_axis(
                jnp.broadcast_to(values, dense.shape), lanes + lane // step, axis=1
            )
            edge_ref[t, row : row + 1, :] = values[:1]
        left = roll(tiles[dx, -1][free + 1 : free + 2], LANES - step - (lanes + width - 1))
        right = roll(tiles[dx, 1][free : free + 1], -lanes)
        edge_ref[2, row : row + 1, :] = jnp.where(lane[:1] < step, right, left)

    tall = b.shape[0]
    zeros = jnp.zeros((GUARD, LANES), jnp.float32)
    for k in range(2):
        e_ref[k, 0:GUARD, :] = zeros
        e_ref[k, GUARD + tall :, :] = zeros

    def shifted(k, by):
        return e_ref[k, GUARD + by : GUARD + by + tall, :]

    e_ref[1, GUARD : GUARD + tall, :] = w
    c_west = jnp.minimum(w, roll(w, 1))
    c_north, c_south = jnp.minimum(w, shifted(1, -1)), jnp.minimum(w, shifted(1, 1))
    c_east = roll(c_west, -1)
    scale = relaxation / (damping + c_north + c_south + c_west + c_east)
    first = scale * b
    c_west, c_east, c_north, c_south = (scale * c for c in (c_west, c_east, c_north, c_south))
    e_ref[0, GUARD : GUARD + tall, :] = first
    trim = TALL // 2
    for sweep in range(SWEEPS - 1):
        k = sweep % 2
        cut = trim if SWEEPS - 1 - sweep <= TALL - trim else 0
        here = slice(cut, tall - cut)
        e, north, south = (shifted(k, by)[here] for by in (0, -1, 1))
        around = (c_west[here] * roll(e, 1) + c_east[here] * roll(e, -1)) + (c_north[here] * north + c_south[here] * south)
        e_ref[1 - k, GUARD + cut : GUARD + tall - cut, :] = ((1.0 - relaxation) * e + first[here]) + around
    return shifted((SWEEPS - 1) % 2, 0)


def up_kernel(all_ref, dense_ref, from_cross, from_pair, own_source, frame_source, own_diagonal, frame_diagonal, *refs):
    count = 4 * (LEVELS - 1)
    body_state, frame_state, ring_state = refs[:count], refs[count : 2 * count], refs[2 * count : 2 * count + 4]
    out_ref, resid_ref = refs[2 * count + 4 : 2 * count + 6]
    ring_pe, body_final, frame_final, sems, e_ref, edge_ref, *inner = refs[2 * count + 6 :]
    outs, inner = inner[:2], inner[2:]
    body_pe, frame_pe = inner[: LEVELS - 1], inner[LEVELS - 1 :]
    rows = out_ref.shape[0] + 2 * TOP
    width = out_ref.shape[1] >> LEVELS
    e = coarse_solve(all_ref, dense_ref, from_cross, from_pair, e_ref, edge_ref, ring_state[3], out_ref.shape[0], width, (out_ref.shape[0] >> LEVELS) // 8)

    level = LEVELS - 1
    step, halo, height = 2**level, TOP >> level, rows >> level
    coarse_rows = (height - 2 * halo) // 2
    picked = e[TALL - 8 : TALL + coarse_rows + 8]
    lane = lane_of(picked)
    for t in range(3):
        group = (lane + t * LANES) // 2**LEVELS
        if t == 2:
            group = jnp.where(lane < LANES // 2, group, group - 3 * LANES // 2**LEVELS)
        taken = jnp.take_along_axis(picked, jnp.clip(group + width, 0, LANES - 1), axis=1)[7 : 7 + coarse_rows + 2]
        ring_pe[t, 0 : 2 * GUARD, :] = jnp.zeros((2 * GUARD, LANES), jnp.float32)
        ring_pe[t, height : height + 2 * GUARD, :] = jnp.zeros((2 * GUARD, LANES), jnp.float32)
        ring_pe[t, pl.ds(GUARD + halo - 2, coarse_rows + 2, stride=2), :] = taken
        ring_pe[t, pl.ds(GUARD + halo - 1, coarse_rows + 2, stride=2), :] = taken

    def climbed(pe, state, start, size, step, edge=None):
        mid, around = beside_of(pe, state[:2], start, size, step)
        scale, smooth = load(state[2], start, size), load(state[3], start, size)
        if edge is not None:
            smooth = load(edge, start, size)
        return [(smooth[t] + (1.0 - relaxation) * mid[t]) + scale[t] * around[t] for t in range(len(mid))]

    def climb_ring(start, size, level=level, step=step):
        ring = spread(climbed(ring_pe, ring_state, start, size, step, edge_ref), step // 2)
        lane = lane_of(ring[0])
        around = jnp.where(
            lane < LANES // 2,
            jnp.where(lane < HALO, roll(ring[2], HALO), roll(ring[0], HALO)),
            jnp.where(lane < LANES - HALO, roll(ring[1], -HALO), roll(ring[2], -HALO)),
        )
        store_twice(body_pe[level - 1], start, size, ring[:2])
        store_twice(frame_pe[level - 1], start, size, [around])

    for_chunks(height, climb_ring, height, height)

    for level in range(LEVELS - 2, -1, -1):
        step, height = 2**level, rows >> level
        groups = ((body_pe, body_state, body_final), (frame_pe, frame_state, frame_final))
        for pes, _, _ in groups:
            clear_guards(pes[level], height)

        def climb(start, size, level=level, step=step, groups=groups):
            for pes, states, final in groups:
                value = climbed(pes[level], states[4 * level : 4 * level + 4], start, size, step)
                if level == 0:
                    store(final, start, size, value)
                else:
                    store_twice(pes[level - 1], start, size, spread(value, step // 2))

        if level > 0:
            for_chunks(height, climb, 2 * CHUNK, PART)

    def last(base, size):
        body, around = beside_of(body_final, body_state[:2], base, size, 1)
        frame, frame_around = beside_of(frame_final, frame_state[:2], base, size, 1)
        b, d = load(own_source, base, size), load(own_diagonal, base, size)
        b_frame, d_frame = load(frame_source, base, size), load(frame_diagonal, base, size)
        body = (body, [(b[t] + around[t]) - d[t] * body[t] for t in range(2)])
        frame = (frame[0], (b_frame[0] + frame_around[0]) - d_frame[0] * frame[0])
        lane = lane_of(frame[0])
        span = pl.ds(base, size)
        for ref, middle, around in ((outs[0], body[0], frame[0]), (outs[1], body[1], frame[1])):
            ref[span, :LANES] = jnp.where(lane < NEAR, roll(around, -HALO), middle[0])
            ref[span, LANES:] = jnp.where(lane >= LANES - NEAR, roll(around, HALO), middle[1])

    count = rows // CHUNK
    ends = [0] + [CHUNK * (p + 1) - LAG - TOP for p in range(count - 1)] + [out_ref.shape[0]]

    spans = [*zip(ends[:-2], ends[1:-1])]
    middle = (ends[-2] + ends[-1]) // 16 * 8
    spans += [(ends[-2], middle), (middle, ends[-1])]
    sent = []
    for p in range(count):
        start, stop = max(p * CHUNK, TOP - 8), min((p + 1) * CHUNK, rows - TOP + 8)
        climb(start, stop - start)
        for first, end in spans[p : p + 1] if p < count - 1 else spans[p:]:
            last(TOP + first, end - first)
            for k, ref in enumerate((out_ref, resid_ref)):
                size = end - first
                source = outs[k].at[pl.ds(TOP + first, size)]
                copy = pltpu.make_async_copy(source, ref.at[pl.ds(first, size)], sems.at[len(sent)])
                copy.start()
                sent.append(copy)
    for copy in sent:
        copy.wait()


def call(kernel, out_shape, scratch, flops, moved, **more):
    return pl.pallas_call(
        kernel,
        out_shape=out_shape,
        scratch_shapes=scratch,
        compiler_params=pltpu.CompilerParams(vmem_limit_bytes=VMEM_LIMIT),
        cost_estimate=pl.CostEstimate(flops=flops, bytes_accessed=moved, transcendentals=0),
        **more,
    )


def swap(x, axis, first):
    pairs = [(i, i + 1) for i in range(first, lax.axis_size(axis) - 1, 2)]
    return lax.ppermute(x, axis, pairs + [(j, i) for i, j in pairs])


def local(rhs, pressure, wet_mask, bathy_class):
    rows, columns = rhs.shape
    cells = rows * columns
    total = rows + 2 * TOP
    levels = range(LEVELS - 1)

    def shape(tiles, level):
        return (tiles, (total >> level) + 2 * GUARD, LANES)

    def out(*dims):
        return jax.ShapeDtypeStruct(dims, jnp.float32)

    def vmem(tiles, level):
        return pltpu.VMEM(shape(tiles, level), jnp.float32)

    def fields(r, p, m, c):
        wet = m.astype(jnp.float32)
        return wet * r, wet * p, wet * (1.0 + 0.5 * c.astype(jnp.float32))

    given = (rhs, pressure, wet_mask, bathy_class)

    def edge(start):
        return jnp.stack(fields(*(lax.dynamic_slice_in_dim(x, start, TOP, axis=0) for x in given)))

    even = lax.axis_index("gx") % 2 == 0
    first_rows = swap(edge(jnp.where(even, 0, rows - TOP)), "gx", 1)
    second_rows = swap(edge(jnp.where(even, rows - TOP, 0)), "gx", 0)
    piece = -(-(rows + 2 * TOP + (rows >> LEVELS) // 2) // (8 * PIECES)) * 8
    own_shapes = [out(*shape(2, 0))] * 3
    laid_out = [*own_shapes, *[out(*shape(1, 0))] * 3, out(3, piece, LANES), out(3, piece, LANES)]
    inner = [vmem(2, level) for level in range(1, LEVELS)]
    begun = call(layout_kernel, laid_out, inner, 10 * cells, 10 * cells)(*fields(*given))
    *own, to_cross, to_pair = call(
        halo_kernel, laid_out, (), cells, cells, input_output_aliases={k: k for k in range(8)}
    )(*begun, first_rows, second_rows)
    own, frames = own[:3], own[3:]
    from_pair = swap(to_pair, "gy", 0)
    from_cross = swap(to_cross, "gy", 1)

    state_count = 4 * (LEVELS - 1)
    *body_state, body_weight, body_source, diagonal = call(
        body_kernel,
        [out(*shape(2, level)) for level in levels for _ in range(4)]
        + [out(*shape(2, LEVELS - 1))] * 2
        + [out(*shape(2, 0))],
        [vmem(2, 0)] * 3 + [vmem(2, level) for level in levels[1:]] * 3,
        100 * cells,
        40 * cells,
    )(*own)
    nx, ny = lax.axis_size("gx"), lax.axis_size("gy")
    ring = LEVELS - 1
    frame_source, _, _, *state, dense, chunks = call(
        frame_kernel,
        [out(*shape(1, 0))] * 3
        + [out(*shape(1, level)) for level in levels for _ in range(4)]
        + [out(*shape(1, 0))]
        + [out(*shape(3, ring))] * 4
        + [out(8, LANES), out(nx, ny, 4, LANES)],
        [vmem(1, 0)] * 2 + [vmem(3, ring)] * 5 + [vmem(1, level) for level in range(1, LEVELS)] * 3,
        50 * cells,
        20 * cells,
        input_output_aliases={k: k for k in range(3)},
    )(*frames, from_pair, from_cross, body_weight, body_source)
    frame_state, frame_diagonal, ring_state = state[:state_count], state[state_count], state[state_count + 1 :]
    gathered = lax.all_to_all(chunks.reshape(nx * ny, 4, LANES), ("gx", "gy"), 0, 0).reshape(chunks.shape)
    return call(
        up_kernel,
        (out(rows, columns), out(rows, columns)),
        [vmem(3, ring), vmem(2, 0), vmem(1, 0), pltpu.SemaphoreType.DMA((16,))]
        + [pltpu.VMEM((2, (rows >> LEVELS) + 2 * TALL + 2 * GUARD, LANES), jnp.float32), vmem(3, ring)]
        + [pltpu.VMEM((total, columns), jnp.float32)] * 2
        + [vmem(2, level) for level in levels]
        + [vmem(1, level) for level in levels],
        60 * cells,
        40 * cells,
        out_specs=[pl.BlockSpec(memory_space=pl.ANY)] * 2,
    )(gathered, dense, from_cross, from_pair, own[0], frame_source, diagonal, frame_diagonal, *body_state, *frame_state, *ring_state)


def solution(mesh):
    placed = (P("gx", "gy"), P("gx", "gy"), P("gx", "gy"), P("gx", "gy"))
    return jax.shard_map(
        local, mesh=mesh, in_specs=placed, out_specs=(P("gx", "gy"), P("gx", "gy")), check_vma=False
    )
```

```python
import jax
import jax.numpy as jnp
from jax import lax
from jax.experimental import pallas as pl
from jax.experimental.pallas import tpu as pltpu
from jax.sharding import PartitionSpec as P

LEVELS = 4
SWEEPS = 12

damping = 0.01
relaxation = 0.8

HALO = 16
NEAR = 20
LANES = 128
INNER = LANES // 2 - HALO
TOP = 16
GUARD = 8
PIECES = 8
CHUNK = 136
PART = CHUNK
LAG = 8
TALL = 16
VMEM_LIMIT = 40 * 1024 * 1024


def lane_of(x):
    return lax.broadcasted_iota(jnp.int32, x.shape, x.ndim - 1)


def roll(x, amount):
    amount %= LANES
    return x if amount == 0 else pltpu.roll(x, amount, x.ndim - 1)


def from_west(tiles, step):
    moved = [roll(t, step) for t in tiles]
    if len(tiles) == 1:
        return moved
    edge = lane_of(tiles[0]) < step
    return [jnp.where(edge, moved[i - 1], moved[i]) for i in range(len(tiles))]


def from_east(tiles, step):
    moved = [roll(t, -step) for t in tiles]
    count = len(tiles)
    if count == 1:
        return moved
    edge = lane_of(tiles[0]) >= LANES - step
    return [jnp.where(edge, moved[(i + 1) % count], moved[i]) for i in range(count)]


def spread(tiles, step):
    second = (lane_of(tiles[0]) // step) % 2 == 1
    return [jnp.where(second, roll(t, step), t) for t in tiles]


def for_parts(start, size, body, part):
    for offset in range(0, size, part):
        body(start + offset, min(part, size - offset))


def for_chunks(rows, body, largest, part):
    sizes = [size for size in range(8, largest + 1, 8) if rows % size == 0]
    if rows <= largest or not sizes:
        for_parts(0, rows, body, part)
        return

    def step(i, carry):
        for_parts(i * sizes[-1], sizes[-1], body, part)
        return carry

    lax.fori_loop(0, rows // sizes[-1], step, 0)


def load(ref, start, size):
    return [ref[t, pl.ds(GUARD + start, size), :] for t in range(ref.shape[0])]


def store(ref, start, size, tiles):
    for t, tile in enumerate(tiles):
        ref[t, pl.ds(GUARD + start, size), :] = tile


def store_twice(ref, start, size, tiles):
    for t, tile in enumerate(tiles):
        ref[t, pl.ds(GUARD + 2 * start, size, stride=2), :] = tile
        ref[t, pl.ds(GUARD + 2 * start + 1, size, stride=2), :] = tile


def clear_guards(ref, rows):
    zeros = jnp.zeros((GUARD, LANES), jnp.float32)
    for t in range(ref.shape[0]):
        ref[t, 0:GUARD, :] = zeros
        ref[t, GUARD + rows : 2 * GUARD + rows, :] = zeros


def beside(mid, north, south, c_west, c_north, c_south, step):
    west = from_west(mid, step)
    east = from_east([c * m for c, m in zip(c_west, mid)], step)
    return [
        (c_west[t] * west[t] + east[t]) + (c_north[t] * north[t] + c_south[t] * south[t]) for t in range(len(mid))
    ]


def beside_of(ref, coeffs, start, size, step):
    c_west_ref, c_north_ref = coeffs
    mid = load(ref, start, size)
    north, south = load(ref, start - 1, size), load(ref, start + 1, size)
    c_west, c_north = load(c_west_ref, start, size), load(c_north_ref, start, size)
    return mid, beside(mid, north, south, c_west, c_north, load(c_north_ref, start + 1, size), step)


def pool_rows(ref, start, size, step):
    out = []
    for t in range(ref.shape[0]):
        even = ref[t, pl.ds(GUARD + start, size // 2, stride=2), :]
        odd = ref[t, pl.ds(GUARD + start + 1, size // 2, stride=2), :]
        both = even + odd
        out.append(both + roll(both, -step))
    return out


def descend(level, height, weight, source, guess, state, diagonal_ref, field, resid, next_weight, next_source, largest, part):
    step = 2**level
    c_west_ref, c_north_ref, scale_ref, smooth_ref = state
    for ref in (weight, field, c_north_ref):
        clear_guards(ref, height)

    def first_pass(start, size):
        w, w_north, w_south = (load(weight, start + k, size) for k in (0, -1, 1))
        c_north = [jnp.minimum(a, b) for a, b in zip(w, w_north)]
        c_south = [jnp.minimum(a, b) for a, b in zip(w, w_south)]
        c_west = [jnp.minimum(a, b) for a, b in zip(w, from_west(w, step))]
        c_east = from_east(c_west, step)
        diagonal = [damping + c_north[t] + c_south[t] + c_west[t] + c_east[t] for t in range(len(w))]
        scale = [relaxation / d for d in diagonal]
        store(c_north_ref, start, size, c_north)
        store(c_west_ref, start, size, c_west)
        store(scale_ref, start, size, scale)
        store(diagonal_ref, start, size, diagonal)
        value = load(source, start, size)
        if guess is None:
            value = [scale[t] * value[t] for t in range(len(w))]
        else:
            mid, north, south = (load(guess, start + k, size) for k in (0, -1, 1))
            around = beside(mid, north, south, c_west, c_north, c_south, step)
            value = [
                (1.0 - relaxation) * mid[t] + scale[t] * (value[t] + around[t]) for t in range(len(w))
            ]
        store(field, start, size, value)
        if next_weight is not None:
            pooled = [0.125 * p for p in pool_rows(weight, start, size, step)]
            store(next_weight, start // 2, size // 2, pooled)

    def second_pass(start, size):
        mid, around = beside_of(field, (c_west_ref, c_north_ref), start, size, step)
        b, scale, diagonal = (load(ref, start, size) for ref in (source, scale_ref, diagonal_ref))
        rest = [(b[t] + around[t]) - diagonal[t] * mid[t] for t in range(len(b))]
        store(smooth_ref, start, size, [mid[t] + scale[t] * rest[t] for t in range(len(b))])
        store(resid, start, size, rest)
        if next_source is not None:
            pooled = [0.25 * p for p in pool_rows(resid, start, size, step)]
            store(next_source, start // 2, size // 2, pooled)

    for_chunks(height, first_pass, largest, part)
    for_chunks(height, second_pass, largest, part)


def descend_all(rows, sources, guess, weights, states, diagonal, field, resid, largest, part):
    for level in range(LEVELS - 1):
        descend(
            level,
            rows >> level,
            weights[level],
            sources[level],
            guess if level == 0 else None,
            states[4 * level : 4 * level + 4],
            diagonal[level],
            field,
            resid,
            weights[level + 1],
            sources[level + 1],
            largest,
            part,
        )


def group_of(x, west):
    return (lane_of(x) // HALO + (1 if west else 0)) % PIECES


def packed(part, p, west):
    return roll(part, p * HALO - HALO if west else p * HALO + HALO)


def to_sides(west, east, cross_ref, pair_ref, k, rows):
    even = lax.axis_index("gy") % 2 == 0
    cross_ref[k, rows, :] = jnp.where(even, west, east)
    pair_ref[k, rows, :] = jnp.where(even, east, west)


def inner_columns(tiles):
    return jnp.where(lane_of(tiles[0]) < LANES // 2, roll(tiles[0], HALO), roll(tiles[1], -HALO))


def layout_kernel(source, guess, weight, *refs):
    owns, frames, (cross_ref, pair_ref, *inner) = refs[:3], refs[3:6], refs[6:]
    rows = source.shape[0]
    piece = cross_ref.shape[1]
    whole = rows // piece
    tail = rows - whole * piece
    for own, frame, block in zip(owns, frames, (source, guess, weight)):
        clear_guards(own, rows + 2 * TOP)
        clear_guards(frame, rows + 2 * TOP)
        tiles = [block[:, t * LANES : (t + 1) * LANES] for t in range(2)]
        for t in range(2):
            own[t, GUARD + TOP : GUARD + TOP + rows, :] = tiles[t]
        frame[0, GUARD + TOP : GUARD + TOP + rows, :] = inner_columns(tiles)
    weights, start, height = (owns[2], *inner), TOP, rows
    for level in range(LEVELS):
        pooled = [0.125 * w for w in pool_rows(weights[level], start, height, 2**level)]
        start, height = start // 2, height // 2
        if level < LEVELS - 1:
            store(weights[level + 1], start, height, pooled)
    lane = lane_of(pooled[0])
    width = HALO // 2
    index = (lane % width) * 2**LEVELS
    coarse = [jnp.take_along_axis(p, index, axis=1) for p in pooled]
    coarse = jnp.where(lane % HALO < width, *coarse)
    for k, block in enumerate((source, guess, weight)):
        sides = []
        for west in (True, False):
            columns = slice(0, LANES) if west else slice(LANES, 2 * LANES)
            below = jnp.zeros((piece - tail, LANES), jnp.float32)
            if k < 2:
                half = coarse[k * height // 2 : (k + 1) * height // 2]
                below = jnp.concatenate((below[: 2 * TOP], half, below[2 * TOP + height // 2 :]), axis=0)
            last = packed(block[whole * piece :, columns], whole, west)
            both = jnp.concatenate((last, below), axis=0)
            for p in range(whole):
                part = packed(block[p * piece : (p + 1) * piece, columns], p, west)
                both = jnp.where(group_of(part, west) == p, part, both)
            sides.append(both)
        to_sides(*sides, cross_ref, pair_ref, k, slice(0, piece))


def halo_kernel(*refs):
    first_rows, second_rows, *own, cross_ref, pair_ref = refs[8:]
    own, frames = own[:3], own[3:]
    total = own[0].shape[1] - 2 * GUARD
    last = PIECES - 1
    first = total - 2 * TOP - last * cross_ref.shape[1]
    even, even_y = lax.axis_index("gx") % 2 == 0, lax.axis_index("gy") % 2 == 0
    for k in range(3):
        above = jnp.where(even, first_rows[k], second_rows[k])
        below = jnp.where(even, second_rows[k], first_rows[k])
        for side, (rows, row) in enumerate(((above, 0), (below, total - TOP))):
            body = [rows[:, t * LANES : (t + 1) * LANES] for t in range(2)]
            for t in range(2):
                own[k][t, GUARD + row : GUARD + row + TOP, :] = body[t]
            frames[k][0, GUARD + row : GUARD + row + TOP, :] = inner_columns(body)
            span = slice(first + side * TOP, first + (side + 1) * TOP)
            parts = []
            for part, west in zip(body, (True, False)):
                here = group_of(part, west) == last
                parts.append((here, packed(part, last, west)))
            (here_west, west), (here_east, east) = parts
            cross, pair = cross_ref[k, span, :], pair_ref[k, span, :]
            cross_ref[k, span, :] = jnp.where(
                even_y, jnp.where(here_west, west, cross), jnp.where(here_east, east, cross)
            )
            pair_ref[k, span, :] = jnp.where(
                even_y, jnp.where(here_east, east, pair), jnp.where(here_west, west, pair)
            )


def body_kernel(source, guess, weight, *refs):
    states = refs[: 4 * (LEVELS - 1)]
    last_weight, last_source, first_diagonal, *refs = refs[4 * (LEVELS - 1) :]
    field, resid, weight_in, *inner = refs
    rows = source.shape[1] - 2 * GUARD
    depth = LEVELS - 2
    weights = (weight_in, *inner[:depth], last_weight)
    sources = (source, *inner[depth : 2 * depth], last_source)
    diagonal = (first_diagonal, *inner[2 * depth :])
    weights[0][...] = weight[...]
    descend_all(rows, sources, guess, weights, states, diagonal, field, resid, 2 * CHUNK, CHUNK)


def frame_kernel(_a, _b, _c, from_pair, from_cross, body_weight, body_source, *refs):
    even = lax.axis_index("gy") % 2 == 0
    frames, states, refs = refs[:3], refs[3 : 3 + 4 * (LEVELS - 1)], refs[3 + 4 * (LEVELS - 1) :]
    frame_source, frame_guess, frame_weight = frames
    first_diagonal, ring_state, dense_ref, chunks_ref, field, resid, *refs = refs[0], refs[1:5], *refs[5:]
    ring_weight, ring_source, ring_field, ring_resid, ring_diagonal, *inner = refs
    rows = frame_source.shape[1] - 2 * GUARD
    depth = LEVELS - 1
    weights = (frame_weight, *inner[:depth])
    sources = (frame_source, *inner[depth : 2 * depth])
    diagonals = (first_diagonal, *inner[2 * depth :])
    piece = from_cross.shape[1]
    for k, frame in enumerate(frames):
        block = rows - 2 * TOP
        last = PIECES - 1
        tail = block - last * piece
        spans = [(p, 0, TOP + p * piece, piece) for p in range(last)]
        spans += [(last, 0, TOP + last * piece, tail)]
        spans += [(last, tail, 0, TOP), (last, tail + TOP, rows - TOP, TOP)]
        for p, first, start, size in spans:
            span = slice(GUARD + start, GUARD + start + size)
            cross, pair = from_cross[k, first : first + size, :], from_pair[k, first : first + size, :]
            from_left = group_of(cross, False) == p
            both = roll(jnp.where(from_left == even, cross, pair), -p * HALO)
            lane = lane_of(both)
            outside = (lane < HALO) | (lane >= LANES - HALO)
            frame[0, span, :] = jnp.where(outside, both, frame[0, span, :])
    descend_all(rows, sources, frame_guess, weights, states, diagonals, field, resid, 4 * CHUNK, CHUNK)

    level = LEVELS - 1
    step, halo, height = 2**level, TOP >> level, rows >> level
    for body, frame, ring in (
        (body_weight, weights[level], ring_weight),
        (body_source, sources[level], ring_source),
    ):
        middle = load(body, 0, height)
        around = load(frame, 0, height)[0]
        lane = lane_of(around)
        ahead, back = roll(around, HALO), roll(around, -HALO)
        store(
            ring,
            0,
            height,
            [
                jnp.where(lane < 2 * step, back, middle[0]),
                jnp.where(lane >= LANES - 2 * step, ahead, middle[1]),
                jnp.where(lane < LANES // 2, ahead, back),
            ],
        )
    descend(
        level,
        height,
        ring_weight,
        ring_source,
        None,
        ring_state,
        ring_diagonal,
        ring_field,
        ring_resid,
        None,
        None,
        height,
        height,
    )

    coarse_rows = (height - 2 * halo) // 2
    dense = jnp.zeros((8, LANES), jnp.float32)
    lane = lane_of(dense)
    per_tile = LANES // 2**LEVELS
    pooled_b = pool_rows(ring_resid, halo, 2 * coarse_rows, step)
    pooled_w = pool_rows(ring_weight, halo, 2 * coarse_rows, step)
    index = (lane % per_tile) * 2**LEVELS
    place = lane // per_tile
    for g in range(coarse_rows // 8):
        for group, (values, factor) in enumerate(((pooled_b, 0.25), (pooled_w, 0.125))):
            for t in range(2):
                taken = jnp.take_along_axis(factor * values[t][8 * g : 8 * g + 8], index, axis=1)
                dense = jnp.where(place == 4 * g + 2 * group + t, taken, dense)
    dense_ref[...] = dense

    width = 2 * per_tile
    index = jnp.minimum(2 * (lane - lane % width) + lane % width, LANES - 1)
    smooth = ring_state[3]
    beside_me = []
    for tile, edge, free in ((0, 0, width - 2), (1, LANES - step, 0)):
        chunk = jnp.take_along_axis(dense, index, axis=1)
        first = GUARD + halo
        pieces = []
        for g in range(coarse_rows // 8):
            for odd in range(2):
                rows_of = smooth[tile, pl.ds(first + 16 * g + odd, 8, stride=2), :]
                pieces.append((g * width + free + odd, rows_of))
        for place, values in pieces:
            chunk = jnp.where(lane == place, roll(values, place - edge), chunk)
        beside_me.append(fold(chunk))
    sublane = lax.broadcasted_iota(jnp.int32, dense.shape, 0)
    beyond = []
    for row, group, free in ((0, 1, 6), (2 * coarse_rows - 1, 2, 0)):
        chunk = dense
        for tile in range(2):
            values = jnp.broadcast_to(smooth[tile, GUARD + halo + row : GUARD + halo + row + 1, :], dense.shape)
            values = jnp.take_along_axis(values, (lane % width) * step, axis=1)
            here = (sublane == free + tile) & (lane // width == 2 * group)
            chunk = jnp.where(here, values, chunk)
        beyond.append(chunk)
    above, below = fold(beyond[0]), fold(roll(beyond[1], -LANES // 2))
    x, y = lax.axis_index("gx"), lax.axis_index("gy")
    for i in range(chunks_ref.shape[0]):
        for j in range(chunks_ref.shape[1]):
            level_with = jnp.where(j < y, beside_me[0], beside_me[1])
            chunks_ref[i, j] = jnp.where(i == x, level_with, jnp.where(i < x, above, below))


def fold(x):
    return jnp.where(lane_of(x) < LANES // 2, x, pltpu.roll(roll(x, LANES // 2), 4, 0))[:4]


def unfold(x):
    return jnp.concatenate((x, roll(x, LANES // 2)), axis=0)


def coarse_solve(all_ref, dense_ref, from_cross, from_pair, e_ref, edge_ref, smooth_ref, rows, width, groups):
    x, nx = lax.axis_index("gx"), lax.axis_size("gx")
    y, ny = lax.axis_index("gy"), lax.axis_size("gy")
    tiles = {}
    for dx in (-1, 0, 1):
        for dy in (-1, 0, 1):
            if dx or dy:
                inside = (x + dx >= 0) & (x + dx < nx) & (y + dy >= 0) & (y + dy < ny)
                tile = unfold(all_ref[jnp.where(inside, x + dx, 0), jnp.where(inside, y + dy, 0)])
                tiles[dx, dy] = jnp.where(inside, tile, 0.0)
    dense = dense_ref[...]
    lane = lane_of(dense)
    even = y % 2 == 0
    half = 4 * groups
    first = rows % from_cross.shape[1] + 2 * TOP
    cross, pair = ([ref[k, first : first + half, :] for k in range(2)] for ref in (from_cross, from_pair))
    cross, pair = jnp.concatenate(cross, axis=0), jnp.concatenate(pair, axis=0)
    weights = {-1: jnp.where(even, cross, pair), 1: jnp.where(even, pair, cross)}
    bands = [(-1, g) for g in range(TALL // 8)] + [(0, g) for g in range(groups)] + [(1, g) for g in range(TALL // 8)]
    b, w = [], []
    for dx, g in bands:
        b_rows = w_rows = jnp.zeros_like(dense)
        for dy in (-1, 0, 1):
            first_lane = (dy + 1) * width
            here = (lane >= first_lane) & (lane < first_lane + width)
            if dx or not dy:
                tile = tiles[dx, dy] if dx else dense
                b_part = roll(tile, first_lane - 2 * g * width)
                w_part = roll(tile, first_lane - (2 * g + 1) * width)
            else:
                b_part = roll(tiles[dx, dy], first_lane - g * width)
                at = (PIECES - 1 - (dy > 0)) * HALO
                w_part = roll(weights[dy][8 * g : 8 * g + 8], first_lane - at)
            b_rows = jnp.where(here, b_part, b_rows)
            w_rows = jnp.where(here, w_part, w_rows)
        b.append(b_rows)
        w.append(w_rows)
    b, w = jnp.concatenate(b, axis=0), jnp.concatenate(w, axis=0)

    step = 2 ** (LEVELS - 1)
    start = GUARD + (TOP >> (LEVELS - 1))
    for t in range(2):
        edge_ref[t] = smooth_ref[t]
    edge_ref[2] = jnp.zeros_like(edge_ref[2])

    def columns(place):
        left = roll(tiles[0, -1], LANES - step - place)
        right = roll(tiles[0, 1], -(place + width - 2))
        return jnp.where(lane < step, right, left)

    for g in range(groups):
        for odd in range(2):
            edge_ref[2, pl.ds(start + 16 * g + odd, 8, stride=2), :] = columns(g * width + odd)
    for dx, row, lanes, free in ((-1, start - 1, 0, 0), (1, start + 16 * groups, 2 * width, 6)):
        for t in range(2):
            values = tiles[dx, 0][free + t : free + t + 1]
            values = jnp.take_along_axis(
                jnp.broadcast_to(values, dense.shape), lanes + lane // step, axis=1
            )
            edge_ref[t, row : row + 1, :] = values[:1]
        left = roll(tiles[dx, -1][free + 1 : free + 2], LANES - step - (lanes + width - 1))
        right = roll(tiles[dx, 1][free : free + 1], -lanes)
        edge_ref[2, row : row + 1, :] = jnp.where(lane[:1] < step, right, left)

    tall = b.shape[0]
    zeros = jnp.zeros((GUARD, LANES), jnp.float32)
    for k in range(2):
        e_ref[k, 0:GUARD, :] = zeros
        e_ref[k, GUARD + tall :, :] = zeros

    def shifted(k, by):
        return e_ref[k, GUARD + by : GUARD + by + tall, :]

    e_ref[1, GUARD : GUARD + tall, :] = w
    c_west = jnp.minimum(w, roll(w, 1))
    c_north, c_south = jnp.minimum(w, shifted(1, -1)), jnp.minimum(w, shifted(1, 1))
    c_east = roll(c_west, -1)
    scale = relaxation / (damping + c_north + c_south + c_west + c_east)
    first = scale * b
    c_west, c_east, c_north, c_south = (scale * c for c in (c_west, c_east, c_north, c_south))
    e_ref[0, GUARD : GUARD + tall, :] = first
    for sweep in range(SWEEPS - 1):
        k = sweep % 2
        e = shifted(k, 0)
        around = (c_west * roll(e, 1) + c_east * roll(e, -1)) + (c_north * shifted(k, -1) + c_south * shifted(k, 1))
        e_ref[1 - k, GUARD : GUARD + tall, :] = ((1.0 - relaxation) * e + first) + around
    return shifted((SWEEPS - 1) % 2, 0)


def up_kernel(all_ref, dense_ref, from_cross, from_pair, own_source, frame_source, own_diagonal, frame_diagonal, *refs):
    count = 4 * (LEVELS - 1)
    body_state, frame_state, ring_state = refs[:count], refs[count : 2 * count], refs[2 * count : 2 * count + 4]
    out_ref, resid_ref = refs[2 * count + 4 : 2 * count + 6]
    ring_pe, body_final, frame_final, sems, e_ref, edge_ref, *inner = refs[2 * count + 6 :]
    outs, inner = inner[:2], inner[2:]
    body_pe, frame_pe = inner[: LEVELS - 1], inner[LEVELS - 1 :]
    rows = out_ref.shape[0] + 2 * TOP
    width = out_ref.shape[1] >> LEVELS
    e = coarse_solve(all_ref, dense_ref, from_cross, from_pair, e_ref, edge_ref, ring_state[3], out_ref.shape[0], width, (out_ref.shape[0] >> LEVELS) // 8)

    level = LEVELS - 1
    step, halo, height = 2**level, TOP >> level, rows >> level
    coarse_rows = (height - 2 * halo) // 2
    picked = e[TALL - 8 : TALL + coarse_rows + 8]
    lane = lane_of(picked)
    for t in range(3):
        group = (lane + t * LANES) // 2**LEVELS
        if t == 2:
            group = jnp.where(lane < LANES // 2, group, group - 3 * LANES // 2**LEVELS)
        taken = jnp.take_along_axis(picked, jnp.clip(group + width, 0, LANES - 1), axis=1)[7 : 7 + coarse_rows + 2]
        ring_pe[t, 0 : 2 * GUARD, :] = jnp.zeros((2 * GUARD, LANES), jnp.float32)
        ring_pe[t, height : height + 2 * GUARD, :] = jnp.zeros((2 * GUARD, LANES), jnp.float32)
        ring_pe[t, pl.ds(GUARD + halo - 2, coarse_rows + 2, stride=2), :] = taken
        ring_pe[t, pl.ds(GUARD + halo - 1, coarse_rows + 2, stride=2), :] = taken

    def climbed(pe, state, start, size, step, edge=None):
        mid, around = beside_of(pe, state[:2], start, size, step)
        scale, smooth = load(state[2], start, size), load(state[3], start, size)
        if edge is not None:
            smooth = load(edge, start, size)
        return [(smooth[t] + (1.0 - relaxation) * mid[t]) + scale[t] * around[t] for t in range(len(mid))]

    def climb_ring(start, size, level=level, step=step):
        ring = spread(climbed(ring_pe, ring_state, start, size, step, edge_ref), step // 2)
        lane = lane_of(ring[0])
        around = jnp.where(
            lane < LANES // 2,
            jnp.where(lane < HALO, roll(ring[2], HALO), roll(ring[0], HALO)),
            jnp.where(lane < LANES - HALO, roll(ring[1], -HALO), roll(ring[2], -HALO)),
        )
        store_twice(body_pe[level - 1], start, size, ring[:2])
        store_twice(frame_pe[level - 1], start, size, [around])

    for_chunks(height, climb_ring, height, height)

    for level in range(LEVELS - 2, -1, -1):
        step, height = 2**level, rows >> level
        groups = ((body_pe, body_state, body_final), (frame_pe, frame_state, frame_final))
        for pes, _, _ in groups:
            clear_guards(pes[level], height)

        def climb(start, size, level=level, step=step, groups=groups):
            for pes, states, final in groups:
                value = climbed(pes[level], states[4 * level : 4 * level + 4], start, size, step)
                if level == 0:
                    store(final, start, size, value)
                else:
                    store_twice(pes[level - 1], start, size, spread(value, step // 2))

        if level > 0:
            for_chunks(height, climb, 2 * CHUNK, PART)

    def last(base, size):
        body, around = beside_of(body_final, body_state[:2], base, size, 1)
        frame, frame_around = beside_of(frame_final, frame_state[:2], base, size, 1)
        b, d = load(own_source, base, size), load(own_diagonal, base, size)
        b_frame, d_frame = load(frame_source, base, size), load(frame_diagonal, base, size)
        body = (body, [(b[t] + around[t]) - d[t] * body[t] for t in range(2)])
        frame = (frame[0], (b_frame[0] + frame_around[0]) - d_frame[0] * frame[0])
        lane = lane_of(frame[0])
        span = pl.ds(base, size)
        for ref, middle, around in ((outs[0], body[0], frame[0]), (outs[1], body[1], frame[1])):
            ref[span, :LANES] = jnp.where(lane < NEAR, roll(around, -HALO), middle[0])
            ref[span, LANES:] = jnp.where(lane >= LANES - NEAR, roll(around, HALO), middle[1])

    count = rows // CHUNK
    ends = [0] + [CHUNK * (p + 1) - LAG - TOP for p in range(count - 1)] + [out_ref.shape[0]]

    spans = [*zip(ends[:-2], ends[1:-1])]
    middle = (ends[-2] + ends[-1]) // 16 * 8
    spans += [(ends[-2], middle), (middle, ends[-1])]
    sent = []
    for p in range(count):
        start, stop = max(p * CHUNK, TOP - 8), min((p + 1) * CHUNK, rows - TOP + 8)
        climb(start, stop - start)
        for first, end in spans[p : p + 1] if p < count - 1 else spans[p:]:
            last(TOP + first, end - first)
            for k, ref in enumerate((out_ref, resid_ref)):
                size = end - first
                source = outs[k].at[pl.ds(TOP + first, size)]
                copy = pltpu.make_async_copy(source, ref.at[pl.ds(first, size)], sems.at[len(sent)])
                copy.start()
                sent.append(copy)
    for copy in sent:
        copy.wait()


def call(kernel, out_shape, scratch, flops, moved, **more):
    return pl.pallas_call(
        kernel,
        out_shape=out_shape,
        scratch_shapes=scratch,
        compiler_params=pltpu.CompilerParams(vmem_limit_bytes=VMEM_LIMIT),
        cost_estimate=pl.CostEstimate(flops=flops, bytes_accessed=moved, transcendentals=0),
        **more,
    )


def swap(x, axis, first):
    pairs = [(i, i + 1) for i in range(first, lax.axis_size(axis) - 1, 2)]
    return lax.ppermute(x, axis, pairs + [(j, i) for i, j in pairs])


def local(rhs, pressure, wet_mask, bathy_class):
    rows, columns = rhs.shape
    cells = rows * columns
    total = rows + 2 * TOP
    levels = range(LEVELS - 1)

    def shape(tiles, level):
        return (tiles, (total >> level) + 2 * GUARD, LANES)

    def out(*dims):
        return jax.ShapeDtypeStruct(dims, jnp.float32)

    def vmem(tiles, level):
        return pltpu.VMEM(shape(tiles, level), jnp.float32)

    def fields(r, p, m, c):
        wet = m.astype(jnp.float32)
        return wet * r, wet * p, wet * (1.0 + 0.5 * c.astype(jnp.float32))

    given = (rhs, pressure, wet_mask, bathy_class)

    def edge(start):
        return jnp.stack(fields(*(lax.dynamic_slice_in_dim(x, start, TOP, axis=0) for x in given)))

    even = lax.axis_index("gx") % 2 == 0
    first_rows = swap(edge(jnp.where(even, 0, rows - TOP)), "gx", 1)
    second_rows = swap(edge(jnp.where(even, rows - TOP, 0)), "gx", 0)
    piece = -(-(rows + 2 * TOP + (rows >> LEVELS) // 2) // (8 * PIECES)) * 8
    own_shapes = [out(*shape(2, 0))] * 3
    laid_out = [*own_shapes, *[out(*shape(1, 0))] * 3, out(3, piece, LANES), out(3, piece, LANES)]
    inner = [vmem(2, level) for level in range(1, LEVELS)]
    begun = call(layout_kernel, laid_out, inner, 10 * cells, 10 * cells)(*fields(*given))
    *own, to_cross, to_pair = call(
        halo_kernel, laid_out, (), cells, cells, input_output_aliases={k: k for k in range(8)}
    )(*begun, first_rows, second_rows)
    own, frames = own[:3], own[3:]
    from_pair = swap(to_pair, "gy", 0)
    from_cross = swap(to_cross, "gy", 1)

    state_count = 4 * (LEVELS - 1)
    *body_state, body_weight, body_source, diagonal = call(
        body_kernel,
        [out(*shape(2, level)) for level in levels for _ in range(4)]
        + [out(*shape(2, LEVELS - 1))] * 2
        + [out(*shape(2, 0))],
        [vmem(2, 0)] * 3 + [vmem(2, level) for level in levels[1:]] * 3,
        100 * cells,
        40 * cells,
    )(*own)
    nx, ny = lax.axis_size("gx"), lax.axis_size("gy")
    ring = LEVELS - 1
    frame_source, _, _, *state, dense, chunks = call(
        frame_kernel,
        [out(*shape(1, 0))] * 3
        + [out(*shape(1, level)) for level in levels for _ in range(4)]
        + [out(*shape(1, 0))]
        + [out(*shape(3, ring))] * 4
        + [out(8, LANES), out(nx, ny, 4, LANES)],
        [vmem(1, 0)] * 2 + [vmem(3, ring)] * 5 + [vmem(1, level) for level in range(1, LEVELS)] * 3,
        50 * cells,
        20 * cells,
        input_output_aliases={k: k for k in range(3)},
    )(*frames, from_pair, from_cross, body_weight, body_source)
    frame_state, frame_diagonal, ring_state = state[:state_count], state[state_count], state[state_count + 1 :]
    gathered = lax.all_to_all(chunks.reshape(nx * ny, 4, LANES), ("gx", "gy"), 0, 0).reshape(chunks.shape)
    return call(
        up_kernel,
        (out(rows, columns), out(rows, columns)),
        [vmem(3, ring), vmem(2, 0), vmem(1, 0), pltpu.SemaphoreType.DMA((16,))]
        + [pltpu.VMEM((2, (rows >> LEVELS) + 2 * TALL + 2 * GUARD, LANES), jnp.float32), vmem(3, ring)]
        + [pltpu.VMEM((total, columns), jnp.float32)] * 2
        + [vmem(2, level) for level in levels]
        + [vmem(1, level) for level in levels],
        60 * cells,
        40 * cells,
        out_specs=[pl.BlockSpec(memory_space=pl.ANY)] * 2,
    )(gathered, dense, from_cross, from_pair, own[0], frame_source, diagonal, frame_diagonal, *body_state, *frame_state, *ring_state)


def solution(mesh):
    placed = (P("gx", "gy"), P("gx", "gy"), P("gx", "gy"), P("gx", "gy"))
    return jax.shard_map(
        local, mesh=mesh, in_specs=placed, out_specs=(P("gx", "gy"), P("gx", "gy")), check_vma=False
    )
```

```python
import jax
import jax.numpy as jnp
from jax import lax
from jax.experimental import pallas as pl
from jax.experimental.pallas import tpu as pltpu
from jax.sharding import PartitionSpec as P

LEVELS = 4
SWEEPS = 12

damping = 0.01
relaxation = 0.8

HALO = 16
NEAR = 20
LANES = 128
INNER = LANES // 2 - HALO
TOP = 16
GUARD = 8
PIECES = 8
CHUNK = 136
PART = CHUNK
LAG = 8
TALL = 16
VMEM_LIMIT = 40 * 1024 * 1024


def lane_of(x):
    return lax.broadcasted_iota(jnp.int32, x.shape, x.ndim - 1)


def roll(x, amount):
    amount %= LANES
    return x if amount == 0 else pltpu.roll(x, amount, x.ndim - 1)


def from_west(tiles, step):
    moved = [roll(t, step) for t in tiles]
    if len(tiles) == 1:
        return moved
    edge = lane_of(tiles[0]) < step
    return [jnp.where(edge, moved[i - 1], moved[i]) for i in range(len(tiles))]


def from_east(tiles, step):
    moved = [roll(t, -step) for t in tiles]
    count = len(tiles)
    if count == 1:
        return moved
    edge = lane_of(tiles[0]) >= LANES - step
    return [jnp.where(edge, moved[(i + 1) % count], moved[i]) for i in range(count)]


def spread(tiles, step):
    second = (lane_of(tiles[0]) // step) % 2 == 1
    return [jnp.where(second, roll(t, step), t) for t in tiles]


def for_parts(start, size, body, part):
    for offset in range(0, size, part):
        body(start + offset, min(part, size - offset))


def for_chunks(rows, body, largest, part):
    sizes = [size for size in range(8, largest + 1, 8) if rows % size == 0]
    if rows <= largest or not sizes:
        for_parts(0, rows, body, part)
        return

    def step(i, carry):
        for_parts(i * sizes[-1], sizes[-1], body, part)
        return carry

    lax.fori_loop(0, rows // sizes[-1], step, 0)


def load(ref, start, size):
    return [ref[t, pl.ds(GUARD + start, size), :] for t in range(ref.shape[0])]


def store(ref, start, size, tiles):
    for t, tile in enumerate(tiles):
        ref[t, pl.ds(GUARD + start, size), :] = tile


def store_twice(ref, start, size, tiles):
    for t, tile in enumerate(tiles):
        ref[t, pl.ds(GUARD + 2 * start, size, stride=2), :] = tile
        ref[t, pl.ds(GUARD + 2 * start + 1, size, stride=2), :] = tile


def clear_guards(ref, rows):
    zeros = jnp.zeros((GUARD, LANES), jnp.float32)
    for t in range(ref.shape[0]):
        ref[t, 0:GUARD, :] = zeros
        ref[t, GUARD + rows : 2 * GUARD + rows, :] = zeros


def beside(mid, north, south, c_west, c_north, c_south, step):
    west = from_west(mid, step)
    east = from_east([c * m for c, m in zip(c_west, mid)], step)
    return [
        (c_west[t] * west[t] + east[t]) + (c_north[t] * north[t] + c_south[t] * south[t]) for t in range(len(mid))
    ]


def beside_of(ref, coeffs, start, size, step):
    c_west_ref, c_north_ref = coeffs
    mid = load(ref, start, size)
    north, south = load(ref, start - 1, size), load(ref, start + 1, size)
    c_west, c_north = load(c_west_ref, start, size), load(c_north_ref, start, size)
    return mid, beside(mid, north, south, c_west, c_north, load(c_north_ref, start + 1, size), step)


def pool_rows(ref, start, size, step):
    out = []
    for t in range(ref.shape[0]):
        even = ref[t, pl.ds(GUARD + start, size // 2, stride=2), :]
        odd = ref[t, pl.ds(GUARD + start + 1, size // 2, stride=2), :]
        both = even + odd
        out.append(both + roll(both, -step))
    return out


def descend(level, height, weight, source, guess, state, diagonal_ref, field, resid, next_weight, next_source, largest, part):
    step = 2**level
    c_west_ref, c_north_ref, scale_ref, smooth_ref = state
    for ref in (weight, field, c_north_ref):
        clear_guards(ref, height)

    def first_pass(start, size):
        w, w_north, w_south = (load(weight, start + k, size) for k in (0, -1, 1))
        c_north = [jnp.minimum(a, b) for a, b in zip(w, w_north)]
        c_south = [jnp.minimum(a, b) for a, b in zip(w, w_south)]
        c_west = [jnp.minimum(a, b) for a, b in zip(w, from_west(w, step))]
        c_east = from_east(c_west, step)
        diagonal = [damping + c_north[t] + c_south[t] + c_west[t] + c_east[t] for t in range(len(w))]
        scale = [relaxation / d for d in diagonal]
        store(c_north_ref, start, size, c_north)
        store(c_west_ref, start, size, c_west)
        store(scale_ref, start, size, scale)
        store(diagonal_ref, start, size, diagonal)
        value = load(source, start, size)
        if guess is None:
            value = [scale[t] * value[t] for t in range(len(w))]
        else:
            mid, north, south = (load(guess, start + k, size) for k in (0, -1, 1))
            around = beside(mid, north, south, c_west, c_north, c_south, step)
            value = [
                (1.0 - relaxation) * mid[t] + scale[t] * (value[t] + around[t]) for t in range(len(w))
            ]
        store(field, start, size, value)
        if next_weight is not None:
            pooled = [0.125 * p for p in pool_rows(weight, start, size, step)]
            store(next_weight, start // 2, size // 2, pooled)

    def second_pass(start, size):
        mid, around = beside_of(field, (c_west_ref, c_north_ref), start, size, step)
        b, scale, diagonal = (load(ref, start, size) for ref in (source, scale_ref, diagonal_ref))
        rest = [(b[t] + around[t]) - diagonal[t] * mid[t] for t in range(len(b))]
        store(smooth_ref, start, size, [mid[t] + scale[t] * rest[t] for t in range(len(b))])
        store(resid, start, size, rest)
        if next_source is not None:
            pooled = [0.25 * p for p in pool_rows(resid, start, size, step)]
            store(next_source, start // 2, size // 2, pooled)

    for_chunks(height, first_pass, largest, part)
    for_chunks(height, second_pass, largest, part)


def descend_all(rows, sources, guess, weights, states, diagonal, field, resid, largest, part):
    for level in range(LEVELS - 1):
        descend(
            level,
            rows >> level,
            weights[level],
            sources[level],
            guess if level == 0 else None,
            states[4 * level : 4 * level + 4],
            diagonal[level],
            field,
            resid,
            weights[level + 1],
            sources[level + 1],
            largest,
            part,
        )


def group_of(x, west):
    return (lane_of(x) // HALO + (1 if west else 0)) % PIECES


def packed(part, p, west):
    return roll(part, p * HALO - HALO if west else p * HALO + HALO)


def to_sides(west, east, cross_ref, pair_ref, k, rows):
    even = lax.axis_index("gy") % 2 == 0
    cross_ref[k, rows, :] = jnp.where(even, west, east)
    pair_ref[k, rows, :] = jnp.where(even, east, west)


def inner_columns(tiles):
    return jnp.where(lane_of(tiles[0]) < LANES // 2, roll(tiles[0], HALO), roll(tiles[1], -HALO))


def layout_kernel(source, guess, weight, *refs):
    owns, frames, (cross_ref, pair_ref, *inner) = refs[:3], refs[3:6], refs[6:]
    rows = source.shape[0]
    piece = cross_ref.shape[1]
    whole = rows // piece
    tail = rows - whole * piece
    for own, frame, block in zip(owns, frames, (source, guess, weight)):
        clear_guards(own, rows + 2 * TOP)
        clear_guards(frame, rows + 2 * TOP)
        tiles = [block[:, t * LANES : (t + 1) * LANES] for t in range(2)]
        for t in range(2):
            own[t, GUARD + TOP : GUARD + TOP + rows, :] = tiles[t]
        frame[0, GUARD + TOP : GUARD + TOP + rows, :] = inner_columns(tiles)
    weights, start, height = (owns[2], *inner), TOP, rows
    for level in range(LEVELS):
        pooled = [0.125 * w for w in pool_rows(weights[level], start, height, 2**level)]
        start, height = start // 2, height // 2
        if level < LEVELS - 1:
            store(weights[level + 1], start, height, pooled)
    lane = lane_of(pooled[0])
    width = HALO // 2
    index = (lane % width) * 2**LEVELS
    coarse = [jnp.take_along_axis(p, index, axis=1) for p in pooled]
    coarse = jnp.where(lane % HALO < width, *coarse)
    for k, block in enumerate((source, guess, weight)):
        sides = []
        for west in (True, False):
            columns = slice(0, LANES) if west else slice(LANES, 2 * LANES)
            below = jnp.zeros((piece - tail, LANES), jnp.float32)
            if k < 2:
                half = coarse[k * height // 2 : (k + 1) * height // 2]
                below = jnp.concatenate((below[: 2 * TOP], half, below[2 * TOP + height // 2 :]), axis=0)
            last = packed(block[whole * piece :, columns], whole, west)
            both = jnp.concatenate((last, below), axis=0)
            for p in range(whole):
                part = packed(block[p * piece : (p + 1) * piece, columns], p, west)
                both = jnp.where(group_of(part, west) == p, part, both)
            sides.append(both)
        to_sides(*sides, cross_ref, pair_ref, k, slice(0, piece))


def halo_kernel(*refs):
    first_rows, second_rows, *own, cross_ref, pair_ref = refs[8:]
    own, frames = own[:3], own[3:]
    total = own[0].shape[1] - 2 * GUARD
    last = PIECES - 1
    first = total - 2 * TOP - last * cross_ref.shape[1]
    even, even_y = lax.axis_index("gx") % 2 == 0, lax.axis_index("gy") % 2 == 0
    for k in range(3):
        above = jnp.where(even, first_rows[k], second_rows[k])
        below = jnp.where(even, second_rows[k], first_rows[k])
        for side, (rows, row) in enumerate(((above, 0), (below, total - TOP))):
            body = [rows[:, t * LANES : (t + 1) * LANES] for t in range(2)]
            for t in range(2):
                own[k][t, GUARD + row : GUARD + row + TOP, :] = body[t]
            frames[k][0, GUARD + row : GUARD + row + TOP, :] = inner_columns(body)
            span = slice(first + side * TOP, first + (side + 1) * TOP)
            parts = []
            for part, west in zip(body, (True, False)):
                here = group_of(part, west) == last
                parts.append((here, packed(part, last, west)))
            (here_west, west), (here_east, east) = parts
            cross, pair = cross_ref[k, span, :], pair_ref[k, span, :]
            cross_ref[k, span, :] = jnp.where(
                even_y, jnp.where(here_west, west, cross), jnp.where(here_east, east, cross)
            )
            pair_ref[k, span, :] = jnp.where(
                even_y, jnp.where(here_east, east, pair), jnp.where(here_west, west, pair)
            )


def body_kernel(source, guess, weight, *refs):
    states = refs[: 4 * (LEVELS - 1)]
    last_weight, last_source, first_diagonal, *refs = refs[4 * (LEVELS - 1) :]
    field, resid, weight_in, *inner = refs
    rows = source.shape[1] - 2 * GUARD
    depth = LEVELS - 2
    weights = (weight_in, *inner[:depth], last_weight)
    sources = (source, *inner[depth : 2 * depth], last_source)
    diagonal = (first_diagonal, *inner[2 * depth :])
    weights[0][...] = weight[...]
    descend_all(rows, sources, guess, weights, states, diagonal, field, resid, 2 * CHUNK, CHUNK)


def frame_kernel(_a, _b, _c, from_pair, from_cross, body_weight, body_source, *refs):
    even = lax.axis_index("gy") % 2 == 0
    frames, states, refs = refs[:3], refs[3 : 3 + 4 * (LEVELS - 1)], refs[3 + 4 * (LEVELS - 1) :]
    frame_source, frame_guess, frame_weight = frames
    first_diagonal, ring_state, dense_ref, chunks_ref, field, resid, *refs = refs[0], refs[1:5], *refs[5:]
    ring_weight, ring_source, ring_field, ring_resid, ring_diagonal, *inner = refs
    rows = frame_source.shape[1] - 2 * GUARD
    depth = LEVELS - 1
    weights = (frame_weight, *inner[:depth])
    sources = (frame_source, *inner[depth : 2 * depth])
    diagonals = (first_diagonal, *inner[2 * depth :])
    piece = from_cross.shape[1]
    for k, frame in enumerate(frames):
        block = rows - 2 * TOP
        last = PIECES - 1
        tail = block - last * piece
        spans = [(p, 0, TOP + p * piece, piece) for p in range(last)]
        spans += [(last, 0, TOP + last * piece, tail)]
        spans += [(last, tail, 0, TOP), (last, tail + TOP, rows - TOP, TOP)]
        for p, first, start, size in spans:
            span = slice(GUARD + start, GUARD + start + size)
            cross, pair = from_cross[k, first : first + size, :], from_pair[k, first : first + size, :]
            from_left = group_of(cross, False) == p
            both = roll(jnp.where(from_left == even, cross, pair), -p * HALO)
            lane = lane_of(both)
            outside = (lane < HALO) | (lane >= LANES - HALO)
            frame[0, span, :] = jnp.where(outside, both, frame[0, span, :])
    descend_all(rows, sources, frame_guess, weights, states, diagonals, field, resid, 4 * CHUNK, 4 * CHUNK)

    level = LEVELS - 1
    step, halo, height = 2**level, TOP >> level, rows >> level
    for body, frame, ring in (
        (body_weight, weights[level], ring_weight),
        (body_source, sources[level], ring_source),
    ):
        middle = load(body, 0, height)
        around = load(frame, 0, height)[0]
        lane = lane_of(around)
        ahead, back = roll(around, HALO), roll(around, -HALO)
        store(
            ring,
            0,
            height,
            [
                jnp.where(lane < 2 * step, back, middle[0]),
                jnp.where(lane >= LANES - 2 * step, ahead, middle[1]),
                jnp.where(lane < LANES // 2, ahead, back),
            ],
        )
    descend(
        level,
        height,
        ring_weight,
        ring_source,
        None,
        ring_state,
        ring_diagonal,
        ring_field,
        ring_resid,
        None,
        None,
        height,
        height,
    )

    coarse_rows = (height - 2 * halo) // 2
    dense = jnp.zeros((8, LANES), jnp.float32)
    lane = lane_of(dense)
    per_tile = LANES // 2**LEVELS
    pooled_b = pool_rows(ring_resid, halo, 2 * coarse_rows, step)
    pooled_w = pool_rows(ring_weight, halo, 2 * coarse_rows, step)
    index = (lane % per_tile) * 2**LEVELS
    place = lane // per_tile
    for g in range(coarse_rows // 8):
        for group, (values, factor) in enumerate(((pooled_b, 0.25), (pooled_w, 0.125))):
            for t in range(2):
                taken = jnp.take_along_axis(factor * values[t][8 * g : 8 * g + 8], index, axis=1)
                dense = jnp.where(place == 4 * g + 2 * group + t, taken, dense)
    dense_ref[...] = dense

    width = 2 * per_tile
    index = jnp.minimum(2 * (lane - lane % width) + lane % width, LANES - 1)
    smooth = ring_state[3]
    beside_me = []
    for tile, edge, free in ((0, 0, width - 2), (1, LANES - step, 0)):
        chunk = jnp.take_along_axis(dense, index, axis=1)
        first = GUARD + halo
        pieces = []
        for g in range(coarse_rows // 8):
            for odd in range(2):
                rows_of = smooth[tile, pl.ds(first + 16 * g + odd, 8, stride=2), :]
                pieces.append((g * width + free + odd, rows_of))
        for place, values in pieces:
            chunk = jnp.where(lane == place, roll(values, place - edge), chunk)
        beside_me.append(fold(chunk))
    sublane = lax.broadcasted_iota(jnp.int32, dense.shape, 0)
    beyond = []
    for row, group, free in ((0, 1, 6), (2 * coarse_rows - 1, 2, 0)):
        chunk = dense
        for tile in range(2):
            values = jnp.broadcast_to(smooth[tile, GUARD + halo + row : GUARD + halo + row + 1, :], dense.shape)
            values = jnp.take_along_axis(values, (lane % width) * step, axis=1)
            here = (sublane == free + tile) & (lane // width == 2 * group)
            chunk = jnp.where(here, values, chunk)
        beyond.append(chunk)
    above, below = fold(beyond[0]), fold(roll(beyond[1], -LANES // 2))
    x, y = lax.axis_index("gx"), lax.axis_index("gy")
    for i in range(chunks_ref.shape[0]):
        for j in range(chunks_ref.shape[1]):
            level_with = jnp.where(j < y, beside_me[0], beside_me[1])
            chunks_ref[i, j] = jnp.where(i == x, level_with, jnp.where(i < x, above, below))


def fold(x):
    return jnp.where(lane_of(x) < LANES // 2, x, pltpu.roll(roll(x, LANES // 2), 4, 0))[:4]


def unfold(x):
    return jnp.concatenate((x, roll(x, LANES // 2)), axis=0)


def coarse_solve(all_ref, dense_ref, from_cross, from_pair, e_ref, edge_ref, smooth_ref, rows, width, groups):
    x, nx = lax.axis_index("gx"), lax.axis_size("gx")
    y, ny = lax.axis_index("gy"), lax.axis_size("gy")
    tiles = {}
    for dx in (-1, 0, 1):
        for dy in (-1, 0, 1):
            if dx or dy:
                inside = (x + dx >= 0) & (x + dx < nx) & (y + dy >= 0) & (y + dy < ny)
                tile = unfold(all_ref[jnp.where(inside, x + dx, 0), jnp.where(inside, y + dy, 0)])
                tiles[dx, dy] = jnp.where(inside, tile, 0.0)
    dense = dense_ref[...]
    lane = lane_of(dense)
    even = y % 2 == 0
    half = 4 * groups
    first = rows % from_cross.shape[1] + 2 * TOP
    cross, pair = ([ref[k, first : first + half, :] for k in range(2)] for ref in (from_cross, from_pair))
    cross, pair = jnp.concatenate(cross, axis=0), jnp.concatenate(pair, axis=0)
    weights = {-1: jnp.where(even, cross, pair), 1: jnp.where(even, pair, cross)}
    bands = [(-1, g) for g in range(TALL // 8)] + [(0, g) for g in range(groups)] + [(1, g) for g in range(TALL // 8)]
    b, w = [], []
    for dx, g in bands:
        b_rows = w_rows = jnp.zeros_like(dense)
        for dy in (-1, 0, 1):
            first_lane = (dy + 1) * width
            here = (lane >= first_lane) & (lane < first_lane + width)
            if dx or not dy:
                tile = tiles[dx, dy] if dx else dense
                b_part = roll(tile, first_lane - 2 * g * width)
                w_part = roll(tile, first_lane - (2 * g + 1) * width)
            else:
                b_part = roll(tiles[dx, dy], first_lane - g * width)
                at = (PIECES - 1 - (dy > 0)) * HALO
                w_part = roll(weights[dy][8 * g : 8 * g + 8], first_lane - at)
            b_rows = jnp.where(here, b_part, b_rows)
            w_rows = jnp.where(here, w_part, w_rows)
        b.append(b_rows)
        w.append(w_rows)
    b, w = jnp.concatenate(b, axis=0), jnp.concatenate(w, axis=0)

    step = 2 ** (LEVELS - 1)
    start = GUARD + (TOP >> (LEVELS - 1))
    for t in range(2):
        edge_ref[t] = smooth_ref[t]
    edge_ref[2] = jnp.zeros_like(edge_ref[2])

    def columns(place):
        left = roll(tiles[0, -1], LANES - step - place)
        right = roll(tiles[0, 1], -(place + width - 2))
        return jnp.where(lane < step, right, left)

    for g in range(groups):
        for odd in range(2):
            edge_ref[2, pl.ds(start + 16 * g + odd, 8, stride=2), :] = columns(g * width + odd)
    for dx, row, lanes, free in ((-1, start - 1, 0, 0), (1, start + 16 * groups, 2 * width, 6)):
        for t in range(2):
            values = tiles[dx, 0][free + t : free + t + 1]
            values = jnp.take_along_axis(
                jnp.broadcast_to(values, dense.shape), lanes + lane // step, axis=1
            )
            edge_ref[t, row : row + 1, :] = values[:1]
        left = roll(tiles[dx, -1][free + 1 : free + 2], LANES - step - (lanes + width - 1))
        right = roll(tiles[dx, 1][free : free + 1], -lanes)
        edge_ref[2, row : row + 1, :] = jnp.where(lane[:1] < step, right, left)

    tall = b.shape[0]
    zeros = jnp.zeros((GUARD, LANES), jnp.float32)
    for k in range(2):
        e_ref[k, 0:GUARD, :] = zeros
        e_ref[k, GUARD + tall :, :] = zeros

    def shifted(k, by):
        return e_ref[k, GUARD + by : GUARD + by + tall, :]

    e_ref[1, GUARD : GUARD + tall, :] = w
    c_west = jnp.minimum(w, roll(w, 1))
    c_north, c_south = jnp.minimum(w, shifted(1, -1)), jnp.minimum(w, shifted(1, 1))
    c_east = roll(c_west, -1)
    scale = relaxation / (damping + c_north + c_south + c_west + c_east)
    first = scale * b
    c_west, c_east, c_north, c_south = (scale * c for c in (c_west, c_east, c_north, c_south))
    e_ref[0, GUARD : GUARD + tall, :] = first
    for sweep in range(SWEEPS - 1):
        k = sweep % 2
        e = shifted(k, 0)
        around = (c_west * roll(e, 1) + c_east * roll(e, -1)) + (c_north * shifted(k, -1) + c_south * shifted(k, 1))
        e_ref[1 - k, GUARD : GUARD + tall, :] = ((1.0 - relaxation) * e + first) + around
    return shifted((SWEEPS - 1) % 2, 0)


def up_kernel(all_ref, dense_ref, from_cross, from_pair, own_source, frame_source, own_diagonal, frame_diagonal, *refs):
    count = 4 * (LEVELS - 1)
    body_state, frame_state, ring_state = refs[:count], refs[count : 2 * count], refs[2 * count : 2 * count + 4]
    out_ref, resid_ref = refs[2 * count + 4 : 2 * count + 6]
    ring_pe, body_final, frame_final, sems, e_ref, edge_ref, *inner = refs[2 * count + 6 :]
    outs, inner = inner[:2], inner[2:]
    body_pe, frame_pe = inner[: LEVELS - 1], inner[LEVELS - 1 :]
    rows = out_ref.shape[0] + 2 * TOP
    width = out_ref.shape[1] >> LEVELS
    e = coarse_solve(all_ref, dense_ref, from_cross, from_pair, e_ref, edge_ref, ring_state[3], out_ref.shape[0], width, (out_ref.shape[0] >> LEVELS) // 8)

    level = LEVELS - 1
    step, halo, height = 2**level, TOP >> level, rows >> level
    coarse_rows = (height - 2 * halo) // 2
    picked = e[TALL - 8 : TALL + coarse_rows + 8]
    lane = lane_of(picked)
    for t in range(3):
        group = (lane + t * LANES) // 2**LEVELS
        if t == 2:
            group = jnp.where(lane < LANES // 2, group, group - 3 * LANES // 2**LEVELS)
        taken = jnp.take_along_axis(picked, jnp.clip(group + width, 0, LANES - 1), axis=1)[7 : 7 + coarse_rows + 2]
        ring_pe[t, 0 : 2 * GUARD, :] = jnp.zeros((2 * GUARD, LANES), jnp.float32)
        ring_pe[t, height : height + 2 * GUARD, :] = jnp.zeros((2 * GUARD, LANES), jnp.float32)
        ring_pe[t, pl.ds(GUARD + halo - 2, coarse_rows + 2, stride=2), :] = taken
        ring_pe[t, pl.ds(GUARD + halo - 1, coarse_rows + 2, stride=2), :] = taken

    def climbed(pe, state, start, size, step, edge=None):
        mid, around = beside_of(pe, state[:2], start, size, step)
        scale, smooth = load(state[2], start, size), load(state[3], start, size)
        if edge is not None:
            smooth = load(edge, start, size)
        return [(smooth[t] + (1.0 - relaxation) * mid[t]) + scale[t] * around[t] for t in range(len(mid))]

    def climb_ring(start, size, level=level, step=step):
        ring = spread(climbed(ring_pe, ring_state, start, size, step, edge_ref), step // 2)
        lane = lane_of(ring[0])
        around = jnp.where(
            lane < LANES // 2,
            jnp.where(lane < HALO, roll(ring[2], HALO), roll(ring[0], HALO)),
            jnp.where(lane < LANES - HALO, roll(ring[1], -HALO), roll(ring[2], -HALO)),
        )
        store_twice(body_pe[level - 1], start, size, ring[:2])
        store_twice(frame_pe[level - 1], start, size, [around])

    for_chunks(height, climb_ring, height, height)

    for level in range(LEVELS - 2, -1, -1):
        step, height = 2**level, rows >> level
        groups = ((body_pe, body_state, body_final), (frame_pe, frame_state, frame_final))
        for pes, _, _ in groups:
            clear_guards(pes[level], height)

        def climb(start, size, level=level, step=step, groups=groups):
            for pes, states, final in groups:
                value = climbed(pes[level], states[4 * level : 4 * level + 4], start, size, step)
                if level == 0:
                    store(final, start, size, value)
                else:
                    store_twice(pes[level - 1], start, size, spread(value, step // 2))

        if level > 0:
            for_chunks(height, climb, 2 * CHUNK, PART)

    def last(base, size):
        body, around = beside_of(body_final, body_state[:2], base, size, 1)
        frame, frame_around = beside_of(frame_final, frame_state[:2], base, size, 1)
        b, d = load(own_source, base, size), load(own_diagonal, base, size)
        b_frame, d_frame = load(frame_source, base, size), load(frame_diagonal, base, size)
        body = (body, [(b[t] + around[t]) - d[t] * body[t] for t in range(2)])
        frame = (frame[0], (b_frame[0] + frame_around[0]) - d_frame[0] * frame[0])
        lane = lane_of(frame[0])
        span = pl.ds(base, size)
        for ref, middle, around in ((outs[0], body[0], frame[0]), (outs[1], body[1], frame[1])):
            ref[span, :LANES] = jnp.where(lane < NEAR, roll(around, -HALO), middle[0])
            ref[span, LANES:] = jnp.where(lane >= LANES - NEAR, roll(around, HALO), middle[1])

    count = rows // CHUNK
    ends = [0] + [CHUNK * (p + 1) - LAG - TOP for p in range(count - 1)] + [out_ref.shape[0]]

    spans = [*zip(ends[:-2], ends[1:-1])]
    middle = (ends[-2] + ends[-1]) // 16 * 8
    spans += [(ends[-2], middle), (middle, ends[-1])]
    sent = []
    for p in range(count):
        start, stop = max(p * CHUNK, TOP - 8), min((p + 1) * CHUNK, rows - TOP + 8)
        climb(start, stop - start)
        for first, end in spans[p : p + 1] if p < count - 1 else spans[p:]:
            last(TOP + first, end - first)
            for k, ref in enumerate((out_ref, resid_ref)):
                size = end - first
                source = outs[k].at[pl.ds(TOP + first, size)]
                copy = pltpu.make_async_copy(source, ref.at[pl.ds(first, size)], sems.at[len(sent)])
                copy.start()
                sent.append(copy)
    for copy in sent:
        copy.wait()


def call(kernel, out_shape, scratch, flops, moved, **more):
    return pl.pallas_call(
        kernel,
        out_shape=out_shape,
        scratch_shapes=scratch,
        compiler_params=pltpu.CompilerParams(vmem_limit_bytes=VMEM_LIMIT),
        cost_estimate=pl.CostEstimate(flops=flops, bytes_accessed=moved, transcendentals=0),
        **more,
    )


def swap(x, axis, first):
    pairs = [(i, i + 1) for i in range(first, lax.axis_size(axis) - 1, 2)]
    return lax.ppermute(x, axis, pairs + [(j, i) for i, j in pairs])


def local(rhs, pressure, wet_mask, bathy_class):
    rows, columns = rhs.shape
    cells = rows * columns
    total = rows + 2 * TOP
    levels = range(LEVELS - 1)

    def shape(tiles, level):
        return (tiles, (total >> level) + 2 * GUARD, LANES)

    def out(*dims):
        return jax.ShapeDtypeStruct(dims, jnp.float32)

    def vmem(tiles, level):
        return pltpu.VMEM(shape(tiles, level), jnp.float32)

    def fields(r, p, m, c):
        wet = m.astype(jnp.float32)
        return wet * r, wet * p, wet * (1.0 + 0.5 * c.astype(jnp.float32))

    given = (rhs, pressure, wet_mask, bathy_class)

    def edge(start):
        return jnp.stack(fields(*(lax.dynamic_slice_in_dim(x, start, TOP, axis=0) for x in given)))

    even = lax.axis_index("gx") % 2 == 0
    first_rows = swap(edge(jnp.where(even, 0, rows - TOP)), "gx", 1)
    second_rows = swap(edge(jnp.where(even, rows - TOP, 0)), "gx", 0)
    piece = -(-(rows + 2 * TOP + (rows >> LEVELS) // 2) // (8 * PIECES)) * 8
    own_shapes = [out(*shape(2, 0))] * 3
    laid_out = [*own_shapes, *[out(*shape(1, 0))] * 3, out(3, piece, LANES), out(3, piece, LANES)]
    inner = [vmem(2, level) for level in range(1, LEVELS)]
    begun = call(layout_kernel, laid_out, inner, 10 * cells, 10 * cells)(*fields(*given))
    *own, to_cross, to_pair = call(
        halo_kernel, laid_out, (), cells, cells, input_output_aliases={k: k for k in range(8)}
    )(*begun, first_rows, second_rows)
    own, frames = own[:3], own[3:]
    from_pair = swap(to_pair, "gy", 0)
    from_cross = swap(to_cross, "gy", 1)

    state_count = 4 * (LEVELS - 1)
    *body_state, body_weight, body_source, diagonal = call(
        body_kernel,
        [out(*shape(2, level)) for level in levels for _ in range(4)]
        + [out(*shape(2, LEVELS - 1))] * 2
        + [out(*shape(2, 0))],
        [vmem(2, 0)] * 3 + [vmem(2, level) for level in levels[1:]] * 3,
        100 * cells,
        40 * cells,
    )(*own)
    nx, ny = lax.axis_size("gx"), lax.axis_size("gy")
    ring = LEVELS - 1
    frame_source, _, _, *state, dense, chunks = call(
        frame_kernel,
        [out(*shape(1, 0))] * 3
        + [out(*shape(1, level)) for level in levels for _ in range(4)]
        + [out(*shape(1, 0))]
        + [out(*shape(3, ring))] * 4
        + [out(8, LANES), out(nx, ny, 4, LANES)],
        [vmem(1, 0)] * 2 + [vmem(3, ring)] * 5 + [vmem(1, level) for level in range(1, LEVELS)] * 3,
        50 * cells,
        20 * cells,
        input_output_aliases={k: k for k in range(3)},
    )(*frames, from_pair, from_cross, body_weight, body_source)
    frame_state, frame_diagonal, ring_state = state[:state_count], state[state_count], state[state_count + 1 :]
    gathered = lax.all_to_all(chunks.reshape(nx * ny, 4, LANES), ("gx", "gy"), 0, 0).reshape(chunks.shape)
    return call(
        up_kernel,
        (out(rows, columns), out(rows, columns)),
        [vmem(3, ring), vmem(2, 0), vmem(1, 0), pltpu.SemaphoreType.DMA((16,))]
        + [pltpu.VMEM((2, (rows >> LEVELS) + 2 * TALL + 2 * GUARD, LANES), jnp.float32), vmem(3, ring)]
        + [pltpu.VMEM((total, columns), jnp.float32)] * 2
        + [vmem(2, level) for level in levels]
        + [vmem(1, level) for level in levels],
        60 * cells,
        40 * cells,
        out_specs=[pl.BlockSpec(memory_space=pl.ANY)] * 2,
    )(gathered, dense, from_cross, from_pair, own[0], frame_source, diagonal, frame_diagonal, *body_state, *frame_state, *ring_state)


def solution(mesh):
    placed = (P("gx", "gy"), P("gx", "gy"), P("gx", "gy"), P("gx", "gy"))
    return jax.shard_map(
        local, mesh=mesh, in_specs=placed, out_specs=(P("gx", "gy"), P("gx", "gy")), check_vma=False
    )
```
